32 devices in a mesh: dp: 16 (over z, x, core), tensor: 2 (over y).
Axes of the slice: x: 2, y: 2, z: 4, core: 2. Of those that a mesh axis runs over, the one named last changes fastest.
Arguments:
- hidden: bfloat16 [16, 1024, 1024], P('dp', 'tensor'), may hold values from -6 to 6
- pre_gain: float32 [1024], replicated, may hold values from 0.5 to 1.5
- zx_weight: bfloat16 [1024, 4096], P('dp', 'tensor'), may hold values from -0.1875 to 0.1875
- bc_weight: bfloat16 [1024, 256], P('dp'), may hold values from -0.1875 to 0.1875
- step_weight: bfloat16 [1024, 32], P('dp', 'tensor'), may hold values from -0.1875 to 0.1875
- conv_x_weight: float32 [4, 2048], P(None, 'tensor'), may hold values from -2 to 2
- conv_x_bias: float32 [2048], P('tensor'), may hold values from -2 to 2
- conv_bc_weight: float32 [4, 256], replicated, may hold values from -2 to 2
- conv_bc_bias: float32 [256], replicated, may hold values from -2 to 2
- step_bias: float32 [32], P('tensor'), may hold values from -6 to -2
- decay_log: float32 [32], P('tensor'), may hold values from 0 to 2.77
- skip_gain: float32 [32], P('tensor'), may hold values from 0.5 to 1.5
- norm_gain: float32 [2048], P('tensor'), may hold values from 0.5 to 1.5
- out_weight: bfloat16 [2048, 1024], P('tensor', 'dp'), may hold values from -0.125 to 0.125
- segment_ids: int32 [16, 1024], P('dp'), may hold values from 0 to 3, never falling along the last dimension, each value on 1 to 512 neighbouring positions
- pad_mask: int32 [16, 1024], P('dp'), may hold values 0 or 1
- grad_out: bfloat16 [16, 1024, 1024], P('dp', 'tensor'), may hold values from -6 to 6
Outputs:
- output: bfloat16 [16, 1024, 1024], P('dp', 'tensor')
- grad_hidden: bfloat16 [16, 1024, 1024], P('dp', 'tensor')
- grad_pre_gain: float32 [1024], replicated
- grad_zx_weight: float32 [1024, 4096], P('dp', 'tensor')
- grad_bc_weight: float32 [1024, 256], P('dp')
- grad_step_weight: float32 [1024, 32], P('dp', 'tensor')
- grad_conv_x_weight: float32 [4, 2048], P(None, 'tensor')
- grad_conv_x_bias: float32 [2048], P('tensor')
- grad_conv_bc_weight: float32 [4, 256], replicated
- grad_conv_bc_bias: float32 [256], replicated
- grad_step_bias: float32 [32], P('tensor')
- grad_decay_log: float32 [32], P('tensor')
- grad_skip_gain: float32 [32], P('tensor')
- grad_norm_gain: float32 [2048], P('tensor')
- grad_out_weight: float32 [2048, 1024], P('tensor', 'dp')
The draws below stay inside these ranges and needn't reach their ends.
Inputs may be any that keep to these rules, and one draw needn't show every extreme that they name: `segment_ids`: along each sequence the ids never fall; a document, a run of equal ids, holds 1 to 512 tokens.
All inputs are finite; a program needn't handle non-finite values. No bound on the sum of `pad_mask` on one device may be relied on, other than what follows from the above.
Results may differ from the reference program's by a relative error of at most 0.012.
The reference program's roundings to bfloat16 on the way count: a program that leaves them out, or rounds other values in their place, can miss the bound.
Values may be sent and summed in bfloat16 or wider, within the bound.
A program may use at most 192 MiB of HBM per device.

```python
import math
import jax
import jax.numpy as jnp
import numpy as np
from jax import lax

D = 1024
HEADS = 32
HEADDIM = 64
STATE = 128
KCONV = 4
SPAN = 256
SEQ_LEN = 1024
INNER = 2048
SEQS = 16


def touch_ends(values, key, least, largest):
    longest = values.shape.index(max(values.shape))
    spots = []
    for shift in (0, 1):
        where = [jax.random.randint(jax.random.fold_in(key, axis), (), 0, length) for axis, length in enumerate(values.shape)]
        where[longest] = (where[longest] + shift) % values.shape[longest]
        spots.append(tuple(where))
    return values.at[spots[0]].set(least).at[spots[1]].set(largest)


def block_scale(stream_key, dims, shards, low, largest):
    def one(dim, blocks):
        heights = jax.random.uniform(jax.random.fold_in(jax.random.fold_in(stream_key, 6), dim), (blocks,), jnp.float32, low / len(shards), largest / len(shards))
        return jnp.repeat(jnp.exp(heights), dims[dim] // blocks).reshape((-1,) + (1,) * (len(dims) - dim - 1))

    gain = one(*shards[0])
    for cut in shards[1:]:
        gain = gain * one(*cut)
    return gain


def split_up(count, total, bound, lean):
    portions = [(1 << 20) // math.isqrt(grade ** lean) + 1 for grade in range(2, count + 1)]
    spare, holding = total - bound - (count - 1), [1] * (count - 1)
    while spare > 0:
        movable = [i for i in range(count - 1) if holding[i] < bound]
        mass, left = sum([portions[i] for i in movable]), spare
        for i in movable:
            more = min(bound - holding[i], max(1, left * portions[i] // mass), spare)
            holding[i] = holding[i] + more
            spare = spare - more
    return np.array([bound] + holding)


def uneven_parts(rng, count, total, reach, skew):
    if count == 2:
        one = jax.random.randint(rng, (), max(1, total - reach), min(reach, total - 1) + 1)
        return jnp.stack([one, total - one])
    sizes = jnp.asarray(split_up(count, total, reach, skew), jnp.int32)
    twos = (count - 1) // 2
    source_of, sink = sizes[1:1 + 2 * twos:2], sizes[2:2 + 2 * twos:2]
    room = jnp.minimum(source_of - 1, reach - sink)
    passed = jax.random.randint(jax.random.fold_in(rng, 1), (twos,), 0, 1 << 20) % (room + 1)
    sizes = sizes.at[1:1 + 2 * twos:2].set(source_of - passed).at[2:2 + 2 * twos:2].set(sink + passed)
    return sizes[jax.random.permutation(jax.random.fold_in(rng, 2), count)]


def scatter_about(own_key, dims, deviation, reach, cuts=(), dtype=jnp.bfloat16):
    values = jax.random.normal(own_key, dims, jnp.float32) * deviation
    if len(cuts) > 0:
        values = block_scale(own_key, dims, cuts, -0.22, 0.18) * values
    return jnp.clip(values, min=-reach, max=reach).astype(dtype)


def setup_inputs(seed: int = 0) -> dict:
    keys = jax.random.split(jax.random.key(seed), 18)
    return {
        "hidden": scatter_about(keys[0], (SEQS, SEQ_LEN, D), 1.0, 6.0, ((0, 16), (1, 2))),
        "pre_gain": jnp.clip(1.0 + 0.1 * jax.random.normal(keys[1], (D,), jnp.float32), 0.5, 1.5),
        "zx_weight": scatter_about(keys[2], (D, 2 * INNER), D ** -0.5, 0.1875, ((0, 16), (1, 2))),
        "bc_weight": scatter_about(keys[3], (D, 2 * STATE), D ** -0.5, 0.1875, ((0, 16),)),
        "step_weight": scatter_about(keys[4], (D, HEADS), D ** -0.5, 0.1875, ((0, 16), (1, 2))),
        "conv_x_weight": scatter_about(keys[5], (KCONV, INNER), 0.4, 2.0, ((1, 2),), jnp.float32),
        "conv_x_bias": scatter_about(keys[6], (INNER,), 0.3, 2.0, ((0, 2),), jnp.float32),
        "conv_bc_weight": scatter_about(keys[7], (KCONV, 2 * STATE), 0.4, 2.0, (), jnp.float32),
        "conv_bc_bias": scatter_about(keys[8], (2 * STATE,), 0.3, 2.0, (), jnp.float32),
        "step_bias": jnp.clip(-6.0 + 4.0 * jax.random.uniform(keys[9], (HEADS,), jnp.float32) ** block_scale(keys[9], (HEADS,), ((0, 2),), -0.2, 0.2), -6.0, -2.0),
        "decay_log": jnp.clip(2.77 * jax.random.uniform(keys[10], (HEADS,), jnp.float32) ** block_scale(keys[10], (HEADS,), ((0, 2),), -0.2, 0.2), 0.0, 2.77),
        "skip_gain": jnp.clip(0.5 + 1.0 * jax.random.uniform(keys[11], (HEADS,), jnp.float32) ** block_scale(keys[11], (HEADS,), ((0, 2),), -0.2, 0.2), 0.5, 1.5),
        "norm_gain": jnp.clip(1.0 + 0.1 * jax.random.normal(keys[12], (INNER,), jnp.float32), 0.5, 1.5),
        "out_weight": scatter_about(keys[13], (INNER, D), INNER ** -0.5, 0.125, ((0, 2), (1, 16))),
        "segment_ids": jax.vmap(lambda own: jnp.searchsorted(jnp.cumsum(uneven_parts(own, 4, SEQ_LEN, SEQ_LEN // 2, 0)), jnp.arange(SEQ_LEN), side="right"))(jax.random.split(keys[14], SEQS)).reshape((SEQS, SEQ_LEN)).astype(jnp.int32),
        "pad_mask": touch_ends((jax.random.randint(keys[15], (SEQS, SEQ_LEN), 0, 8) < 7).astype(jnp.int32), jax.random.fold_in(keys[15], 1), 0, 1),
        "grad_out": scatter_about(keys[16], (SEQS, SEQ_LEN, D), 1.0, 6.0, ((0, 16), (1, 2))),
    }


epsilon = 1e-05
highest_precision = lax.Precision.HIGHEST

@jax.custom_vjp
def low(v):
    return lax.optimization_barrier(v.astype(jnp.bfloat16)).astype(jnp.float32)

@jax.custom_vjp
def low_back(v):
    return v

def low_keep(v):
    return (low(v), None)

def low_pass(kept, grad):
    return (grad,)

def back_keep(v):
    return (v, None)

def back_low(kept, grad):
    return (low(grad),)
low.defvjp(low_keep, low_pass)
low_back.defvjp(back_keep, back_low)

def project(left_operand, right_operand):
    return jnp.einsum('zbp,py->zby', left_operand, right_operand, precision=highest_precision)

def filter_kernel_length(inputs, weight, bias_row, segment):
    length = inputs.shape[1]
    summed = bias_row + weight[0] * inputs
    for offset in range(1, weight.shape[0]):
        shifted = jnp.pad(inputs, ((0, 0), (offset, 0), (0, 0)))[:, :length]
        earlier = jnp.pad(segment, ((0, 0), (offset, 0)), constant_values=-1)[:, :length]
        summed = summed + weight[offset] * jnp.where((earlier == segment)[:, :, None], shifted, 0.0)
    return summed

def state_scan(values_in, keys_in, queries_in, step_size, rates, segment):
    seq_count, length, head_count, head_width = values_in.shape
    blocks = length // SPAN

    def to_blocks(array):
        return jnp.moveaxis(array.reshape((seq_count, blocks, SPAN) + array.shape[2:]), 1, 0)
    positions = jnp.arange(SPAN)
    causal = positions[:, None] >= positions[None, :]

    def advance(carry_in, block):
        carry_state, last_doc = carry_in
        block_values, block_keys, block_queries, block_steps, block_docs = block
        log_decay = jnp.cumsum(block_steps * rates, axis=1)
        inside = (causal[None] & (block_docs[:, :, None] == block_docs[:, None, :]))[..., None]
        spread = log_decay[:, :, None, :] - log_decay[:, None, :, :]
        forgetting_factors = jnp.where(inside, jnp.exp(jnp.where(inside, spread, 0.0)), 0.0)
        scores = jnp.einsum('stn,sun->stu', block_queries, block_keys, precision=highest_precision)
        mixing = scores[..., None] * forgetting_factors * block_steps[:, None, :, :]
        result = jnp.einsum('stuh,suhp->sthp', mixing, block_values, precision=highest_precision)
        carried = jnp.where((block_docs == last_doc[:, None])[..., None], jnp.exp(log_decay), 0.0)
        result = result + carried[..., None] * jnp.einsum('stn,shpn->sthp', block_queries, carry_state, precision=highest_precision)
        tail_doc = block_docs[:, -1]
        tail_keep = (block_docs == tail_doc[:, None])[..., None]
        toward = jnp.where(tail_keep, jnp.exp(jnp.where(tail_keep, log_decay[:, -1:, :] - log_decay, 0.0)), 0.0) * block_steps
        persist = jnp.where((tail_doc == last_doc)[:, None], jnp.exp(log_decay[:, -1, :]), 0.0)
        new_state = persist[:, :, None, None] * carry_state + jnp.einsum('suh,suhp,sun->shpn', toward, block_values, block_keys, precision=highest_precision)
        return ((new_state, tail_doc), result)
    start = (jnp.zeros((seq_count, head_count, head_width, keys_in.shape[-1]), jnp.float32), jnp.full((seq_count,), -1, jnp.int32))
    ignored, pieces = lax.scan(jax.checkpoint(advance), start, (to_blocks(values_in), to_blocks(keys_in), to_blocks(queries_in), to_blocks(step_size), to_blocks(segment)))
    return jnp.moveaxis(pieces, 0, 1).reshape(seq_count, length, head_count, head_width)

def block_forward(hidden_f, segment, pad_f, params):
    pre_gain, zx_weight, bc_weight, step_weight, conv_x_weight, conv_x_bias, conv_bc_weight, conv_bc_bias, step_bias, decay_log, skip_gain, norm_gain, out_weight = params
    seq_count, length = (hidden_f.shape[0], hidden_f.shape[1])
    inv_rms = lax.rsqrt(lax.optimization_barrier(jnp.mean(hidden_f * hidden_f, axis=-1, keepdims=True)) + epsilon)
    normalized_input = low(hidden_f * inv_rms * pre_gain)
    proj_zx = low(low_back(project(normalized_input, zx_weight))).reshape(seq_count, length, HEADS, 2, HEADDIM)
    unactivated_step = low_back(project(normalized_input, step_weight))
    proj_bc = low(low_back(project(normalized_input, bc_weight)))
    gate_in = proj_zx[:, :, :, 0, :].reshape(seq_count, length, INNER)
    value_in = proj_zx[:, :, :, 1, :].reshape(seq_count, length, INNER) * pad_f[..., None]
    conv_values = low(jax.nn.silu(filter_kernel_length(value_in, conv_x_weight, conv_x_bias, segment)))
    conv_bc = low(jax.nn.silu(filter_kernel_length(proj_bc * pad_f[..., None], conv_bc_weight, conv_bc_bias, segment)))
    step_size = jax.nn.softplus(unactivated_step + step_bias) * pad_f[..., None]
    rates = -jnp.exp(decay_log)
    values4 = conv_values.reshape(seq_count, length, HEADS, HEADDIM)
    mixed = state_scan(values4, conv_bc[..., :STATE], conv_bc[..., STATE:], step_size, rates, segment) + skip_gain[:, None] * values4
    gated = mixed.reshape(seq_count, length, INNER) * jax.nn.silu(gate_in)
    gate_rms = lax.rsqrt(lax.optimization_barrier(jnp.mean(gated * gated, axis=-1, keepdims=True)) + epsilon)
    rescaled_mixer_result = low(gated * gate_rms * norm_gain)
    return hidden_f + project(rescaled_mixer_result, out_weight)

def reference(hidden, pre_gain, zx_weight, bc_weight, step_weight, conv_x_weight, conv_x_bias, conv_bc_weight, conv_bc_bias, step_bias, decay_log, skip_gain, norm_gain, out_weight, segment_ids, pad_mask, grad_out):
    per_group = 4
    group_count = SEQS // per_group
    params = (pre_gain, zx_weight.astype(jnp.float32), bc_weight.astype(jnp.float32), step_weight.astype(jnp.float32), conv_x_weight, conv_x_bias, conv_bc_weight, conv_bc_bias, step_bias, decay_log, skip_gain, norm_gain, out_weight.astype(jnp.float32))
    latent_memory_everywhere = hidden.astype(jnp.float32).reshape(group_count, per_group, SEQ_LEN, D)
    segment_all = segment_ids.astype(jnp.int32).reshape(group_count, per_group, SEQ_LEN)
    pad_all = pad_mask.astype(jnp.float32).reshape(group_count, per_group, SEQ_LEN)

    def whole(hidden_in, weights):

        def single(item):
            return block_forward(item[0], item[1], item[2], weights)
        return lax.map(jax.checkpoint(single), (hidden_in, segment_all, pad_all))
    output, pullback = jax.vjp(whole, latent_memory_everywhere, params)
    grad_in, grads = pullback(grad_out.astype(jnp.float32).reshape(group_count, per_group, SEQ_LEN, D))
    return (output.reshape(SEQS, SEQ_LEN, D).astype(jnp.bfloat16), grad_in.reshape(SEQS, SEQ_LEN, D).astype(jnp.bfloat16), grads[0], grads[1], grads[2], grads[3], grads[4], grads[5], grads[6], grads[7], grads[8], grads[9], grads[10], grads[11], grads[12])
```

```python
import functools
import jax
import jax.numpy as jnp
from jax import lax
from jax.experimental import pallas as pl
from jax.experimental.pallas import tpu as pltpu
from jax.sharding import PartitionSpec as P

HEADDIM = 64
STATE = 128
CHUNK = 128
TAPS = 4
HALO = 8
AUX = 16
LOG2E = 1.4426950408889634
FAR = -1e30
epsilon = 1e-05
BF = jnp.bfloat16
F32 = jnp.float32


def sigmoid(v):
    return 0.5 * jnp.tanh(0.5 * v) + 0.5


def split3(v):
    a = v.astype(BF)
    r = v - a.astype(F32)
    b = r.astype(BF)
    c = (r - b.astype(F32)).astype(BF)
    return a, b, c


def dot_nn(a, b):
    return lax.dot_general(a, b, (((1,), (0,)), ((), ())), preferred_element_type=F32)


def dot_nt(a, b):
    return lax.dot_general(a, b, (((1,), (1,)), ((), ())), preferred_element_type=F32)


def exact_dot(v, ones):
    rows = v.shape[0]
    out = dot_nn(jnp.concatenate(split3(v), axis=0), ones)
    return out[:rows] + out[rows : 2 * rows] + out[2 * rows :]


def iota2(shape, dim):
    return lax.broadcasted_iota(jnp.int32, shape, dim)


def pieces(raw, bias, rate, aux, tri):
    pad = aux[1:2]
    pre = raw + bias
    soft = jnp.maximum(pre, 0.0) + jnp.log1p(jnp.exp(-jnp.abs(pre)))
    dt = soft * pad
    cum = exact_dot(dt * rate, tri) * LOG2E
    carried = jnp.exp2(cum) * aux[5:6]
    toward = jnp.exp2(cum[:, CHUNK - 1 : CHUNK] - cum) * aux[6:7]
    return dt, cum, carried, toward


def expander(heads, inner, place):
    row = lax.rem(iota2((256, inner), 0), 128)
    head = lax.div(iota2((256, inner), 1), HEADDIM)
    return jnp.where(row == head + place, 1.0, 0.0).astype(BF)


def collector(inner, place):
    head = lax.div(iota2((inner, 128), 0), HEADDIM)
    lane = iota2((inner, 128), 1)
    return jnp.where(lane == head + place, 1.0, 0.0).astype(BF)


def hi_lo(cols):
    hi = cols.astype(BF)
    return jnp.concatenate([hi, (cols - hi.astype(F32)).astype(BF)], axis=1)


def compact(rows_list):
    used = sum(r.shape[0] for r in rows_list)
    if used < 128:
        rows_list = list(rows_list) + [jnp.zeros((128 - used, CHUNK), F32)]
    return jnp.concatenate(rows_list, axis=0).T


def split_pair(first, second, low):
    gate = jnp.where(low, first, pltpu.roll(second, HEADDIM, 1))
    value = jnp.where(low, pltpu.roll(first, HEADDIM, 1), second)
    return gate, value


def forward_kernel(
    heads, zx_ref, bc_ref, raw_ref, aux_ref, g_ref, cw_ref, cbw_ref, hp_ref,
    mixed_ref, gated_ref, cv_ref, pre_ref, cbc_ref, pbc_ref, st_ref, stat_ref,
    state, ubuf, bbuf, vd, yint, expand, tri_ref,
):
    inner = heads * HEADDIM
    pairs = heads // 2
    first = (pl.program_id(0) == 0) & (pl.program_id(1) == 0)

    @pl.when(first)
    def _():
        for i, place in enumerate((AUX + heads, AUX + 2 * heads, AUX + 3 * heads)):
            expand[i] = expander(heads, inner, place)
        tri_ref[...] = jnp.where(iota2((CHUNK, CHUNK), 0) <= iota2((CHUNK, CHUNK), 1), 1.0, 0.0).astype(BF)

    @pl.when(pl.program_id(1) == 0)
    def _():
        state[...] = jnp.zeros_like(state)
        ubuf[0:HALO] = jnp.zeros((HALO, inner), F32)
        bbuf[0:HALO] = jnp.zeros((HALO, 2 * STATE), F32)

    aux = aux_ref[0]
    dt, cum, carried, toward = pieces(raw_ref[0], hp_ref[0], hp_ref[1], aux, tri_ref[...])
    cols = compact([aux, cum, dt, carried, toward])
    both = hi_lo(cols)
    dtx = dot_nn(both, expand[0])
    carx = dot_nn(both, expand[1])
    towx = dot_nn(both, expand[2])
    pad = cols[:, 1:2]
    same = [None] + [cols[:, 1 + k : 2 + k] for k in range(1, TAPS)]
    low = iota2((CHUNK, 128), 1) < HEADDIM

    bbuf[HALO:] = bc_ref[0].astype(F32) * pad
    maps = cbw_ref[TAPS : TAPS + 1] + cbw_ref[0:1] * bbuf[HALO:]
    for k in range(1, TAPS):
        maps = maps + cbw_ref[k : k + 1] * (same[k] * bbuf[HALO - k : HALO - k + CHUNK])
    pbc_ref[0] = maps.astype(BF)
    maps = (maps * sigmoid(maps)).astype(BF)
    cbc_ref[0] = maps
    bbuf[0:HALO] = bbuf[CHUNK : CHUNK + HALO]
    keys, queries = maps[:, :STATE], maps[:, STATE:]
    scores = dot_nt(queries, keys)
    keys_t = keys.astype(F32).T.astype(BF)

    for p in range(pairs):
        s = slice(128 * p, 128 * p + 128)
        x0 = zx_ref[0, :, 256 * p : 256 * p + 128].astype(F32)
        x1 = zx_ref[0, :, 256 * p + 128 : 256 * p + 256].astype(F32)
        value = jnp.where(low, pltpu.roll(x0, HEADDIM, 1), x1)
        ubuf[HALO:, s] = value * pad
        pre = cw_ref[TAPS : TAPS + 1, s] + cw_ref[0:1, s] * ubuf[HALO:, s]
        for k in range(1, TAPS):
            pre = pre + cw_ref[k : k + 1, s] * (same[k] * ubuf[HALO - k : HALO - k + CHUNK, s])
        pre_ref[0, :, s] = pre.astype(BF)
        cv = (pre * sigmoid(pre)).astype(BF)
        cv_ref[0, :, s] = cv
        vd[:, s] = (cv.astype(F32) * dtx[:, s]).astype(BF)
    ubuf[0:HALO] = ubuf[CHUNK : CHUNK + HALO]

    old = state[...]
    old_b = old.astype(BF)
    st_ref[0, 0] = old_b
    yint[...] = dot_nn(queries, old_b) * carx
    state[...] = carx[CHUNK - 1 : CHUNK] * old + dot_nn(keys_t, (vd[...].astype(F32) * towx).astype(BF))

    inside = (iota2((CHUNK, CHUNK), 0) >= iota2((CHUNK, CHUNK), 1)) & (cols[:, 0:1] == aux[0:1])
    fence = jnp.where(inside, 0.0, FAR)
    squares = jnp.zeros((CHUNK, 128), F32)
    cross = jnp.zeros((CHUNK, 128), F32)
    for p in range(pairs):
        s = slice(128 * p, 128 * p + 128)
        mix = []
        for h in (2 * p, 2 * p + 1):
            decay = jnp.exp2(cols[:, AUX + h : AUX + h + 1] - cum[h : h + 1] + fence)
            mix.append((scores * decay).astype(BF))
        v = vd[:, s]
        zero = jnp.zeros_like(v)
        stacked = jnp.concatenate([jnp.where(low, v, zero), jnp.where(low, zero, v)], axis=0)
        y = dot_nn(jnp.concatenate(mix, axis=1), stacked)
        mixed = y + yint[:, s] + cw_ref[5:6, s] * cv_ref[0, :, s].astype(F32)
        x0 = zx_ref[0, :, 256 * p : 256 * p + 128].astype(F32)
        x1 = zx_ref[0, :, 256 * p + 128 : 256 * p + 256].astype(F32)
        gate = jnp.where(low, x0, pltpu.roll(x1, HEADDIM, 1))
        gated = mixed * (gate * sigmoid(gate))
        mixed_ref[0, :, s] = mixed.astype(BF)
        gated_ref[0, :, s] = gated.astype(BF)
        squares = squares + gated * gated
        cross = cross + gated * (g_ref[0, :, s].astype(F32) * cw_ref[6:7, s])
    lane = iota2((CHUNK, 128), 1)
    sums = jnp.where(lane == 0, jnp.sum(squares, axis=1, keepdims=True), 0.0)
    sums = jnp.where(lane == 1, jnp.sum(cross, axis=1, keepdims=True), sums)
    stat_ref[0] = sums.T[0:8]


def backward_kernel(
    heads, zx_ref, bc_ref, raw_ref, aux_ref, g_ref, mixed_ref, cv_ref, pre_ref, cbc_ref, pbc_ref,
    st_ref, stat_ref, cw_ref, cbw_ref, hp_ref,
    gzx_ref, gbc_ref, gstep_ref, gch_ref, gmap_ref, ghead_ref,
    dstate, cbuf, dbuf, vd, gm_s, gmc_s, ggate_s, cs_s, bs_s, expand, collect, tri_ref, suf_ref,
):
    inner = heads * HEADDIM
    pairs = heads // 2
    first = (pl.program_id(0) == 0) & (pl.program_id(1) == 0)

    @pl.when(first)
    def _():
        for i, place in enumerate((AUX + heads, AUX + 2 * heads, AUX + 3 * heads)):
            expand[i] = expander(heads, inner, place)
        collect[0] = collector(inner, heads)
        collect[1] = collector(inner, 2 * heads)
        r, c = iota2((CHUNK, CHUNK), 0), iota2((CHUNK, CHUNK), 1)
        tri_ref[...] = jnp.where(r <= c, 1.0, 0.0).astype(BF)
        suf_ref[...] = jnp.where(r >= c, 1.0, 0.0).astype(BF)
        gch_ref[...] = jnp.zeros_like(gch_ref)
        gmap_ref[...] = jnp.zeros_like(gmap_ref)
        ghead_ref[...] = jnp.zeros_like(ghead_ref)

    @pl.when(pl.program_id(1) == 0)
    def _():
        dstate[...] = jnp.zeros_like(dstate)
        cbuf[CHUNK:] = jnp.zeros((HALO, inner), F32)
        dbuf[CHUNK:] = jnp.zeros((HALO, 2 * STATE), F32)

    aux = aux_ref[0]
    rate = hp_ref[1]
    dt, cum, carried, toward = pieces(raw_ref[0], hp_ref[0], rate, aux, tri_ref[...])
    cols = compact([aux, cum, dt, carried, toward, stat_ref[0]])
    both = hi_lo(cols)
    dtx = dot_nn(both, expand[0])
    carx = dot_nn(both, expand[1])
    towx = dot_nn(both, expand[2])
    pad = cols[:, 1:2]
    ahead = [None] + [cols[:, 7 + k : 8 + k] for k in range(1, TAPS)]
    base = AUX + 4 * heads
    rms, pull = cols[:, base : base + 1], cols[:, base + 1 : base + 2]
    low = iota2((CHUNK, 128), 1) < HEADDIM
    maps = cbc_ref[0]
    keys, queries = maps[:, :STATE], maps[:, STATE:]
    queries_t = queries.astype(F32).T.astype(BF)
    scores_t = dot_nt(keys, queries)

    for p in range(pairs):
        s = slice(128 * p, 128 * p + 128)
        x0 = zx_ref[0, :, 256 * p : 256 * p + 128].astype(F32)
        x1 = zx_ref[0, :, 256 * p + 128 : 256 * p + 256].astype(F32)
        gate = jnp.where(low, x0, pltpu.roll(x1, HEADDIM, 1))
        sig = sigmoid(gate)
        act = gate * sig
        mixed = mixed_ref[0, :, s].astype(F32)
        gated = mixed * act
        g = g_ref[0, :, s].astype(F32)
        grad_gated = rms * (g * cw_ref[6:7, s]) - gated * pull
        gm = grad_gated * act
        ggate_s[:, s] = (grad_gated * mixed * (sig * (1.0 + gate * (1.0 - sig)))).astype(BF)
        gm_s[:, s] = gm.astype(BF)
        gmc_s[:, s] = (gm * carx[:, s]).astype(BF)
        cv = cv_ref[0, :, s].astype(F32)
        vd[:, s] = (cv * dtx[:, s]).astype(BF)
        gch_ref[5:6, s] += jnp.sum(gm * cv, axis=0, keepdims=True)
        gch_ref[6:7, s] += jnp.sum(gated * rms * g, axis=0, keepdims=True)

    ds = dstate[...]
    ds_b = ds.astype(BF)
    st = st_ref[0, 0]
    gmc = gmc_s[...]
    cs = dot_nn(queries, st)
    bs = dot_nn(keys, ds_b) * towx
    bs_s[...] = bs
    reach = dot_nn((gmc.astype(F32) * cs).astype(BF), collect[1])
    reach = reach + dot_nn((bs * cv_ref[0].astype(F32)).astype(BF), collect[0])
    grad_q = dot_nt(gmc, st)
    grad_k = dot_nt((vd[...].astype(F32) * towx).astype(BF), ds_b)
    keep = carx[CHUNK - 1 : CHUNK]
    held = jnp.sum(st.astype(F32) * ds, axis=0, keepdims=True) * keep
    dstate[...] = keep * ds + dot_nn(queries_t, gmc)

    inside = (iota2((CHUNK, CHUNK), 0) <= iota2((CHUNK, CHUNK), 1)) & (cols[:, 0:1] == aux[0:1])
    fence = jnp.where(inside, 0.0, FAR)
    grad_scores_t = jnp.zeros((CHUNK, CHUNK), F32)
    lane = iota2((CHUNK, 128), 1)
    gathered = reach
    row_sums = []
    for p in range(pairs):
        s = slice(128 * p, 128 * p + 128)
        gm_b = gm_s[:, s]
        zero = jnp.zeros_like(gm_b)
        gm_two = jnp.concatenate([jnp.where(low, gm_b, zero), jnp.where(low, zero, gm_b)], axis=0)
        near = dot_nt(vd[:, s], gm_two)
        mix = []
        for j in range(2):
            h = 2 * p + j
            decay = jnp.exp2(cum[h : h + 1] - cols[:, AUX + h : AUX + h + 1] + fence)
            mix.append((scores_t * decay).astype(BF))
            weighed = decay * near[:, CHUNK * j : CHUNK * j + CHUNK]
            grad_scores_t = grad_scores_t + weighed
            pairs_g = weighed * scores_t
            row_sums.append(jnp.sum(pairs_g, axis=0, keepdims=True))
            gathered = jnp.where(lane == h, jnp.sum(pairs_g, axis=1, keepdims=True), gathered)
        z = dot_nn(jnp.concatenate(mix, axis=1), gm_two)
        gm = gm_b.astype(F32)
        grad_v = cw_ref[5:6, s] * gm + dtx[:, s] * (z + bs_s[:, s])
        x0 = zx_ref[0, :, 256 * p : 256 * p + 128].astype(F32)
        x1 = zx_ref[0, :, 256 * p + 128 : 256 * p + 256].astype(F32)
        u = jnp.where(low, pltpu.roll(x0, HEADDIM, 1), x1) * pad
        pre = pre_ref[0, :, s].astype(F32)
        sig = sigmoid(pre)
        c = grad_v * (sig * (1.0 + pre * (1.0 - sig)))
        cbuf[0:CHUNK, s] = c
        gu = cw_ref[0:1, s] * c
        gch_ref[4:5, s] += jnp.sum(c, axis=0, keepdims=True)
        gch_ref[0:1, s] += jnp.sum(c * u, axis=0, keepdims=True)
        for k in range(1, TAPS):
            shifted = ahead[k] * cbuf[k : k + CHUNK, s]
            gu = gu + cw_ref[k : k + 1, s] * shifted
            gch_ref[k : k + 1, s] += jnp.sum(shifted * u, axis=0, keepdims=True)
        gu = gu * pad
        ggate = ggate_s[:, s].astype(F32)
        gzx_ref[0, :, 256 * p : 256 * p + 128] = jnp.where(low, ggate, pltpu.roll(gu, HEADDIM, 1)).astype(BF)
        gzx_ref[0, :, 256 * p + 128 : 256 * p + 256] = jnp.where(low, pltpu.roll(ggate, HEADDIM, 1), gu).astype(BF)
    cbuf[CHUNK:] = cbuf[0:HALO]

    gst = grad_scores_t.astype(BF)
    grad_k = grad_k + dot_nn(gst, queries)
    grad_q = grad_q + dot_nn(grad_scores_t.T.astype(BF), keys)
    pbc = pbc_ref[0].astype(F32)
    sig = sigmoid(pbc)
    c = jnp.concatenate([grad_k, grad_q], axis=1) * (sig * (1.0 + pbc * (1.0 - sig)))
    dbuf[0:CHUNK] = c
    u = bc_ref[0].astype(F32) * pad
    gu = cbw_ref[0:1] * c
    gmap_ref[4:5] += jnp.sum(c, axis=0, keepdims=True)
    gmap_ref[0:1] += jnp.sum(c * u, axis=0, keepdims=True)
    for k in range(1, TAPS):
        shifted = ahead[k] * dbuf[k : k + CHUNK]
        gu = gu + cbw_ref[k : k + 1] * shifted
        gmap_ref[k : k + 1] += jnp.sum(shifted * u, axis=0, keepdims=True)
    gbc_ref[0] = gu * pad
    dbuf[CHUNK:] = dbuf[0:HALO]

    across = gathered.T
    col_sum = across[0:heads]
    kx = across[heads : 2 * heads]
    rint = across[2 * heads : 3 * heads]
    row_sum = jnp.concatenate(row_sums, axis=0)
    k_all = kx * dt
    held_head = exact_dot(jnp.broadcast_to(held, (16, inner)), collect[0])
    held_col = jnp.broadcast_to(held_head[0:1], (CHUNK, 128)).T[heads : 2 * heads]
    diff = row_sum + rint - col_sum - k_all
    grad_a = exact_dot(diff, suf_ref[...]) + jnp.sum(k_all, axis=1, keepdims=True) + held_col
    direct = jnp.where(dt > 0.0, col_sum / jnp.where(dt > 0.0, dt, 1.0), 0.0)
    grad_dt = direct + kx + rate * grad_a
    graw = grad_dt * aux[1:2] * sigmoid(raw_ref[0] + hp_ref[0])
    gstep_ref[0] = graw
    ghead_ref[0] += graw
    ghead_ref[1] += rate * dt * grad_a


def mixer_forward(zx, bc, raw, aux, g, cw, cbw, hp):
    seqs, length, wide = zx.shape
    inner = wide // 2
    heads = inner // HEADDIM
    chunks = length // CHUNK
    token = lambda width: pl.BlockSpec((1, CHUNK, width), lambda s, c: (s, c, 0))
    row = lambda high: pl.BlockSpec((1, high, CHUNK), lambda s, c: (s, 0, c))
    whole = lambda *shape: pl.BlockSpec(shape, lambda s, c: (0,) * len(shape))
    sds = jax.ShapeDtypeStruct
    return pl.pallas_call(
        functools.partial(forward_kernel, heads),
        grid=(seqs, chunks),
        in_specs=[
            token(wide), token(2 * STATE), row(heads), row(AUX), token(inner),
            whole(8, inner), whole(8, 2 * STATE), whole(2, heads, 128),
        ],
        out_specs=[
            token(inner), token(inner), token(inner), token(inner), token(2 * STATE), token(2 * STATE),
            pl.BlockSpec((1, 1, STATE, inner), lambda s, c: (s, c, 0, 0)), row(8),
        ],
        out_shape=[
            sds((seqs, length, inner), BF), sds((seqs, length, inner), BF), sds((seqs, length, inner), BF),
            sds((seqs, length, inner), BF), sds((seqs, length, 2 * STATE), BF), sds((seqs, length, 2 * STATE), BF),
            sds((seqs, chunks, STATE, inner), BF), sds((seqs, 8, length), F32),
        ],
        scratch_shapes=[
            pltpu.VMEM((STATE, inner), F32), pltpu.VMEM((HALO + CHUNK, inner), F32),
            pltpu.VMEM((HALO + CHUNK, 2 * STATE), F32), pltpu.VMEM((CHUNK, inner), BF),
            pltpu.VMEM((CHUNK, inner), F32), pltpu.VMEM((3, 256, inner), BF), pltpu.VMEM((CHUNK, CHUNK), BF),
        ],
        compiler_params=pltpu.CompilerParams(vmem_limit_bytes=40 * 1024 * 1024),
        name="mixer_forward",
    )(zx, bc, raw, aux, g, cw, cbw, hp)


def mixer_backward(zx, bc, raw, aux, g, mixed, cv, pre, cbc, pbc, st, stat, cw, cbw, hp):
    seqs, length, wide = zx.shape
    inner = wide // 2
    heads = inner // HEADDIM
    chunks = length // CHUNK
    last = chunks - 1
    token = lambda width: pl.BlockSpec((1, CHUNK, width), lambda s, c: (s, last - c, 0))
    row = lambda high: pl.BlockSpec((1, high, CHUNK), lambda s, c: (s, 0, last - c))
    whole = lambda *shape: pl.BlockSpec(shape, lambda s, c: (0,) * len(shape))
    sds = jax.ShapeDtypeStruct
    return pl.pallas_call(
        functools.partial(backward_kernel, heads),
        grid=(seqs, chunks),
        in_specs=[
            token(wide), token(2 * STATE), row(heads), row(AUX), token(inner), token(inner), token(inner),
            token(inner), token(2 * STATE), token(2 * STATE),
            pl.BlockSpec((1, 1, STATE, inner), lambda s, c: (s, last - c, 0, 0)), row(8),
            whole(8, inner), whole(8, 2 * STATE), whole(2, heads, 128),
        ],
        out_specs=[
            token(wide), token(2 * STATE), row(heads),
            whole(8, inner), whole(8, 2 * STATE), whole(2, heads, 128),
        ],
        out_shape=[
            sds((seqs, length, wide), BF), sds((seqs, length, 2 * STATE), F32), sds((seqs, heads, length), F32),
            sds((8, inner), F32), sds((8, 2 * STATE), F32), sds((2, heads, 128), F32),
        ],
        scratch_shapes=[
            pltpu.VMEM((STATE, inner), F32), pltpu.VMEM((CHUNK + HALO, inner), F32),
            pltpu.VMEM((CHUNK + HALO, 2 * STATE), F32), pltpu.VMEM((CHUNK, inner), BF),
            pltpu.VMEM((CHUNK, inner), BF), pltpu.VMEM((CHUNK, inner), BF), pltpu.VMEM((CHUNK, inner), BF),
            pltpu.VMEM((CHUNK, inner), F32), pltpu.VMEM((CHUNK, inner), F32),
            pltpu.VMEM((3, 256, inner), BF), pltpu.VMEM((2, inner, 128), BF),
            pltpu.VMEM((CHUNK, CHUNK), BF), pltpu.VMEM((CHUNK, CHUNK), BF),
        ],
        compiler_params=pltpu.CompilerParams(vmem_limit_bytes=40 * 1024 * 1024),
        name="mixer_backward",
    )(zx, bc, raw, aux, g, mixed, cv, pre, cbc, pbc, st, stat, cw, cbw, hp)


def doc_flags(segment, pad_mask):
    seqs, length = segment.shape
    position = lax.broadcasted_iota(jnp.int32, segment.shape, 1)
    rows = [segment.astype(F32), pad_mask.astype(F32)]
    back = []
    for k in range(1, TAPS):
        earlier = jnp.pad(segment, ((0, 0), (k, 0)), constant_values=-1)[:, :length]
        back.append(earlier == segment)
    rows += [b.astype(F32) for b in back]
    blocks = segment.reshape(seqs, length // CHUNK, CHUNK)
    tail = blocks[:, :, CHUNK - 1 :]
    previous = jnp.pad(tail, ((0, 0), (1, 0), (0, 0)), constant_values=-1)[:, :-1]
    rows.append((blocks == previous).reshape(seqs, length).astype(F32))
    rows.append((blocks == tail).reshape(seqs, length).astype(F32))
    rows.append(jnp.zeros_like(rows[0]))
    for k in range(1, TAPS):
        later = jnp.pad(segment, ((0, 0), (0, k)), constant_values=-1)[:, k:]
        rows.append((later == segment).astype(F32))
    rows += [jnp.zeros_like(rows[0])] * (AUX - len(rows))
    return jnp.stack(rows, axis=1)


def gather_tokens(own, n, me):
    if n != 2:
        return lax.all_gather(own, "tensor", axis=1, tiled=True)
    other = lax.ppermute(own, "tensor", [(0, 1), (1, 0)])
    seqs, here, width = own.shape
    full = jnp.zeros((seqs, 2 * here, width), own.dtype)
    full = lax.dynamic_update_slice(full, own, (0, me * here, 0))
    return lax.dynamic_update_slice(full, other, (0, (1 - me) * here, 0))


def scatter_sum(make, size, n, me, dim):
    if n != 2:
        blocks = [make(i * size) for i in range(n)]
        return lax.psum_scatter(jnp.concatenate(blocks, axis=dim), "tensor", scatter_dimension=dim, tiled=True)
    away = lax.ppermute(make((1 - me) * size).astype(BF), "tensor", [(0, 1), (1, 0)])
    return make(me * size) + away.astype(F32)


def swap_sum(value, n):
    if n != 2:
        return lax.psum(value, "tensor")
    return value + lax.ppermute(value, "tensor", [(0, 1), (1, 0)])


def body(
    hidden, pre_gain, zx_weight, bc_weight, step_weight, conv_x_weight, conv_x_bias, conv_bc_weight, conv_bc_bias,
    step_bias, decay_log, skip_gain, norm_gain, out_weight, segment_ids, pad_mask, grad_out,
):
    n = lax.axis_size("tensor")
    me = lax.axis_index("tensor")
    heads = step_weight.shape[1]
    inner = heads * HEADDIM
    inner_all = inner * n
    here = hidden.shape[1]
    width = hidden.shape[2]
    maps_here = 2 * STATE // n

    zx_all = lax.all_gather(zx_weight, "dp", axis=0, tiled=True)
    small_all = lax.all_gather(jnp.concatenate([bc_weight, step_weight], axis=1), "dp", axis=0, tiled=True)
    out_all = lax.all_gather(out_weight.T, "dp", axis=0, tiled=True)
    bc_all, step_all = small_all[:, : 2 * STATE], small_all[:, 2 * STATE :]

    hidden_f = hidden.astype(F32)
    inv_rms = lax.rsqrt(jnp.mean(hidden_f * hidden_f, axis=-1, keepdims=True) + epsilon)
    normed = gather_tokens((hidden_f * inv_rms * pre_gain).astype(BF), n, me)
    cotangent = gather_tokens(grad_out, n, me)

    aux = doc_flags(segment_ids, pad_mask)
    cw = jnp.concatenate(
        [conv_x_weight, conv_x_bias[None], jnp.repeat(skip_gain, HEADDIM)[None], norm_gain[None], jnp.zeros((1, inner), F32)]
    )
    cbw = jnp.concatenate([conv_bc_weight, conv_bc_bias[None], jnp.zeros((3, 2 * STATE), F32)])
    rate = -jnp.exp(decay_log)
    hp = jnp.broadcast_to(jnp.stack([step_bias, rate])[:, :, None], (2, heads, 128))

    zx = jnp.einsum("stp,py->sty", normed, zx_all, preferred_element_type=F32).astype(BF)
    bc = jnp.einsum("stp,py->sty", normed, bc_all, preferred_element_type=F32).astype(BF)
    raw = jnp.einsum("stp,ph->sht", normed, step_all, preferred_element_type=F32)
    g = jnp.einsum("str,rc->stc", cotangent, out_all, preferred_element_type=F32).astype(BF)

    mixed, gated, cv, pre, cbc, pbc, st, stat = mixer_forward(zx, bc, raw, aux, g, cw, cbw, hp)
    stat = swap_sum(stat, n)
    gate_rms = lax.rsqrt(stat[:, 0] / inner_all + epsilon)
    back = jnp.stack([gate_rms, gate_rms**3 * (stat[:, 1] / inner_all)] + [jnp.zeros_like(gate_rms)] * 6, axis=1)

    normed_out = (gated.astype(F32) * gate_rms[..., None] * norm_gain).astype(BF)

    def out_part(start):
        rows = lax.dynamic_slice_in_dim(normed_out, start, here, axis=1)
        return jnp.einsum("stc,rc->str", rows, out_all, preferred_element_type=F32)

    output = (hidden_f + scatter_sum(out_part, here, n, me, 1)).astype(BF)
    out_grad = jnp.einsum("str,stc->rc", cotangent, normed_out, preferred_element_type=F32).astype(BF)
    grad_out_weight = lax.psum_scatter(out_grad, "dp", scatter_dimension=0, tiled=True).astype(F32).T

    gzx, gbc, gstep, gch, gmap, ghead = mixer_backward(
        zx, bc, raw, aux, g, mixed, cv, pre, cbc, pbc, st, back, cw, cbw, hp
    )
    gstep = gstep.astype(BF)
    gbc_own = scatter_sum(
        lambda start: lax.dynamic_slice_in_dim(gbc, start, maps_here, axis=2), maps_here, n, me, 2
    ).astype(BF)
    bc_own = lax.dynamic_slice_in_dim(bc_all, me * maps_here, maps_here, axis=1)

    def in_part(start):
        cut = lambda rows, dim: lax.dynamic_slice_in_dim(rows, start, here, axis=dim)
        return (
            jnp.einsum("sty,py->stp", cut(gzx, 1), zx_all, preferred_element_type=F32)
            + jnp.einsum("sty,py->stp", cut(gbc_own, 1), bc_own, preferred_element_type=F32)
            + jnp.einsum("sht,ph->stp", cut(gstep, 2), step_all, preferred_element_type=F32)
        )

    grad_normed = scatter_sum(in_part, here, n, me, 1)
    zx_grad = jnp.einsum("stp,sty->py", normed, gzx, preferred_element_type=F32).astype(BF)
    small_grad = jnp.concatenate(
        [
            jnp.einsum("stp,sty->py", normed, gbc_own, preferred_element_type=F32),
            jnp.einsum("stp,sht->ph", normed, gstep, preferred_element_type=F32),
        ],
        axis=1,
    ).astype(BF)
    grad_zx_weight = lax.psum_scatter(zx_grad, "dp", scatter_dimension=0, tiled=True).astype(F32)
    small_rows = lax.psum_scatter(small_grad, "dp", scatter_dimension=0, tiled=True).astype(F32)
    grad_bc_weight = lax.all_gather(small_rows[:, :maps_here], "tensor", axis=1, tiled=True)
    grad_step_weight = small_rows[:, maps_here:]

    scaled_in = hidden_f * inv_rms
    grad_pre = jnp.sum(scaled_in * grad_normed, axis=(0, 1))
    gain_grad = grad_normed * pre_gain
    grad_hidden = (
        grad_out.astype(F32)
        + inv_rms * gain_grad
        - hidden_f * inv_rms**3 * jnp.mean(hidden_f * gain_grad, axis=-1, keepdims=True)
    ).astype(BF)

    head_sums = jnp.sum(ghead, axis=-1)
    skip_sums = jnp.sum(gch[5].reshape(heads, HEADDIM), axis=-1)
    flat = jnp.concatenate(
        [gmap[:5].reshape(-1), grad_pre, gch[:5].reshape(-1), gch[6], head_sums.reshape(-1), skip_sums]
    )
    flat = lax.psum(flat, "dp")
    shared_size = 5 * 2 * STATE + width
    shared = swap_sum(flat[:shared_size], n)
    shared_map = shared[: 5 * 2 * STATE].reshape(5, 2 * STATE)
    rest = flat[shared_size:]
    channel = rest[: 6 * inner].reshape(6, inner)
    per_head = rest[6 * inner :].reshape(3, heads)
    return (
        output, grad_hidden, shared[5 * 2 * STATE :], grad_zx_weight, grad_bc_weight, grad_step_weight,
        channel[:4], channel[4], shared_map[:4], shared_map[4], per_head[0], per_head[1], per_head[2],
        channel[5], grad_out_weight,
    )


def solution(mesh):
    placed = (
        P("dp", "tensor", None), P(), P("dp", "tensor"), P("dp", None), P("dp", "tensor"), P(None, "tensor"),
        P("tensor"), P(), P(), P("tensor"), P("tensor"), P("tensor"), P("tensor"), P("tensor", "dp"),
        P("dp", None), P("dp", None), P("dp", "tensor", None),
    )
    return jax.shard_map(
        body,
        mesh=mesh,
        in_specs=placed,
        out_specs=(
            P("dp", "tensor", None), P("dp", "tensor", None), P(), P("dp", "tensor"), P("dp", None), P("dp", "tensor"),
            P(None, "tensor"), P("tensor"), P(), P(), P("tensor"), P("tensor"), P("tensor"), P("tensor"),
            P("tensor", "dp"),
        ),
        check_vma=False,
    )
```

```python
import functools
import jax
import jax.numpy as jnp
from jax import lax
from jax.experimental import pallas as pl
from jax.experimental.pallas import tpu as pltpu
from jax.sharding import PartitionSpec as P

HEADDIM = 64
STATE = 128
CHUNK = 128
TAPS = 4
HALO = 8
AUX = 16
LOG2E = 1.4426950408889634
FAR = -1e30
BLOCK = 256
VMEM_LIMIT = 44 * 1024 * 1024
epsilon = 1e-05
BF = jnp.bfloat16
F32 = jnp.float32


def sigmoid(v):
    return 0.5 * jnp.tanh(0.5 * v) + 0.5


def split3(v):
    a = v.astype(BF)
    r = v - a.astype(F32)
    b = r.astype(BF)
    c = (r - b.astype(F32)).astype(BF)
    return a, b, c


def dot_nn(a, b):
    return lax.dot_general(a, b, (((1,), (0,)), ((), ())), preferred_element_type=F32)


def dot_nt(a, b):
    return lax.dot_general(a, b, (((1,), (1,)), ((), ())), preferred_element_type=F32)


def exact_dot(v, ones):
    rows = v.shape[0]
    out = dot_nn(jnp.concatenate(split3(v), axis=0), ones)
    return out[:rows] + out[rows : 2 * rows] + out[2 * rows :]


def iota2(shape, dim):
    return lax.broadcasted_iota(jnp.int32, shape, dim)


def pieces(raw, bias, rate, aux, tri):
    pad = aux[1:2]
    pre = raw + bias
    soft = jnp.maximum(pre, 0.0) + jnp.log1p(jnp.exp(-jnp.abs(pre)))
    dt = soft * pad
    cum = exact_dot(dt * rate, tri) * LOG2E
    carried = jnp.exp2(cum) * aux[5:6]
    toward = jnp.exp2(cum[:, CHUNK - 1 : CHUNK] - cum) * aux[6:7]
    return dt, cum, carried, toward


def expander(heads, inner, place):
    row = lax.rem(iota2((256, inner), 0), 128)
    head = lax.div(iota2((256, inner), 1), HEADDIM)
    return jnp.where(row == head + place, 1.0, 0.0).astype(BF)


def collector(inner, place):
    head = lax.div(iota2((inner, 128), 0), HEADDIM)
    lane = iota2((inner, 128), 1)
    return jnp.where(lane == head + place, 1.0, 0.0).astype(BF)


def hi_lo(cols):
    hi = cols.astype(BF)
    return jnp.concatenate([hi, (cols - hi.astype(F32)).astype(BF)], axis=1)


def compact(rows_list):
    used = sum(r.shape[0] for r in rows_list)
    if used < 128:
        rows_list = list(rows_list) + [jnp.zeros((128 - used, CHUNK), F32)]
    return jnp.concatenate(rows_list, axis=0).T


def split_pair(first, second, low):
    gate = jnp.where(low, first, pltpu.roll(second, HEADDIM, 1))
    value = jnp.where(low, pltpu.roll(first, HEADDIM, 1), second)
    return gate, value


def forward_kernel(
    heads, tok_ref, w_ref, aux_ref, cw_ref, cbw_ref, hp_ref,
    pz_ref, raw_ref, mixed_ref, gated_ref, cv_ref, pre_ref, cbc_ref, pbc_ref, st_ref, stat_ref,
    state, ubuf, bbuf, vd, yint, expand, tri_ref,
):
    inner = heads * HEADDIM
    pairs = heads // 2
    wide = 2 * inner
    first = (pl.program_id(0) == 0) & (pl.program_id(1) == 0)

    @pl.when(first)
    def _():
        for i, place in enumerate((AUX + heads, AUX + 2 * heads, AUX + 3 * heads)):
            expand[i] = expander(heads, inner, place)
        tri_ref[...] = jnp.where(iota2((CHUNK, CHUNK), 0) <= iota2((CHUNK, CHUNK), 1), 1.0, 0.0).astype(BF)

    @pl.when(pl.program_id(1) == 0)
    def _():
        state[...] = jnp.zeros_like(state)
        ubuf[0:HALO] = jnp.zeros((HALO, inner), F32)
        bbuf[0:HALO] = jnp.zeros((HALO, 2 * STATE), F32)

    tok = tok_ref[0]
    side = dot_nn(tok, w_ref[:, wide:])
    raw_ref[0] = side[:, 2 * STATE :].T[0:heads]
    pz_ref[0, :, wide:] = side[:, : 2 * STATE].astype(BF)
    for p in range(pairs):
        pz_ref[0, :, 256 * p : 256 * p + 256] = dot_nn(tok, w_ref[:, 256 * p : 256 * p + 256]).astype(BF)

    def chunk_step(step, carry):
        here = pl.ds(pl.multiple_of(step * CHUNK, CHUNK), CHUNK)
        aux = aux_ref[0, :, here]
        raw = raw_ref[0, :, here]
        bc = pz_ref[0, here, wide:]
        dt, cum, carried, toward = pieces(raw, hp_ref[0], hp_ref[1], aux, tri_ref[...])
        cols = compact([aux, cum, dt, carried, toward])
        both = hi_lo(cols)
        dtx = dot_nn(both, expand[0])
        carx = dot_nn(both, expand[1])
        towx = dot_nn(both, expand[2])
        pad = cols[:, 1:2]
        same = [None] + [cols[:, 1 + k : 2 + k] for k in range(1, TAPS)]
        low = iota2((CHUNK, 128), 1) < HEADDIM

        bbuf[HALO:] = bc.astype(F32) * pad
        maps = cbw_ref[TAPS : TAPS + 1] + cbw_ref[0:1] * bbuf[HALO:]
        for k in range(1, TAPS):
            maps = maps + cbw_ref[k : k + 1] * (same[k] * bbuf[HALO - k : HALO - k + CHUNK])
        pbc_ref[0, here] = maps.astype(BF)
        maps = (maps * sigmoid(maps)).astype(BF)
        cbc_ref[0, here] = maps
        bbuf[0:HALO] = bbuf[CHUNK : CHUNK + HALO]
        keys, queries = maps[:, :STATE], maps[:, STATE:]
        scores = dot_nt(queries, keys)
        keys_t = keys.astype(F32).T.astype(BF)

        for p in range(pairs):
            s = slice(128 * p, 128 * p + 128)
            x0 = pz_ref[0, here, 256 * p : 256 * p + 128].astype(F32)
            x1 = pz_ref[0, here, 256 * p + 128 : 256 * p + 256].astype(F32)
            value = jnp.where(low, pltpu.roll(x0, HEADDIM, 1), x1)
            ubuf[HALO:, s] = value * pad
            pre = cw_ref[TAPS : TAPS + 1, s] + cw_ref[0:1, s] * ubuf[HALO:, s]
            for k in range(1, TAPS):
                pre = pre + cw_ref[k : k + 1, s] * (same[k] * ubuf[HALO - k : HALO - k + CHUNK, s])
            pre_ref[0, here, s] = pre.astype(BF)
            cv = (pre * sigmoid(pre)).astype(BF)
            cv_ref[0, here, s] = cv
            vd[:, s] = (cv.astype(F32) * dtx[:, s]).astype(BF)
        ubuf[0:HALO] = ubuf[CHUNK : CHUNK + HALO]

        old = state[...]
        old_b = old.astype(BF)
        st_ref[0, step] = old_b
        yint[...] = dot_nn(queries, old_b) * carx
        state[...] = carx[CHUNK - 1 : CHUNK] * old + dot_nn(keys_t, (vd[...].astype(F32) * towx).astype(BF))

        inside = (iota2((CHUNK, CHUNK), 0) >= iota2((CHUNK, CHUNK), 1)) & (cols[:, 0:1] == aux[0:1])
        fence = jnp.where(inside, 0.0, FAR)
        squares = jnp.zeros((CHUNK, 128), F32)
        for p in range(pairs):
            s = slice(128 * p, 128 * p + 128)
            mix = []
            for h in (2 * p, 2 * p + 1):
                decay = jnp.exp2(cols[:, AUX + h : AUX + h + 1] - cum[h : h + 1] + fence)
                mix.append((scores * decay).astype(BF))
            v = vd[:, s]
            zero = jnp.zeros_like(v)
            stacked = jnp.concatenate([jnp.where(low, v, zero), jnp.where(low, zero, v)], axis=0)
            y = dot_nn(jnp.concatenate(mix, axis=1), stacked)
            mixed = y + yint[:, s] + cw_ref[5:6, s] * cv_ref[0, here, s].astype(F32)
            x0 = pz_ref[0, here, 256 * p : 256 * p + 128].astype(F32)
            x1 = pz_ref[0, here, 256 * p + 128 : 256 * p + 256].astype(F32)
            gate = jnp.where(low, x0, pltpu.roll(x1, HEADDIM, 1))
            gated = mixed * (gate * sigmoid(gate))
            mixed_ref[0, here, s] = mixed.astype(BF)
            gated_ref[0, here, s] = (gated * cw_ref[6:7, s]).astype(BF)
            squares = squares + gated * gated
        lane = iota2((CHUNK, 128), 1)
        sums = jnp.where(lane == 0, jnp.sum(squares, axis=1, keepdims=True), 0.0)
        stat_ref[0, :, here] = sums.T[0:8]
        return carry

    lax.fori_loop(0, BLOCK // CHUNK, chunk_step, 0)


def backward_kernel(
    heads, pz_ref, raw_ref, aux_ref, cot_ref, mixed_ref, cv_ref, pre_ref, cbc_ref, pbc_ref,
    st_ref, stat_ref, cw_ref, cbw_ref, hp_ref, out_ref, w_ref, tok_ref,
    ge_ref, dg_ref, gch_ref, gmap_ref, ghead_ref, gpre_ref,
    g_s, dstate, cbuf, dbuf, vd, gm_s, gmc_s, ggate_s, cs_s, bs_s, expand, collect, tri_ref, suf_ref,
):
    inner = heads * HEADDIM
    pairs = heads // 2
    wide = 2 * inner
    first = (pl.program_id(0) == 0) & (pl.program_id(1) == 0)

    @pl.when(first)
    def _():
        for i, place in enumerate((AUX + heads, AUX + 2 * heads, AUX + 3 * heads)):
            expand[i] = expander(heads, inner, place)
        collect[0] = collector(inner, heads)
        collect[1] = collector(inner, 2 * heads)
        r, c = iota2((CHUNK, CHUNK), 0), iota2((CHUNK, CHUNK), 1)
        tri_ref[...] = jnp.where(r <= c, 1.0, 0.0).astype(BF)
        suf_ref[...] = jnp.where(r >= c, 1.0, 0.0).astype(BF)
        gch_ref[...] = jnp.zeros_like(gch_ref)
        gmap_ref[...] = jnp.zeros_like(gmap_ref)
        ghead_ref[...] = jnp.zeros_like(ghead_ref)
        gpre_ref[...] = jnp.zeros_like(gpre_ref)

    @pl.when(pl.program_id(1) == 0)
    def _():
        dstate[...] = jnp.zeros_like(dstate)
        cbuf[CHUNK:] = jnp.zeros((HALO, inner), F32)
        dbuf[CHUNK:] = jnp.zeros((HALO, 2 * STATE), F32)

    g_s[...] = dot_nn(cot_ref[0], out_ref[...])

    def chunk_step(step, carry):
        here = pl.ds(pl.multiple_of(BLOCK - CHUNK - step * CHUNK, CHUNK), CHUNK)
        aux = aux_ref[0, :, here]
        rate = hp_ref[1]
        dt, cum, carried, toward = pieces(raw_ref[0, :, here], hp_ref[0], rate, aux, tri_ref[...])
        cols = compact([aux, cum, dt, carried, toward, stat_ref[0, :, here]])
        both = hi_lo(cols)
        dtx = dot_nn(both, expand[0])
        carx = dot_nn(both, expand[1])
        towx = dot_nn(both, expand[2])
        pad = cols[:, 1:2]
        ahead = [None] + [cols[:, 7 + k : 8 + k] for k in range(1, TAPS)]
        base = AUX + 4 * heads
        rms, pull = cols[:, base : base + 1], cols[:, base + 1 : base + 2]
        low = iota2((CHUNK, 128), 1) < HEADDIM
        maps = cbc_ref[0, here]
        keys, queries = maps[:, :STATE], maps[:, STATE:]
        queries_t = queries.astype(F32).T.astype(BF)
        scores_t = dot_nt(keys, queries)

        for p in range(pairs):
            s = slice(128 * p, 128 * p + 128)
            x0 = pz_ref[0, here, 256 * p : 256 * p + 128].astype(F32)
            x1 = pz_ref[0, here, 256 * p + 128 : 256 * p + 256].astype(F32)
            gate = jnp.where(low, x0, pltpu.roll(x1, HEADDIM, 1))
            sig = sigmoid(gate)
            act = gate * sig
            mixed = mixed_ref[0, here, s].astype(F32)
            gated = mixed * act
            g = g_s[here, s]
            grad_gated = rms * (g * cw_ref[6:7, s]) - gated * pull
            gm = grad_gated * act
            ggate_s[:, s] = (grad_gated * mixed * (sig * (1.0 + gate * (1.0 - sig)))).astype(BF)
            gm_s[:, s] = gm.astype(BF)
            gmc_s[:, s] = (gm * carx[:, s]).astype(BF)
            cv = cv_ref[0, here, s].astype(F32)
            vd[:, s] = (cv * dtx[:, s]).astype(BF)
            gch_ref[5:6, s] += jnp.sum(gm * cv, axis=0, keepdims=True)
            gch_ref[6:7, s] += jnp.sum(gated * rms * g, axis=0, keepdims=True)

        ds = dstate[...]
        ds_b = ds.astype(BF)
        st = st_ref[0, BLOCK // CHUNK - 1 - step]
        gmc = gmc_s[...]
        cs = dot_nn(queries, st)
        bs = dot_nn(keys, ds_b) * towx
        bs_s[...] = bs
        reach = dot_nn((gmc.astype(F32) * cs).astype(BF), collect[1])
        reach = reach + dot_nn((bs * cv_ref[0, here].astype(F32)).astype(BF), collect[0])
        grad_q = dot_nt(gmc, st)
        grad_k = dot_nt((vd[...].astype(F32) * towx).astype(BF), ds_b)
        keep = carx[CHUNK - 1 : CHUNK]
        held = jnp.sum(st.astype(F32) * ds, axis=0, keepdims=True) * keep
        dstate[...] = keep * ds + dot_nn(queries_t, gmc)

        inside = (iota2((CHUNK, CHUNK), 0) <= iota2((CHUNK, CHUNK), 1)) & (cols[:, 0:1] == aux[0:1])
        fence = jnp.where(inside, 0.0, FAR)
        grad_scores_t = jnp.zeros((CHUNK, CHUNK), F32)
        lane = iota2((CHUNK, 128), 1)
        gathered = reach
        row_sums = []
        for p in range(pairs):
            s = slice(128 * p, 128 * p + 128)
            gm_b = gm_s[:, s]
            zero = jnp.zeros_like(gm_b)
            gm_two = jnp.concatenate([jnp.where(low, gm_b, zero), jnp.where(low, zero, gm_b)], axis=0)
            near = dot_nt(vd[:, s], gm_two)
            mix = []
            for j in range(2):
                h = 2 * p + j
                decay = jnp.exp2(cum[h : h + 1] - cols[:, AUX + h : AUX + h + 1] + fence)
                mix.append((scores_t * decay).astype(BF))
                weighed = decay * near[:, CHUNK * j : CHUNK * j + CHUNK]
                grad_scores_t = grad_scores_t + weighed
                pairs_g = weighed * scores_t
                row_sums.append(jnp.sum(pairs_g, axis=0, keepdims=True))
                gathered = jnp.where(lane == h, jnp.sum(pairs_g, axis=1, keepdims=True), gathered)
            z = dot_nn(jnp.concatenate(mix, axis=1), gm_two)
            gm = gm_b.astype(F32)
            grad_v = cw_ref[5:6, s] * gm + dtx[:, s] * (z + bs_s[:, s])
            x0 = pz_ref[0, here, 256 * p : 256 * p + 128].astype(F32)
            x1 = pz_ref[0, here, 256 * p + 128 : 256 * p + 256].astype(F32)
            u = jnp.where(low, pltpu.roll(x0, HEADDIM, 1), x1) * pad
            pre = pre_ref[0, here, s].astype(F32)
            sig = sigmoid(pre)
            c = grad_v * (sig * (1.0 + pre * (1.0 - sig)))
            cbuf[0:CHUNK, s] = c
            gu = cw_ref[0:1, s] * c
            gch_ref[4:5, s] += jnp.sum(c, axis=0, keepdims=True)
            gch_ref[0:1, s] += jnp.sum(c * u, axis=0, keepdims=True)
            for k in range(1, TAPS):
                shifted = ahead[k] * cbuf[k : k + CHUNK, s]
                gu = gu + cw_ref[k : k + 1, s] * shifted
                gch_ref[k : k + 1, s] += jnp.sum(shifted * u, axis=0, keepdims=True)
            gu = gu * pad
            ggate = ggate_s[:, s].astype(F32)
            ge_ref[0, here, 256 * p : 256 * p + 128] = jnp.where(low, ggate, pltpu.roll(gu, HEADDIM, 1)).astype(BF)
            ge_ref[0, here, 256 * p + 128 : 256 * p + 256] = jnp.where(low, pltpu.roll(ggate, HEADDIM, 1), gu).astype(BF)
        cbuf[CHUNK:] = cbuf[0:HALO]

        gst = grad_scores_t.astype(BF)
        grad_k = grad_k + dot_nn(gst, queries)
        grad_q = grad_q + dot_nn(grad_scores_t.T.astype(BF), keys)
        pbc = pbc_ref[0, here].astype(F32)
        sig = sigmoid(pbc)
        c = jnp.concatenate([grad_k, grad_q], axis=1) * (sig * (1.0 + pbc * (1.0 - sig)))
        dbuf[0:CHUNK] = c
        u = pz_ref[0, here, wide:].astype(F32) * pad
        gu = cbw_ref[0:1] * c
        gmap_ref[4:5] += jnp.sum(c, axis=0, keepdims=True)
        gmap_ref[0:1] += jnp.sum(c * u, axis=0, keepdims=True)
        for k in range(1, TAPS):
            shifted = ahead[k] * dbuf[k : k + CHUNK]
            gu = gu + cbw_ref[k : k + 1] * shifted
            gmap_ref[k : k + 1] += jnp.sum(shifted * u, axis=0, keepdims=True)
        ge_ref[0, here, wide : wide + 2 * STATE] = (gu * pad).astype(BF)
        dbuf[CHUNK:] = dbuf[0:HALO]

        across = gathered.T
        col_sum = across[0:heads]
        kx = across[heads : 2 * heads]
        rint = across[2 * heads : 3 * heads]
        row_sum = jnp.concatenate(row_sums, axis=0)
        k_all = kx * dt
        held_head = exact_dot(jnp.broadcast_to(held, (16, inner)), collect[0])
        held_col = jnp.broadcast_to(held_head[0:1], (CHUNK, 128)).T[heads : 2 * heads]
        diff = row_sum + rint - col_sum - k_all
        grad_a = exact_dot(diff, suf_ref[...]) + jnp.sum(k_all, axis=1, keepdims=True) + held_col
        direct = jnp.where(dt > 0.0, col_sum / jnp.where(dt > 0.0, dt, 1.0), 0.0)
        grad_dt = direct + kx + rate * grad_a
        graw = grad_dt * aux[1:2] * sigmoid(raw_ref[0, :, here] + hp_ref[0])
        ge_ref[0, here, wide + 2 * STATE :] = compact([graw]).astype(BF)
        ghead_ref[0] += graw
        ghead_ref[1] += rate * dt * grad_a
        return carry

    lax.fori_loop(0, BLOCK // CHUNK, chunk_step, 0)
    dg = dot_nt(ge_ref[0], w_ref[...])
    dg_ref[0] = dg.astype(BF)
    gpre_ref[0:1] += jnp.sum(dg * tok_ref[0].astype(F32), axis=0, keepdims=True)


def whole_once(*shape):
    return pl.BlockSpec(shape, lambda s, c: (0,) * len(shape), pipeline_mode=pl.Buffered(1))


def mixer_forward(tok, weights, aux, cw, cbw, hp):
    seqs, length, width = tok.shape
    heads, inner = hp.shape[1], cw.shape[1]
    wide = 2 * inner + 2 * STATE
    chunks = length // CHUNK
    token = lambda size: pl.BlockSpec((1, BLOCK, size), lambda s, c: (s, c, 0))
    row = lambda high: pl.BlockSpec((1, high, BLOCK), lambda s, c: (s, 0, c))
    sds = jax.ShapeDtypeStruct
    return pl.pallas_call(
        functools.partial(forward_kernel, heads),
        grid=(seqs, length // BLOCK),
        in_specs=[
            token(width), whole_once(*weights.shape), row(AUX),
            whole_once(8, inner), whole_once(8, 2 * STATE), whole_once(2, heads, 128),
        ],
        out_specs=[
            token(wide), row(heads), token(inner), token(inner), token(inner), token(inner), token(2 * STATE),
            token(2 * STATE), pl.BlockSpec((1, BLOCK // CHUNK, STATE, inner), lambda s, c: (s, c, 0, 0)), row(8),
        ],
        out_shape=[
            sds((seqs, length, wide), BF), sds((seqs, heads, length), F32),
            sds((seqs, length, inner), BF), sds((seqs, length, inner), BF), sds((seqs, length, inner), BF),
            sds((seqs, length, inner), BF), sds((seqs, length, 2 * STATE), BF), sds((seqs, length, 2 * STATE), BF),
            sds((seqs, chunks, STATE, inner), BF), sds((seqs, 8, length), F32),
        ],
        scratch_shapes=[
            pltpu.VMEM((STATE, inner), F32), pltpu.VMEM((HALO + CHUNK, inner), F32),
            pltpu.VMEM((HALO + CHUNK, 2 * STATE), F32), pltpu.VMEM((CHUNK, inner), BF),
            pltpu.VMEM((CHUNK, inner), F32), pltpu.VMEM((3, 256, inner), BF), pltpu.VMEM((CHUNK, CHUNK), BF),
        ],
        compiler_params=pltpu.CompilerParams(vmem_limit_bytes=VMEM_LIMIT),
        name="mixer_forward",
    )(tok, weights, aux, cw, cbw, hp)


def mixer_backward(pz, raw, aux, cot, mixed, cv, pre, cbc, pbc, st, stat, cw, cbw, hp, out_all, weights, tok):
    seqs, length, width = cot.shape
    heads, inner = hp.shape[1], cw.shape[1]
    last = length // BLOCK - 1
    token = lambda size: pl.BlockSpec((1, BLOCK, size), lambda s, c: (s, last - c, 0))
    row = lambda high: pl.BlockSpec((1, high, BLOCK), lambda s, c: (s, 0, last - c))
    whole = lambda *shape: pl.BlockSpec(shape, lambda s, c: (0,) * len(shape))
    sds = jax.ShapeDtypeStruct
    return pl.pallas_call(
        functools.partial(backward_kernel, heads),
        grid=(seqs, length // BLOCK),
        in_specs=[
            token(pz.shape[2]), row(heads), row(AUX), token(width), token(inner), token(inner),
            token(inner), token(2 * STATE), token(2 * STATE),
            pl.BlockSpec((1, BLOCK // CHUNK, STATE, inner), lambda s, c: (s, last - c, 0, 0)), row(8),
            whole_once(8, inner), whole_once(8, 2 * STATE), whole_once(2, heads, 128),
            whole_once(*out_all.shape), whole_once(*weights.shape), token(width),
        ],
        out_specs=[
            token(weights.shape[1]), token(width),
            whole(8, inner), whole(8, 2 * STATE), whole(2, heads, 128), whole(8, width),
        ],
        out_shape=[
            sds((seqs, length, weights.shape[1]), BF), sds((seqs, length, width), BF),
            sds((8, inner), F32), sds((8, 2 * STATE), F32), sds((2, heads, 128), F32), sds((8, width), F32),
        ],
        scratch_shapes=[
            pltpu.VMEM((BLOCK, inner), F32),
            pltpu.VMEM((STATE, inner), F32), pltpu.VMEM((CHUNK + HALO, inner), F32),
            pltpu.VMEM((CHUNK + HALO, 2 * STATE), F32), pltpu.VMEM((CHUNK, inner), BF),
            pltpu.VMEM((CHUNK, inner), BF), pltpu.VMEM((CHUNK, inner), BF), pltpu.VMEM((CHUNK, inner), BF),
            pltpu.VMEM((CHUNK, inner), F32), pltpu.VMEM((CHUNK, inner), F32),
            pltpu.VMEM((3, 256, inner), BF), pltpu.VMEM((2, inner, 128), BF),
            pltpu.VMEM((CHUNK, CHUNK), BF), pltpu.VMEM((CHUNK, CHUNK), BF),
        ],
        compiler_params=pltpu.CompilerParams(vmem_limit_bytes=VMEM_LIMIT),
        name="mixer_backward",
    )(pz, raw, aux, cot, mixed, cv, pre, cbc, pbc, st, stat, cw, cbw, hp, out_all, weights, tok)


def out_kernel(gn_ref, cot_ref, out_ref, stat_ref, y_ref, stat_out_ref):
    y = dot_nt(gn_ref[0], out_ref[...])
    y_ref[0] = y.astype(BF)
    cross = jnp.sum(y * cot_ref[0].astype(F32), axis=1, keepdims=True)
    row = jnp.broadcast_to(cross, (cross.shape[0], 128)).T[0:8]
    stat_out_ref[0] = jnp.where(iota2(row.shape, 0) == 1, row, stat_ref[0])


def out_project(gn, cot, out_all, stat):
    seqs, length, inner = gn.shape
    width = cot.shape[2]
    size = 256
    token = lambda last: pl.BlockSpec((1, size, last), lambda s, c: (s, c, 0))
    row = pl.BlockSpec((1, 8, size), lambda s, c: (s, 0, c))
    sds = jax.ShapeDtypeStruct
    return pl.pallas_call(
        out_kernel,
        grid=(seqs, length // size),
        in_specs=[token(inner), token(width), whole_once(*out_all.shape), row],
        out_specs=[token(width), row],
        out_shape=[sds((seqs, length, width), BF), sds((seqs, 8, length), F32)],
        compiler_params=pltpu.CompilerParams(vmem_limit_bytes=VMEM_LIMIT),
        name="out_project",
    )(gn, cot, out_all, stat)


def doc_flags(segment, pad_mask):
    seqs, length = segment.shape
    position = lax.broadcasted_iota(jnp.int32, segment.shape, 1)
    rows = [segment.astype(F32), pad_mask.astype(F32)]
    back = []
    for k in range(1, TAPS):
        earlier = jnp.pad(segment, ((0, 0), (k, 0)), constant_values=-1)[:, :length]
        back.append(earlier == segment)
    rows += [b.astype(F32) for b in back]
    blocks = segment.reshape(seqs, length // CHUNK, CHUNK)
    tail = blocks[:, :, CHUNK - 1 :]
    previous = jnp.pad(tail, ((0, 0), (1, 0), (0, 0)), constant_values=-1)[:, :-1]
    rows.append((blocks == previous).reshape(seqs, length).astype(F32))
    rows.append((blocks == tail).reshape(seqs, length).astype(F32))
    rows.append(jnp.zeros_like(rows[0]))
    for k in range(1, TAPS):
        later = jnp.pad(segment, ((0, 0), (0, k)), constant_values=-1)[:, k:]
        rows.append((later == segment).astype(F32))
    rows += [jnp.zeros_like(rows[0])] * (AUX - len(rows))
    return jnp.stack(rows, axis=1)


MESH = pl.DeviceIdType.MESH


def factors(size):
    first = 4 if size % 8 == 0 else 1
    return first, size // (2 * first)


def gather_sites(first, second):
    return (2 + second) + (first - 1) * 2 * (1 + second) + (2 * first - 1) * (second - 1)


def gather_kernel(first, second, pair, arrays, *refs):
    own = refs[:arrays]
    tok = refs[arrays]
    full = refs[arrays + 1 : 2 * arrays + 1]
    tok_full = refs[2 * arrays + 1]
    send_sem, recv_sem, local_sem, tok_sem = refs[2 * arrays + 2 :]
    index = lax.axis_index("dp")
    me = lax.axis_index("tensor")
    a = lax.div(index, 2 * second)
    b = lax.rem(lax.div(index, 2), second)
    c = lax.rem(index, 2)
    at = lambda i, j, k: (i * second + j) * 2 + k
    sibling = at(a, b, 1 - c)
    has_up, has_down = a < first - 1, a > 0

    barrier = pltpu.get_barrier_semaphore()
    greet = lambda dp, t: pl.semaphore_signal(barrier, inc=1, device_id=(dp, t), device_id_type=MESH)
    greet(sibling, me)
    for j in range(1, second):
        greet(at(a, lax.rem(b + j, second), c), me)
    for i in range(1, first):
        greet(at(lax.rem(a + i, first), b, c), me)
    if pair:
        greet(index, 1 - me)
    pl.semaphore_wait(barrier, first + second - 1 + (1 if pair else 0))

    def place(which, shard):
        rows = own[which].shape[0]
        return full[which].at[pl.ds(pl.multiple_of(shard * rows, rows), rows)]

    def copies(site, shard, target, mine):
        return [
            pltpu.make_async_remote_copy(
                src_ref=own[w] if mine else place(w, shard),
                dst_ref=place(w, shard),
                send_sem=send_sem.at[w, site],
                recv_sem=recv_sem.at[w, shard],
                device_id=(target, me),
                device_id_type=MESH,
            )
            for w in range(arrays)
        ]

    sites = []

    def send(valid, shard, target, mine=False):
        site = len(sites)
        sites.append((valid, shard, target, mine))

        def start():
            for copy in copies(site, shard, target, mine):
                copy.start()

        start() if valid is None else pl.when(valid)(start)

    def arrived(shard):
        for copy in copies(0, shard, sibling, False):
            copy.wait_recv()

    def both(left, right):
        return right if left is None else left & right

    if pair:
        here = tok.shape[1]
        token_copy = pltpu.make_async_remote_copy(
            src_ref=tok,
            dst_ref=tok_full.at[:, pl.ds(pl.multiple_of(me * here, here), here)],
            send_sem=tok_sem.at[0],
            recv_sem=tok_sem.at[1],
            device_id=(index, 1 - me),
            device_id_type=MESH,
        )
        token_copy.start()
        token_local = pltpu.make_async_copy(
            tok, tok_full.at[:, pl.ds(pl.multiple_of(me * here, here), here)], tok_sem.at[2]
        )
        token_local.start()
    send(has_up, index, at(a + 1, b, c), True)
    send(has_down, index, at(a - 1, b, c), True)
    for j in range(1, second):
        send(None, index, at(a, lax.rem(b + j, second), c), True)
    send(None, index, sibling, True)
    local = [pltpu.make_async_copy(own[w], place(w, index), local_sem.at[w]) for w in range(arrays)]
    for copy in local:
        copy.start()

    steps = [(None, index)]
    for s in range(1, first):
        below, above = a - s >= 0, a + s < first
        steps += [(below, a - s), (above, a + s)]
        for valid, other, onward, target in (
            (below, a - s, has_up, at(a + 1, b, c)),
            (above, a + s, has_down, at(a - 1, b, c)),
        ):
            shard = at(other, b, c)
            pl.when(valid)(functools.partial(arrived, shard))
            send(valid & onward, shard, target)
            for j in range(1, second):
                send(valid, shard, at(a, lax.rem(b + j, second), c))
            send(valid, shard, sibling)
    for j in range(1, second):
        column = lax.rem(b + j, second)
        for s, (valid, other) in enumerate(steps):
            shard = at(a if s == 0 else other, column, c)
            arrived(shard) if valid is None else pl.when(valid)(functools.partial(arrived, shard))
            send(valid, shard, sibling)
    for i in range(first):
        for j in range(second):
            arrived(at(i, j, 1 - c))
    for site, (valid, shard, target, mine) in enumerate(sites):

        def finish(site=site, shard=shard, target=target, mine=mine):
            for copy in copies(site, shard, target, mine):
                copy.wait_send()

        finish() if valid is None else pl.when(valid)(finish)
    for copy in local:
        copy.wait()
    if pair:
        token_copy.wait()
        token_local.wait()


def gather_all(shards, tokens, size, n):
    first, second = factors(size)
    pair = n == 2
    arrays = len(shards)
    any_space = pl.BlockSpec(memory_space=pl.ANY)
    sds = jax.ShapeDtypeStruct
    seqs, here, width = tokens.shape
    out_shape = [sds((size * s.shape[0], s.shape[1]), s.dtype) for s in shards]
    out_shape.append(sds((seqs, 2 * here, width) if pair else (8, 128), tokens.dtype))
    *full, tok_full = pl.pallas_call(
        functools.partial(gather_kernel, first, second, pair, arrays),
        in_specs=[any_space] * arrays + [pl.BlockSpec(memory_space=pltpu.VMEM)],
        out_specs=[any_space] * (arrays + 1),
        out_shape=out_shape,
        scratch_shapes=[
            pltpu.SemaphoreType.DMA((arrays, gather_sites(first, second))),
            pltpu.SemaphoreType.DMA((arrays, size)),
            pltpu.SemaphoreType.DMA((arrays,)),
            pltpu.SemaphoreType.DMA((3,)),
        ],
        compiler_params=pltpu.CompilerParams(collective_id=0, has_side_effects=True),
        name="gather_all",
    )(*shards, tokens)
    return full, tok_full if pair else lax.all_gather(tokens, "tensor", axis=1, tiled=True)


def reduce_kernel(
    first, second, pair, shared, part_ref, flat_ref, out_ref, sum_ref,
    core_buf, x_buf, z_buf, y_flat, core_flat, x_flat, z_flat, stage,
    core_send, core_recv, x_send, x_recv, z_send, z_recv, flat_send, flat_recv,
):
    index = lax.axis_index("dp")
    me = lax.axis_index("tensor")
    a = lax.div(index, 2 * second)
    b = lax.rem(lax.div(index, 2), second)
    c = lax.rem(index, 2)
    rows = out_ref.shape[0]
    at = lambda i, j, k: (i * second + j) * 2 + k
    around = lambda i: lax.rem(a + i, first)
    aside = lambda j: lax.rem(b + j, second)
    sibling = at(a, b, 1 - c)
    columns = [at(a, aside(j), c) for j in range(1, second)]
    lines = [at(around(i), b, c) for i in range(1, first)]

    barrier = pltpu.get_barrier_semaphore()
    greet = lambda dp, t: pl.semaphore_signal(barrier, inc=1, device_id=(dp, t), device_id_type=MESH)
    for other in [sibling] + columns + lines:
        greet(other, me)
    if pair:
        greet(index, 1 - me)
    pl.semaphore_wait(barrier, first + second - 1 + (1 if pair else 0))

    started = []

    def send(src, dst, ss, rs, target, tensor=me):
        copy = pltpu.make_async_remote_copy(
            src_ref=src, dst_ref=dst, send_sem=ss, recv_sem=rs, device_id=(target, tensor), device_id_type=MESH
        )
        copy.start()
        started.append(copy)

    def arrived(dst, rs):
        pltpu.make_async_remote_copy(
            src_ref=dst, dst_ref=dst, send_sem=core_send.at[0], recv_sem=rs,
            device_id=(sibling, me), device_id_type=MESH,
        ).wait_recv()

    def block(i, j, k):
        return part_ref.at[pl.ds(pl.multiple_of(at(i, j, k) * rows, rows), rows)]

    order = [around(i) for i in range(1, first)] + [a]
    slot = lambda i, j: i * second + j
    if pair:
        send(flat_ref.at[0:shared], y_flat, flat_send.at[0], flat_recv.at[0], index, 1 - me)
    for j in list(range(1, second)) + [0]:
        for i in order:
            s = slot(i, aside(j))
            send(block(i, aside(j), 1 - c), core_buf.at[s], core_send.at[s], core_recv.at[s], sibling)
    if pair:
        arrived(y_flat, flat_recv.at[0])
        stage[0, 0:shared] = flat_ref[0:shared] + y_flat[...]
    else:
        stage[0, 0:shared] = flat_ref[0:shared]
    stage[0, shared:] = flat_ref[shared:]
    send(stage.at[0], core_flat, flat_send.at[1], flat_recv.at[1], sibling)
    for j in range(1, second):
        for i in order:
            s = slot(i, aside(j))
            arrived(core_buf.at[s], core_recv.at[s])
            core_buf[s] = (block(i, aside(j), c)[...].astype(F32) + core_buf[s].astype(F32)).astype(BF)
            t = i * (second - 1) + (second - j - 1)
            send(core_buf.at[s], x_buf.at[t], x_send.at[i * (second - 1) + j - 1], x_recv.at[t], at(a, aside(j), c))
    arrived(core_flat, flat_recv.at[1])
    stage[1] = stage[0] + core_flat[...]
    x_flat[b] = stage[1]
    for j in range(1, second):
        send(stage.at[1], x_flat.at[b], flat_send.at[1 + j], flat_recv.at[2 + b], at(a, aside(j), c))
    for n, i in enumerate(order):
        s = slot(i, b)
        arrived(core_buf.at[s], core_recv.at[s])
        total = block(i, b, c)[...].astype(F32) + core_buf[s].astype(F32)
        for j in range(1, second):
            t = i * (second - 1) + j - 1
            arrived(x_buf.at[t], x_recv.at[t])
            total = total + x_buf[t].astype(F32)
        if n < first - 1:
            core_buf[s] = total.astype(BF)
            send(core_buf.at[s], z_buf.at[a], z_send.at[n], z_recv.at[a], at(i, b, c))
        else:
            out_ref[...] = total
    for j in range(1, second):
        arrived(x_flat.at[aside(j)], flat_recv.at[2 + aside(j)])
    total = x_flat[0]
    for j in range(1, second):
        total = total + x_flat[j]
    stage[2] = total
    z_flat[a] = total
    for i in range(1, first):
        send(stage.at[2], z_flat.at[a], flat_send.at[second + i], flat_recv.at[2 + second + a], at(around(i), b, c))
    for i in range(1, first):
        arrived(z_buf.at[around(i)], z_recv.at[around(i)])
        out_ref[...] = out_ref[...] + z_buf[around(i)].astype(F32)
    for i in range(1, first):
        arrived(z_flat.at[around(i)], flat_recv.at[2 + second + around(i)])
    total = z_flat[0]
    for i in range(1, first):
        total = total + z_flat[i]
    sum_ref[...] = total
    for copy in started:
        copy.wait_send()


def reduce_all(part, flat, shared, size, n):
    first, second = factors(size)
    pair = n == 2
    if not pair:
        flat = jnp.concatenate([lax.psum(flat[:shared], "tensor"), flat[shared:]])
    rows, width = part.shape[0] // size, part.shape[1]
    sds = jax.ShapeDtypeStruct
    vmem = pl.BlockSpec(memory_space=pltpu.VMEM)
    blocks = first * second
    return pl.pallas_call(
        functools.partial(reduce_kernel, first, second, pair, shared),
        in_specs=[vmem, vmem],
        out_specs=[vmem, vmem],
        out_shape=[sds((rows, width), F32), sds(flat.shape, F32)],
        scratch_shapes=[
            pltpu.VMEM((blocks, rows, width), BF),
            pltpu.VMEM((first * max(second - 1, 1), rows, width), BF),
            pltpu.VMEM((first, rows, width), BF),
            pltpu.VMEM((shared, flat.shape[1]), F32),
            pltpu.VMEM(flat.shape, F32),
            pltpu.VMEM((second,) + flat.shape, F32),
            pltpu.VMEM((first,) + flat.shape, F32),
            pltpu.VMEM((3,) + flat.shape, F32),
            pltpu.SemaphoreType.DMA((blocks,)),
            pltpu.SemaphoreType.DMA((blocks,)),
            pltpu.SemaphoreType.DMA((first * max(second - 1, 1),)),
            pltpu.SemaphoreType.DMA((first * max(second - 1, 1),)),
            pltpu.SemaphoreType.DMA((first,)),
            pltpu.SemaphoreType.DMA((first,)),
            pltpu.SemaphoreType.DMA((1 + first + second,)),
            pltpu.SemaphoreType.DMA((2 + first + second,)),
        ],
        compiler_params=pltpu.CompilerParams(collective_id=1, has_side_effects=True, vmem_limit_bytes=VMEM_LIMIT),
        name="reduce_all",
    )(part, flat)


def gather_tokens(own, n, me):
    if n != 2:
        return lax.all_gather(own, "tensor", axis=1, tiled=True)
    other = lax.ppermute(own, "tensor", [(0, 1), (1, 0)])
    seqs, here, width = own.shape
    full = jnp.zeros((seqs, 2 * here, width), own.dtype)
    full = lax.dynamic_update_slice(full, own, (0, me * here, 0))
    return lax.dynamic_update_slice(full, other, (0, (1 - me) * here, 0))


def scatter_sum(make, size, n, me, dim):
    if n != 2:
        blocks = [make(i * size) for i in range(n)]
        return lax.psum_scatter(jnp.concatenate(blocks, axis=dim), "tensor", scatter_dimension=dim, tiled=True)
    away = lax.ppermute(make((1 - me) * size).astype(BF), "tensor", [(0, 1), (1, 0)])
    return make(me * size) + away.astype(F32)


def swap_sum(value, n):
    if n != 2:
        return lax.psum(value, "tensor")
    return value + lax.ppermute(value, "tensor", [(0, 1), (1, 0)])


def body(
    hidden, pre_gain, zx_weight, bc_weight, step_weight, conv_x_weight, conv_x_bias, conv_bc_weight, conv_bc_bias,
    step_bias, decay_log, skip_gain, norm_gain, out_weight, segment_ids, pad_mask, grad_out,
):
    n = lax.axis_size("tensor")
    me = lax.axis_index("tensor")
    heads = step_weight.shape[1]
    inner = heads * HEADDIM
    inner_all = inner * n
    here = hidden.shape[1]
    width = hidden.shape[2]
    size = lax.axis_size("dp")
    hidden_f = hidden.astype(F32)
    inv_rms = lax.rsqrt(jnp.mean(hidden_f * hidden_f, axis=-1, keepdims=True) + epsilon)
    normed_own = (hidden_f * inv_rms * pre_gain).astype(BF)
    shard = jnp.concatenate(
        [zx_weight, bc_weight, step_weight, jnp.zeros((zx_weight.shape[0], 128 - heads), BF)], axis=1
    )
    (weights,), normed = gather_all([shard], normed_own, size, n)
    out_own, cot_own, normed = lax.optimization_barrier((out_weight.T, grad_out, normed))
    out_all = lax.all_gather(out_own, "dp", axis=0, tiled=True)
    cot = gather_tokens(cot_own, n, me)

    aux = doc_flags(segment_ids, pad_mask)
    cw = jnp.concatenate(
        [conv_x_weight, conv_x_bias[None], jnp.repeat(skip_gain, HEADDIM)[None], norm_gain[None], jnp.zeros((1, inner), F32)]
    )
    cbw = jnp.concatenate([conv_bc_weight, conv_bc_bias[None], jnp.zeros((3, 2 * STATE), F32)])
    rate = -jnp.exp(decay_log)
    hp = jnp.broadcast_to(jnp.stack([step_bias, rate])[:, :, None], (2, heads, 128))

    pz, raw, mixed, gn, cv, pre, cbc, pbc, st, stat = mixer_forward(normed, weights, aux, cw, cbw, hp)
    y, stat = out_project(gn, cot, out_all, stat)
    stat = swap_sum(stat, n)
    gate_rms = lax.rsqrt(stat[:, 0] / inner_all + epsilon)
    back = jnp.stack([gate_rms, gate_rms**3 * (stat[:, 1] / inner_all)] + [jnp.zeros_like(gate_rms)] * 6, axis=1)
    y, back = lax.optimization_barrier((y, back))

    part = lambda rows: lambda start: lax.dynamic_slice_in_dim(rows, start, here, axis=1).astype(F32)
    rms_own = lax.dynamic_slice_in_dim(gate_rms, me * here, here, axis=1)[..., None]
    output = (hidden_f + rms_own * scatter_sum(part(y), here, n, me, 1)).astype(BF)
    cot_scaled = (cot.astype(F32) * gate_rms[..., None]).astype(BF)
    out_grad = jnp.einsum("str,stc->rc", cot_scaled, gn, preferred_element_type=F32).astype(BF)
    grad_out_weight = lax.psum_scatter(out_grad, "dp", scatter_dimension=0, tiled=True).astype(F32).T

    ge, dg, gch, gmap, ghead, gpre = mixer_backward(
        pz, raw, aux, cot, mixed, cv, pre, cbc, pbc, st, back, cw, cbw, hp, out_all, weights, normed
    )
    grad_normed = scatter_sum(part(dg), here, n, me, 1)
    weight_grad = jnp.einsum("stp,sty->py", normed, ge, preferred_element_type=F32).astype(BF)

    def rows_of(*vectors):
        flat = jnp.concatenate([v.reshape(-1) for v in vectors])
        rows = -(-flat.shape[0] // 8192) * 8
        return jnp.pad(flat, (0, rows * 1024 - flat.shape[0])).reshape(rows, 1024)

    shared = rows_of(gmap[:5], gpre[0] / pre_gain)
    skip_sums = jnp.sum(gch[5].reshape(heads, HEADDIM), axis=-1)
    flat = jnp.concatenate([shared, rows_of(gch[:5], gch[6], jnp.sum(ghead, axis=-1), skip_sums)])
    own_rows, flat = reduce_all(weight_grad, flat, shared.shape[0], size, n)
    wide = 2 * inner
    grad_zx_weight = own_rows[:, :wide]
    grad_step_weight = own_rows[:, wide + 2 * STATE :][:, :heads]
    grad_bc_weight = swap_sum(own_rows[:, wide : wide + 2 * STATE], n)

    gain_grad = grad_normed * pre_gain
    grad_hidden = (
        grad_out.astype(F32)
        + inv_rms * gain_grad
        - hidden_f * inv_rms**3 * jnp.mean(hidden_f * gain_grad, axis=-1, keepdims=True)
    ).astype(BF)

    sums = flat[: shared.shape[0]].reshape(-1)
    shared_map = sums[: 5 * 2 * STATE].reshape(5, 2 * STATE)
    grad_pre = sums[5 * 2 * STATE :][:width]
    rest = flat[shared.shape[0] :].reshape(-1)
    channel = rest[: 6 * inner].reshape(6, inner)
    per_head = rest[6 * inner :][: 3 * heads].reshape(3, heads)
    return (
        output, grad_hidden, grad_pre, grad_zx_weight, grad_bc_weight, grad_step_weight,
        channel[:4], channel[4], shared_map[:4], shared_map[4], per_head[0], per_head[1], per_head[2],
        channel[5], grad_out_weight,
    )


def solution(mesh):
    placed = (
        P("dp", "tensor", None), P(), P("dp", "tensor"), P("dp", None), P("dp", "tensor"), P(None, "tensor"),
        P("tensor"), P(), P(), P("tensor"), P("tensor"), P("tensor"), P("tensor"), P("tensor", "dp"),
        P("dp", None), P("dp", None), P("dp", "tensor", None),
    )
    return jax.shard_map(
        body,
        mesh=mesh,
        in_specs=placed,
        out_specs=(
            P("dp", "tensor", None), P("dp", "tensor", None), P(), P("dp", "tensor"), P("dp", None), P("dp", "tensor"),
            P(None, "tensor"), P("tensor"), P(), P(), P("tensor"), P("tensor"), P("tensor"), P("tensor"),
            P("tensor", "dp"),
        ),
        check_vma=False,
    )
```

```python
import functools
import jax
import jax.numpy as jnp
from jax import lax
from jax.experimental import pallas as pl
from jax.experimental.pallas import tpu as pltpu
from jax.sharding import PartitionSpec as P

HEADDIM = 64
STATE = 128
CHUNK = 128
TAPS = 4
HALO = 8
AUX = 16
LOG2E = 1.4426950408889634
FAR = -1e30
BLOCK = 256
VMEM_LIMIT = 58 * 1024 * 1024
epsilon = 1e-05
BF = jnp.bfloat16
F32 = jnp.float32


def sigmoid(v):
    return 0.5 * jnp.tanh(0.5 * v) + 0.5


def split3(v):
    a = v.astype(BF)
    r = v - a.astype(F32)
    b = r.astype(BF)
    c = (r - b.astype(F32)).astype(BF)
    return a, b, c


def dot_nn(a, b):
    return lax.dot_general(a, b, (((1,), (0,)), ((), ())), preferred_element_type=F32)


def dot_nt(a, b):
    return lax.dot_general(a, b, (((1,), (1,)), ((), ())), preferred_element_type=F32)


def exact_dot(v, ones):
    rows = v.shape[0]
    out = dot_nn(jnp.concatenate(split3(v), axis=0), ones)
    return out[:rows] + out[rows : 2 * rows] + out[2 * rows :]


def iota2(shape, dim):
    return lax.broadcasted_iota(jnp.int32, shape, dim)


def pieces(raw, bias, rate, aux, tri):
    pad = aux[1:2]
    pre = raw + bias
    soft = jnp.maximum(pre, 0.0) + jnp.log1p(jnp.exp(-jnp.abs(pre)))
    dt = soft * pad
    cum = exact_dot(dt * rate, tri) * LOG2E
    carried = jnp.exp2(cum) * aux[5:6]
    toward = jnp.exp2(cum[:, CHUNK - 1 : CHUNK] - cum) * aux[6:7]
    return dt, cum, carried, toward


def expander(heads, inner, place):
    row = lax.rem(iota2((256, inner), 0), 128)
    head = lax.div(iota2((256, inner), 1), HEADDIM)
    return jnp.where(row == head + place, 1.0, 0.0).astype(BF)


def collector(inner, place):
    head = lax.div(iota2((inner, 128), 0), HEADDIM)
    lane = iota2((inner, 128), 1)
    return jnp.where(lane == head + place, 1.0, 0.0).astype(BF)


def hi_lo(cols):
    hi = cols.astype(BF)
    return jnp.concatenate([hi, (cols - hi.astype(F32)).astype(BF)], axis=1)


def compact(rows_list):
    used = sum(r.shape[0] for r in rows_list)
    if used < 128:
        rows_list = list(rows_list) + [jnp.zeros((128 - used, CHUNK), F32)]
    return jnp.concatenate(rows_list, axis=0).T


def split_pair(first, second, low):
    gate = jnp.where(low, first, pltpu.roll(second, HEADDIM, 1))
    value = jnp.where(low, pltpu.roll(first, HEADDIM, 1), second)
    return gate, value


def forward_kernel(
    heads, tok_ref, w_ref, aux_ref, cw_ref, cbw_ref, hp_ref,
    pz_ref, raw_ref, mixed_ref, gated_ref, cv_ref, pre_ref, cbc_ref, pbc_ref, st_ref, stat_ref,
    state, ubuf, bbuf, vd, yint, expand, tri_ref,
):
    inner = heads * HEADDIM
    pairs = heads // 2
    wide = 2 * inner
    first = (pl.program_id(0) == 0) & (pl.program_id(1) == 0)

    @pl.when(first)
    def _():
        for i, place in enumerate((AUX + heads, AUX + 2 * heads, AUX + 3 * heads)):
            expand[i] = expander(heads, inner, place)
        tri_ref[...] = jnp.where(iota2((CHUNK, CHUNK), 0) <= iota2((CHUNK, CHUNK), 1), 1.0, 0.0).astype(BF)

    @pl.when(pl.program_id(1) == 0)
    def _():
        state[...] = jnp.zeros_like(state)
        ubuf[0:HALO] = jnp.zeros((HALO, inner), F32)
        bbuf[0:HALO] = jnp.zeros((HALO, 2 * STATE), F32)

    tok = tok_ref[0]
    side = dot_nn(tok, w_ref[:, wide:])
    raw_ref[0] = side[:, 2 * STATE :].T[0:heads]
    pz_ref[0, :, wide:] = side[:, : 2 * STATE].astype(BF)
    for p in range(pairs):
        pz_ref[0, :, 256 * p : 256 * p + 256] = dot_nn(tok, w_ref[:, 256 * p : 256 * p + 256]).astype(BF)

    def chunk_step(step, carry):
        here = pl.ds(pl.multiple_of(step * CHUNK, CHUNK), CHUNK)
        aux = aux_ref[0, :, here]
        raw = raw_ref[0, :, here]
        bc = pz_ref[0, here, wide:]
        dt, cum, carried, toward = pieces(raw, hp_ref[0], hp_ref[1], aux, tri_ref[...])
        cols = compact([aux, cum, dt, carried, toward])
        both = hi_lo(cols)
        dtx = dot_nn(both, expand[0])
        carx = dot_nn(both, expand[1])
        towx = dot_nn(both, expand[2])
        pad = cols[:, 1:2]
        same = [None] + [cols[:, 1 + k : 2 + k] for k in range(1, TAPS)]
        low = iota2((CHUNK, 128), 1) < HEADDIM

        bbuf[HALO:] = bc.astype(F32) * pad
        maps = cbw_ref[TAPS : TAPS + 1] + cbw_ref[0:1] * bbuf[HALO:]
        for k in range(1, TAPS):
            maps = maps + cbw_ref[k : k + 1] * (same[k] * bbuf[HALO - k : HALO - k + CHUNK])
        pbc_ref[0, here] = maps.astype(BF)
        maps = (maps * sigmoid(maps)).astype(BF)
        cbc_ref[0, here] = maps
        bbuf[0:HALO] = bbuf[CHUNK : CHUNK + HALO]
        keys, queries = maps[:, :STATE], maps[:, STATE:]
        scores = dot_nt(queries, keys)
        keys_t = keys.astype(F32).T.astype(BF)

        for p in range(pairs):
            s = slice(128 * p, 128 * p + 128)
            x0 = pz_ref[0, here, 256 * p : 256 * p + 128].astype(F32)
            x1 = pz_ref[0, here, 256 * p + 128 : 256 * p + 256].astype(F32)
            value = jnp.where(low, pltpu.roll(x0, HEADDIM, 1), x1)
            ubuf[HALO:, s] = value * pad
            pre = cw_ref[TAPS : TAPS + 1, s] + cw_ref[0:1, s] * ubuf[HALO:, s]
            for k in range(1, TAPS):
                pre = pre + cw_ref[k : k + 1, s] * (same[k] * ubuf[HALO - k : HALO - k + CHUNK, s])
            pre_ref[0, here, s] = pre.astype(BF)
            cv = (pre * sigmoid(pre)).astype(BF)
            cv_ref[0, here, s] = cv
            vd[:, s] = (cv.astype(F32) * dtx[:, s]).astype(BF)
        ubuf[0:HALO] = ubuf[CHUNK : CHUNK + HALO]

        old = state[...]
        old_b = old.astype(BF)
        st_ref[0, step] = old_b
        yint[...] = dot_nn(queries, old_b) * carx
        state[...] = carx[CHUNK - 1 : CHUNK] * old + dot_nn(keys_t, (vd[...].astype(F32) * towx).astype(BF))

        inside = (iota2((CHUNK, CHUNK), 0) >= iota2((CHUNK, CHUNK), 1)) & (cols[:, 0:1] == aux[0:1])
        fence = jnp.where(inside, 0.0, FAR)
        squares = jnp.zeros((CHUNK, 128), F32)
        for p in range(pairs):
            s = slice(128 * p, 128 * p + 128)
            mix = []
            for h in (2 * p, 2 * p + 1):
                decay = jnp.exp2(cols[:, AUX + h : AUX + h + 1] - cum[h : h + 1] + fence)
                mix.append((scores * decay).astype(BF))
            v = vd[:, s]
            zero = jnp.zeros_like(v)
            stacked = jnp.concatenate([jnp.where(low, v, zero), jnp.where(low, zero, v)], axis=0)
            y = dot_nn(jnp.concatenate(mix, axis=1), stacked)
            mixed = y + yint[:, s] + cw_ref[5:6, s] * cv_ref[0, here, s].astype(F32)
            x0 = pz_ref[0, here, 256 * p : 256 * p + 128].astype(F32)
            x1 = pz_ref[0, here, 256 * p + 128 : 256 * p + 256].astype(F32)
            gate = jnp.where(low, x0, pltpu.roll(x1, HEADDIM, 1))
            gated = mixed * (gate * sigmoid(gate))
            mixed_ref[0, here, s] = mixed.astype(BF)
            gated_ref[0, here, s] = (gated * cw_ref[6:7, s]).astype(BF)
            squares = squares + gated * gated
        lane = iota2((CHUNK, 128), 1)
        sums = jnp.where(lane == 0, jnp.sum(squares, axis=1, keepdims=True), 0.0)
        stat_ref[0, :, here] = sums.T[0:8]
        return carry

    lax.fori_loop(0, BLOCK // CHUNK, chunk_step, 0)


def backward_kernel(
    heads, pz_ref, raw_ref, aux_ref, cot_ref, mixed_ref, cv_ref, pre_ref, cbc_ref, pbc_ref,
    st_ref, stat_ref, cw_ref, cbw_ref, hp_ref, out_ref, w_ref, tok_ref,
    ge_ref, dg_ref, gch_ref, gmap_ref, ghead_ref, gpre_ref,
    g_s, dstate, cbuf, dbuf, vd, gm_s, gmc_s, ggate_s, cs_s, bs_s, expand, collect, tri_ref, suf_ref,
):
    inner = heads * HEADDIM
    pairs = heads // 2
    wide = 2 * inner
    first = (pl.program_id(0) == 0) & (pl.program_id(1) == 0)

    @pl.when(first)
    def _():
        for i, place in enumerate((AUX + heads, AUX + 2 * heads, AUX + 3 * heads)):
            expand[i] = expander(heads, inner, place)
        collect[0] = collector(inner, heads)
        collect[1] = collector(inner, 2 * heads)
        r, c = iota2((CHUNK, CHUNK), 0), iota2((CHUNK, CHUNK), 1)
        tri_ref[...] = jnp.where(r <= c, 1.0, 0.0).astype(BF)
        suf_ref[...] = jnp.where(r >= c, 1.0, 0.0).astype(BF)
        gch_ref[...] = jnp.zeros_like(gch_ref)
        gmap_ref[...] = jnp.zeros_like(gmap_ref)
        ghead_ref[...] = jnp.zeros_like(ghead_ref)
        gpre_ref[...] = jnp.zeros_like(gpre_ref)

    @pl.when(pl.program_id(1) == 0)
    def _():
        dstate[...] = jnp.zeros_like(dstate)
        cbuf[CHUNK:] = jnp.zeros((HALO, inner), F32)
        dbuf[CHUNK:] = jnp.zeros((HALO, 2 * STATE), F32)

    g_s[...] = dot_nn(cot_ref[0], out_ref[...])

    def chunk_step(step, carry):
        here = pl.ds(pl.multiple_of(BLOCK - CHUNK - step * CHUNK, CHUNK), CHUNK)
        aux = aux_ref[0, :, here]
        rate = hp_ref[1]
        dt, cum, carried, toward = pieces(raw_ref[0, :, here], hp_ref[0], rate, aux, tri_ref[...])
        cols = compact([aux, cum, dt, carried, toward, stat_ref[0, :, here]])
        both = hi_lo(cols)
        dtx = dot_nn(both, expand[0])
        carx = dot_nn(both, expand[1])
        towx = dot_nn(both, expand[2])
        pad = cols[:, 1:2]
        ahead = [None] + [cols[:, 7 + k : 8 + k] for k in range(1, TAPS)]
        base = AUX + 4 * heads
        rms, pull = cols[:, base : base + 1], cols[:, base + 1 : base + 2]
        low = iota2((CHUNK, 128), 1) < HEADDIM
        maps = cbc_ref[0, here]
        keys, queries = maps[:, :STATE], maps[:, STATE:]
        queries_t = queries.astype(F32).T.astype(BF)
        scores_t = dot_nt(keys, queries)

        for p in range(pairs):
            s = slice(128 * p, 128 * p + 128)
            x0 = pz_ref[0, here, 256 * p : 256 * p + 128].astype(F32)
            x1 = pz_ref[0, here, 256 * p + 128 : 256 * p + 256].astype(F32)
            gate = jnp.where(low, x0, pltpu.roll(x1, HEADDIM, 1))
            sig = sigmoid(gate)
            act = gate * sig
            mixed = mixed_ref[0, here, s].astype(F32)
            gated = mixed * act
            g = g_s[here, s]
            grad_gated = rms * (g * cw_ref[6:7, s]) - gated * pull
            gm = grad_gated * act
            ggate_s[:, s] = (grad_gated * mixed * (sig * (1.0 + gate * (1.0 - sig)))).astype(BF)
            gm_s[:, s] = gm.astype(BF)
            gmc_s[:, s] = (gm * carx[:, s]).astype(BF)
            cv = cv_ref[0, here, s].astype(F32)
            vd[:, s] = (cv * dtx[:, s]).astype(BF)
            gch_ref[5:6, s] += jnp.sum(gm * cv, axis=0, keepdims=True)
            gch_ref[6:7, s] += jnp.sum(gated * rms * g, axis=0, keepdims=True)

        ds = dstate[...]
        ds_b = ds.astype(BF)
        st = st_ref[0, BLOCK // CHUNK - 1 - step]
        gmc = gmc_s[...]
        cs = dot_nn(queries, st)
        bs = dot_nn(keys, ds_b) * towx
        bs_s[...] = bs
        reach = dot_nn((gmc.astype(F32) * cs).astype(BF), collect[1])
        reach = reach + dot_nn((bs * cv_ref[0, here].astype(F32)).astype(BF), collect[0])
        grad_q = dot_nt(gmc, st)
        grad_k = dot_nt((vd[...].astype(F32) * towx).astype(BF), ds_b)
        keep = carx[CHUNK - 1 : CHUNK]
        held = jnp.sum(st.astype(F32) * ds, axis=0, keepdims=True) * keep
        dstate[...] = keep * ds + dot_nn(queries_t, gmc)

        inside = (iota2((CHUNK, CHUNK), 0) <= iota2((CHUNK, CHUNK), 1)) & (cols[:, 0:1] == aux[0:1])
        fence = jnp.where(inside, 0.0, FAR)
        grad_scores_t = jnp.zeros((CHUNK, CHUNK), F32)
        lane = iota2((CHUNK, 128), 1)
        gathered = reach
        row_sums = []
        for p in range(pairs):
            s = slice(128 * p, 128 * p + 128)
            gm_b = gm_s[:, s]
            zero = jnp.zeros_like(gm_b)
            gm_two = jnp.concatenate([jnp.where(low, gm_b, zero), jnp.where(low, zero, gm_b)], axis=0)
            near = dot_nt(vd[:, s], gm_two)
            mix = []
            for j in range(2):
                h = 2 * p + j
                decay = jnp.exp2(cum[h : h + 1] - cols[:, AUX + h : AUX + h + 1] + fence)
                mix.append((scores_t * decay).astype(BF))
                weighed = decay * near[:, CHUNK * j : CHUNK * j + CHUNK]
                grad_scores_t = grad_scores_t + weighed
                pairs_g = weighed * scores_t
                row_sums.append(jnp.sum(pairs_g, axis=0, keepdims=True))
                gathered = jnp.where(lane == h, jnp.sum(pairs_g, axis=1, keepdims=True), gathered)
            z = dot_nn(jnp.concatenate(mix, axis=1), gm_two)
            gm = gm_b.astype(F32)
            grad_v = cw_ref[5:6, s] * gm + dtx[:, s] * (z + bs_s[:, s])
            x0 = pz_ref[0, here, 256 * p : 256 * p + 128].astype(F32)
            x1 = pz_ref[0, here, 256 * p + 128 : 256 * p + 256].astype(F32)
            u = jnp.where(low, pltpu.roll(x0, HEADDIM, 1), x1) * pad
            pre = pre_ref[0, here, s].astype(F32)
            sig = sigmoid(pre)
            c = grad_v * (sig * (1.0 + pre * (1.0 - sig)))
            cbuf[0:CHUNK, s] = c
            gu = cw_ref[0:1, s] * c
            gch_ref[4:5, s] += jnp.sum(c, axis=0, keepdims=True)
            gch_ref[0:1, s] += jnp.sum(c * u, axis=0, keepdims=True)
            for k in range(1, TAPS):
                shifted = ahead[k] * cbuf[k : k + CHUNK, s]
                gu = gu + cw_ref[k : k + 1, s] * shifted
                gch_ref[k : k + 1, s] += jnp.sum(shifted * u, axis=0, keepdims=True)
            gu = gu * pad
            ggate = ggate_s[:, s].astype(F32)
            ge_ref[0, here, 256 * p : 256 * p + 128] = jnp.where(low, ggate, pltpu.roll(gu, HEADDIM, 1)).astype(BF)
            ge_ref[0, here, 256 * p + 128 : 256 * p + 256] = jnp.where(low, pltpu.roll(ggate, HEADDIM, 1), gu).astype(BF)
        cbuf[CHUNK:] = cbuf[0:HALO]

        gst = grad_scores_t.astype(BF)
        grad_k = grad_k + dot_nn(gst, queries)
        grad_q = grad_q + dot_nn(grad_scores_t.T.astype(BF), keys)
        pbc = pbc_ref[0, here].astype(F32)
        sig = sigmoid(pbc)
        c = jnp.concatenate([grad_k, grad_q], axis=1) * (sig * (1.0 + pbc * (1.0 - sig)))
        dbuf[0:CHUNK] = c
        u = pz_ref[0, here, wide:].astype(F32) * pad
        gu = cbw_ref[0:1] * c
        gmap_ref[4:5] += jnp.sum(c, axis=0, keepdims=True)
        gmap_ref[0:1] += jnp.sum(c * u, axis=0, keepdims=True)
        for k in range(1, TAPS):
            shifted = ahead[k] * dbuf[k : k + CHUNK]
            gu = gu + cbw_ref[k : k + 1] * shifted
            gmap_ref[k : k + 1] += jnp.sum(shifted * u, axis=0, keepdims=True)
        ge_ref[0, here, wide : wide + 2 * STATE] = (gu * pad).astype(BF)
        dbuf[CHUNK:] = dbuf[0:HALO]

        across = gathered.T
        col_sum = across[0:heads]
        kx = across[heads : 2 * heads]
        rint = across[2 * heads : 3 * heads]
        row_sum = jnp.concatenate(row_sums, axis=0)
        k_all = kx * dt
        held_head = exact_dot(jnp.broadcast_to(held, (16, inner)), collect[0])
        held_col = jnp.broadcast_to(held_head[0:1], (CHUNK, 128)).T[heads : 2 * heads]
        diff = row_sum + rint - col_sum - k_all
        grad_a = exact_dot(diff, suf_ref[...]) + jnp.sum(k_all, axis=1, keepdims=True) + held_col
        direct = jnp.where(dt > 0.0, col_sum / jnp.where(dt > 0.0, dt, 1.0), 0.0)
        grad_dt = direct + kx + rate * grad_a
        graw = grad_dt * aux[1:2] * sigmoid(raw_ref[0, :, here] + hp_ref[0])
        ge_ref[0, here, wide + 2 * STATE :] = compact([graw]).astype(BF)
        ghead_ref[0] += graw
        ghead_ref[1] += rate * dt * grad_a
        return carry

    lax.fori_loop(0, BLOCK // CHUNK, chunk_step, 0)
    dg = dot_nt(ge_ref[0], w_ref[...])
    dg_ref[0] = dg.astype(BF)
    gpre_ref[0:1] += jnp.sum(dg * tok_ref[0].astype(F32), axis=0, keepdims=True)


def whole_once(*shape):
    return pl.BlockSpec(shape, lambda s, c: (0,) * len(shape), pipeline_mode=pl.Buffered(1))


def mixer_forward(tok, weights, aux, cw, cbw, hp):
    seqs, length, width = tok.shape
    heads, inner = hp.shape[1], cw.shape[1]
    wide = 2 * inner + 2 * STATE
    chunks = length // CHUNK
    token = lambda size: pl.BlockSpec((1, BLOCK, size), lambda s, c: (s, c, 0))
    row = lambda high: pl.BlockSpec((1, high, BLOCK), lambda s, c: (s, 0, c))
    sds = jax.ShapeDtypeStruct
    return pl.pallas_call(
        functools.partial(forward_kernel, heads),
        grid=(seqs, length // BLOCK),
        in_specs=[
            token(width), whole_once(*weights.shape), row(AUX),
            whole_once(8, inner), whole_once(8, 2 * STATE), whole_once(2, heads, 128),
        ],
        out_specs=[
            token(wide), row(heads), token(inner), token(inner), token(inner), token(inner), token(2 * STATE),
            token(2 * STATE), pl.BlockSpec((1, BLOCK // CHUNK, STATE, inner), lambda s, c: (s, c, 0, 0)), row(8),
        ],
        out_shape=[
            sds((seqs, length, wide), BF), sds((seqs, heads, length), F32),
            sds((seqs, length, inner), BF), sds((seqs, length, inner), BF), sds((seqs, length, inner), BF),
            sds((seqs, length, inner), BF), sds((seqs, length, 2 * STATE), BF), sds((seqs, length, 2 * STATE), BF),
            sds((seqs, chunks, STATE, inner), BF), sds((seqs, 8, length), F32),
        ],
        scratch_shapes=[
            pltpu.VMEM((STATE, inner), F32), pltpu.VMEM((HALO + CHUNK, inner), F32),
            pltpu.VMEM((HALO + CHUNK, 2 * STATE), F32), pltpu.VMEM((CHUNK, inner), BF),
            pltpu.VMEM((CHUNK, inner), F32), pltpu.VMEM((3, 256, inner), BF), pltpu.VMEM((CHUNK, CHUNK), BF),
        ],
        compiler_params=pltpu.CompilerParams(vmem_limit_bytes=VMEM_LIMIT),
        name="mixer_forward",
    )(tok, weights, aux, cw, cbw, hp)


def mixer_backward(pz, raw, aux, cot, mixed, cv, pre, cbc, pbc, st, stat, cw, cbw, hp, out_all, weights, tok):
    seqs, length, width = cot.shape
    heads, inner = hp.shape[1], cw.shape[1]
    last = length // BLOCK - 1
    token = lambda size: pl.BlockSpec((1, BLOCK, size), lambda s, c: (s, last - c, 0))
    row = lambda high: pl.BlockSpec((1, high, BLOCK), lambda s, c: (s, 0, last - c))
    whole = lambda *shape: pl.BlockSpec(shape, lambda s, c: (0,) * len(shape))
    sds = jax.ShapeDtypeStruct
    return pl.pallas_call(
        functools.partial(backward_kernel, heads),
        grid=(seqs, length // BLOCK),
        in_specs=[
            token(pz.shape[2]), row(heads), row(AUX), token(width), token(inner), token(inner),
            token(inner), token(2 * STATE), token(2 * STATE),
            pl.BlockSpec((1, BLOCK // CHUNK, STATE, inner), lambda s, c: (s, last - c, 0, 0)), row(8),
            whole_once(8, inner), whole_once(8, 2 * STATE), whole_once(2, heads, 128),
            whole_once(*out_all.shape), whole_once(*weights.shape), token(width),
        ],
        out_specs=[
            token(weights.shape[1]), token(width),
            whole(8, inner), whole(8, 2 * STATE), whole(2, heads, 128), whole(8, width),
        ],
        out_shape=[
            sds((seqs, length, weights.shape[1]), BF), sds((seqs, length, width), BF),
            sds((8, inner), F32), sds((8, 2 * STATE), F32), sds((2, heads, 128), F32), sds((8, width), F32),
        ],
        scratch_shapes=[
            pltpu.VMEM((BLOCK, inner), F32),
            pltpu.VMEM((STATE, inner), F32), pltpu.VMEM((CHUNK + HALO, inner), F32),
            pltpu.VMEM((CHUNK + HALO, 2 * STATE), F32), pltpu.VMEM((CHUNK, inner), BF),
            pltpu.VMEM((CHUNK, inner), BF), pltpu.VMEM((CHUNK, inner), BF), pltpu.VMEM((CHUNK, inner), BF),
            pltpu.VMEM((CHUNK, inner), F32), pltpu.VMEM((CHUNK, inner), F32),
            pltpu.VMEM((3, 256, inner), BF), pltpu.VMEM((2, inner, 128), BF),
            pltpu.VMEM((CHUNK, CHUNK), BF), pltpu.VMEM((CHUNK, CHUNK), BF),
        ],
        compiler_params=pltpu.CompilerParams(vmem_limit_bytes=VMEM_LIMIT),
        name="mixer_backward",
    )(pz, raw, aux, cot, mixed, cv, pre, cbc, pbc, st, stat, cw, cbw, hp, out_all, weights, tok)


def out_kernel(gn_ref, cot_ref, out_ref, stat_ref, y_ref, stat_out_ref):
    y = dot_nt(gn_ref[0], out_ref[...])
    y_ref[0] = y.astype(BF)
    cross = jnp.sum(y * cot_ref[0].astype(F32), axis=1, keepdims=True)
    row = jnp.broadcast_to(cross, (cross.shape[0], 128)).T[0:8]
    stat_out_ref[0] = jnp.where(iota2(row.shape, 0) == 1, row, stat_ref[0])


def out_project(gn, cot, out_all, stat):
    seqs, length, inner = gn.shape
    width = cot.shape[2]
    size = 256
    token = lambda last: pl.BlockSpec((1, size, last), lambda s, c: (s, c, 0))
    row = pl.BlockSpec((1, 8, size), lambda s, c: (s, 0, c))
    sds = jax.ShapeDtypeStruct
    return pl.pallas_call(
        out_kernel,
        grid=(seqs, length // size),
        in_specs=[token(inner), token(width), whole_once(*out_all.shape), row],
        out_specs=[token(width), row],
        out_shape=[sds((seqs, length, width), BF), sds((seqs, 8, length), F32)],
        compiler_params=pltpu.CompilerParams(vmem_limit_bytes=VMEM_LIMIT),
        name="out_project",
    )(gn, cot, out_all, stat)


def doc_flags(segment, pad_mask):
    seqs, length = segment.shape
    position = lax.broadcasted_iota(jnp.int32, segment.shape, 1)
    rows = [segment.astype(F32), pad_mask.astype(F32)]
    back = []
    for k in range(1, TAPS):
        earlier = jnp.pad(segment, ((0, 0), (k, 0)), constant_values=-1)[:, :length]
        back.append(earlier == segment)
    rows += [b.astype(F32) for b in back]
    blocks = segment.reshape(seqs, length // CHUNK, CHUNK)
    tail = blocks[:, :, CHUNK - 1 :]
    previous = jnp.pad(tail, ((0, 0), (1, 0), (0, 0)), constant_values=-1)[:, :-1]
    rows.append((blocks == previous).reshape(seqs, length).astype(F32))
    rows.append((blocks == tail).reshape(seqs, length).astype(F32))
    rows.append(jnp.zeros_like(rows[0]))
    for k in range(1, TAPS):
        later = jnp.pad(segment, ((0, 0), (0, k)), constant_values=-1)[:, k:]
        rows.append((later == segment).astype(F32))
    rows += [jnp.zeros_like(rows[0])] * (AUX - len(rows))
    return jnp.stack(rows, axis=1)


MESH = pl.DeviceIdType.MESH


def factors(size):
    first = 4 if size % 8 == 0 else 1
    return first, size // (2 * first)


def gather_sites(first, second):
    return (2 + second) + (first - 1) * 2 * (1 + second) + (2 * first - 1) * (second - 1)


def gather_kernel(first, second, pair, arrays, *refs):
    own = refs[:arrays]
    tok = refs[arrays]
    full = refs[arrays + 1 : 2 * arrays + 1]
    tok_full = refs[2 * arrays + 1]
    send_sem, recv_sem, local_sem, tok_sem = refs[2 * arrays + 2 :]
    index = lax.axis_index("dp")
    me = lax.axis_index("tensor")
    a = lax.div(index, 2 * second)
    b = lax.rem(lax.div(index, 2), second)
    c = lax.rem(index, 2)
    at = lambda i, j, k: (i * second + j) * 2 + k
    sibling = at(a, b, 1 - c)
    has_up, has_down = a < first - 1, a > 0

    barrier = pltpu.get_barrier_semaphore()
    greet = lambda dp, t: pl.semaphore_signal(barrier, inc=1, device_id=(dp, t), device_id_type=MESH)
    greet(sibling, me)
    for j in range(1, second):
        greet(at(a, lax.rem(b + j, second), c), me)
    for i in range(1, first):
        greet(at(lax.rem(a + i, first), b, c), me)
    if pair:
        greet(index, 1 - me)
    pl.semaphore_wait(barrier, first + second - 1 + (1 if pair else 0))

    def place(which, shard):
        rows = own[which].shape[0]
        return full[which].at[pl.ds(pl.multiple_of(shard * rows, rows), rows)]

    def copies(site, shard, target, mine):
        return [
            pltpu.make_async_remote_copy(
                src_ref=own[w] if mine else place(w, shard),
                dst_ref=place(w, shard),
                send_sem=send_sem.at[w, site],
                recv_sem=recv_sem.at[w, shard],
                device_id=(target, me),
                device_id_type=MESH,
            )
            for w in range(arrays)
        ]

    sites = []

    def send(valid, shard, target, mine=False):
        site = len(sites)
        sites.append((valid, shard, target, mine))

        def start():
            for copy in copies(site, shard, target, mine):
                copy.start()

        start() if valid is None else pl.when(valid)(start)

    def arrived(shard):
        for copy in copies(0, shard, sibling, False):
            copy.wait_recv()

    def both(left, right):
        return right if left is None else left & right

    if pair:
        here = tok.shape[1]
        token_copy = pltpu.make_async_remote_copy(
            src_ref=tok,
            dst_ref=tok_full.at[:, pl.ds(pl.multiple_of(me * here, here), here)],
            send_sem=tok_sem.at[0],
            recv_sem=tok_sem.at[1],
            device_id=(index, 1 - me),
            device_id_type=MESH,
        )
        token_copy.start()
        token_local = pltpu.make_async_copy(
            tok, tok_full.at[:, pl.ds(pl.multiple_of(me * here, here), here)], tok_sem.at[2]
        )
        token_local.start()
    send(has_up, index, at(a + 1, b, c), True)
    send(has_down, index, at(a - 1, b, c), True)
    for j in range(1, second):
        send(None, index, at(a, lax.rem(b + j, second), c), True)
    send(None, index, sibling, True)
    local = [pltpu.make_async_copy(own[w], place(w, index), local_sem.at[w]) for w in range(arrays)]
    for copy in local:
        copy.start()

    steps = [(None, index)]
    for s in range(1, first):
        below, above = a - s >= 0, a + s < first
        steps += [(below, a - s), (above, a + s)]
        for valid, other, onward, target in (
            (below, a - s, has_up, at(a + 1, b, c)),
            (above, a + s, has_down, at(a - 1, b, c)),
        ):
            shard = at(other, b, c)
            pl.when(valid)(functools.partial(arrived, shard))
            send(valid & onward, shard, target)
            for j in range(1, second):
                send(valid, shard, at(a, lax.rem(b + j, second), c))
            send(valid, shard, sibling)
    for j in range(1, second):
        column = lax.rem(b + j, second)
        for s, (valid, other) in enumerate(steps):
            shard = at(a if s == 0 else other, column, c)
            arrived(shard) if valid is None else pl.when(valid)(functools.partial(arrived, shard))
            send(valid, shard, sibling)
    for i in range(first):
        for j in range(second):
            arrived(at(i, j, 1 - c))
    for site, (valid, shard, target, mine) in enumerate(sites):

        def finish(site=site, shard=shard, target=target, mine=mine):
            for copy in copies(site, shard, target, mine):
                copy.wait_send()

        finish() if valid is None else pl.when(valid)(finish)
    for copy in local:
        copy.wait()
    if pair:
        token_copy.wait()
        token_local.wait()


def gather_all(shards, tokens, size, n):
    first, second = factors(size)
    pair = n == 2
    arrays = len(shards)
    any_space = pl.BlockSpec(memory_space=pl.ANY)
    sds = jax.ShapeDtypeStruct
    seqs, here, width = tokens.shape
    out_shape = [sds((size * s.shape[0], s.shape[1]), s.dtype) for s in shards]
    out_shape.append(sds((seqs, 2 * here, width) if pair else (8, 128), tokens.dtype))
    *full, tok_full = pl.pallas_call(
        functools.partial(gather_kernel, first, second, pair, arrays),
        in_specs=[any_space] * arrays + [pl.BlockSpec(memory_space=pltpu.VMEM)],
        out_specs=[any_space] * (arrays + 1),
        out_shape=out_shape,
        scratch_shapes=[
            pltpu.SemaphoreType.DMA((arrays, gather_sites(first, second))),
            pltpu.SemaphoreType.DMA((arrays, size)),
            pltpu.SemaphoreType.DMA((arrays,)),
            pltpu.SemaphoreType.DMA((3,)),
        ],
        compiler_params=pltpu.CompilerParams(collective_id=0, has_side_effects=True),
        name="gather_all",
    )(*shards, tokens)
    return full, tok_full if pair else lax.all_gather(tokens, "tensor", axis=1, tiled=True)


PIECES = 2


def reduce_kernel(
    first, second, pair, fused, shared, tok_ref, ge_ref, flat_ref, dg_ref, hidden_ref, cot_ref, gain_ref,
    out_ref, sum_ref, gh_ref,
    part_buf, core_buf, x_buf, z_buf, acc, dg_buf, y_flat, core_flat, x_flat, z_flat, stage,
    core_send, core_recv, x_send, x_recv, z_send, z_recv, flat_send, flat_recv, dg_sem,
):
    index = lax.axis_index("dp")
    me = lax.axis_index("tensor")
    a = lax.div(index, 2 * second)
    b = lax.rem(lax.div(index, 2), second)
    c = lax.rem(index, 2)
    rows = out_ref.shape[0] // PIECES
    at = lambda i, j, k: (i * second + j) * 2 + k
    around = lambda i: lax.rem(a + i, first)
    aside = lambda j: lax.rem(b + j, second)
    sibling = at(a, b, 1 - c)
    part_ref = part_buf if fused else ge_ref

    barrier = pltpu.get_barrier_semaphore()
    greet = lambda dp, t: pl.semaphore_signal(barrier, inc=1, device_id=(dp, t), device_id_type=MESH)
    greet(sibling, me)
    for j in range(1, second):
        greet(at(a, aside(j), c), me)
    for i in range(1, first):
        greet(at(around(i), b, c), me)
    if pair:
        greet(index, 1 - me)
    pl.semaphore_wait(barrier, first + second - 1 + (1 if pair else 0))

    started = []

    def send(src, dst, ss, rs, target, tensor=me):
        copy = pltpu.make_async_remote_copy(
            src_ref=src, dst_ref=dst, send_sem=ss, recv_sem=rs, device_id=(target, tensor), device_id_type=MESH
        )
        copy.start()
        started.append(copy)

    def arrived(dst, rs):
        pltpu.make_async_remote_copy(
            src_ref=dst, dst_ref=dst, send_sem=core_send.at[0], recv_sem=rs,
            device_id=(sibling, me), device_id_type=MESH,
        ).wait_recv()

    def block(i, j, k, q):
        return part_ref.at[pl.ds(pl.multiple_of((at(i, j, k) * PIECES + q) * rows, rows), rows)]

    if first == 4:
        near = jnp.minimum(a, 3 - a)
        order = [jnp.where(a < 2, d, 3 - d) for d in (3 + 0 * a, 2 - 2 * near, 1 + near)] + [a]
    else:
        order = [a]
    slot = lambda i, j, q: (i * second + j) * PIECES + q
    pieces_of = [(n, i, q) for n, i in enumerate(order) for q in range(PIECES)]

    if pair:
        send(flat_ref.at[0:shared], y_flat, flat_send.at[0], flat_recv.at[0], index, 1 - me)
        here = hidden_ref.shape[1]
        own_rows = pl.ds(pl.multiple_of(me * here, here), here)
        away_rows = pl.ds(pl.multiple_of((1 - me) * here, here), here)
        send(dg_ref.at[:, away_rows], dg_buf, dg_sem.at[0], dg_sem.at[1], index, 1 - me)

    def produce(i, j):
        if fused:
            there = pl.ds(pl.multiple_of(at(i, aside(j), 0) * rows * PIECES, 128), 2 * rows * PIECES)
            part_buf[there] = lax.dot_general(
                tok_ref[:, there], ge_ref[...], (((0,), (0,)), ((), ())), preferred_element_type=F32
            ).astype(BF)
        for q in range(PIECES):
            s = slot(i, aside(j), q)
            send(block(i, aside(j), 1 - c, q), core_buf.at[s], core_send.at[s], core_recv.at[s], sibling)

    def cross_over(i, j):
        for q in range(PIECES):
            s = slot(i, aside(j), q)
            arrived(core_buf.at[s], core_recv.at[s])
            core_buf[s] = (block(i, aside(j), c, q)[...].astype(F32) + core_buf[s].astype(F32)).astype(BF)
            t = (i * (second - 1) + second - j - 1) * PIECES + q
            u = (i * (second - 1) + j - 1) * PIECES + q
            send(core_buf.at[s], x_buf.at[t], x_send.at[u], x_recv.at[t], at(a, aside(j), c))

    work = [(i, j) for j in list(range(1, second)) + [0] for i in order]
    for n, (i, j) in enumerate(work):
        produce(i, j)
        if n >= 1 and work[n - 1][1] > 0:
            cross_over(*work[n - 1])

    if pair:
        arrived(y_flat, flat_recv.at[0])
        stage[0, 0:shared] = flat_ref[0:shared] + y_flat[...]
    else:
        stage[0, 0:shared] = flat_ref[0:shared]
    stage[0, shared:] = flat_ref[shared:]
    send(stage.at[0], core_flat, flat_send.at[1], flat_recv.at[1], sibling)
    arrived(core_flat, flat_recv.at[1])
    stage[1] = stage[0] + core_flat[...]
    x_flat[b] = stage[1]
    for j in range(1, second):
        send(stage.at[1], x_flat.at[b], flat_send.at[1 + j], flat_recv.at[2 + b], at(a, aside(j), c))

    for n, i, q in pieces_of:
        s = slot(i, b, q)
        arrived(core_buf.at[s], core_recv.at[s])
        total = block(i, b, c, q)[...].astype(F32) + core_buf[s].astype(F32)
        for j in range(1, second):
            t = (i * (second - 1) + j - 1) * PIECES + q
            arrived(x_buf.at[t], x_recv.at[t])
            total = total + x_buf[t].astype(F32)
        if n < first - 1:
            down = jnp.where(i > a, 0, 1)
            z = (down * first + i) * PIECES + q
            acc[...] = total

            @pl.when(jnp.where(i > a, a, first - 1 - a) > 0)
            def _():
                arrived(z_buf.at[z], z_recv.at[z])
                acc[...] = acc[...] + z_buf[z].astype(F32)

            core_buf[s] = acc[...].astype(BF)
            send(
                core_buf.at[s], z_buf.at[z], z_send.at[n * PIECES + q], z_recv.at[z], at(a + 1 - 2 * down, b, c)
            )
        else:
            out_ref[q * rows : (q + 1) * rows] = total
    for j in range(1, second):
        arrived(x_flat.at[aside(j)], flat_recv.at[2 + aside(j)])
    total = x_flat[0]
    for j in range(1, second):
        total = total + x_flat[j]
    stage[2] = total
    z_flat[a] = total
    for i in range(1, first):
        send(stage.at[2], z_flat.at[a], flat_send.at[second + i], flat_recv.at[2 + second + a], at(around(i), b, c))

    if pair:
        arrived(dg_buf, dg_sem.at[1])
        size = 128

        def norm_rows(step, carry):
            seq, cut = lax.div(step, here // size), lax.rem(step, here // size)
            mine = pl.ds(pl.multiple_of(cut * size, size), size)
            full = pl.ds(pl.multiple_of(me * here + cut * size, size), size)
            hid = hidden_ref[seq, mine].astype(F32)
            inv = lax.rsqrt(jnp.mean(hid * hid, axis=-1, keepdims=True) + epsilon)
            gain = (dg_ref[seq, full].astype(F32) + dg_buf[seq, mine].astype(F32)) * gain_ref[0:1]
            pull = inv * inv * inv * jnp.mean(hid * gain, axis=-1, keepdims=True)
            gh_ref[seq, mine] = (cot_ref[seq, mine].astype(F32) + inv * gain - hid * pull).astype(BF)
            return carry

        lax.fori_loop(0, hidden_ref.shape[0] * (here // size), norm_rows, 0)
    else:
        gh_ref[...] = jnp.zeros_like(gh_ref)

    for q in range(PIECES):
        cut_rows = slice(q * rows, (q + 1) * rows)
        for down, there in ((0, a), (1, first - 1 - a)):
            z = (down * first + a) * PIECES + q

            @pl.when(there > 0)
            def _(z=z, cut_rows=cut_rows):
                arrived(z_buf.at[z], z_recv.at[z])
                out_ref[cut_rows] = out_ref[cut_rows] + z_buf[z].astype(F32)

    for i in range(1, first):
        arrived(z_flat.at[around(i)], flat_recv.at[2 + second + around(i)])
    total = z_flat[0]
    for i in range(1, first):
        total = total + z_flat[i]
    sum_ref[...] = total
    for copy in started:
        copy.wait_send()


def reduce_all(tok, ge, flat, shared, dg, hidden, cot_own, pre_gain, size, n):
    first, second = factors(size)
    pair = n == 2
    seqs, length, depth = tok.shape
    width = ge.shape[2]
    rows = depth // size
    fused = (2 * rows) % 128 == 0
    if not pair:
        flat = jnp.concatenate([lax.psum(flat[:shared], "tensor"), flat[shared:]])
        dg, hidden, cot_own = [jnp.zeros((1, 16, depth), BF)] * 3
    if fused:
        tok, ge = tok.reshape(seqs * length, depth), ge.reshape(seqs * length, width)
    else:
        ge = jnp.einsum("stp,sty->py", tok, ge, preferred_element_type=F32).astype(BF)
        tok = tok[0, :16]
    sds = jax.ShapeDtypeStruct
    vmem = pl.BlockSpec(memory_space=pltpu.VMEM)
    blocks = first * second * PIECES
    columns = first * max(second - 1, 1) * PIECES
    lines = 2 * first * PIECES
    cut = rows // PIECES
    dma = pltpu.SemaphoreType.DMA
    return pl.pallas_call(
        functools.partial(reduce_kernel, first, second, pair, fused, shared),
        in_specs=[vmem] * 7,
        out_specs=[vmem] * 3,
        out_shape=[sds((rows, width), F32), sds(flat.shape, F32), sds(hidden.shape, BF)],
        scratch_shapes=[
            pltpu.VMEM((depth, width) if fused else (16, 128), BF),
            pltpu.VMEM((blocks, cut, width), BF),
            pltpu.VMEM((columns, cut, width), BF),
            pltpu.VMEM((lines, cut, width), BF),
            pltpu.VMEM((cut, width), F32),
            pltpu.VMEM(hidden.shape, BF),
            pltpu.VMEM((shared, flat.shape[1]), F32),
            pltpu.VMEM(flat.shape, F32),
            pltpu.VMEM((second,) + flat.shape, F32),
            pltpu.VMEM((first,) + flat.shape, F32),
            pltpu.VMEM((3,) + flat.shape, F32),
            dma((blocks,)), dma((blocks,)), dma((columns,)), dma((columns,)),
            dma((first * PIECES,)), dma((lines,)), dma((1 + first + second,)), dma((2 + first + second,)), dma((2,)),
        ],
        compiler_params=pltpu.CompilerParams(collective_id=1, has_side_effects=True, vmem_limit_bytes=VMEM_LIMIT),
        name="reduce_all",
    )(tok, ge, flat, dg, hidden, cot_own, jnp.broadcast_to(pre_gain[None], (8, depth)))


def gather_tokens(own, n, me):
    if n != 2:
        return lax.all_gather(own, "tensor", axis=1, tiled=True)
    other = lax.ppermute(own, "tensor", [(0, 1), (1, 0)])
    seqs, here, width = own.shape
    full = jnp.zeros((seqs, 2 * here, width), own.dtype)
    full = lax.dynamic_update_slice(full, own, (0, me * here, 0))
    return lax.dynamic_update_slice(full, other, (0, (1 - me) * here, 0))


def scatter_sum(make, size, n, me, dim):
    if n != 2:
        blocks = [make(i * size) for i in range(n)]
        return lax.psum_scatter(jnp.concatenate(blocks, axis=dim), "tensor", scatter_dimension=dim, tiled=True)
    away = lax.ppermute(make((1 - me) * size).astype(BF), "tensor", [(0, 1), (1, 0)])
    return make(me * size) + away.astype(F32)


def swap_sum(value, n):
    if n != 2:
        return lax.psum(value, "tensor")
    return value + lax.ppermute(value, "tensor", [(0, 1), (1, 0)])


def body(
    hidden, pre_gain, zx_weight, bc_weight, step_weight, conv_x_weight, conv_x_bias, conv_bc_weight, conv_bc_bias,
    step_bias, decay_log, skip_gain, norm_gain, out_weight, segment_ids, pad_mask, grad_out,
):
    n = lax.axis_size("tensor")
    me = lax.axis_index("tensor")
    heads = step_weight.shape[1]
    inner = heads * HEADDIM
    inner_all = inner * n
    here = hidden.shape[1]
    width = hidden.shape[2]
    size = lax.axis_size("dp")
    hidden_f = hidden.astype(F32)
    inv_rms = lax.rsqrt(jnp.mean(hidden_f * hidden_f, axis=-1, keepdims=True) + epsilon)
    normed_own = (hidden_f * inv_rms * pre_gain).astype(BF)
    shard = jnp.concatenate(
        [zx_weight, bc_weight, step_weight, jnp.zeros((zx_weight.shape[0], 128 - heads), BF)], axis=1
    )
    (weights,), normed = gather_all([shard], normed_own, size, n)
    out_own, cot_own, normed = lax.optimization_barrier((out_weight.T, grad_out, normed))
    out_all = lax.all_gather(out_own, "dp", axis=0, tiled=True)
    cot = gather_tokens(cot_own, n, me)

    aux = doc_flags(segment_ids, pad_mask)
    cw = jnp.concatenate(
        [conv_x_weight, conv_x_bias[None], jnp.repeat(skip_gain, HEADDIM)[None], norm_gain[None], jnp.zeros((1, inner), F32)]
    )
    cbw = jnp.concatenate([conv_bc_weight, conv_bc_bias[None], jnp.zeros((3, 2 * STATE), F32)])
    rate = -jnp.exp(decay_log)
    hp = jnp.broadcast_to(jnp.stack([step_bias, rate])[:, :, None], (2, heads, 128))

    pz, raw, mixed, gn, cv, pre, cbc, pbc, st, stat = mixer_forward(normed, weights, aux, cw, cbw, hp)
    y, stat = out_project(gn, cot, out_all, stat)
    stat = swap_sum(stat, n)
    gate_rms = lax.rsqrt(stat[:, 0] / inner_all + epsilon)
    back = jnp.stack([gate_rms, gate_rms**3 * (stat[:, 1] / inner_all)] + [jnp.zeros_like(gate_rms)] * 6, axis=1)
    y, back = lax.optimization_barrier((y, back))

    part = lambda rows: lambda start: lax.dynamic_slice_in_dim(rows, start, here, axis=1).astype(F32)
    rms_own = lax.dynamic_slice_in_dim(gate_rms, me * here, here, axis=1)[..., None]
    output = (hidden_f + rms_own * scatter_sum(part(y), here, n, me, 1)).astype(BF)
    cot_scaled = (cot.astype(F32) * gate_rms[..., None]).astype(BF)
    out_grad = jnp.einsum("str,stc->rc", cot_scaled, gn, preferred_element_type=F32).astype(BF)
    grad_out_weight = lax.psum_scatter(out_grad, "dp", scatter_dimension=0, tiled=True).astype(F32).T

    ge, dg, gch, gmap, ghead, gpre = mixer_backward(
        pz, raw, aux, cot, mixed, cv, pre, cbc, pbc, st, back, cw, cbw, hp, out_all, weights, normed
    )
    ge, output = lax.optimization_barrier((ge, output))

    def rows_of(*vectors):
        flat = jnp.concatenate([v.reshape(-1) for v in vectors])
        rows = -(-flat.shape[0] // 8192) * 8
        return jnp.pad(flat, (0, rows * 1024 - flat.shape[0])).reshape(rows, 1024)

    shared = rows_of(gmap[:5], gpre[0] / pre_gain)
    skip_sums = jnp.sum(gch[5].reshape(heads, HEADDIM), axis=-1)
    flat = jnp.concatenate([shared, rows_of(gch[:5], gch[6], jnp.sum(ghead, axis=-1), skip_sums)])
    own_rows, flat, grad_hidden = reduce_all(
        normed, ge, flat, shared.shape[0], dg, hidden, grad_out, pre_gain, size, n
    )
    wide = 2 * inner
    grad_zx_weight = own_rows[:, :wide]
    grad_step_weight = own_rows[:, wide + 2 * STATE :][:, :heads]
    grad_bc_weight = swap_sum(own_rows[:, wide : wide + 2 * STATE], n)

    if n != 2:
        gain_grad = scatter_sum(part(dg), here, n, me, 1) * pre_gain
        grad_hidden = (
            grad_out.astype(F32)
            + inv_rms * gain_grad
            - hidden_f * inv_rms**3 * jnp.mean(hidden_f * gain_grad, axis=-1, keepdims=True)
        ).astype(BF)

    sums = flat[: shared.shape[0]].reshape(-1)
    shared_map = sums[: 5 * 2 * STATE].reshape(5, 2 * STATE)
    grad_pre = sums[5 * 2 * STATE :][:width]
    rest = flat[shared.shape[0] :].reshape(-1)
    channel = rest[: 6 * inner].reshape(6, inner)
    per_head = rest[6 * inner :][: 3 * heads].reshape(3, heads)
    return (
        output, grad_hidden, grad_pre, grad_zx_weight, grad_bc_weight, grad_step_weight,
        channel[:4], channel[4], shared_map[:4], shared_map[4], per_head[0], per_head[1], per_head[2],
        channel[5], grad_out_weight,
    )


def solution(mesh):
    placed = (
        P("dp", "tensor", None), P(), P("dp", "tensor"), P("dp", None), P("dp", "tensor"), P(None, "tensor"),
        P("tensor"), P(), P(), P("tensor"), P("tensor"), P("tensor"), P("tensor"), P("tensor", "dp"),
        P("dp", None), P("dp", None), P("dp", "tensor", None),
    )
    return jax.shard_map(
        body,
        mesh=mesh,
        in_specs=placed,
        out_specs=(
            P("dp", "tensor", None), P("dp", "tensor", None), P(), P("dp", "tensor"), P("dp", None), P("dp", "tensor"),
            P(None, "tensor"), P("tensor"), P(), P(), P("tensor"), P("tensor"), P("tensor"), P("tensor"),
            P("tensor", "dp"),
        ),
        check_vma=False,
    )
```

```python
import collections
import functools
import jax
import jax.numpy as jnp
from jax import lax
from jax.experimental import pallas as pl
from jax.experimental.pallas import tpu as pltpu
from jax.sharding import PartitionSpec as P

HEADDIM = 64
STATE = 128
CHUNK = 128
TAPS = 4
HALO = 8
AUX = 16
LOG2E = 1.4426950408889634
FAR = -1e30
BLOCK = 256
VMEM_LIMIT = 58 * 1024 * 1024
MESH = pl.DeviceIdType.MESH
PIECES = 2
epsilon = 1e-05
BF = jnp.bfloat16
F32 = jnp.float32


def sigmoid(v):
    return 0.5 * jnp.tanh(0.5 * v) + 0.5


def split3(v):
    a = v.astype(BF)
    r = v - a.astype(F32)
    b = r.astype(BF)
    c = (r - b.astype(F32)).astype(BF)
    return a, b, c


def dot_nn(a, b):
    return lax.dot_general(a, b, (((1,), (0,)), ((), ())), preferred_element_type=F32)


def dot_nt(a, b):
    return lax.dot_general(a, b, (((1,), (1,)), ((), ())), preferred_element_type=F32)


def exact_dot(v, ones):
    rows = v.shape[0]
    out = dot_nn(jnp.concatenate(split3(v), axis=0), ones)
    return out[:rows] + out[rows : 2 * rows] + out[2 * rows :]


def iota2(shape, dim):
    return lax.broadcasted_iota(jnp.int32, shape, dim)


def pieces(raw, bias, rate, aux, tri):
    pad = aux[1:2]
    pre = raw + bias
    soft = jnp.maximum(pre, 0.0) + jnp.log1p(jnp.exp(-jnp.abs(pre)))
    dt = soft * pad
    cum = exact_dot(dt * rate, tri) * LOG2E
    carried = jnp.exp2(cum) * aux[5:6]
    toward = jnp.exp2(cum[:, CHUNK - 1 : CHUNK] - cum) * aux[6:7]
    return dt, cum, carried, toward


def expander(heads, inner, place):
    row = lax.rem(iota2((256, inner), 0), 128)
    head = lax.div(iota2((256, inner), 1), HEADDIM)
    return jnp.where(row == head + place, 1.0, 0.0).astype(BF)


def collector(inner, place):
    head = lax.div(iota2((inner, 128), 0), HEADDIM)
    lane = iota2((inner, 128), 1)
    return jnp.where(lane == head + place, 1.0, 0.0).astype(BF)


def hi_lo(cols):
    hi = cols.astype(BF)
    return jnp.concatenate([hi, (cols - hi.astype(F32)).astype(BF)], axis=1)


def compact(rows_list):
    used = sum(r.shape[0] for r in rows_list)
    if used < 128:
        rows_list = list(rows_list) + [jnp.zeros((128 - used, CHUNK), F32)]
    return jnp.concatenate(rows_list, axis=0).T


def split_pair(first, second, low):
    gate = jnp.where(low, first, pltpu.roll(second, HEADDIM, 1))
    value = jnp.where(low, pltpu.roll(first, HEADDIM, 1), second)
    return gate, value


Place = collections.namedtuple("Place", ("first", "second", "pair", "fused", "steps", "length"))


def factors(size):
    first = 4 if size % 8 == 0 else 1
    return first, size // (2 * first)


class Spot:
    def __init__(self, place):
        self.first, self.second = place.first, place.second
        self.index = lax.axis_index("dp")
        self.me = lax.axis_index("tensor")
        self.a = lax.div(self.index, 2 * self.second)
        self.b = lax.rem(lax.div(self.index, 2), self.second)
        self.c = lax.rem(self.index, 2)

    def at(self, i, j, k):
        return (i * self.second + j) * 2 + k

    def around(self, i):
        return lax.rem(self.a + i, self.first)

    def aside(self, j):
        return lax.rem(self.b + j, self.second)

    @property
    def sibling(self):
        return self.at(self.a, self.b, 1 - self.c)

    def greet(self, pair):
        barrier = pltpu.get_barrier_semaphore()
        peers = [(self.sibling, self.me)]
        peers += [(self.at(self.a, self.aside(j), self.c), self.me) for j in range(1, self.second)]
        peers += [(self.at(self.around(i), self.b, self.c), self.me) for i in range(1, self.first)]
        if pair:
            peers.append((self.index, 1 - self.me))
        for peer in peers:
            pl.semaphore_signal(barrier, inc=1, device_id=peer, device_id_type=MESH)
        pl.semaphore_wait(barrier, len(peers))

    def copy(self, src, dst, ss, rs, target, tensor=None):
        return pltpu.make_async_remote_copy(
            src_ref=src, dst_ref=dst, send_sem=ss, recv_sem=rs,
            device_id=(target, self.me if tensor is None else tensor), device_id_type=MESH,
        )

    def arrived(self, dst, rs):
        self.copy(dst, dst, rs, rs, self.sibling).wait_recv()


def when(valid, run):
    def quiet():
        run()

    quiet() if valid is None else pl.when(valid)(quiet)


def gather_sites(first, second):
    return (2 + second) + (first - 1) * 2 * (1 + second) + (2 * first - 1) * (second - 1)


class LineGather:
    def __init__(self, spot, arrays, send_sem, recv_sem, local_sem):
        self.spot, self.arrays = spot, arrays
        self.send_sem, self.recv_sem, self.local_sem = send_sem, recv_sem, local_sem
        self.sites = []

    def rows(self, which, shard):
        own, full = self.arrays[which]
        rows = own.shape[0]
        return full.at[pl.ds(pl.multiple_of(shard * rows, rows), rows)]

    def copies(self, site, shard, target, mine=False):
        return [
            self.spot.copy(
                own if mine else self.rows(w, shard), self.rows(w, shard),
                self.send_sem.at[w, site], self.recv_sem.at[w, shard], target,
            )
            for w, (own, full) in enumerate(self.arrays)
        ]

    def send(self, valid, shard, target, mine=False):
        site = len(self.sites)
        self.sites.append((valid, shard, target, mine))
        when(valid and valid(), lambda: [copy.start() for copy in self.copies(site, shard(), target(), mine)])

    def arrive(self, valid, shard):
        def wait():
            for w in range(len(self.arrays)):
                self.spot.arrived(self.rows(w, shard), self.recv_sem.at[w, shard])

        when(valid, wait)

    def local(self):
        return [
            pltpu.make_async_copy(own, self.rows(w, self.spot.index), self.local_sem.at[w])
            for w, (own, full) in enumerate(self.arrays)
        ]

    def begin(self):
        s = self.spot
        self.send(lambda: s.a < s.first - 1, lambda: s.index, lambda: s.at(s.a + 1, s.b, s.c), True)
        self.send(lambda: s.a > 0, lambda: s.index, lambda: s.at(s.a - 1, s.b, s.c), True)
        for j in range(1, s.second):
            self.send(None, lambda: s.index, lambda j=j: s.at(s.a, s.aside(j), s.c), True)
        self.send(None, lambda: s.index, lambda: s.sibling, True)
        for copy in self.local():
            copy.start()

    def sides(self, hop):
        s = self.spot
        if hop == 0:
            return [(None, lambda: s.a, None, None)]
        return [
            (lambda: s.a - hop >= 0, lambda: s.a - hop, lambda: s.a < s.first - 1, lambda: s.at(s.a + 1, s.b, s.c)),
            (lambda: s.a + hop < s.first, lambda: s.a + hop, lambda: s.a > 0, lambda: s.at(s.a - 1, s.b, s.c)),
        ]

    def along(self, hop):
        s = self.spot
        for valid, origin, onward, target in self.sides(hop):
            shard = lambda origin=origin: s.at(origin(), s.b, s.c)
            self.arrive(valid(), shard())
            self.send(lambda valid=valid, onward=onward: valid() & onward(), shard, target)
            for j in range(1, s.second):
                self.send(valid, shard, lambda j=j: s.at(s.a, s.aside(j), s.c))
            self.send(valid, shard, lambda: s.sibling)

    def across(self, hop):
        s = self.spot
        for j in range(1, s.second):
            for valid, origin, onward, target in self.sides(hop):
                shard = lambda origin=origin, j=j: s.at(origin(), s.aside(j), s.c)
                self.arrive(valid and valid(), shard())
                self.send(valid, shard, lambda: s.sibling)

    def finish(self):
        s = self.spot
        for i in range(s.first):
            for j in range(s.second):
                self.arrive(None, s.at(i, j, 1 - s.c))
        for site, (valid, shard, target, mine) in enumerate(self.sites):
            when(
                valid and valid(),
                lambda site=site, shard=shard, target=target, mine=mine: [
                    copy.wait_send() for copy in self.copies(site, shard(), target(), mine)
                ],
            )
        for copy in self.local():
            copy.wait()


class TokenSwap:
    def __init__(self, spot, own, full, sem):
        self.spot, self.own, self.full, self.sem = spot, own, full, sem

    def target(self):
        here = self.own.shape[1]
        return self.full.at[:, pl.ds(pl.multiple_of(self.spot.me * here, here), here)]

    def remote(self):
        s = self.spot
        return s.copy(self.own, self.target(), self.sem.at[0], self.sem.at[1], s.index, 1 - s.me)

    def local(self):
        return pltpu.make_async_copy(self.own, self.target(), self.sem.at[2])

    def begin(self):
        self.remote().start()
        self.local().start()

    def finish(self):
        self.remote().wait()
        self.local().wait()


class HalfSwap:
    def __init__(self, spot, whole, away, sem):
        self.spot, self.whole, self.away, self.sem = spot, whole, away, sem

    def remote(self):
        s = self.spot
        here = self.away.shape[1]
        rows = self.whole.at[:, pl.ds(pl.multiple_of((1 - s.me) * here, here), here)]
        return s.copy(rows, self.away, self.sem.at[0], self.sem.at[1], s.index, 1 - s.me)

    def begin(self):
        self.remote().start()

    def finish(self):
        self.remote().wait()


class LineScatter:
    def __init__(
        self, spot, part, core_buf, x_buf, z_buf, out, core_send, core_recv, x_send, x_recv, z_send, z_recv, cuts=1
    ):
        self.spot, self.part, self.out, self.cuts = spot, part, out, cuts
        self.core_buf, self.x_buf, self.z_buf = core_buf, x_buf, z_buf
        self.sems = (core_send, core_recv, x_send, x_recv, z_send, z_recv)
        self.rows = out.shape[0] // cuts
        self.copies = []
        a = spot.a
        if spot.first == 4:
            near = jnp.minimum(a, 3 - a)
            self.order = [jnp.where(a < 2, d, 3 - d) for d in (3 + 0 * a, 2 - 2 * near, 1 + near)] + [a]
        else:
            self.order = [a]

    def block(self, i, j, k, q):
        rows = self.rows
        return self.part.at[pl.ds(pl.multiple_of((self.spot.at(i, j, k) * self.cuts + q) * rows, rows), rows)]

    def slot(self, i, j, q):
        return (i * self.spot.second + j) * self.cuts + q

    def start(self, make):
        make().start()
        self.copies.append(make)

    def give(self, n, j):
        s, i = self.spot, self.order[n]
        for q in range(self.cuts):

            def make(q=q):
                t = self.slot(i, s.aside(j), q)
                return s.copy(
                    self.block(i, s.aside(j), 1 - s.c, q), self.core_buf.at[t], self.sems[0].at[t],
                    self.sems[1].at[t], s.sibling,
                )

            self.start(make)

    def terms(self, n, j):
        rows = 2 * self.rows * self.cuts
        first_row = self.spot.at(self.order[n], self.spot.aside(j), 0) * self.rows * self.cuts
        return pl.ds(pl.multiple_of(first_row, rows), rows)

    def cross_over(self, n, j):
        s, i = self.spot, self.order[n]
        for q in range(self.cuts):
            t = self.slot(i, s.aside(j), q)
            s.arrived(self.core_buf.at[t], self.sems[1].at[t])
            own = self.block(i, s.aside(j), s.c, q)[...].astype(F32)
            self.core_buf[t] = (own + self.core_buf[t].astype(F32)).astype(BF)

            def make(q=q):
                t = self.slot(i, s.aside(j), q)
                there = (i * (s.second - 1) + s.second - j - 1) * self.cuts + q
                here = (i * (s.second - 1) + j - 1) * self.cuts + q
                return s.copy(
                    self.core_buf.at[t], self.x_buf.at[there], self.sems[2].at[here], self.sems[3].at[there],
                    s.at(s.a, s.aside(j), s.c),
                )

            self.start(make)

    def column_sum(self, n, q):
        s, i = self.spot, self.order[n]
        t = self.slot(i, s.b, q)
        s.arrived(self.core_buf.at[t], self.sems[1].at[t])
        total = self.block(i, s.b, s.c, q)[...].astype(F32) + self.core_buf[t].astype(F32)
        for j in range(1, s.second):
            u = (i * (s.second - 1) + j - 1) * self.cuts + q
            s.arrived(self.x_buf.at[u], self.sems[3].at[u])
            total = total + self.x_buf[u].astype(F32)
        return total

    def produce(self, make_terms, far):
        s = self.spot
        for j in range(1, s.second) if far else [0]:
            for n in range(s.first):
                make_terms(self.terms(n, j))
                self.give(n, j)

    def cross(self):
        for j in range(1, self.spot.second):
            for n in range(self.spot.first):
                self.cross_over(n, j)

    def along(self):
        s = self.spot
        for n in range(s.first):
            for q in range(self.cuts):
                total = self.column_sum(n, q)
                if n == s.first - 1:
                    self.out[q * self.rows : (q + 1) * self.rows] = total
                    continue
                self.core_buf[self.slot(self.order[n], s.b, q)] = total.astype(BF)

                def make(n=n, q=q):
                    z = s.a * self.cuts + q
                    return s.copy(
                        self.core_buf.at[self.slot(self.order[n], s.b, q)], self.z_buf.at[z],
                        self.sems[4].at[n * self.cuts + q], self.sems[5].at[z], s.at(self.order[n], s.b, s.c),
                    )

                self.start(make)

    def chain(self, acc):
        s = self.spot
        for n in range(s.first):
            for q in range(self.cuts):
                i = self.order[n]
                total = self.column_sum(n, q)
                if n == s.first - 1:
                    self.out[q * self.rows : (q + 1) * self.rows] = total
                    continue
                down = jnp.where(i > s.a, 0, 1)
                z = (down * s.first + i) * self.cuts + q
                acc[...] = total

                @pl.when(jnp.where(i > s.a, s.a, s.first - 1 - s.a) > 0)
                def _(z=z):
                    s.arrived(self.z_buf.at[z], self.sems[5].at[z])
                    acc[...] = acc[...] + self.z_buf[z].astype(F32)

                self.core_buf[self.slot(i, s.b, q)] = acc[...].astype(BF)

                def make(n=n, q=q, i=i, down=down, z=z):
                    return s.copy(
                        self.core_buf.at[self.slot(i, s.b, q)], self.z_buf.at[z],
                        self.sems[4].at[n * self.cuts + q], self.sems[5].at[z], s.at(s.a + 1 - 2 * down, s.b, s.c),
                    )

                self.start(make)

    def finish_chain(self):
        s = self.spot
        for q in range(self.cuts):
            cut = slice(q * self.rows, (q + 1) * self.rows)
            for down, there in ((0, s.a), (1, s.first - 1 - s.a)):
                z = (down * s.first + s.a) * self.cuts + q

                @pl.when(there > 0)
                def _(z=z, cut=cut):
                    s.arrived(self.z_buf.at[z], self.sems[5].at[z])
                    self.out[cut] = self.out[cut] + self.z_buf[z].astype(F32)

    def wait_sends(self):
        for make in self.copies:
            make().wait_send()

    def finish(self):
        s = self.spot
        for i in range(1, s.first):
            for q in range(self.cuts):
                z = s.around(i) * self.cuts + q
                s.arrived(self.z_buf.at[z], self.sems[5].at[z])
                cut = slice(q * self.rows, (q + 1) * self.rows)
                self.out[cut] = self.out[cut] + self.z_buf[z].astype(F32)
        self.wait_sends()


def forward_kernel(
    place, heads, tok_ref, w_ref, aux_ref, cw_ref, cbw_ref, hp_ref, cot_own, out_own,
    pz_ref, raw_ref, mixed_ref, gated_ref, cv_ref, pre_ref, cbc_ref, pbc_ref, st_ref, stat_ref, out_all, cot_full,
    state, ubuf, bbuf, vd, yint, expand, tri_ref, send_sem, recv_sem, local_sem, cot_sem,
):
    inner = heads * HEADDIM
    pairs = heads // 2
    wide = 2 * inner
    now = pl.program_id(0) * pl.num_programs(1) + pl.program_id(1)
    last = place.steps - 1
    first = now == 0
    spot = Spot(place)
    gather = LineGather(spot, [(out_own, out_all)], send_sem, recv_sem, local_sem)
    swap = TokenSwap(spot, cot_own, cot_full, cot_sem) if place.pair else None

    @pl.when(first)
    def _():
        spot.greet(place.pair)
        gather.begin()
        if swap:
            swap.begin()

    for hop in range(1, place.first):

        @pl.when(now == min(hop, last))
        def _(hop=hop):
            gather.along(hop)
            gather.across(hop - 1)

    @pl.when(first)
    def _():
        for i, place in enumerate((AUX + heads, AUX + 2 * heads, AUX + 3 * heads)):
            expand[i] = expander(heads, inner, place)
        tri_ref[...] = jnp.where(iota2((CHUNK, CHUNK), 0) <= iota2((CHUNK, CHUNK), 1), 1.0, 0.0).astype(BF)

    @pl.when(pl.program_id(1) == 0)
    def _():
        state[...] = jnp.zeros_like(state)
        ubuf[0:HALO] = jnp.zeros((HALO, inner), F32)
        bbuf[0:HALO] = jnp.zeros((HALO, 2 * STATE), F32)

    tok = tok_ref[0]
    side = dot_nn(tok, w_ref[:, wide:])
    raw_ref[0] = side[:, 2 * STATE :].T[0:heads]
    pz_ref[0, :, wide:] = side[:, : 2 * STATE].astype(BF)
    for p in range(pairs):
        pz_ref[0, :, 256 * p : 256 * p + 256] = dot_nn(tok, w_ref[:, 256 * p : 256 * p + 256]).astype(BF)

    def chunk_step(step, carry):
        here = pl.ds(pl.multiple_of(step * CHUNK, CHUNK), CHUNK)
        aux = aux_ref[0, :, here]
        raw = raw_ref[0, :, here]
        bc = pz_ref[0, here, wide:]
        dt, cum, carried, toward = pieces(raw, hp_ref[0], hp_ref[1], aux, tri_ref[...])
        cols = compact([aux, cum, dt, carried, toward])
        both = hi_lo(cols)
        dtx = dot_nn(both, expand[0])
        carx = dot_nn(both, expand[1])
        towx = dot_nn(both, expand[2])
        pad = cols[:, 1:2]
        same = [None] + [cols[:, 1 + k : 2 + k] for k in range(1, TAPS)]
        low = iota2((CHUNK, 128), 1) < HEADDIM

        bbuf[HALO:] = bc.astype(F32) * pad
        maps = cbw_ref[TAPS : TAPS + 1] + cbw_ref[0:1] * bbuf[HALO:]
        for k in range(1, TAPS):
            maps = maps + cbw_ref[k : k + 1] * (same[k] * bbuf[HALO - k : HALO - k + CHUNK])
        pbc_ref[0, here] = maps.astype(BF)
        maps = (maps * sigmoid(maps)).astype(BF)
        cbc_ref[0, here] = maps
        bbuf[0:HALO] = bbuf[CHUNK : CHUNK + HALO]
        keys, queries = maps[:, :STATE], maps[:, STATE:]
        scores = dot_nt(queries, keys)
        keys_t = keys.astype(F32).T.astype(BF)

        for p in range(pairs):
            s = slice(128 * p, 128 * p + 128)
            x0 = pz_ref[0, here, 256 * p : 256 * p + 128].astype(F32)
            x1 = pz_ref[0, here, 256 * p + 128 : 256 * p + 256].astype(F32)
            value = jnp.where(low, pltpu.roll(x0, HEADDIM, 1), x1)
            ubuf[HALO:, s] = value * pad
            pre = cw_ref[TAPS : TAPS + 1, s] + cw_ref[0:1, s] * ubuf[HALO:, s]
            for k in range(1, TAPS):
                pre = pre + cw_ref[k : k + 1, s] * (same[k] * ubuf[HALO - k : HALO - k + CHUNK, s])
            pre_ref[0, here, s] = pre.astype(BF)
            cv = (pre * sigmoid(pre)).astype(BF)
            cv_ref[0, here, s] = cv
            vd[:, s] = (cv.astype(F32) * dtx[:, s]).astype(BF)
        ubuf[0:HALO] = ubuf[CHUNK : CHUNK + HALO]

        old = state[...]
        old_b = old.astype(BF)
        st_ref[0, step] = old_b
        yint[...] = dot_nn(queries, old_b) * carx
        state[...] = carx[CHUNK - 1 : CHUNK] * old + dot_nn(keys_t, (vd[...].astype(F32) * towx).astype(BF))

        inside = (iota2((CHUNK, CHUNK), 0) >= iota2((CHUNK, CHUNK), 1)) & (cols[:, 0:1] == aux[0:1])
        fence = jnp.where(inside, 0.0, FAR)
        squares = jnp.zeros((CHUNK, 128), F32)
        for p in range(pairs):
            s = slice(128 * p, 128 * p + 128)
            mix = []
            for h in (2 * p, 2 * p + 1):
                decay = jnp.exp2(cols[:, AUX + h : AUX + h + 1] - cum[h : h + 1] + fence)
                mix.append((scores * decay).astype(BF))
            v = vd[:, s]
            zero = jnp.zeros_like(v)
            stacked = jnp.concatenate([jnp.where(low, v, zero), jnp.where(low, zero, v)], axis=0)
            y = dot_nn(jnp.concatenate(mix, axis=1), stacked)
            mixed = y + yint[:, s] + cw_ref[5:6, s] * cv_ref[0, here, s].astype(F32)
            x0 = pz_ref[0, here, 256 * p : 256 * p + 128].astype(F32)
            x1 = pz_ref[0, here, 256 * p + 128 : 256 * p + 256].astype(F32)
            gate = jnp.where(low, x0, pltpu.roll(x1, HEADDIM, 1))
            gated = mixed * (gate * sigmoid(gate))
            mixed_ref[0, here, s] = mixed.astype(BF)
            gated_ref[0, here, s] = (gated * cw_ref[6:7, s]).astype(BF)
            squares = squares + gated * gated
        lane = iota2((CHUNK, 128), 1)
        sums = jnp.where(lane == 0, jnp.sum(squares, axis=1, keepdims=True), 0.0)
        stat_ref[0, :, here] = sums.T[0:8]
        return carry

    lax.fori_loop(0, BLOCK // CHUNK, chunk_step, 0)

    @pl.when(now == last)
    def _():
        gather.across(place.first - 1)
        gather.finish()
        if swap:
            swap.finish()


def backward_kernel(
    place, heads, pz_ref, raw_ref, aux_ref, cot_ref, mixed_ref, cv_ref, pre_ref, cbc_ref, pbc_ref,
    st_ref, stat_ref, cw_ref, cbw_ref, hp_ref, out_ref, w_ref, tok_ref, y_ref, gn_all, cot_all, stat_all,
    ge_ref, dg_ref, flat_ref, y_away, grad_rows,
    g_s, dstate, cbuf, dbuf, vd, gm_s, gmc_s, ggate_s, bs_s, expand, collect, tri_ref, suf_ref, ghead_ref,
    normed_s, part_buf, core_buf, x_buf, z_buf, core_send, core_recv, x_send, x_recv, z_send, z_recv, y_sem,
):
    inner = heads * HEADDIM
    pairs = heads // 2
    wide = 2 * inner
    now = pl.program_id(0) * pl.num_programs(1) + pl.program_id(1)
    last = place.steps - 1
    first = now == 0
    gch_ref = flat_ref.at[8:16, 0:inner]
    gmap_ref = flat_ref.at[0:8, 0 : 2 * STATE]
    gpre_ref = flat_ref.at[5:6]
    spot = Spot(place)
    scatter = None
    if place.fused:
        scatter = LineScatter(
            spot, part_buf, core_buf, x_buf, z_buf, grad_rows, core_send, core_recv, x_send, x_recv, z_send, z_recv
        )

        def out_terms(there):
            part_buf[there] = lax.dot_general(
                cot_all[:, there], normed_s[...], (((0,), (0,)), ((), ())), preferred_element_type=F32
            ).astype(BF)

    if place.fused or place.pair:

        @pl.when(first)
        def _():
            spot.greet(place.pair)

    if place.pair:
        half = HalfSwap(spot, y_ref, y_away, y_sem)
        pl.when(first)(half.begin)

    if place.fused:

        @pl.when(first)
        def _():
            def scale(step, carry):
                rows = pl.ds(pl.multiple_of(step * CHUNK, CHUNK), CHUNK)
                seq = lax.div(step, place.length // CHUNK)
                there = pl.ds(pl.multiple_of(lax.rem(step, place.length // CHUNK) * CHUNK, CHUNK), CHUNK)
                rms_col = compact([stat_all[seq, :, there]])[:, 0:1]
                normed_s[rows] = (gn_all[rows].astype(F32) * rms_col).astype(BF)
                return carry

            lax.fori_loop(0, normed_s.shape[0] // CHUNK, scale, 0)
            scatter.produce(out_terms, True)

        @pl.when(now == min(1, last))
        def _():
            scatter.cross()
            scatter.produce(out_terms, False)

        @pl.when(now == min(2, last))
        def _():
            scatter.along()

    @pl.when(first)
    def _():
        for i, place in enumerate((AUX + heads, AUX + 2 * heads, AUX + 3 * heads)):
            expand[i] = expander(heads, inner, place)
        collect[0] = collector(inner, heads)
        collect[1] = collector(inner, 2 * heads)
        r, c = iota2((CHUNK, CHUNK), 0), iota2((CHUNK, CHUNK), 1)
        tri_ref[...] = jnp.where(r <= c, 1.0, 0.0).astype(BF)
        suf_ref[...] = jnp.where(r >= c, 1.0, 0.0).astype(BF)
        flat_ref[...] = jnp.zeros_like(flat_ref)
        ghead_ref[...] = jnp.zeros_like(ghead_ref)

    @pl.when(pl.program_id(1) == 0)
    def _():
        dstate[...] = jnp.zeros_like(dstate)
        cbuf[CHUNK:] = jnp.zeros((HALO, inner), F32)
        dbuf[CHUNK:] = jnp.zeros((HALO, 2 * STATE), F32)

    g_s[...] = dot_nn(cot_ref[0], out_ref[...])

    def chunk_step(step, carry):
        here = pl.ds(pl.multiple_of(BLOCK - CHUNK - step * CHUNK, CHUNK), CHUNK)
        aux = aux_ref[0, :, here]
        rate = hp_ref[1]
        dt, cum, carried, toward = pieces(raw_ref[0, :, here], hp_ref[0], rate, aux, tri_ref[...])
        cols = compact([aux, cum, dt, carried, toward, stat_ref[0, :, here]])
        both = hi_lo(cols)
        dtx = dot_nn(both, expand[0])
        carx = dot_nn(both, expand[1])
        towx = dot_nn(both, expand[2])
        pad = cols[:, 1:2]
        ahead = [None] + [cols[:, 7 + k : 8 + k] for k in range(1, TAPS)]
        base = AUX + 4 * heads
        rms, pull = cols[:, base : base + 1], cols[:, base + 1 : base + 2]
        low = iota2((CHUNK, 128), 1) < HEADDIM
        maps = cbc_ref[0, here]
        keys, queries = maps[:, :STATE], maps[:, STATE:]
        queries_t = queries.astype(F32).T.astype(BF)
        scores_t = dot_nt(keys, queries)

        for p in range(pairs):
            s = slice(128 * p, 128 * p + 128)
            x0 = pz_ref[0, here, 256 * p : 256 * p + 128].astype(F32)
            x1 = pz_ref[0, here, 256 * p + 128 : 256 * p + 256].astype(F32)
            gate = jnp.where(low, x0, pltpu.roll(x1, HEADDIM, 1))
            sig = sigmoid(gate)
            act = gate * sig
            mixed = mixed_ref[0, here, s].astype(F32)
            gated = mixed * act
            g = g_s[here, s]
            grad_gated = rms * (g * cw_ref[6:7, s]) - gated * pull
            gm = grad_gated * act
            ggate_s[:, s] = (grad_gated * mixed * (sig * (1.0 + gate * (1.0 - sig)))).astype(BF)
            gm_s[:, s] = gm.astype(BF)
            gmc_s[:, s] = (gm * carx[:, s]).astype(BF)
            cv = cv_ref[0, here, s].astype(F32)
            vd[:, s] = (cv * dtx[:, s]).astype(BF)
            gch_ref[5:6, s] += jnp.sum(gm * cv, axis=0, keepdims=True)
            gch_ref[6:7, s] += jnp.sum(gated * rms * g, axis=0, keepdims=True)

        ds = dstate[...]
        ds_b = ds.astype(BF)
        st = st_ref[0, BLOCK // CHUNK - 1 - step]
        gmc = gmc_s[...]
        cs = dot_nn(queries, st)
        bs = dot_nn(keys, ds_b) * towx
        bs_s[...] = bs
        reach = dot_nn((gmc.astype(F32) * cs).astype(BF), collect[1])
        reach = reach + dot_nn((bs * cv_ref[0, here].astype(F32)).astype(BF), collect[0])
        grad_q = dot_nt(gmc, st)
        grad_k = dot_nt((vd[...].astype(F32) * towx).astype(BF), ds_b)
        keep = carx[CHUNK - 1 : CHUNK]
        held = jnp.sum(st.astype(F32) * ds, axis=0, keepdims=True) * keep
        dstate[...] = keep * ds + dot_nn(queries_t, gmc)

        inside = (iota2((CHUNK, CHUNK), 0) <= iota2((CHUNK, CHUNK), 1)) & (cols[:, 0:1] == aux[0:1])
        fence = jnp.where(inside, 0.0, FAR)
        grad_scores_t = jnp.zeros((CHUNK, CHUNK), F32)
        lane = iota2((CHUNK, 128), 1)
        gathered = reach
        row_sums = []
        for p in range(pairs):
            s = slice(128 * p, 128 * p + 128)
            gm_b = gm_s[:, s]
            zero = jnp.zeros_like(gm_b)
            gm_two = jnp.concatenate([jnp.where(low, gm_b, zero), jnp.where(low, zero, gm_b)], axis=0)
            near = dot_nt(vd[:, s], gm_two)
            mix = []
            for j in range(2):
                h = 2 * p + j
                decay = jnp.exp2(cum[h : h + 1] - cols[:, AUX + h : AUX + h + 1] + fence)
                mix.append((scores_t * decay).astype(BF))
                weighed = decay * near[:, CHUNK * j : CHUNK * j + CHUNK]
                grad_scores_t = grad_scores_t + weighed
                pairs_g = weighed * scores_t
                row_sums.append(jnp.sum(pairs_g, axis=0, keepdims=True))
                gathered = jnp.where(lane == h, jnp.sum(pairs_g, axis=1, keepdims=True), gathered)
            z = dot_nn(jnp.concatenate(mix, axis=1), gm_two)
            gm = gm_b.astype(F32)
            grad_v = cw_ref[5:6, s] * gm + dtx[:, s] * (z + bs_s[:, s])
            x0 = pz_ref[0, here, 256 * p : 256 * p + 128].astype(F32)
            x1 = pz_ref[0, here, 256 * p + 128 : 256 * p + 256].astype(F32)
            u = jnp.where(low, pltpu.roll(x0, HEADDIM, 1), x1) * pad
            pre = pre_ref[0, here, s].astype(F32)
            sig = sigmoid(pre)
            c = grad_v * (sig * (1.0 + pre * (1.0 - sig)))
            cbuf[0:CHUNK, s] = c
            gu = cw_ref[0:1, s] * c
            gch_ref[4:5, s] += jnp.sum(c, axis=0, keepdims=True)
            gch_ref[0:1, s] += jnp.sum(c * u, axis=0, keepdims=True)
            for k in range(1, TAPS):
                shifted = ahead[k] * cbuf[k : k + CHUNK, s]
                gu = gu + cw_ref[k : k + 1, s] * shifted
                gch_ref[k : k + 1, s] += jnp.sum(shifted * u, axis=0, keepdims=True)
            gu = gu * pad
            ggate = ggate_s[:, s].astype(F32)
            ge_ref[0, here, 256 * p : 256 * p + 128] = jnp.where(low, ggate, pltpu.roll(gu, HEADDIM, 1)).astype(BF)
            ge_ref[0, here, 256 * p + 128 : 256 * p + 256] = jnp.where(low, pltpu.roll(ggate, HEADDIM, 1), gu).astype(BF)
        cbuf[CHUNK:] = cbuf[0:HALO]

        gst = grad_scores_t.astype(BF)
        grad_k = grad_k + dot_nn(gst, queries)
        grad_q = grad_q + dot_nn(grad_scores_t.T.astype(BF), keys)
        pbc = pbc_ref[0, here].astype(F32)
        sig = sigmoid(pbc)
        c = jnp.concatenate([grad_k, grad_q], axis=1) * (sig * (1.0 + pbc * (1.0 - sig)))
        dbuf[0:CHUNK] = c
        u = pz_ref[0, here, wide:].astype(F32) * pad
        gu = cbw_ref[0:1] * c
        gmap_ref[4:5] += jnp.sum(c, axis=0, keepdims=True)
        gmap_ref[0:1] += jnp.sum(c * u, axis=0, keepdims=True)
        for k in range(1, TAPS):
            shifted = ahead[k] * dbuf[k : k + CHUNK]
            gu = gu + cbw_ref[k : k + 1] * shifted
            gmap_ref[k : k + 1] += jnp.sum(shifted * u, axis=0, keepdims=True)
        ge_ref[0, here, wide : wide + 2 * STATE] = (gu * pad).astype(BF)
        dbuf[CHUNK:] = dbuf[0:HALO]

        across = gathered.T
        col_sum = across[0:heads]
        kx = across[heads : 2 * heads]
        rint = across[2 * heads : 3 * heads]
        row_sum = jnp.concatenate(row_sums, axis=0)
        k_all = kx * dt
        held_head = exact_dot(jnp.broadcast_to(held, (16, inner)), collect[0])
        held_col = jnp.broadcast_to(held_head[0:1], (CHUNK, 128)).T[heads : 2 * heads]
        diff = row_sum + rint - col_sum - k_all
        grad_a = exact_dot(diff, suf_ref[...]) + jnp.sum(k_all, axis=1, keepdims=True) + held_col
        direct = jnp.where(dt > 0.0, col_sum / jnp.where(dt > 0.0, dt, 1.0), 0.0)
        grad_dt = direct + kx + rate * grad_a
        graw = grad_dt * aux[1:2] * sigmoid(raw_ref[0, :, here] + hp_ref[0])
        ge_ref[0, here, wide + 2 * STATE :] = compact([graw]).astype(BF)
        ghead_ref[0] += graw
        ghead_ref[1] += rate * dt * grad_a
        return carry

    lax.fori_loop(0, BLOCK // CHUNK, chunk_step, 0)
    dg = dot_nt(ge_ref[0], w_ref[...])
    dg_ref[0] = dg.astype(BF)
    gpre_ref[...] += jnp.sum(dg * tok_ref[0].astype(F32), axis=0, keepdims=True)

    @pl.when(now == last)
    def _():
        for i in range(2):
            sums = jnp.broadcast_to(jnp.sum(ghead_ref[i], axis=1, keepdims=True), (heads, 128))
            flat_ref[15:16, 128 * i : 128 * i + 128] = compact([sums])[0:1]
        if place.fused:
            scatter.finish()
        else:
            grad_rows[...] = jnp.zeros_like(grad_rows)
        if place.pair:
            half.finish()


def gather_kernel(
    place, heads, zx_ref, bc_ref, step_ref, hidden_ref, gain_ref, cxw_ref, cxb_ref, cbw_ref, cbb_ref, head_ref,
    ngain_ref, seg_ref, pad_ref,
    w_all, tok_full, aux_ref, cw_ref, cbw_out, hp_ref,
    shard, tok_own, square, send_sem, recv_sem, local_sem, tok_sem,
):
    inner = heads * HEADDIM
    wide = 2 * inner
    spot = Spot(place)
    rows = zx_ref.shape[0]
    shard[:, 0:wide] = zx_ref[...]
    shard[:, wide : wide + 2 * STATE] = bc_ref[...]
    square[...] = jnp.zeros_like(square)
    square[0:heads, 0:rows] = step_ref[...].astype(F32)
    shard[:, wide + 2 * STATE :] = square[...].T[0:rows].astype(BF)
    spot.greet(place.pair)
    gather = LineGather(spot, [(shard, w_all)], send_sem, recv_sem, local_sem)
    gather.begin()

    size = 64
    seqs, here = hidden_ref.shape[0], hidden_ref.shape[1]

    def norm_rows(step, carry):
        seq, cut = lax.div(step, here // size), lax.rem(step, here // size)
        mine = pl.ds(pl.multiple_of(cut * size, size), size)
        hid = hidden_ref[seq, mine].astype(F32)
        inv = lax.rsqrt(jnp.mean(hid * hid, axis=-1, keepdims=True) + epsilon)
        tok_own[seq, mine] = (hid * inv * gain_ref[...]).astype(BF)
        return carry

    lax.fori_loop(0, seqs * (here // size), norm_rows, 0)
    if place.pair:
        swap = TokenSwap(spot, tok_own, tok_full, tok_sem)
        swap.begin()
    else:
        copy = pltpu.make_async_copy(tok_own, tok_full, tok_sem.at[2])
        copy.start()

    square[...] = jnp.zeros_like(square)
    square[0:3, 0:heads] = head_ref[...]
    per_head = square[...].T
    hp_ref[0] = jnp.broadcast_to(per_head[0:heads, 0:1], (heads, 128))
    hp_ref[1] = jnp.broadcast_to(-jnp.exp(per_head[0:heads, 1:2]), (heads, 128))
    cw_ref[0:TAPS] = cxw_ref[...]
    cw_ref[TAPS : TAPS + 1] = cxb_ref[...]
    cw_ref[5:6] = exact_dot(square[0:16], expander(heads, inner, 0)[0:128])[2:3]
    cw_ref[6:7] = ngain_ref[...]
    cw_ref[7:8] = jnp.zeros((1, inner), F32)
    cbw_out[...] = jnp.zeros_like(cbw_out)
    cbw_out[0:TAPS] = cbw_ref[...]
    cbw_out[TAPS : TAPS + 1] = cbb_ref[...]

    length = place.length
    lane = iota2((8, length), 1)
    flag = lambda condition: jnp.where(condition, 1.0, 0.0)[0:1]
    for seq in range(aux_ref.shape[0]):
        seg = jnp.broadcast_to(seg_ref[seq : seq + 1], (8, length))
        aux_ref[seq] = jnp.zeros((AUX, length), F32)
        aux_ref[seq, 0:1] = seg[0:1].astype(F32)
        aux_ref[seq, 1:2] = pad_ref[seq : seq + 1].astype(F32)
        for k in range(1, TAPS):
            aux_ref[seq, 1 + k : 2 + k] = flag((pltpu.roll(seg, k, 1) == seg) & (lane >= k))
            aux_ref[seq, 7 + k : 8 + k] = flag((pltpu.roll(seg, length - k, 1) == seg) & (lane < length - k))
        before = jnp.full((8, CHUNK), -1, jnp.int32)
        for chunk in range(length // CHUNK):
            cut = slice(chunk * CHUNK, (chunk + 1) * CHUNK)
            block = seg[:, cut]
            tail = jnp.broadcast_to(block[:, CHUNK - 1 : CHUNK], (8, CHUNK))
            aux_ref[seq, 5:6, cut] = flag(block == before)
            aux_ref[seq, 6:7, cut] = flag(block == tail)
            before = tail

    gather.across(0) if place.first == 1 else None
    for hop in range(1, place.first):
        gather.along(hop)
        gather.across(hop - 1)
    if place.first > 1:
        gather.across(place.first - 1)
    gather.finish()
    swap.finish() if place.pair else copy.wait()


def out_kernel(place, inner_all, gn_ref, cot_ref, out_ref, stat_ref, y_ref, back_ref, sums, theirs, sem):
    seq, block = pl.program_id(0), pl.program_id(1)
    now = seq * pl.num_programs(1) + block
    if place.pair:
        s = Spot(place)
        barrier = pltpu.get_barrier_semaphore()

        @pl.when(now == 0)
        def _():
            pl.semaphore_signal(barrier, inc=1, device_id=(s.index, 1 - s.me), device_id_type=MESH)
            pl.semaphore_wait(barrier, 1)

    y = dot_nt(gn_ref[0], out_ref[...])
    y_ref[0] = y.astype(BF)
    cross = jnp.sum(y * cot_ref[0].astype(F32), axis=1, keepdims=True)
    row = jnp.broadcast_to(cross, (cross.shape[0], 128)).T[0:8]
    there = pl.ds(pl.multiple_of(block * BLOCK, BLOCK), BLOCK)
    sums[seq, :, there] = jnp.where(iota2(row.shape, 0) == 1, row, stat_ref[0])

    @pl.when(now == place.steps - 1)
    def _():
        total = sums[...]
        if place.pair:
            copy = s.copy(sums, theirs, sem.at[0], sem.at[1], s.index, 1 - s.me)
            copy.start()
            copy.wait()
            total = total + theirs[...]
        back_ref[...] = finish_sums(total, inner_all) if place.pair else total


def finish_sums(total, inner_all):
    lines = lax.broadcasted_iota(jnp.int32, total.shape, 1)
    rms = lax.rsqrt(total[:, 0:1] / inner_all + epsilon)
    pull = rms * rms * rms * (total[:, 1:2] / inner_all)
    return jnp.where(lines == 0, rms, jnp.where(lines == 1, pull, 0.0))


def reduce_kernel(
    place, tok_ref, ge_ref, flat_ref, dg_ref, hidden_ref, cot_ref, gain_ref, y_ref, y_away, back_ref,
    own_ref, sum_ref, gh_ref, output_ref,
    part_buf, core_buf, x_buf, z_buf, acc, dg_buf, bc_buf, bc_send, y_flat, core_flat, x_flat, z_flat, stage,
    core_send, core_recv, x_send, x_recv, z_send, z_recv, flat_send, flat_recv, dg_sem, bc_sem,
):
    spot = Spot(place)
    a, b, c, me, index = spot.a, spot.b, spot.c, spot.me, spot.index
    first, second = place.first, place.second
    scatter = LineScatter(
        spot, part_buf if place.fused else ge_ref, core_buf, x_buf, z_buf, own_ref,
        core_send, core_recv, x_send, x_recv, z_send, z_recv, PIECES,
    )
    spot.greet(place.pair)
    started = []

    def send(*args):
        copy = spot.copy(*args)
        copy.start()
        started.append(copy)

    if place.pair:
        send(flat_ref.at[0:8], y_flat, flat_send.at[0], flat_recv.at[0], index, 1 - me)
        swap = HalfSwap(spot, dg_ref, dg_buf, dg_sem)
        swap.begin()

    def terms(there):
        if place.fused:
            part_buf[there] = lax.dot_general(
                tok_ref[:, there], ge_ref[...], (((0,), (0,)), ((), ())), preferred_element_type=F32
            ).astype(BF)

    work = [(n, j) for j in list(range(1, second)) + [0] for n in range(first)]
    for k, (n, j) in enumerate(work):
        terms(scatter.terms(n, j))
        scatter.give(n, j)
        if k >= 1 and work[k - 1][1] > 0:
            scatter.cross_over(*work[k - 1])

    if place.pair:
        spot.arrived(y_flat, flat_recv.at[0])
        stage[0, 0:8] = flat_ref[0:8] + y_flat[...]
    else:
        stage[0, 0:8] = flat_ref[0:8]
    stage[0, 8:] = flat_ref[8:]
    send(stage.at[0], core_flat, flat_send.at[1], flat_recv.at[1], spot.sibling)
    spot.arrived(core_flat, flat_recv.at[1])
    stage[1] = stage[0] + core_flat[...]
    x_flat[b] = stage[1]
    for j in range(1, second):
        send(stage.at[1], x_flat.at[b], flat_send.at[1 + j], flat_recv.at[2 + b], spot.at(a, spot.aside(j), c))

    scatter.chain(acc)
    for j in range(1, second):
        spot.arrived(x_flat.at[spot.aside(j)], flat_recv.at[2 + spot.aside(j)])
    total = x_flat[0]
    for j in range(1, second):
        total = total + x_flat[j]
    stage[2] = total
    z_flat[a] = total
    for i in range(1, first):
        send(
            stage.at[2], z_flat.at[a], flat_send.at[second + i], flat_recv.at[2 + second + a],
            spot.at(spot.around(i), b, c),
        )

    if place.pair:
        swap.finish()
        here = hidden_ref.shape[1]
        size = 128

        def token_rows(step, carry):
            seq, cut = lax.div(step, here // size), lax.rem(step, here // size)
            mine = pl.ds(pl.multiple_of(cut * size, size), size)
            full = pl.ds(pl.multiple_of(me * here + cut * size, size), size)
            hid = hidden_ref[seq, mine].astype(F32)
            inv = lax.rsqrt(jnp.mean(hid * hid, axis=-1, keepdims=True) + epsilon)
            gain = (dg_ref[seq, full].astype(F32) + dg_buf[seq, mine].astype(F32)) * gain_ref[...]
            pull = inv * inv * inv * jnp.mean(hid * gain, axis=-1, keepdims=True)
            gh_ref[seq, mine] = (cot_ref[seq, mine].astype(F32) + inv * gain - hid * pull).astype(BF)
            rms = compact([back_ref[seq, :, full]])[:, 0:1]
            mixed = y_ref[seq, full].astype(F32) + y_away[seq, mine].astype(F32)
            output_ref[seq, mine] = (hid + rms * mixed).astype(BF)
            return carry

        lax.fori_loop(0, hidden_ref.shape[0] * (here // size), token_rows, 0)
    else:
        gh_ref[...] = jnp.zeros_like(gh_ref)
        output_ref[...] = jnp.zeros_like(output_ref)

    scatter.finish_chain()
    if place.pair:
        edge = own_ref.shape[1] - 128 - 2 * STATE
        bc_send[...] = own_ref[:, edge : edge + 2 * STATE]
        swap_bc = spot.copy(bc_send, bc_buf, bc_sem.at[0], bc_sem.at[1], index, 1 - me)
        swap_bc.start()
    for i in range(1, first):
        spot.arrived(z_flat.at[spot.around(i)], flat_recv.at[2 + second + spot.around(i)])
    total = z_flat[0]
    for i in range(1, first):
        total = total + z_flat[i]
    sum_ref[...] = total
    scatter.wait_sends()
    for copy in started:
        copy.wait_send()
    if place.pair:
        swap_bc.wait()
        own_ref[:, edge : edge + 2 * STATE] = bc_send[...] + bc_buf[...]


def last_kernel(
    heads, own_ref, sum_ref, gh_in, output_in, out_rows, gain_ref,
    output_ref, gh_ref, pre_ref, zx_ref, bc_ref, step_ref, cxw_ref, cxb_ref, cbw_ref, cbb_ref, head_ref, ngain_ref,
    out_ref,
):
    inner = heads * HEADDIM
    wide = 2 * inner
    rows = own_ref.shape[0]
    output_ref[...] = output_in[...]
    gh_ref[...] = gh_in[...]
    pre_ref[...] = sum_ref[5:6] / gain_ref[...]
    zx_ref[...] = own_ref[:, 0:wide]
    bc_ref[...] = own_ref[:, wide : wide + 2 * STATE]
    steps = own_ref[:, wide + 2 * STATE :]
    if rows < 128:
        steps = jnp.concatenate([steps, jnp.zeros((128 - rows, 128), F32)], axis=0)
    step_ref[...] = steps.T[0:heads, 0:rows]
    cxw_ref[...] = sum_ref[8 : 8 + TAPS, 0:inner]
    cxb_ref[...] = sum_ref[8 + TAPS : 9 + TAPS, 0:inner]
    cbw_ref[...] = sum_ref[0:TAPS, 0 : 2 * STATE]
    cbb_ref[...] = sum_ref[TAPS : TAPS + 1, 0 : 2 * STATE]
    skip = exact_dot(jnp.broadcast_to(sum_ref[13:14, 0:inner], (16, inner)), collector(inner, 0))
    head_ref[0:1] = sum_ref[15:16, 0:heads]
    head_ref[1:2] = sum_ref[15:16, 128 : 128 + heads]
    head_ref[2:3] = skip[0:1, 0:heads]
    ngain_ref[...] = sum_ref[14:15, 0:inner]
    out_ref[...] = out_rows[...]


SDS = jax.ShapeDtypeStruct
DMA = pltpu.SemaphoreType.DMA
ANY = pl.BlockSpec(memory_space=pl.ANY)
WHOLE = pl.BlockSpec(memory_space=pltpu.VMEM)


def params(collective=None):
    if collective is None:
        return pltpu.CompilerParams(vmem_limit_bytes=VMEM_LIMIT)
    return pltpu.CompilerParams(vmem_limit_bytes=VMEM_LIMIT, collective_id=collective, has_side_effects=True)


def whole_once(*shape):
    return pl.BlockSpec(shape, lambda s, c: (0,) * len(shape), pipeline_mode=pl.Buffered(1))


def line_sems(place, cuts, lines):
    columns = place.first * max(place.second - 1, 1) * cuts
    blocks = place.first * place.second * cuts
    return [DMA((blocks,)), DMA((blocks,)), DMA((columns,)), DMA((columns,)), DMA((place.first * cuts,)), DMA((lines,))]


def gather_all(place, size, zx, bc, step_t, hidden, gain, cxw, cxb, cbw, cbb, head, ngain, seg, pad):
    seqs, here, width = hidden.shape
    heads, inner = head.shape[1], cxw.shape[1]
    total = 2 * inner + 2 * STATE + 128
    rows = zx.shape[0]
    return pl.pallas_call(
        functools.partial(gather_kernel, place, heads),
        in_specs=[WHOLE] * 13,
        out_specs=[ANY, ANY] + [WHOLE] * 4,
        out_shape=[
            SDS((size * rows, total), BF), SDS((seqs, place.length if place.pair else here, width), BF),
            SDS((seqs, AUX, place.length), F32), SDS((8, inner), F32), SDS((8, 2 * STATE), F32), SDS((2, heads, 128), F32),
        ],
        scratch_shapes=[
            pltpu.VMEM((rows, total), BF), pltpu.VMEM(hidden.shape, BF), pltpu.VMEM((128, 128), F32),
            DMA((1, gather_sites(place.first, place.second))), DMA((1, size)), DMA((1,)), DMA((3,)),
        ],
        compiler_params=params(0),
        name="gather_all",
    )(zx, bc, step_t, hidden, gain, cxw, cxb, cbw, cbb, head, ngain, seg, pad)


def mixer_forward(place, size, tok, weights, aux, cw, cbw, hp, cot_own, out_own):
    seqs, length, width = tok.shape
    heads, inner = hp.shape[1], cw.shape[1]
    wide = 2 * inner + 2 * STATE
    chunks = length // CHUNK
    token = lambda size: pl.BlockSpec((1, BLOCK, size), lambda s, c: (s, c, 0))
    row = lambda high: pl.BlockSpec((1, high, BLOCK), lambda s, c: (s, 0, c))
    return pl.pallas_call(
        functools.partial(forward_kernel, place, heads),
        grid=(seqs, length // BLOCK),
        in_specs=[
            token(width), whole_once(*weights.shape), row(AUX),
            whole_once(8, inner), whole_once(8, 2 * STATE), whole_once(2, heads, 128), WHOLE, ANY,
        ],
        out_specs=[
            token(wide), row(heads), token(inner), token(inner), token(inner), token(inner), token(2 * STATE),
            token(2 * STATE), pl.BlockSpec((1, BLOCK // CHUNK, STATE, inner), lambda s, c: (s, c, 0, 0)), row(8),
            ANY, ANY,
        ],
        out_shape=[
            SDS((seqs, length, wide), BF), SDS((seqs, heads, length), F32),
            SDS((seqs, length, inner), BF), SDS((seqs, length, inner), BF), SDS((seqs, length, inner), BF),
            SDS((seqs, length, inner), BF), SDS((seqs, length, 2 * STATE), BF), SDS((seqs, length, 2 * STATE), BF),
            SDS((seqs, chunks, STATE, inner), BF), SDS((seqs, 8, length), F32),
            SDS((size * out_own.shape[0], inner), BF), SDS((seqs, length, width) if place.pair else (8, 128), BF),
        ],
        scratch_shapes=[
            pltpu.VMEM((STATE, inner), F32), pltpu.VMEM((HALO + CHUNK, inner), F32),
            pltpu.VMEM((HALO + CHUNK, 2 * STATE), F32), pltpu.VMEM((CHUNK, inner), BF),
            pltpu.VMEM((CHUNK, inner), F32), pltpu.VMEM((3, 256, inner), BF), pltpu.VMEM((CHUNK, CHUNK), BF),
            DMA((1, gather_sites(place.first, place.second))), DMA((1, size)), DMA((1,)), DMA((3,)),
        ],
        compiler_params=params(1),
        name="mixer_forward",
    )(tok, weights, aux, cw, cbw, hp, cot_own, out_own)


def out_project(place, inner_all, gn, cot, out_all, stat):
    seqs, length, inner = gn.shape
    width = cot.shape[2]
    token = lambda last: pl.BlockSpec((1, BLOCK, last), lambda s, c: (s, c, 0))
    row = pl.BlockSpec((1, 8, BLOCK), lambda s, c: (s, 0, c))
    shape = (seqs, 8, length)
    return pl.pallas_call(
        functools.partial(out_kernel, place, inner_all),
        grid=(seqs, length // BLOCK),
        in_specs=[token(inner), token(width), whole_once(*out_all.shape), row],
        out_specs=[token(width), pl.BlockSpec(shape, lambda s, c: (0, 0, 0))],
        out_shape=[SDS((seqs, length, width), BF), SDS(shape, F32)],
        scratch_shapes=[pltpu.VMEM(shape, F32), pltpu.VMEM(shape, F32), DMA((2,))],
        compiler_params=params(2 if place.pair else None),
        name="out_project",
    )(gn, cot, out_all, stat)


def mixer_backward(
    place, size, pz, raw, aux, cot, mixed, cv, pre, cbc, pbc, st, stat, cw, cbw, hp, out_all, weights, tok, y, gn
):
    seqs, length, width = cot.shape
    heads, inner = hp.shape[1], cw.shape[1]
    last = length // BLOCK - 1
    here = length // 2 if place.pair else 16
    rows = width // size
    tokens = seqs * length
    fused = place.fused
    token = lambda size: pl.BlockSpec((1, BLOCK, size), lambda s, c: (s, last - c, 0))
    row = lambda high: pl.BlockSpec((1, high, BLOCK), lambda s, c: (s, 0, last - c))
    fixed = lambda *shape: pl.BlockSpec(shape, lambda s, c: (0,) * len(shape))
    gn_all, cot_all = (gn, cot) if fused else (gn[:1, :16], cot[:1, :16])
    gn_all, cot_all = gn_all.reshape(-1, inner), cot_all.reshape(-1, width)
    blocks = place.first * place.second
    columns = place.first * max(place.second - 1, 1)
    rs = lambda count: pltpu.VMEM((count, rows, inner) if fused else (1, 16, 128), BF)
    return pl.pallas_call(
        functools.partial(backward_kernel, place, heads),
        grid=(seqs, length // BLOCK),
        in_specs=[
            token(pz.shape[2]), row(heads), row(AUX), token(width), token(inner), token(inner),
            token(inner), token(2 * STATE), token(2 * STATE),
            pl.BlockSpec((1, BLOCK // CHUNK, STATE, inner), lambda s, c: (s, last - c, 0, 0)), row(8),
            whole_once(8, inner), whole_once(8, 2 * STATE), whole_once(2, heads, 128),
            whole_once(*out_all.shape), whole_once(*weights.shape), token(width), ANY,
            whole_once(*gn_all.shape), whole_once(*cot_all.shape), whole_once(*stat.shape),
        ],
        out_specs=[token(weights.shape[1]), token(width), fixed(16, width), ANY, fixed(rows, inner)],
        out_shape=[
            SDS((seqs, length, weights.shape[1]), BF), SDS((seqs, length, width), BF), SDS((16, width), F32),
            SDS((seqs, here, width), BF), SDS((rows, inner), F32),
        ],
        scratch_shapes=[
            pltpu.VMEM((BLOCK, inner), F32),
            pltpu.VMEM((STATE, inner), F32), pltpu.VMEM((CHUNK + HALO, inner), F32),
            pltpu.VMEM((CHUNK + HALO, 2 * STATE), F32), pltpu.VMEM((CHUNK, inner), BF),
            pltpu.VMEM((CHUNK, inner), BF), pltpu.VMEM((CHUNK, inner), BF), pltpu.VMEM((CHUNK, inner), BF),
            pltpu.VMEM((CHUNK, inner), F32),
            pltpu.VMEM((3, 256, inner), BF), pltpu.VMEM((2, inner, 128), BF),
            pltpu.VMEM((CHUNK, CHUNK), BF), pltpu.VMEM((CHUNK, CHUNK), BF), pltpu.VMEM((2, heads, 128), F32),
            pltpu.VMEM((tokens, inner) if fused else (16, 128), BF),
            pltpu.VMEM((width, inner) if fused else (16, 128), BF),
            rs(blocks), rs(columns), rs(place.first),
        ] + line_sems(place, 1, place.first) + [DMA((2,))],
        compiler_params=params(3 if place.fused or place.pair else None),
        name="mixer_backward",
    )(
        pz, raw, aux, cot, mixed, cv, pre, cbc, pbc, st, stat, cw, cbw, hp, out_all, weights, tok, y,
        gn_all, cot_all, stat,
    )


def reduce_all(place, size, tok, ge, flat, dg, hidden, cot_own, gain, y, y_away, back):
    seqs, length, depth = tok.shape
    width = ge.shape[2]
    rows = depth // size
    if place.fused:
        tok, ge = tok.reshape(seqs * length, depth), ge.reshape(seqs * length, width)
    else:
        ge = jnp.einsum("stp,sty->py", tok, ge, preferred_element_type=F32).astype(BF)
        tok = tok[0, :16]
    if not place.pair:
        flat = jnp.concatenate([lax.psum(flat[:8], "tensor"), flat[8:]])
        dg, hidden, cot_own, y, y_away = [jnp.zeros((1, 16, depth), BF)] * 5
        back = back[:1, :, :128]
    blocks = place.first * place.second * PIECES
    columns = place.first * max(place.second - 1, 1) * PIECES
    lines = 2 * place.first * PIECES
    cut = rows // PIECES
    own, flat, gh, output = pl.pallas_call(
        functools.partial(reduce_kernel, place),
        in_specs=[WHOLE] * 10,
        out_specs=[WHOLE] * 4,
        out_shape=[SDS((rows, width), F32), SDS(flat.shape, F32), SDS(hidden.shape, BF), SDS(hidden.shape, BF)],
        scratch_shapes=[
            pltpu.VMEM((depth, width) if place.fused else (16, 128), BF),
            pltpu.VMEM((blocks, cut, width), BF),
            pltpu.VMEM((columns, cut, width), BF),
            pltpu.VMEM((lines, cut, width), BF),
            pltpu.VMEM((cut, width), F32),
            pltpu.VMEM(hidden.shape, BF),
            pltpu.VMEM((rows, 2 * STATE), F32),
            pltpu.VMEM((rows, 2 * STATE), F32),
            pltpu.VMEM((8, flat.shape[1]), F32),
            pltpu.VMEM(flat.shape, F32),
            pltpu.VMEM((place.second,) + flat.shape, F32),
            pltpu.VMEM((place.first,) + flat.shape, F32),
            pltpu.VMEM((3,) + flat.shape, F32),
        ] + line_sems(place, PIECES, lines) + [
            DMA((1 + place.first + place.second,)), DMA((2 + place.first + place.second,)), DMA((2,)), DMA((2,)),
        ],
        compiler_params=params(4),
        name="reduce_all",
    )(tok, ge, flat, dg, hidden, cot_own, gain, y, y_away, back)
    if not place.pair:
        edge = width - 128 - 2 * STATE
        own = own.at[:, edge : edge + 2 * STATE].set(lax.psum(own[:, edge : edge + 2 * STATE], "tensor"))
    return own, flat, gh, output


def body(
    hidden, pre_gain, zx_weight, bc_weight, step_weight, conv_x_weight, conv_x_bias, conv_bc_weight, conv_bc_bias,
    step_bias, decay_log, skip_gain, norm_gain, out_weight, segment_ids, pad_mask, grad_out,
):
    n, size = lax.axis_size("tensor"), lax.axis_size("dp")
    heads = step_weight.shape[1]
    inner = heads * HEADDIM
    seqs, here, width = hidden.shape
    length = segment_ids.shape[1]
    first, second = factors(size)
    place = Place(first, second, n == 2, (2 * width // size) % 128 == 0, seqs * length // BLOCK, length)
    line = lambda vector: vector.reshape(1, -1)
    gain = line(pre_gain)

    weights, tok, aux, cw, cbw, hp = gather_all(
        place, size, zx_weight, bc_weight, step_weight.T, hidden, gain, conv_x_weight, line(conv_x_bias),
        conv_bc_weight, line(conv_bc_bias), jnp.stack([step_bias, decay_log, skip_gain]), line(norm_gain),
        segment_ids, pad_mask,
    )
    if not place.pair:
        tok = lax.all_gather(tok, "tensor", axis=1, tiled=True)
    pz, raw, mixed, gn, cv, pre, cbc, pbc, st, stat, out_all, cot = mixer_forward(
        place, size, tok, weights, aux, cw, cbw, hp, grad_out, out_weight.T
    )
    if not place.pair:
        cot = lax.all_gather(grad_out, "tensor", axis=1, tiled=True)
    y, back = out_project(place, inner * n, gn, cot, out_all, stat)
    if not place.pair:
        back = finish_sums(lax.psum(back, "tensor"), inner * n)
    ge, dg, flat, y_away, out_rows = mixer_backward(
        place, size, pz, raw, aux, cot, mixed, cv, pre, cbc, pbc, st, back, cw, cbw, hp, out_all, weights, tok, y, gn
    )
    if not place.fused:
        normed_out = (gn.astype(F32) * back[:, 0, :, None]).astype(BF)
        terms = jnp.einsum("str,stc->rc", cot, normed_out, preferred_element_type=F32).astype(BF)
        out_rows = lax.psum_scatter(terms, "dp", scatter_dimension=0, tiled=True).astype(F32)
    own, sums, grad_hidden, output = reduce_all(
        place, size, tok, ge, flat, dg, hidden, grad_out, gain, y, y_away, back
    )
    if not place.pair:
        hidden_f = hidden.astype(F32)
        inv_rms = lax.rsqrt(jnp.mean(hidden_f * hidden_f, axis=-1, keepdims=True) + epsilon)
        scatter = lambda rows: lax.psum_scatter(rows.astype(F32), "tensor", scatter_dimension=1, tiled=True)
        gain_grad = scatter(dg) * pre_gain
        pull = inv_rms**3 * jnp.mean(hidden_f * gain_grad, axis=-1, keepdims=True)
        grad_hidden = (grad_out.astype(F32) + inv_rms * gain_grad - hidden_f * pull).astype(BF)
        output = (hidden_f + scatter(y.astype(F32) * back[:, 0, :, None])).astype(BF)
    rows = own.shape[0]
    output, grad_hidden, grad_pre, gzx, gbc, gstep, gcxw, gcxb, gcbw, gcbb, ghead, gnorm, gout = pl.pallas_call(
        functools.partial(last_kernel, heads),
        in_specs=[WHOLE] * 6,
        out_specs=[WHOLE] * 13,
        out_shape=[
            SDS(hidden.shape, BF), SDS(hidden.shape, BF), SDS((1, width), F32), SDS((rows, 2 * inner), F32),
            SDS((rows, 2 * STATE), F32), SDS((heads, rows), F32), SDS((TAPS, inner), F32), SDS((1, inner), F32),
            SDS((TAPS, 2 * STATE), F32), SDS((1, 2 * STATE), F32), SDS((3, heads), F32), SDS((1, inner), F32),
            SDS((rows, inner), F32),
        ],
        compiler_params=params(),
        name="outputs",
    )(own, sums, grad_hidden, output, out_rows, gain)
    return (
        output, grad_hidden, grad_pre[0], gzx, gbc, gstep.T, gcxw, gcxb[0], gcbw, gcbb[0], ghead[0], ghead[1], ghead[2],
        gnorm[0], gout.T,
    )


def solution(mesh):
    placed = (
        P("dp", "tensor", None), P(), P("dp", "tensor"), P("dp", None), P("dp", "tensor"), P(None, "tensor"),
        P("tensor"), P(), P(), P("tensor"), P("tensor"), P("tensor"), P("tensor"), P("tensor", "dp"),
        P("dp", None), P("dp", None), P("dp", "tensor", None),
    )
    return jax.shard_map(
        body,
        mesh=mesh,
        in_specs=placed,
        out_specs=(
            P("dp", "tensor", None), P("dp", "tensor", None), P(), P("dp", "tensor"), P("dp", None), P("dp", "tensor"),
            P(None, "tensor"), P("tensor"), P(), P(), P("tensor"), P("tensor"), P("tensor"), P("tensor"),
            P("tensor", "dp"),
        ),
        check_vma=False,
    )
```

```python
import collections
import functools
import jax
import jax.numpy as jnp
from jax import lax
from jax.experimental import pallas as pl
from jax.experimental.pallas import tpu as pltpu
from jax.sharding import PartitionSpec as P

HEADDIM = 64
STATE = 128
CHUNK = 128
TAPS = 4
HALO = 8
AUX = 16
LOG2E = 1.4426950408889634
FAR = -1e30
BLOCK = 256
VMEM_LIMIT = 58 * 1024 * 1024
MESH = pl.DeviceIdType.MESH
PIECES = 2
epsilon = 1e-05
BF = jnp.bfloat16
F32 = jnp.float32


def sigmoid(v):
    return 0.5 * jnp.tanh(0.5 * v) + 0.5


def split3(v):
    a = v.astype(BF)
    r = v - a.astype(F32)
    b = r.astype(BF)
    c = (r - b.astype(F32)).astype(BF)
    return a, b, c


def dot_nn(a, b):
    return lax.dot_general(a, b, (((1,), (0,)), ((), ())), preferred_element_type=F32)


def dot_nt(a, b):
    return lax.dot_general(a, b, (((1,), (1,)), ((), ())), preferred_element_type=F32)


def exact_dot(v, ones):
    rows = v.shape[0]
    out = dot_nn(jnp.concatenate(split3(v), axis=0), ones)
    return out[:rows] + out[rows : 2 * rows] + out[2 * rows :]


def iota2(shape, dim):
    return lax.broadcasted_iota(jnp.int32, shape, dim)


def pieces(raw, bias, rate, aux, tri):
    pad = aux[1:2]
    pre = raw + bias
    soft = jnp.maximum(pre, 0.0) + jnp.log1p(jnp.exp(-jnp.abs(pre)))
    dt = soft * pad
    cum = exact_dot(dt * rate, tri) * LOG2E
    carried = jnp.exp2(cum) * aux[5:6]
    toward = jnp.exp2(cum[:, CHUNK - 1 : CHUNK] - cum) * aux[6:7]
    return dt, cum, carried, toward


def expander(heads, inner, place):
    row = lax.rem(iota2((256, inner), 0), 128)
    head = lax.div(iota2((256, inner), 1), HEADDIM)
    return jnp.where(row == head + place, 1.0, 0.0).astype(BF)


def collector(inner, place):
    head = lax.div(iota2((inner, 128), 0), HEADDIM)
    lane = iota2((inner, 128), 1)
    return jnp.where(lane == head + place, 1.0, 0.0).astype(BF)


def hi_lo(cols):
    hi = cols.astype(BF)
    return jnp.concatenate([hi, (cols - hi.astype(F32)).astype(BF)], axis=1)


def compact(rows_list):
    used = sum(r.shape[0] for r in rows_list)
    if used < 128:
        rows_list = list(rows_list) + [jnp.zeros((128 - used, CHUNK), F32)]
    return jnp.concatenate(rows_list, axis=0).T


def split_pair(first, second, low):
    gate = jnp.where(low, first, pltpu.roll(second, HEADDIM, 1))
    value = jnp.where(low, pltpu.roll(first, HEADDIM, 1), second)
    return gate, value


Place = collections.namedtuple("Place", ("first", "second", "pair", "steps", "length"))


def factors(size):
    first = 4 if size % 8 == 0 else 1
    return first, size // (2 * first)


class Spot:
    def __init__(self, place):
        self.first, self.second = place.first, place.second
        self.index = lax.axis_index("dp")
        self.me = lax.axis_index("tensor")
        self.a = lax.div(self.index, 2 * self.second)
        self.b = lax.rem(lax.div(self.index, 2), self.second)
        self.c = lax.rem(self.index, 2)

    def at(self, i, j, k):
        return (i * self.second + j) * 2 + k

    def around(self, i):
        return lax.rem(self.a + i, self.first)

    def aside(self, j):
        return lax.rem(self.b + j, self.second)

    @property
    def sibling(self):
        return self.at(self.a, self.b, 1 - self.c)

    def greet(self, pair):
        barrier = pltpu.get_barrier_semaphore()
        peers = [(self.sibling, self.me)]
        peers += [(self.at(self.a, self.aside(j), self.c), self.me) for j in range(1, self.second)]
        peers += [(self.at(self.around(i), self.b, self.c), self.me) for i in range(1, self.first)]
        if pair:
            peers.append((self.index, 1 - self.me))
        for peer in peers:
            pl.semaphore_signal(barrier, inc=1, device_id=peer, device_id_type=MESH)
        pl.semaphore_wait(barrier, len(peers))

    def copy(self, src, dst, ss, rs, target, tensor=None):
        return pltpu.make_async_remote_copy(
            src_ref=src, dst_ref=dst, send_sem=ss, recv_sem=rs,
            device_id=(target, self.me if tensor is None else tensor), device_id_type=MESH,
        )

    def arrived(self, dst, rs):
        self.copy(dst, dst, rs, rs, self.sibling).wait_recv()


def when(valid, run):
    def quiet():
        run()

    quiet() if valid is None else pl.when(valid)(quiet)


def gather_sites(first, second):
    return (2 + second) + (first - 1) * 2 * (1 + second) + (2 * first - 1) * (second - 1)


class LineGather:
    def __init__(self, spot, arrays, send_sem, recv_sem, local_sem):
        self.spot, self.arrays = spot, arrays
        self.send_sem, self.recv_sem, self.local_sem = send_sem, recv_sem, local_sem
        self.sites = []

    def rows(self, which, shard):
        own, full = self.arrays[which]
        rows = own.shape[0]
        return full.at[pl.ds(pl.multiple_of(shard * rows, rows), rows)]

    def copies(self, site, shard, target, mine=False):
        return [
            self.spot.copy(
                own if mine else self.rows(w, shard), self.rows(w, shard),
                self.send_sem.at[w, site], self.recv_sem.at[w, shard], target,
            )
            for w, (own, full) in enumerate(self.arrays)
        ]

    def send(self, valid, shard, target, mine=False):
        site = len(self.sites)
        self.sites.append((valid, shard, target, mine))
        when(valid and valid(), lambda: [copy.start() for copy in self.copies(site, shard(), target(), mine)])

    def arrive(self, valid, shard):
        def wait():
            for w in range(len(self.arrays)):
                self.spot.arrived(self.rows(w, shard), self.recv_sem.at[w, shard])

        when(valid, wait)

    def local(self):
        return [
            pltpu.make_async_copy(own, self.rows(w, self.spot.index), self.local_sem.at[w])
            for w, (own, full) in enumerate(self.arrays)
        ]

    def begin(self):
        s = self.spot
        self.send(lambda: s.a < s.first - 1, lambda: s.index, lambda: s.at(s.a + 1, s.b, s.c), True)
        self.send(lambda: s.a > 0, lambda: s.index, lambda: s.at(s.a - 1, s.b, s.c), True)
        for j in range(1, s.second):
            self.send(None, lambda: s.index, lambda j=j: s.at(s.a, s.aside(j), s.c), True)
        self.send(None, lambda: s.index, lambda: s.sibling, True)
        for copy in self.local():
            copy.start()

    def sides(self, hop):
        s = self.spot
        if hop == 0:
            return [(None, lambda: s.a, None, None)]
        return [
            (lambda: s.a - hop >= 0, lambda: s.a - hop, lambda: s.a < s.first - 1, lambda: s.at(s.a + 1, s.b, s.c)),
            (lambda: s.a + hop < s.first, lambda: s.a + hop, lambda: s.a > 0, lambda: s.at(s.a - 1, s.b, s.c)),
        ]

    def along(self, hop):
        s = self.spot
        for valid, origin, onward, target in self.sides(hop):
            shard = lambda origin=origin: s.at(origin(), s.b, s.c)
            self.arrive(valid(), shard())
            self.send(lambda valid=valid, onward=onward: valid() & onward(), shard, target)
            for j in range(1, s.second):
                self.send(valid, shard, lambda j=j: s.at(s.a, s.aside(j), s.c))
            self.send(valid, shard, lambda: s.sibling)

    def across(self, hop):
        s = self.spot
        for j in range(1, s.second):
            for valid, origin, onward, target in self.sides(hop):
                shard = lambda origin=origin, j=j: s.at(origin(), s.aside(j), s.c)
                self.arrive(valid and valid(), shard())
                self.send(valid, shard, lambda: s.sibling)

    def finish(self):
        s = self.spot
        for i in range(s.first):
            for j in range(s.second):
                self.arrive(None, s.at(i, j, 1 - s.c))
        for site, (valid, shard, target, mine) in enumerate(self.sites):
            when(
                valid and valid(),
                lambda site=site, shard=shard, target=target, mine=mine: [
                    copy.wait_send() for copy in self.copies(site, shard(), target(), mine)
                ],
            )
        for copy in self.local():
            copy.wait()


class TokenSwap:
    def __init__(self, spot, own, full, sem):
        self.spot, self.own, self.full, self.sem = spot, own, full, sem

    def target(self):
        here = self.own.shape[1]
        return self.full.at[:, pl.ds(pl.multiple_of(self.spot.me * here, here), here)]

    def remote(self):
        s = self.spot
        return s.copy(self.own, self.target(), self.sem.at[0], self.sem.at[1], s.index, 1 - s.me)

    def local(self):
        return pltpu.make_async_copy(self.own, self.target(), self.sem.at[2])

    def begin(self):
        self.remote().start()
        self.local().start()

    def finish(self):
        self.remote().wait()
        self.local().wait()


class HalfSwap:
    def __init__(self, spot, whole, away, sem):
        self.spot, self.whole, self.away, self.sem = spot, whole, away, sem

    def remote(self):
        s = self.spot
        here = self.away.shape[1]
        rows = self.whole.at[:, pl.ds(pl.multiple_of((1 - s.me) * here, here), here)]
        return s.copy(rows, self.away, self.sem.at[0], self.sem.at[1], s.index, 1 - s.me)

    def begin(self):
        self.remote().start()

    def finish(self):
        self.remote().wait()


class LineScatter:
    def __init__(
        self, spot, part, core_buf, x_buf, z_buf, out, core_send, core_recv, x_send, x_recv, z_send, z_recv, cuts=1
    ):
        self.spot, self.part, self.out, self.cuts = spot, part, out, cuts
        self.core_buf, self.x_buf, self.z_buf = core_buf, x_buf, z_buf
        self.sems = (core_send, core_recv, x_send, x_recv, z_send, z_recv)
        self.rows = out.shape[0] // cuts
        self.copies = []
        a = spot.a
        if spot.first == 4:
            near = jnp.minimum(a, 3 - a)
            self.order = [jnp.where(a < 2, d, 3 - d) for d in (3 + 0 * a, 2 - 2 * near, 1 + near)] + [a]
        else:
            self.order = [a]

    def block(self, i, j, k, q):
        rows = self.rows
        return self.part.at[pl.ds(pl.multiple_of((self.spot.at(i, j, k) * self.cuts + q) * rows, rows), rows)]

    def slot(self, i, j, q):
        return (i * self.spot.second + j) * self.cuts + q

    def start(self, make):
        make().start()
        self.copies.append(make)

    def give(self, n, j):
        s, i = self.spot, self.order[n]
        for q in range(self.cuts):

            def make(q=q):
                t = self.slot(i, s.aside(j), q)
                return s.copy(
                    self.block(i, s.aside(j), 1 - s.c, q), self.core_buf.at[t], self.sems[0].at[t],
                    self.sems[1].at[t], s.sibling,
                )

            self.start(make)

    def terms(self, n, j):
        rows = 2 * self.rows * self.cuts
        first_row = self.spot.at(self.order[n], self.spot.aside(j), 0) * self.rows * self.cuts
        return pl.ds(pl.multiple_of(first_row, rows), rows)

    def cross_over(self, n, j):
        s, i = self.spot, self.order[n]
        for q in range(self.cuts):
            t = self.slot(i, s.aside(j), q)
            s.arrived(self.core_buf.at[t], self.sems[1].at[t])
            own = self.block(i, s.aside(j), s.c, q)[...].astype(F32)
            self.core_buf[t] = (own + self.core_buf[t].astype(F32)).astype(BF)

            def make(q=q):
                t = self.slot(i, s.aside(j), q)
                there = (i * (s.second - 1) + s.second - j - 1) * self.cuts + q
                here = (i * (s.second - 1) + j - 1) * self.cuts + q
                return s.copy(
                    self.core_buf.at[t], self.x_buf.at[there], self.sems[2].at[here], self.sems[3].at[there],
                    s.at(s.a, s.aside(j), s.c),
                )

            self.start(make)

    def column_sum(self, n, q):
        s, i = self.spot, self.order[n]
        t = self.slot(i, s.b, q)
        s.arrived(self.core_buf.at[t], self.sems[1].at[t])
        total = self.block(i, s.b, s.c, q)[...].astype(F32) + self.core_buf[t].astype(F32)
        for j in range(1, s.second):
            u = (i * (s.second - 1) + j - 1) * self.cuts + q
            s.arrived(self.x_buf.at[u], self.sems[3].at[u])
            total = total + self.x_buf[u].astype(F32)
        return total

    def produce(self, make_terms, far):
        s = self.spot
        for j in range(1, s.second) if far else [0]:
            for n in range(s.first):
                make_terms(self.terms(n, j))
                self.give(n, j)

    def cross(self):
        for j in range(1, self.spot.second):
            for n in range(self.spot.first):
                self.cross_over(n, j)

    def along(self):
        s = self.spot
        for n in range(s.first):
            for q in range(self.cuts):
                total = self.column_sum(n, q)
                if n == s.first - 1:
                    self.out[q * self.rows : (q + 1) * self.rows] = total
                    continue
                self.core_buf[self.slot(self.order[n], s.b, q)] = total.astype(BF)

                def make(n=n, q=q):
                    z = s.a * self.cuts + q
                    return s.copy(
                        self.core_buf.at[self.slot(self.order[n], s.b, q)], self.z_buf.at[z],
                        self.sems[4].at[n * self.cuts + q], self.sems[5].at[z], s.at(self.order[n], s.b, s.c),
                    )

                self.start(make)

    def chain(self, acc, order):
        s = self.spot
        for n in order:
            for q in range(self.cuts):
                i = self.order[n]
                total = self.column_sum(n, q)
                if n == s.first - 1:
                    self.out[q * self.rows : (q + 1) * self.rows] = total
                    continue
                down = jnp.where(i > s.a, 0, 1)
                z = (down * s.first + i) * self.cuts + q
                acc[...] = total

                @pl.when(jnp.where(i > s.a, s.a, s.first - 1 - s.a) > 0)
                def _(z=z):
                    s.arrived(self.z_buf.at[z], self.sems[5].at[z])
                    acc[...] = acc[...] + self.z_buf[z].astype(F32)

                self.core_buf[self.slot(i, s.b, q)] = acc[...].astype(BF)

                def make(n=n, q=q, i=i, down=down, z=z):
                    return s.copy(
                        self.core_buf.at[self.slot(i, s.b, q)], self.z_buf.at[z],
                        self.sems[4].at[n * self.cuts + q], self.sems[5].at[z], s.at(s.a + 1 - 2 * down, s.b, s.c),
                    )

                self.start(make)

    def finish_chain(self):
        s = self.spot
        for q in range(self.cuts):
            cut = slice(q * self.rows, (q + 1) * self.rows)
            for down, there in ((0, s.a), (1, s.first - 1 - s.a)):
                z = (down * s.first + s.a) * self.cuts + q

                @pl.when(there > 0)
                def _(z=z, cut=cut):
                    s.arrived(self.z_buf.at[z], self.sems[5].at[z])
                    self.out[cut] = self.out[cut] + self.z_buf[z].astype(F32)

    def wait_sends(self):
        for make in self.copies:
            make().wait_send()

    def finish(self):
        s = self.spot
        for i in range(1, s.first):
            for q in range(self.cuts):
                z = s.around(i) * self.cuts + q
                s.arrived(self.z_buf.at[z], self.sems[5].at[z])
                cut = slice(q * self.rows, (q + 1) * self.rows)
                self.out[cut] = self.out[cut] + self.z_buf[z].astype(F32)
        self.wait_sends()


def forward_kernel(
    place, heads, tok_ref, w_ref, aux_ref, cw_ref, cbw_ref, hp_ref, cot_own, out_own,
    pz_ref, raw_ref, mixed_ref, gated_ref, cv_ref, pre_ref, cbc_ref, pbc_ref, st_ref, stat_ref, out_all, cot_full,
    state, ubuf, bbuf, vd, yint, expand, tri_ref, send_sem, recv_sem, local_sem, cot_sem,
):
    inner = heads * HEADDIM
    pairs = heads // 2
    wide = 2 * inner
    now = pl.program_id(0) * pl.num_programs(1) + pl.program_id(1)
    last = place.steps - 1
    first = now == 0
    spot = Spot(place)
    gather = LineGather(spot, [(out_own, out_all)], send_sem, recv_sem, local_sem)
    swap = TokenSwap(spot, cot_own, cot_full, cot_sem) if place.pair else None

    @pl.when(first)
    def _():
        spot.greet(place.pair)
        gather.begin()
        if swap:
            swap.begin()

    for hop in range(1, place.first):

        @pl.when(now == min(hop, last))
        def _(hop=hop):
            gather.along(hop)
            gather.across(hop - 1)

    @pl.when(first)
    def _():
        for i, place in enumerate((AUX + heads, AUX + 2 * heads, AUX + 3 * heads)):
            expand[i] = expander(heads, inner, place)
        tri_ref[...] = jnp.where(iota2((CHUNK, CHUNK), 0) <= iota2((CHUNK, CHUNK), 1), 1.0, 0.0).astype(BF)

    @pl.when(pl.program_id(1) == 0)
    def _():
        state[...] = jnp.zeros_like(state)
        ubuf[0:HALO] = jnp.zeros((HALO, inner), F32)
        bbuf[0:HALO] = jnp.zeros((HALO, 2 * STATE), F32)

    tok = tok_ref[0]
    side = dot_nn(tok, w_ref[:, wide:])
    raw_ref[0] = side[:, 2 * STATE :].T[0:heads]
    pz_ref[0, :, wide:] = side[:, : 2 * STATE].astype(BF)
    for p in range(pairs):
        pz_ref[0, :, 256 * p : 256 * p + 256] = dot_nn(tok, w_ref[:, 256 * p : 256 * p + 256]).astype(BF)

    def chunk_step(step, carry):
        here = pl.ds(pl.multiple_of(step * CHUNK, CHUNK), CHUNK)
        aux = aux_ref[0, :, here]
        raw = raw_ref[0, :, here]
        bc = pz_ref[0, here, wide:]
        dt, cum, carried, toward = pieces(raw, hp_ref[0], hp_ref[1], aux, tri_ref[...])
        cols = compact([aux, cum, dt, carried, toward])
        both = hi_lo(cols)
        dtx = dot_nn(both, expand[0])
        carx = dot_nn(both, expand[1])
        towx = dot_nn(both, expand[2])
        pad = cols[:, 1:2]
        same = [None] + [cols[:, 1 + k : 2 + k] for k in range(1, TAPS)]
        low = iota2((CHUNK, 128), 1) < HEADDIM

        bbuf[HALO:] = bc.astype(F32) * pad
        maps = cbw_ref[TAPS : TAPS + 1] + cbw_ref[0:1] * bbuf[HALO:]
        for k in range(1, TAPS):
            maps = maps + cbw_ref[k : k + 1] * (same[k] * bbuf[HALO - k : HALO - k + CHUNK])
        pbc_ref[0, here] = maps.astype(BF)
        maps = (maps * sigmoid(maps)).astype(BF)
        cbc_ref[0, here] = maps
        bbuf[0:HALO] = bbuf[CHUNK : CHUNK + HALO]
        keys, queries = maps[:, :STATE], maps[:, STATE:]
        scores = dot_nt(queries, keys)
        keys_t = keys.astype(F32).T.astype(BF)

        for p in range(pairs):
            s = slice(128 * p, 128 * p + 128)
            x0 = pz_ref[0, here, 256 * p : 256 * p + 128].astype(F32)
            x1 = pz_ref[0, here, 256 * p + 128 : 256 * p + 256].astype(F32)
            value = jnp.where(low, pltpu.roll(x0, HEADDIM, 1), x1)
            ubuf[HALO:, s] = value * pad
            pre = cw_ref[TAPS : TAPS + 1, s] + cw_ref[0:1, s] * ubuf[HALO:, s]
            for k in range(1, TAPS):
                pre = pre + cw_ref[k : k + 1, s] * (same[k] * ubuf[HALO - k : HALO - k + CHUNK, s])
            pre_ref[0, here, s] = pre.astype(BF)
            cv = (pre * sigmoid(pre)).astype(BF)
            cv_ref[0, here, s] = cv
            vd[:, s] = (cv.astype(F32) * dtx[:, s]).astype(BF)
        ubuf[0:HALO] = ubuf[CHUNK : CHUNK + HALO]

        old = state[...]
        old_b = old.astype(BF)
        st_ref[0, step] = old_b
        yint[...] = dot_nn(queries, old_b) * carx
        state[...] = carx[CHUNK - 1 : CHUNK] * old + dot_nn(keys_t, (vd[...].astype(F32) * towx).astype(BF))

        inside = (iota2((CHUNK, CHUNK), 0) >= iota2((CHUNK, CHUNK), 1)) & (cols[:, 0:1] == aux[0:1])
        fence = jnp.where(inside, 0.0, FAR)
        squares = jnp.zeros((CHUNK, 128), F32)
        for p in range(pairs):
            s = slice(128 * p, 128 * p + 128)
            mix = []
            for h in (2 * p, 2 * p + 1):
                decay = jnp.exp2(cols[:, AUX + h : AUX + h + 1] - cum[h : h + 1] + fence)
                mix.append((scores * decay).astype(BF))
            v = vd[:, s]
            zero = jnp.zeros_like(v)
            stacked = jnp.concatenate([jnp.where(low, v, zero), jnp.where(low, zero, v)], axis=0)
            y = dot_nn(jnp.concatenate(mix, axis=1), stacked)
            mixed = y + yint[:, s] + cw_ref[5:6, s] * cv_ref[0, here, s].astype(F32)
            x0 = pz_ref[0, here, 256 * p : 256 * p + 128].astype(F32)
            x1 = pz_ref[0, here, 256 * p + 128 : 256 * p + 256].astype(F32)
            gate = jnp.where(low, x0, pltpu.roll(x1, HEADDIM, 1))
            gated = mixed * (gate * sigmoid(gate))
            mixed_ref[0, here, s] = mixed.astype(BF)
            gated_ref[0, here, s] = (gated * cw_ref[6:7, s]).astype(BF)
            squares = squares + gated * gated
        lane = iota2((CHUNK, 128), 1)
        sums = jnp.where(lane == 0, jnp.sum(squares, axis=1, keepdims=True), 0.0)
        stat_ref[0, :, here] = sums.T[0:8]
        return carry

    lax.fori_loop(0, BLOCK // CHUNK, chunk_step, 0, unroll=True)

    @pl.when(now == last)
    def _():
        gather.across(place.first - 1)
        gather.finish()
        if swap:
            swap.finish()


def backward_kernel(
    place, heads, inner_all, pz_ref, raw_ref, aux_ref, mixed_ref, cv_ref, pre_ref, cbc_ref, pbc_ref,
    st_ref, stat_ref, cw_ref, cbw_ref, hp_ref, g_ref, out_ref, gn_all, cot_all,
    ge_ref, flat_ref, y_keep, y_away, back_ref, grad_rows,
    dstate, cbuf, dbuf, vd, gm_s, gmc_s, ggate_s, bs_s, expand, collect, tri_ref, suf_ref, ghead_ref,
    y_s, g_s, fold, sums, theirs, normed_s, part_buf, core_buf, x_buf, z_buf,
    core_send, core_recv, x_send, x_recv, z_send, z_recv, y_sem, stat_sem,
):
    inner = heads * HEADDIM
    pairs = heads // 2
    wide = 2 * inner
    now = pl.program_id(0) * pl.num_programs(1) + pl.program_id(1)
    last = place.steps - 1
    first = now == 0
    gch_ref = flat_ref.at[8:16, 0:inner]
    gmap_ref = flat_ref.at[0:8, 0 : 2 * STATE]
    spot = Spot(place)
    if place.pair:
        scatter = LineScatter(
            spot, part_buf, core_buf, x_buf, z_buf, grad_rows, core_send, core_recv, x_send, x_recv, z_send, z_recv
        )
        half = HalfSwap(spot, y_s, y_away, y_sem)
        here_len = y_keep.shape[1]
        seqs = y_keep.shape[0]
        per_seq = place.length // CHUNK

        def out_terms(there):
            part_buf[there] = lax.dot_general(
                cot_all[:, there], normed_s[...], (((0,), (0,)), ((), ())), preferred_element_type=F32
            ).astype(BF)

        def keep():
            rows = y_s.at[:, pl.ds(pl.multiple_of(spot.me * here_len, here_len), here_len)]
            return pltpu.make_async_copy(rows, y_keep, y_sem.at[2])

        @pl.when(first)
        def _():
            spot.greet(True)
            for cut in range(out_ref.shape[0] // 256):
                cols = slice(256 * cut, 256 * cut + 256)
                for seq in range(seqs):
                    rows = slice(seq * place.length, (seq + 1) * place.length)
                    y = dot_nt(gn_all[rows], out_ref[cols])
                    y_s[seq, :, cols] = y.astype(BF)
                    y = y * cot_all[rows, cols].astype(F32)
                    y = y[:, :128] + y[:, 128:]
                    fold[rows] = y if cut == 0 else fold[rows] + y

            for step in range(seqs * per_seq):
                rows = slice(step * CHUNK, (step + 1) * CHUNK)
                seq, cut = divmod(step, per_seq)
                there = slice(cut * CHUNK, (cut + 1) * CHUNK)
                cross = jnp.sum(fold[rows], axis=1, keepdims=True)
                row = jnp.broadcast_to(cross, (CHUNK, 128)).T[0:8]
                sums[seq, :, there] = jnp.where(iota2(row.shape, 0) == 1, row, stat_ref[seq, :, there])
            swap = spot.copy(sums, theirs, stat_sem.at[0], stat_sem.at[1], spot.index, 1 - spot.me)
            swap.start()

            def out_back(step, carry):
                rows = pl.ds(pl.multiple_of(step * BLOCK, BLOCK), BLOCK)
                g_s[rows] = dot_nn(cot_all[rows], out_ref[...]).astype(BF)
                return carry

            lax.fori_loop(0, seqs * place.length // BLOCK, out_back, 0)
            swap.wait()
            half.begin()
            keep().start()
            back_ref[...] = finish_sums(sums[...] + theirs[...], inner_all)

            for step in range(seqs * per_seq):
                rows = slice(step * CHUNK, (step + 1) * CHUNK)
                seq, cut = divmod(step, per_seq)
                rms_col = compact([back_ref[seq, :, cut * CHUNK : (cut + 1) * CHUNK]])[:, 0:1]
                normed_s[rows] = (gn_all[rows].astype(F32) * rms_col).astype(BF)
            scatter.produce(out_terms, True)
            scatter.produce(out_terms, False)
            scatter.cross()

        @pl.when(now == min(2, last))
        def _():
            scatter.along()
    else:
        pl.when(first)(lambda: back_ref.__setitem__(Ellipsis, stat_ref[...]))

    @pl.when(first)
    def _():
        for i, place in enumerate((AUX + heads, AUX + 2 * heads, AUX + 3 * heads)):
            expand[i] = expander(heads, inner, place)
        collect[0] = collector(inner, heads)
        collect[1] = collector(inner, 2 * heads)
        r, c = iota2((CHUNK, CHUNK), 0), iota2((CHUNK, CHUNK), 1)
        tri_ref[...] = jnp.where(r <= c, 1.0, 0.0).astype(BF)
        suf_ref[...] = jnp.where(r >= c, 1.0, 0.0).astype(BF)
        flat_ref[...] = jnp.zeros_like(flat_ref)
        ghead_ref[...] = jnp.zeros_like(ghead_ref)

    @pl.when(pl.program_id(1) == 0)
    def _():
        dstate[...] = jnp.zeros_like(dstate)
        cbuf[CHUNK:] = jnp.zeros((HALO, inner), F32)
        dbuf[CHUNK:] = jnp.zeros((HALO, 2 * STATE), F32)

    seq_now = pl.program_id(0)
    block_start = (pl.num_programs(1) - 1 - pl.program_id(1)) * BLOCK

    def chunk_step(step, carry):
        here = pl.ds(pl.multiple_of(BLOCK - CHUNK - step * CHUNK, CHUNK), CHUNK)
        there = pl.ds(pl.multiple_of(block_start + BLOCK - CHUNK - step * CHUNK, CHUNK), CHUNK)
        flat_rows = pl.ds(pl.multiple_of(seq_now * place.length + block_start + BLOCK - CHUNK - step * CHUNK, CHUNK), CHUNK)
        aux = aux_ref[0, :, here]
        rate = hp_ref[1]
        dt, cum, carried, toward = pieces(raw_ref[0, :, here], hp_ref[0], rate, aux, tri_ref[...])
        cols = compact([aux, cum, dt, carried, toward, back_ref[seq_now, :, there]])
        both = hi_lo(cols)
        dtx = dot_nn(both, expand[0])
        carx = dot_nn(both, expand[1])
        towx = dot_nn(both, expand[2])
        pad = cols[:, 1:2]
        ahead = [None] + [cols[:, 7 + k : 8 + k] for k in range(1, TAPS)]
        base = AUX + 4 * heads
        rms, pull = cols[:, base : base + 1], cols[:, base + 1 : base + 2]
        low = iota2((CHUNK, 128), 1) < HEADDIM
        maps = cbc_ref[0, here]
        keys, queries = maps[:, :STATE], maps[:, STATE:]
        queries_t = queries.astype(F32).T.astype(BF)
        scores_t = dot_nt(keys, queries)

        for p in range(pairs):
            s = slice(128 * p, 128 * p + 128)
            x0 = pz_ref[0, here, 256 * p : 256 * p + 128].astype(F32)
            x1 = pz_ref[0, here, 256 * p + 128 : 256 * p + 256].astype(F32)
            gate = jnp.where(low, x0, pltpu.roll(x1, HEADDIM, 1))
            sig = sigmoid(gate)
            act = gate * sig
            mixed = mixed_ref[0, here, s].astype(F32)
            gated = mixed * act
            g = (g_s[flat_rows, s] if place.pair else g_ref[0, here, s]).astype(F32)
            grad_gated = rms * (g * cw_ref[6:7, s]) - gated * pull
            gm = grad_gated * act
            ggate_s[:, s] = (grad_gated * mixed * (sig * (1.0 + gate * (1.0 - sig)))).astype(BF)
            gm_s[:, s] = gm.astype(BF)
            gmc_s[:, s] = (gm * carx[:, s]).astype(BF)
            cv = cv_ref[0, here, s].astype(F32)
            vd[:, s] = (cv * dtx[:, s]).astype(BF)
            gch_ref[5:6, s] += jnp.sum(gm * cv, axis=0, keepdims=True)
            gch_ref[6:7, s] += jnp.sum(gated * rms * g, axis=0, keepdims=True)

        ds = dstate[...]
        ds_b = ds.astype(BF)
        st = st_ref[0, BLOCK // CHUNK - 1 - step]
        gmc = gmc_s[...]
        cs = dot_nn(queries, st)
        bs = dot_nn(keys, ds_b) * towx
        bs_s[...] = bs
        reach = dot_nn((gmc.astype(F32) * cs).astype(BF), collect[1])
        reach = reach + dot_nn((bs * cv_ref[0, here].astype(F32)).astype(BF), collect[0])
        grad_q = dot_nt(gmc, st)
        grad_k = dot_nt((vd[...].astype(F32) * towx).astype(BF), ds_b)
        keep = carx[CHUNK - 1 : CHUNK]
        held = jnp.sum(st.astype(F32) * ds, axis=0, keepdims=True) * keep
        dstate[...] = keep * ds + dot_nn(queries_t, gmc)

        inside = (iota2((CHUNK, CHUNK), 0) <= iota2((CHUNK, CHUNK), 1)) & (cols[:, 0:1] == aux[0:1])
        fence = jnp.where(inside, 0.0, FAR)
        grad_scores_t = jnp.zeros((CHUNK, CHUNK), F32)
        lane = iota2((CHUNK, 128), 1)
        gathered = reach
        row_sums = []
        for p in range(pairs):
            s = slice(128 * p, 128 * p + 128)
            gm_b = gm_s[:, s]
            zero = jnp.zeros_like(gm_b)
            gm_two = jnp.concatenate([jnp.where(low, gm_b, zero), jnp.where(low, zero, gm_b)], axis=0)
            near = dot_nt(vd[:, s], gm_two)
            mix = []
            for j in range(2):
                h = 2 * p + j
                decay = jnp.exp2(cum[h : h + 1] - cols[:, AUX + h : AUX + h + 1] + fence)
                mix.append((scores_t * decay).astype(BF))
                weighed = decay * near[:, CHUNK * j : CHUNK * j + CHUNK]
                grad_scores_t = grad_scores_t + weighed
                pairs_g = weighed * scores_t
                row_sums.append(jnp.sum(pairs_g, axis=0, keepdims=True))
                gathered = jnp.where(lane == h, jnp.sum(pairs_g, axis=1, keepdims=True), gathered)
            z = dot_nn(jnp.concatenate(mix, axis=1), gm_two)
            gm = gm_b.astype(F32)
            grad_v = cw_ref[5:6, s] * gm + dtx[:, s] * (z + bs_s[:, s])
            x0 = pz_ref[0, here, 256 * p : 256 * p + 128].astype(F32)
            x1 = pz_ref[0, here, 256 * p + 128 : 256 * p + 256].astype(F32)
            u = jnp.where(low, pltpu.roll(x0, HEADDIM, 1), x1) * pad
            pre = pre_ref[0, here, s].astype(F32)
            sig = sigmoid(pre)
            c = grad_v * (sig * (1.0 + pre * (1.0 - sig)))
            cbuf[0:CHUNK, s] = c
            gu = cw_ref[0:1, s] * c
            gch_ref[4:5, s] += jnp.sum(c, axis=0, keepdims=True)
            gch_ref[0:1, s] += jnp.sum(c * u, axis=0, keepdims=True)
            for k in range(1, TAPS):
                shifted = ahead[k] * cbuf[k : k + CHUNK, s]
                gu = gu + cw_ref[k : k + 1, s] * shifted
                gch_ref[k : k + 1, s] += jnp.sum(shifted * u, axis=0, keepdims=True)
            gu = gu * pad
            ggate = ggate_s[:, s].astype(F32)
            ge_ref[0, here, 256 * p : 256 * p + 128] = jnp.where(low, ggate, pltpu.roll(gu, HEADDIM, 1)).astype(BF)
            ge_ref[0, here, 256 * p + 128 : 256 * p + 256] = jnp.where(low, pltpu.roll(ggate, HEADDIM, 1), gu).astype(BF)
        cbuf[CHUNK:] = cbuf[0:HALO]

        gst = grad_scores_t.astype(BF)
        grad_k = grad_k + dot_nn(gst, queries)
        grad_q = grad_q + dot_nn(grad_scores_t.T.astype(BF), keys)
        pbc = pbc_ref[0, here].astype(F32)
        sig = sigmoid(pbc)
        c = jnp.concatenate([grad_k, grad_q], axis=1) * (sig * (1.0 + pbc * (1.0 - sig)))
        dbuf[0:CHUNK] = c
        u = pz_ref[0, here, wide:].astype(F32) * pad
        gu = cbw_ref[0:1] * c
        gmap_ref[4:5] += jnp.sum(c, axis=0, keepdims=True)
        gmap_ref[0:1] += jnp.sum(c * u, axis=0, keepdims=True)
        for k in range(1, TAPS):
            shifted = ahead[k] * dbuf[k : k + CHUNK]
            gu = gu + cbw_ref[k : k + 1] * shifted
            gmap_ref[k : k + 1] += jnp.sum(shifted * u, axis=0, keepdims=True)
        ge_ref[0, here, wide : wide + 2 * STATE] = (gu * pad).astype(BF)
        dbuf[CHUNK:] = dbuf[0:HALO]

        across = gathered.T
        col_sum = across[0:heads]
        kx = across[heads : 2 * heads]
        rint = across[2 * heads : 3 * heads]
        row_sum = jnp.concatenate(row_sums, axis=0)
        k_all = kx * dt
        held_head = exact_dot(jnp.broadcast_to(held, (16, inner)), collect[0])
        held_col = jnp.broadcast_to(held_head[0:1], (CHUNK, 128)).T[heads : 2 * heads]
        diff = row_sum + rint - col_sum - k_all
        grad_a = exact_dot(diff, suf_ref[...]) + jnp.sum(k_all, axis=1, keepdims=True) + held_col
        direct = jnp.where(dt > 0.0, col_sum / jnp.where(dt > 0.0, dt, 1.0), 0.0)
        grad_dt = direct + kx + rate * grad_a
        graw = grad_dt * aux[1:2] * sigmoid(raw_ref[0, :, here] + hp_ref[0])
        ge_ref[0, here, wide + 2 * STATE :] = compact([graw]).astype(BF)
        ghead_ref[0] += graw
        ghead_ref[1] += rate * dt * grad_a
        return carry

    lax.fori_loop(0, BLOCK // CHUNK, chunk_step, 0)
    @pl.when(now == last)
    def _():
        for i in range(2):
            sums = jnp.broadcast_to(jnp.sum(ghead_ref[i], axis=1, keepdims=True), (heads, 128))
            flat_ref[15:16, 128 * i : 128 * i + 128] = compact([sums])[0:1]
        if place.pair:
            scatter.finish()
            half.finish()
            keep().wait()
        else:
            grad_rows[...] = jnp.zeros_like(grad_rows)


def gather_kernel(
    place, heads, zx_ref, bc_ref, step_ref, hidden_ref, gain_ref, cxw_ref, cxb_ref, cbw_ref, cbb_ref, bias_ref, decay_ref,
    skip_ref, ngain_ref, seg_ref, pad_ref,
    w_all, tok_full, aux_ref, cw_ref, cbw_out, hp_ref,
    shard, tok_own, square, send_sem, recv_sem, local_sem, tok_sem,
):
    inner = heads * HEADDIM
    wide = 2 * inner
    spot = Spot(place)
    rows = zx_ref.shape[0]
    shard[:, 0:wide] = zx_ref[...]
    shard[:, wide : wide + 2 * STATE] = bc_ref[...]
    square[...] = jnp.zeros_like(square)
    square[0:heads, 0:rows] = step_ref[...].astype(F32)
    shard[:, wide + 2 * STATE :] = square[...].T[0:rows].astype(BF)
    spot.greet(place.pair)
    gather = LineGather(spot, [(shard, w_all)], send_sem, recv_sem, local_sem)
    gather.begin()

    size = 64
    seqs, here = hidden_ref.shape[0], hidden_ref.shape[1]

    def norm_rows(step, carry):
        seq, cut = lax.div(step, here // size), lax.rem(step, here // size)
        mine = pl.ds(pl.multiple_of(cut * size, size), size)
        hid = hidden_ref[seq, mine].astype(F32)
        inv = lax.rsqrt(jnp.mean(hid * hid, axis=-1, keepdims=True) + epsilon)
        tok_own[seq, mine] = (hid * inv * gain_ref[...]).astype(BF)
        return carry

    lax.fori_loop(0, seqs * (here // size), norm_rows, 0)
    if place.pair:
        swap = TokenSwap(spot, tok_own, tok_full, tok_sem)
        swap.begin()
    else:
        copy = pltpu.make_async_copy(tok_own, tok_full, tok_sem.at[2])
        copy.start()

    square[...] = jnp.zeros_like(square)
    square[0:1, 0:heads] = bias_ref[...]
    square[1:2, 0:heads] = decay_ref[...]
    square[2:3, 0:heads] = skip_ref[...]
    per_head = square[...].T
    hp_ref[0] = jnp.broadcast_to(per_head[0:heads, 0:1], (heads, 128))
    hp_ref[1] = jnp.broadcast_to(-jnp.exp(per_head[0:heads, 1:2]), (heads, 128))
    cw_ref[0:TAPS] = cxw_ref[...]
    cw_ref[TAPS : TAPS + 1] = cxb_ref[...]
    cw_ref[5:6] = exact_dot(square[0:16], expander(heads, inner, 0)[0:128])[2:3]
    cw_ref[6:7] = ngain_ref[...]
    cw_ref[7:8] = jnp.zeros((1, inner), F32)
    cbw_out[...] = jnp.zeros_like(cbw_out)
    cbw_out[0:TAPS] = cbw_ref[...]
    cbw_out[TAPS : TAPS + 1] = cbb_ref[...]

    length = place.length
    lane = iota2((8, length), 1)
    flag = lambda condition: jnp.where(condition, 1.0, 0.0)[0:1]
    for seq in range(aux_ref.shape[0]):
        seg = jnp.broadcast_to(seg_ref[seq : seq + 1], (8, length))
        aux_ref[seq] = jnp.zeros((AUX, length), F32)
        aux_ref[seq, 0:1] = seg[0:1].astype(F32)
        aux_ref[seq, 1:2] = pad_ref[seq : seq + 1].astype(F32)
        for k in range(1, TAPS):
            aux_ref[seq, 1 + k : 2 + k] = flag((pltpu.roll(seg, k, 1) == seg) & (lane >= k))
            aux_ref[seq, 7 + k : 8 + k] = flag((pltpu.roll(seg, length - k, 1) == seg) & (lane < length - k))
        before = jnp.full((8, CHUNK), -1, jnp.int32)
        for chunk in range(length // CHUNK):
            cut = slice(chunk * CHUNK, (chunk + 1) * CHUNK)
            block = seg[:, cut]
            tail = jnp.broadcast_to(block[:, CHUNK - 1 : CHUNK], (8, CHUNK))
            aux_ref[seq, 5:6, cut] = flag(block == before)
            aux_ref[seq, 6:7, cut] = flag(block == tail)
            before = tail

    gather.across(0) if place.first == 1 else None
    for hop in range(1, place.first):
        gather.along(hop)
        gather.across(hop - 1)
    if place.first > 1:
        gather.across(place.first - 1)
    gather.finish()
    swap.finish() if place.pair else copy.wait()


def finish_sums(total, inner_all):
    lines = lax.broadcasted_iota(jnp.int32, total.shape, 1)
    rms = lax.rsqrt(total[:, 0:1] / inner_all + epsilon)
    pull = rms * rms * rms * (total[:, 1:2] / inner_all)
    return jnp.where(lines == 0, rms, jnp.where(lines == 1, pull, 0.0))


def reduce_kernel(
    place, tok_ref, ge_ref, flat_ref, gain_ref, back_ref, w_hbm, hidden_hbm, cot_hbm, keep_hbm, away_hbm,
    own_ref, sum_ref, gh_ref, output_ref,
    w_ref, hidden_ref, cot_ref, keep_ref, away_ref, dg_ref, dg_send, dg_buf,
    part_buf, core_buf, x_buf, z_buf, acc, bc_buf, bc_send, y_flat, core_flat, x_flat, z_flat, stage,
    core_send, core_recv, x_send, x_recv, z_send, z_recv, flat_send, flat_recv, dg_sem, load_sem,
):
    spot = Spot(place)
    a, b, c, me, index = spot.a, spot.b, spot.c, spot.me, spot.index
    first, second = place.first, place.second
    scatter = LineScatter(
        spot, part_buf if place.pair else ge_ref, core_buf, x_buf, z_buf, own_ref,
        core_send, core_recv, x_send, x_recv, z_send, z_recv, PIECES,
    )
    loads = []
    if place.pair:
        pairs = ((w_hbm, w_ref), (hidden_hbm, hidden_ref), (cot_hbm, cot_ref), (keep_hbm, keep_ref), (away_hbm, away_ref))
        for k, (far, near) in enumerate(pairs):
            loads.append(pltpu.make_async_copy(far, near, load_sem.at[k]))
        loads[0].start()
    spot.greet(place.pair)
    started = []

    def send(*args):
        copy = spot.copy(*args)
        copy.start()
        started.append(copy)

    def terms(there):
        if place.pair:
            part_buf[there] = lax.dot_general(
                tok_ref[:, there], ge_ref[...], (((0,), (0,)), ((), ())), preferred_element_type=F32
            ).astype(BF)

    stage[0] = flat_ref[...]
    here = hidden_ref.shape[1]

    def token_gradient(side, to):
        for seq in range(hidden_ref.shape[0]):
            rows = pl.ds(pl.multiple_of(seq * place.length + side * here, here), here)
            for cut in range(w_ref.shape[0] // 256):
                cols = slice(256 * cut, 256 * cut + 256)
                dg = dot_nt(ge_ref[rows], w_ref[cols])
                to[seq, :, cols] = dg.astype(BF)
                stage[0, 5:6, cols] += jnp.sum(dg * tok_ref[rows, cols].astype(F32), axis=0, keepdims=True)

    far = [(n, j) for j in range(1, second) for n in range(first)]
    near = [(n, 0) for n in range(first)]
    for k, (n, j) in enumerate(far + near[:1]):
        terms(scatter.terms(n, j))
        scatter.give(n, j)
        if 1 <= k <= len(far):
            scatter.cross_over(*far[k - 1])
    if place.pair:
        loads[0].wait()
        for load in loads[1:]:
            load.start()
        token_gradient(1 - me, dg_send)
        send(dg_send, dg_buf, dg_sem.at[0], dg_sem.at[1], index, 1 - me)
    for n, j in near[1:]:
        terms(scatter.terms(n, j))
        scatter.give(n, j)
    scatter.chain(acc, range(1))
    if place.pair:
        token_gradient(me, dg_ref)

    send(stage.at[0], core_flat, flat_send.at[1], flat_recv.at[1], spot.sibling)
    spot.arrived(core_flat, flat_recv.at[1])
    stage[1] = stage[0] + core_flat[...]
    x_flat[b] = stage[1]
    for j in range(1, second):
        send(stage.at[1], x_flat.at[b], flat_send.at[1 + j], flat_recv.at[2 + b], spot.at(a, spot.aside(j), c))

    scatter.chain(acc, range(1, first))
    for j in range(1, second):
        spot.arrived(x_flat.at[spot.aside(j)], flat_recv.at[2 + spot.aside(j)])
    total = x_flat[0]
    for j in range(1, second):
        total = total + x_flat[j]
    stage[2] = total
    z_flat[a] = total
    for i in range(1, first):
        send(
            stage.at[2], z_flat.at[a], flat_send.at[second + i], flat_recv.at[2 + second + a],
            spot.at(spot.around(i), b, c),
        )

    if place.pair:
        for load in loads[1:]:
            load.wait()
        spot.arrived(dg_buf, dg_sem.at[1])
        size = 128

        def token_rows(step, carry):
            seq, cut = lax.div(step, here // size), lax.rem(step, here // size)
            mine = pl.ds(pl.multiple_of(cut * size, size), size)
            full = pl.ds(pl.multiple_of(me * here + cut * size, size), size)
            hid = hidden_ref[seq, mine].astype(F32)
            inv = lax.rsqrt(jnp.mean(hid * hid, axis=-1, keepdims=True) + epsilon)
            gain = (dg_ref[seq, mine].astype(F32) + dg_buf[seq, mine].astype(F32)) * gain_ref[...]
            pull = inv * inv * inv * jnp.mean(hid * gain, axis=-1, keepdims=True)
            gh_ref[seq, mine] = (cot_ref[seq, mine].astype(F32) + inv * gain - hid * pull).astype(BF)
            rms = compact([back_ref[seq, :, full]])[:, 0:1]
            mixed = keep_ref[seq, mine].astype(F32) + away_ref[seq, mine].astype(F32)
            output_ref[seq, mine] = (hid + rms * mixed).astype(BF)
            return carry

        lax.fori_loop(0, hidden_ref.shape[0] * (here // size), token_rows, 0)
    else:
        gh_ref[...] = jnp.zeros_like(gh_ref)
        output_ref[...] = jnp.zeros_like(output_ref)

    for i in range(1, first):
        spot.arrived(z_flat.at[spot.around(i)], flat_recv.at[2 + second + spot.around(i)])
    total = z_flat[0]
    for i in range(1, first):
        total = total + z_flat[i]
    sum_ref[...] = total
    if place.pair:
        stage[3, 0:8] = total[0:8]
        send(stage.at[3, 0:8], y_flat, flat_send.at[0], flat_recv.at[0], index, 1 - me)
    scatter.finish_chain()
    if place.pair:
        edge = own_ref.shape[1] - 128 - 2 * STATE
        bc_send[...] = own_ref[:, edge : edge + 2 * STATE]
        send(bc_send, bc_buf, dg_sem.at[2], dg_sem.at[3], index, 1 - me)
    scatter.wait_sends()
    if place.pair:
        spot.arrived(y_flat, flat_recv.at[0])
        sum_ref[0:8] = stage[3, 0:8] + y_flat[...]
        spot.arrived(bc_buf, dg_sem.at[3])
        own_ref[:, edge : edge + 2 * STATE] = bc_send[...] + bc_buf[...]
    for copy in started:
        copy.wait_send()


def last_kernel(
    heads, own_ref, sum_ref, gh_in, output_in, out_rows, gain_ref,
    output_ref, gh_ref, pre_ref, zx_ref, bc_ref, step_ref, cxw_ref, cxb_ref, cbw_ref, cbb_ref, bias_ref, decay_ref,
    skip_ref, ngain_ref, out_ref,
):
    inner = heads * HEADDIM
    wide = 2 * inner
    rows = own_ref.shape[0]
    output_ref[...] = output_in[...]
    gh_ref[...] = gh_in[...]
    pre_ref[...] = sum_ref[5:6] / gain_ref[...]
    zx_ref[...] = own_ref[:, 0:wide]
    bc_ref[...] = own_ref[:, wide : wide + 2 * STATE]
    steps = own_ref[:, wide + 2 * STATE :]
    if rows < 128:
        steps = jnp.concatenate([steps, jnp.zeros((128 - rows, 128), F32)], axis=0)
    step_ref[...] = steps.T[0:heads, 0:rows]
    cxw_ref[...] = sum_ref[8 : 8 + TAPS, 0:inner]
    cxb_ref[...] = sum_ref[8 + TAPS : 9 + TAPS, 0:inner]
    cbw_ref[...] = sum_ref[0:TAPS, 0 : 2 * STATE]
    cbb_ref[...] = sum_ref[TAPS : TAPS + 1, 0 : 2 * STATE]
    skip = exact_dot(jnp.broadcast_to(sum_ref[13:14, 0:inner], (16, inner)), collector(inner, 0))
    bias_ref[...] = sum_ref[15:16, 0:heads]
    decay_ref[...] = sum_ref[15:16, 128 : 128 + heads]
    skip_ref[...] = skip[0:1, 0:heads]
    ngain_ref[...] = sum_ref[14:15, 0:inner]
    out_ref[...] = out_rows[...]


SDS = jax.ShapeDtypeStruct
DMA = pltpu.SemaphoreType.DMA
ANY = pl.BlockSpec(memory_space=pl.ANY)
WHOLE = pl.BlockSpec(memory_space=pltpu.VMEM)


def params(collective=None):
    if collective is None:
        return pltpu.CompilerParams(vmem_limit_bytes=VMEM_LIMIT)
    return pltpu.CompilerParams(vmem_limit_bytes=VMEM_LIMIT, collective_id=collective, has_side_effects=True)


def whole_once(*shape):
    return pl.BlockSpec(shape, lambda s, c: (0,) * len(shape), pipeline_mode=pl.Buffered(1))


def line_sems(place, cuts, lines):
    columns = place.first * max(place.second - 1, 1) * cuts
    blocks = place.first * place.second * cuts
    return [DMA((blocks,)), DMA((blocks,)), DMA((columns,)), DMA((columns,)), DMA((place.first * cuts,)), DMA((lines,))]


def gather_all(place, size, zx, bc, step_t, hidden, gain, cxw, cxb, cbw, cbb, bias, decay, skip, ngain, seg, pad):
    seqs, here, width = hidden.shape
    heads, inner = bias.shape[1], cxw.shape[1]
    total = 2 * inner + 2 * STATE + 128
    rows = zx.shape[0]
    return pl.pallas_call(
        functools.partial(gather_kernel, place, heads),
        in_specs=[WHOLE] * 15,
        out_specs=[ANY, ANY] + [WHOLE] * 4,
        out_shape=[
            SDS((size * rows, total), BF), SDS((seqs, place.length if place.pair else here, width), BF),
            SDS((seqs, AUX, place.length), F32), SDS((8, inner), F32), SDS((8, 2 * STATE), F32), SDS((2, heads, 128), F32),
        ],
        scratch_shapes=[
            pltpu.VMEM((rows, total), BF), pltpu.VMEM(hidden.shape, BF), pltpu.VMEM((128, 128), F32),
            DMA((1, gather_sites(place.first, place.second))), DMA((1, size)), DMA((1,)), DMA((3,)),
        ],
        compiler_params=params(0),
        name="gather_all",
    )(zx, bc, step_t, hidden, gain, cxw, cxb, cbw, cbb, bias, decay, skip, ngain, seg, pad)


def mixer_forward(place, size, tok, weights, aux, cw, cbw, hp, cot_own, out_own):
    seqs, length, width = tok.shape
    heads, inner = hp.shape[1], cw.shape[1]
    wide = 2 * inner + 2 * STATE
    chunks = length // CHUNK
    token = lambda size: pl.BlockSpec((1, BLOCK, size), lambda s, c: (s, c, 0))
    row = lambda high: pl.BlockSpec((1, high, BLOCK), lambda s, c: (s, 0, c))
    return pl.pallas_call(
        functools.partial(forward_kernel, place, heads),
        grid=(seqs, length // BLOCK),
        in_specs=[
            token(width), whole_once(*weights.shape), row(AUX),
            whole_once(8, inner), whole_once(8, 2 * STATE), whole_once(2, heads, 128), WHOLE, ANY,
        ],
        out_specs=[
            token(wide), row(heads), token(inner), token(inner), token(inner), token(inner), token(2 * STATE),
            token(2 * STATE), pl.BlockSpec((1, BLOCK // CHUNK, STATE, inner), lambda s, c: (s, c, 0, 0)), row(8),
            ANY, ANY,
        ],
        out_shape=[
            SDS((seqs, length, wide), BF), SDS((seqs, heads, length), F32),
            SDS((seqs, length, inner), BF), SDS((seqs, length, inner), BF), SDS((seqs, length, inner), BF),
            SDS((seqs, length, inner), BF), SDS((seqs, length, 2 * STATE), BF), SDS((seqs, length, 2 * STATE), BF),
            SDS((seqs, chunks, STATE, inner), BF), SDS((seqs, 8, length), F32),
            SDS((size * out_own.shape[0], inner), BF), SDS((seqs, length, width) if place.pair else (8, 128), BF),
        ],
        scratch_shapes=[
            pltpu.VMEM((STATE, inner), F32), pltpu.VMEM((HALO + CHUNK, inner), F32),
            pltpu.VMEM((HALO + CHUNK, 2 * STATE), F32), pltpu.VMEM((CHUNK, inner), BF),
            pltpu.VMEM((CHUNK, inner), F32), pltpu.VMEM((3, 256, inner), BF), pltpu.VMEM((CHUNK, CHUNK), BF),
            DMA((1, gather_sites(place.first, place.second))), DMA((1, size)), DMA((1,)), DMA((3,)),
        ],
        compiler_params=params(1),
        name="mixer_forward",
    )(tok, weights, aux, cw, cbw, hp, cot_own, out_own)


def mixer_backward(
    place, size, inner_all, pz, raw, aux, mixed, cv, pre, cbc, pbc, st, stat, cw, cbw, hp, g, out_all, gn, cot
):
    seqs, length, inner = mixed.shape
    width, wide = out_all.shape[0], pz.shape[2] + 128
    heads = hp.shape[1]
    last = length // BLOCK - 1
    pair = place.pair
    here = length // 2 if pair else 16
    rows = width // size
    tokens = seqs * length
    token = lambda size: pl.BlockSpec((1, BLOCK, size), lambda s, c: (s, last - c, 0))
    row = lambda high: pl.BlockSpec((1, high, BLOCK), lambda s, c: (s, 0, last - c))
    fixed = lambda *shape: pl.BlockSpec(shape, lambda s, c: (0,) * len(shape))
    if pair:
        g = cbw
        gn_all, cot_all = gn.reshape(-1, inner), cot.reshape(-1, width)
    else:
        gn_all, cot_all, out_all = gn[0, :16, :128], cot[0, :16, :128], out_all[:16, :128]
    blocks = place.first * place.second
    columns = place.first * max(place.second - 1, 1)
    tile = lambda *shape: pltpu.VMEM(shape if pair else (1,) * (len(shape) - 2) + (16, 128), BF)
    rowed = pltpu.VMEM((seqs, 8, length), F32)
    return pl.pallas_call(
        functools.partial(backward_kernel, place, heads, inner_all),
        grid=(seqs, length // BLOCK),
        in_specs=[
            token(pz.shape[2]), row(heads), row(AUX), token(inner), token(inner),
            token(inner), token(2 * STATE), token(2 * STATE),
            pl.BlockSpec((1, BLOCK // CHUNK, STATE, inner), lambda s, c: (s, last - c, 0, 0)), whole_once(*stat.shape),
            whole_once(8, inner), whole_once(8, 2 * STATE), whole_once(2, heads, 128),
            whole_once(*g.shape) if pair else token(inner),
            whole_once(*out_all.shape), whole_once(*gn_all.shape), whole_once(*cot_all.shape),
        ],
        out_specs=[token(wide), fixed(16, width), ANY, ANY, fixed(seqs, 8, length), fixed(rows, inner)],
        out_shape=[
            SDS((seqs, length, wide), BF), SDS((16, width), F32), SDS((seqs, here, width), BF),
            SDS((seqs, here, width), BF), SDS((seqs, 8, length), F32), SDS((rows, inner), F32),
        ],
        scratch_shapes=[
            pltpu.VMEM((STATE, inner), F32), pltpu.VMEM((CHUNK + HALO, inner), F32),
            pltpu.VMEM((CHUNK + HALO, 2 * STATE), F32), pltpu.VMEM((CHUNK, inner), BF),
            pltpu.VMEM((CHUNK, inner), BF), pltpu.VMEM((CHUNK, inner), BF), pltpu.VMEM((CHUNK, inner), BF),
            pltpu.VMEM((CHUNK, inner), F32),
            pltpu.VMEM((3, 256, inner), BF), pltpu.VMEM((2, inner, 128), BF),
            pltpu.VMEM((CHUNK, CHUNK), BF), pltpu.VMEM((CHUNK, CHUNK), BF), pltpu.VMEM((2, heads, 128), F32),
            tile(seqs, length, width), tile(tokens, inner), pltpu.VMEM((tokens, 128), F32), rowed, rowed,
            tile(tokens, inner), tile(width, inner),
            tile(blocks, rows, inner), tile(columns, rows, inner), tile(place.first, rows, inner),
        ] + line_sems(place, 1, place.first) + [DMA((3,)), DMA((2,))],
        compiler_params=params(3 if pair else None),
        name="mixer_backward",
    )(
        pz, raw, aux, mixed, cv, pre, cbc, pbc, st, stat, cw, cbw, hp, g, out_all, gn_all, cot_all,
    )


def reduce_all(place, size, tok, ge, flat, gain, back, weights, hidden, cot_own, y_keep, y_away):
    seqs, length, depth = tok.shape
    width = ge.shape[2]
    rows = depth // size
    pair = place.pair
    if pair:
        tok, ge = tok.reshape(seqs * length, depth), ge.reshape(seqs * length, width)
    else:
        ge = jnp.einsum("stp,sty->py", tok, ge, preferred_element_type=F32).astype(BF)
        tok, weights = tok[0, :16], weights[:16, :128]
        flat = jnp.concatenate([lax.psum(flat[:8], "tensor"), flat[8:]])
        hidden, cot_own, y_keep, y_away = [jnp.zeros((1, 16, depth), BF)] * 4
        back = back[:1, :, :128]
    blocks = place.first * place.second * PIECES
    columns = place.first * max(place.second - 1, 1) * PIECES
    lines = 2 * place.first * PIECES
    cut = rows // PIECES
    tokens = pltpu.VMEM(hidden.shape, BF)
    small = pltpu.VMEM((rows, 2 * STATE), F32)
    own, flat, gh, output = pl.pallas_call(
        functools.partial(reduce_kernel, place),
        in_specs=[WHOLE] * 5 + [ANY] * 5,
        out_specs=[WHOLE] * 4,
        out_shape=[SDS((rows, width), F32), SDS(flat.shape, F32), SDS(hidden.shape, BF), SDS(hidden.shape, BF)],
        scratch_shapes=[
            pltpu.VMEM(weights.shape, BF), tokens, tokens, tokens, tokens, tokens, tokens, tokens,
            pltpu.VMEM((depth, width) if pair else (16, 128), BF),
            pltpu.VMEM((blocks, cut, width), BF),
            pltpu.VMEM((columns, cut, width), BF),
            pltpu.VMEM((lines, cut, width), BF),
            pltpu.VMEM((cut, width), F32),
            small, small,
            pltpu.VMEM((8, flat.shape[1]), F32),
            pltpu.VMEM(flat.shape, F32),
            pltpu.VMEM((place.second,) + flat.shape, F32),
            pltpu.VMEM((place.first,) + flat.shape, F32),
            pltpu.VMEM((4,) + flat.shape, F32),
        ] + line_sems(place, PIECES, lines) + [
            DMA((1 + place.first + place.second,)), DMA((2 + place.first + place.second,)), DMA((4,)), DMA((5,)),
        ],
        compiler_params=params(4),
        name="reduce_all",
    )(tok, ge, flat, gain, back, weights, hidden, cot_own, y_keep, y_away)
    if not pair:
        edge = width - 128 - 2 * STATE
        own = own.at[:, edge : edge + 2 * STATE].set(lax.psum(own[:, edge : edge + 2 * STATE], "tensor"))
    return own, flat, gh, output


def body(
    hidden, pre_gain, zx_weight, bc_weight, step_weight, conv_x_weight, conv_x_bias, conv_bc_weight, conv_bc_bias,
    step_bias, decay_log, skip_gain, norm_gain, out_weight, segment_ids, pad_mask, grad_out,
):
    n, size = lax.axis_size("tensor"), lax.axis_size("dp")
    heads = step_weight.shape[1]
    inner = heads * HEADDIM
    seqs, here, width = hidden.shape
    length = segment_ids.shape[1]
    first, second = factors(size)
    place = Place(first, second, n == 2 and (2 * width // size) % 128 == 0, seqs * length // BLOCK, length)
    line = lambda vector: vector.reshape(1, -1)
    gain = line(pre_gain)

    weights, tok, aux, cw, cbw, hp = gather_all(
        place, size, zx_weight, bc_weight, step_weight.T, hidden, gain, conv_x_weight, line(conv_x_bias),
        conv_bc_weight, line(conv_bc_bias), line(step_bias), line(decay_log), line(skip_gain), line(norm_gain),
        segment_ids, pad_mask,
    )
    if not place.pair:
        tok = lax.all_gather(tok, "tensor", axis=1, tiled=True)
    pz, raw, mixed, gn, cv, pre, cbc, pbc, st, stat, out_all, cot = mixer_forward(
        place, size, tok, weights, aux, cw, cbw, hp, grad_out, out_weight.T
    )
    if not place.pair:
        cot = lax.all_gather(grad_out, "tensor", axis=1, tiled=True)
    g = y = None
    if not place.pair:
        y = jnp.einsum("stc,rc->str", gn, out_all, preferred_element_type=F32)
        cross = jnp.sum(y * cot.astype(F32), axis=-1)
        stat = finish_sums(lax.psum(stat.at[:, 1].set(cross), "tensor"), inner * n)
        g = jnp.einsum("str,rc->stc", cot, out_all, preferred_element_type=F32).astype(BF)
    ge, flat, y_keep, y_away, back, out_rows = mixer_backward(
        place, size, inner * n, pz, raw, aux, mixed, cv, pre, cbc, pbc, st, stat, cw, cbw, hp, g, out_all, gn, cot
    )
    if not place.pair:
        normed_out = (gn.astype(F32) * back[:, 0, :, None]).astype(BF)
        terms = jnp.einsum("str,stc->rc", cot, normed_out, preferred_element_type=F32).astype(BF)
        out_rows = lax.psum_scatter(terms, "dp", scatter_dimension=0, tiled=True).astype(F32)
        dg = jnp.einsum("sty,py->stp", ge, weights, preferred_element_type=F32)
        flat = flat.at[5].add(jnp.sum(dg * tok.astype(F32), axis=(0, 1)))
    own, sums, grad_hidden, output = reduce_all(
        place, size, tok, ge, flat, gain, back, weights, hidden, grad_out, y_keep, y_away
    )
    if not place.pair:
        hidden_f = hidden.astype(F32)
        inv_rms = lax.rsqrt(jnp.mean(hidden_f * hidden_f, axis=-1, keepdims=True) + epsilon)
        scatter = lambda rows: lax.psum_scatter(rows, "tensor", scatter_dimension=1, tiled=True)
        gain_grad = scatter(dg) * pre_gain
        pull = inv_rms**3 * jnp.mean(hidden_f * gain_grad, axis=-1, keepdims=True)
        grad_hidden = (grad_out.astype(F32) + inv_rms * gain_grad - hidden_f * pull).astype(BF)
        output = (hidden_f + scatter(y * back[:, 0, :, None])).astype(BF)
    rows = own.shape[0]
    output, grad_hidden, grad_pre, gzx, gbc, gstep, gcxw, gcxb, gcbw, gcbb, gbias, gdecay, gskip, gnorm, gout = pl.pallas_call(
        functools.partial(last_kernel, heads),
        in_specs=[WHOLE] * 6,
        out_specs=[WHOLE] * 15,
        out_shape=[
            SDS(hidden.shape, BF), SDS(hidden.shape, BF), SDS((1, width), F32), SDS((rows, 2 * inner), F32),
            SDS((rows, 2 * STATE), F32), SDS((heads, rows), F32), SDS((TAPS, inner), F32), SDS((1, inner), F32),
            SDS((TAPS, 2 * STATE), F32), SDS((1, 2 * STATE), F32), SDS((1, heads), F32), SDS((1, heads), F32),
            SDS((1, heads), F32), SDS((1, inner), F32), SDS((rows, inner), F32),
        ],
        compiler_params=params(),
        name="outputs",
    )(own, sums, grad_hidden, output, out_rows, gain)
    return (
        output, grad_hidden, grad_pre[0], gzx, gbc, gstep.T, gcxw, gcxb[0], gcbw, gcbb[0], gbias[0], gdecay[0],
        gskip[0], gnorm[0], gout.T,
    )


def solution(mesh):
    placed = (
        P("dp", "tensor", None), P(), P("dp", "tensor"), P("dp", None), P("dp", "tensor"), P(None, "tensor"),
        P("tensor"), P(), P(), P("tensor"), P("tensor"), P("tensor"), P("tensor"), P("tensor", "dp"),
        P("dp", None), P("dp", None), P("dp", "tensor", None),
    )
    return jax.shard_map(
        body,
        mesh=mesh,
        in_specs=placed,
        out_specs=(
            P("dp", "tensor", None), P("dp", "tensor", None), P(), P("dp", "tensor"), P("dp", None), P("dp", "tensor"),
            P(None, "tensor"), P("tensor"), P(), P(), P("tensor"), P("tensor"), P("tensor"), P("tensor"),
            P("tensor", "dp"),
        ),
        check_vma=False,
    )
```

```python
import collections
import functools
import jax
import jax.numpy as jnp
from jax import lax
from jax.experimental import pallas as pl
from jax.experimental.pallas import tpu as pltpu
from jax.sharding import PartitionSpec as P

HEADDIM = 64
STATE = 128
CHUNK = 128
TAPS = 4
HALO = 8
AUX = 16
LOG2E = 1.4426950408889634
FAR = -1e30
BLOCK = 256
VMEM_LIMIT = 58 * 1024 * 1024
MESH = pl.DeviceIdType.MESH
PIECES = 2
epsilon = 1e-05
BF = jnp.bfloat16
F32 = jnp.float32


def sigmoid(v):
    return 0.5 * jnp.tanh(0.5 * v) + 0.5


def split3(v):
    a = v.astype(BF)
    r = v - a.astype(F32)
    b = r.astype(BF)
    c = (r - b.astype(F32)).astype(BF)
    return a, b, c


def dot_nn(a, b):
    return lax.dot_general(a, b, (((1,), (0,)), ((), ())), preferred_element_type=F32)


def dot_nt(a, b):
    return lax.dot_general(a, b, (((1,), (1,)), ((), ())), preferred_element_type=F32)


def exact_dot(v, ones):
    rows = v.shape[0]
    out = dot_nn(jnp.concatenate(split3(v), axis=0), ones)
    return out[:rows] + out[rows : 2 * rows] + out[2 * rows :]


def iota2(shape, dim):
    return lax.broadcasted_iota(jnp.int32, shape, dim)


def pieces(raw, bias, rate, aux, tri):
    pad = aux[1:2]
    pre = raw + bias
    soft = jnp.maximum(pre, 0.0) + jnp.log1p(jnp.exp(-jnp.abs(pre)))
    dt = soft * pad
    cum = exact_dot(dt * rate, tri) * LOG2E
    carried = jnp.exp2(cum) * aux[5:6]
    toward = jnp.exp2(cum[:, CHUNK - 1 : CHUNK] - cum) * aux[6:7]
    return dt, cum, carried, toward


def expander(heads, inner, place):
    row = lax.rem(iota2((256, inner), 0), 128)
    head = lax.div(iota2((256, inner), 1), HEADDIM)
    return jnp.where(row == head + place, 1.0, 0.0).astype(BF)


def collector(inner, place):
    head = lax.div(iota2((inner, 128), 0), HEADDIM)
    lane = iota2((inner, 128), 1)
    return jnp.where(lane == head + place, 1.0, 0.0).astype(BF)


def hi_lo(cols):
    hi = cols.astype(BF)
    return jnp.concatenate([hi, (cols - hi.astype(F32)).astype(BF)], axis=1)


def compact(rows_list):
    used = sum(r.shape[0] for r in rows_list)
    if used < 128:
        rows_list = list(rows_list) + [jnp.zeros((128 - used, CHUNK), F32)]
    return jnp.concatenate(rows_list, axis=0).T


def split_pair(first, second, low):
    gate = jnp.where(low, first, pltpu.roll(second, HEADDIM, 1))
    value = jnp.where(low, pltpu.roll(first, HEADDIM, 1), second)
    return gate, value


Place = collections.namedtuple("Place", ("first", "second", "pair", "steps", "length"))


def factors(size):
    first = 4 if size % 8 == 0 else 1
    return first, size // (2 * first)


class Spot:
    def __init__(self, place):
        self.first, self.second = place.first, place.second
        self.index = lax.axis_index("dp")
        self.me = lax.axis_index("tensor")
        self.a = lax.div(self.index, 2 * self.second)
        self.b = lax.rem(lax.div(self.index, 2), self.second)
        self.c = lax.rem(self.index, 2)

    def at(self, i, j, k):
        return (i * self.second + j) * 2 + k

    def around(self, i):
        return lax.rem(self.a + i, self.first)

    def aside(self, j):
        return lax.rem(self.b + j, self.second)

    @property
    def sibling(self):
        return self.at(self.a, self.b, 1 - self.c)

    def greet(self, pair):
        barrier = pltpu.get_barrier_semaphore()
        peers = [(self.sibling, self.me)]
        peers += [(self.at(self.a, self.aside(j), self.c), self.me) for j in range(1, self.second)]
        peers += [(self.at(self.around(i), self.b, self.c), self.me) for i in range(1, self.first)]
        if pair:
            peers.append((self.index, 1 - self.me))
        for peer in peers:
            pl.semaphore_signal(barrier, inc=1, device_id=peer, device_id_type=MESH)
        pl.semaphore_wait(barrier, len(peers))

    def copy(self, src, dst, ss, rs, target, tensor=None):
        return pltpu.make_async_remote_copy(
            src_ref=src, dst_ref=dst, send_sem=ss, recv_sem=rs,
            device_id=(target, self.me if tensor is None else tensor), device_id_type=MESH,
        )

    def arrived(self, dst, rs):
        self.copy(dst, dst, rs, rs, self.sibling).wait_recv()


def when(valid, run):
    def quiet():
        run()

    quiet() if valid is None else pl.when(valid)(quiet)


def gather_sites(first, second):
    return (2 + second) + (first - 1) * 2 * (1 + second) + (2 * first - 1) * (second - 1)


def row_sites(first, second):
    return (2 + second) + 3 * (second - 1) + (first - 1) * 4 * second


class LineGather:
    def __init__(self, spot, arrays, send_sem, recv_sem, local_sem, columns=None, part=0, parts=1):
        self.spot, self.arrays, self.columns = spot, arrays, columns
        self.part, self.parts = part, parts
        self.send_sem, self.recv_sem, self.local_sem = send_sem, recv_sem, local_sem
        self.sites = []

    def rows(self, which, shard):
        own, full = self.arrays[which]
        rows = own.shape[0]
        there = pl.ds(pl.multiple_of((shard * self.parts + self.part) * rows, rows), rows)
        return full.at[there] if self.columns is None else full.at[there, self.columns]

    def copies(self, site, shard, target, mine=False):
        return [
            self.spot.copy(
                own if mine else self.rows(w, shard), self.rows(w, shard),
                self.send_sem.at[w, site], self.recv_sem.at[w, shard], target,
            )
            for w, (own, full) in enumerate(self.arrays)
        ]

    def send(self, valid, shard, target, mine=False):
        site = len(self.sites)
        self.sites.append((valid, shard, target, mine))
        when(valid and valid(), lambda: [copy.start() for copy in self.copies(site, shard(), target(), mine)])

    def arrive(self, valid, shard):
        def wait():
            for w in range(len(self.arrays)):
                self.spot.arrived(self.rows(w, shard), self.recv_sem.at[w, shard])

        when(valid, wait)

    def local(self):
        return [
            pltpu.make_async_copy(own, self.rows(w, self.spot.index), self.local_sem.at[w])
            for w, (own, full) in enumerate(self.arrays)
        ]

    def begin(self):
        s = self.spot
        self.send(lambda: s.a < s.first - 1, lambda: s.index, lambda: s.at(s.a + 1, s.b, s.c), True)
        self.send(lambda: s.a > 0, lambda: s.index, lambda: s.at(s.a - 1, s.b, s.c), True)
        for j in range(1, s.second):
            self.send(None, lambda: s.index, lambda j=j: s.at(s.a, s.aside(j), s.c), True)
        self.send(None, lambda: s.index, lambda: s.sibling, True)
        for copy in self.local():
            copy.start()

    def sides(self, hop):
        s = self.spot
        if hop == 0:
            return [(None, lambda: s.a, None, None)]
        return [
            (lambda: s.a - hop >= 0, lambda: s.a - hop, lambda: s.a < s.first - 1, lambda: s.at(s.a + 1, s.b, s.c)),
            (lambda: s.a + hop < s.first, lambda: s.a + hop, lambda: s.a > 0, lambda: s.at(s.a - 1, s.b, s.c)),
        ]

    def along(self, hop):
        s = self.spot
        for valid, origin, onward, target in self.sides(hop):
            shard = lambda origin=origin: s.at(origin(), s.b, s.c)
            self.arrive(valid(), shard())
            self.send(lambda valid=valid, onward=onward: valid() & onward(), shard, target)
            for j in range(1, s.second):
                self.send(valid, shard, lambda j=j: s.at(s.a, s.aside(j), s.c))
            self.send(valid, shard, lambda: s.sibling)

    def across(self, hop):
        s = self.spot
        for j in range(1, s.second):
            for valid, origin, onward, target in self.sides(hop):
                shard = lambda origin=origin, j=j: s.at(origin(), s.aside(j), s.c)
                self.arrive(valid and valid(), shard())
                self.send(valid, shard, lambda: s.sibling)

    def finish(self):
        s = self.spot
        for i in range(s.first):
            for j in range(s.second):
                self.arrive(None, s.at(i, j, 1 - s.c))
        for site, (valid, shard, target, mine) in enumerate(self.sites):
            when(
                valid and valid(),
                lambda site=site, shard=shard, target=target, mine=mine: [
                    copy.wait_send() for copy in self.copies(site, shard(), target(), mine)
                ],
            )
        for copy in self.local():
            copy.wait()


class RowGather(LineGather):
    def cross(self):
        s = self.spot
        for j in range(1, s.second):
            shard = lambda j=j: s.at(s.a, s.aside(j), s.c)
            self.arrive(None, shard())
            self.send(lambda: s.a < s.first - 1, shard, lambda: s.at(s.a + 1, s.b, s.c))
            self.send(lambda: s.a > 0, shard, lambda: s.at(s.a - 1, s.b, s.c))
            self.send(None, shard, lambda: s.sibling)

    def along(self, hop):
        s = self.spot
        for j in range(s.second):
            for valid, origin, onward, target in self.sides(hop):
                shard = lambda origin=origin, j=j: s.at(origin(), s.aside(j), s.c)
                self.arrive(valid(), shard())
                self.send(lambda valid=valid, onward=onward: valid() & onward(), shard, target)
                self.send(valid, shard, lambda: s.sibling)


class TokenSwap:
    def __init__(self, spot, own, full, sem):
        self.spot, self.own, self.full, self.sem = spot, own, full, sem

    def target(self):
        here = self.own.shape[1]
        return self.full.at[:, pl.ds(pl.multiple_of(self.spot.me * here, here), here)]

    def remote(self):
        s = self.spot
        return s.copy(self.own, self.target(), self.sem.at[0], self.sem.at[1], s.index, 1 - s.me)

    def local(self):
        return pltpu.make_async_copy(self.own, self.target(), self.sem.at[2])

    def begin(self):
        self.remote().start()
        self.local().start()

    def finish(self):
        self.remote().wait()
        self.local().wait()


class HalfSwap:
    def __init__(self, spot, whole, away, sem):
        self.spot, self.whole, self.away, self.sem = spot, whole, away, sem

    def remote(self):
        s = self.spot
        here = self.away.shape[1]
        rows = self.whole.at[:, pl.ds(pl.multiple_of((1 - s.me) * here, here), here)]
        return s.copy(rows, self.away, self.sem.at[0], self.sem.at[1], s.index, 1 - s.me)

    def begin(self):
        self.remote().start()

    def finish(self):
        self.remote().wait()


class LineScatter:
    def __init__(
        self, spot, part, core_buf, x_buf, z_buf, out, core_send, core_recv, x_send, x_recv, z_send, z_recv, cuts=1
    ):
        self.spot, self.part, self.out, self.cuts = spot, part, out, cuts
        self.core_buf, self.x_buf, self.z_buf = core_buf, x_buf, z_buf
        self.sems = (core_send, core_recv, x_send, x_recv, z_send, z_recv)
        self.rows = out.shape[0] // cuts
        self.copies = []
        a = spot.a
        if spot.first == 4:
            near = jnp.minimum(a, 3 - a)
            self.order = [jnp.where(a < 2, d, 3 - d) for d in (3 + 0 * a, 2 - 2 * near, 1 + near)] + [a]
        else:
            self.order = [a]

    def block(self, i, j, k, q):
        rows = self.rows
        return self.part.at[pl.ds(pl.multiple_of((self.spot.at(i, j, k) * self.cuts + q) * rows, rows), rows)]

    def slot(self, i, j, q):
        return (i * self.spot.second + j) * self.cuts + q

    def start(self, make):
        make().start()
        self.copies.append(make)

    def give(self, n, j):
        s, i = self.spot, self.order[n]
        for q in range(self.cuts):

            def make(q=q):
                t = self.slot(i, s.aside(j), q)
                return s.copy(
                    self.block(i, s.aside(j), 1 - s.c, q), self.core_buf.at[t], self.sems[0].at[t],
                    self.sems[1].at[t], s.sibling,
                )

            self.start(make)

    def terms(self, n, j):
        rows = 2 * self.rows * self.cuts
        first_row = self.spot.at(self.order[n], self.spot.aside(j), 0) * self.rows * self.cuts
        return pl.ds(pl.multiple_of(first_row, rows), rows)

    def cross_over(self, n, j):
        s, i = self.spot, self.order[n]
        for q in range(self.cuts):
            t = self.slot(i, s.aside(j), q)
            s.arrived(self.core_buf.at[t], self.sems[1].at[t])
            own = self.block(i, s.aside(j), s.c, q)[...].astype(F32)
            self.core_buf[t] = (own + self.core_buf[t].astype(F32)).astype(BF)

            def make(q=q):
                t = self.slot(i, s.aside(j), q)
                there = (i * (s.second - 1) + s.second - j - 1) * self.cuts + q
                here = (i * (s.second - 1) + j - 1) * self.cuts + q
                return s.copy(
                    self.core_buf.at[t], self.x_buf.at[there], self.sems[2].at[here], self.sems[3].at[there],
                    s.at(s.a, s.aside(j), s.c),
                )

            self.start(make)

    def column_sum(self, n, q):
        s, i = self.spot, self.order[n]
        t = self.slot(i, s.b, q)
        s.arrived(self.core_buf.at[t], self.sems[1].at[t])
        total = self.block(i, s.b, s.c, q)[...].astype(F32) + self.core_buf[t].astype(F32)
        for j in range(1, s.second):
            u = (i * (s.second - 1) + j - 1) * self.cuts + q
            s.arrived(self.x_buf.at[u], self.sems[3].at[u])
            total = total + self.x_buf[u].astype(F32)
        return total

    def produce(self, make_terms, far):
        s = self.spot
        for j in range(1, s.second) if far else [0]:
            for n in range(s.first):
                make_terms(self.terms(n, j))
                self.give(n, j)

    def cross(self):
        for j in range(1, self.spot.second):
            for n in range(self.spot.first):
                self.cross_over(n, j)

    def along(self):
        s = self.spot
        for n in range(s.first):
            for q in range(self.cuts):
                total = self.column_sum(n, q)
                if n == s.first - 1:
                    self.out[q * self.rows : (q + 1) * self.rows] = total
                    continue
                self.core_buf[self.slot(self.order[n], s.b, q)] = total.astype(BF)

                def make(n=n, q=q):
                    z = s.a * self.cuts + q
                    return s.copy(
                        self.core_buf.at[self.slot(self.order[n], s.b, q)], self.z_buf.at[z],
                        self.sems[4].at[n * self.cuts + q], self.sems[5].at[z], s.at(self.order[n], s.b, s.c),
                    )

                self.start(make)

    def chain(self, acc, order):
        s = self.spot
        for n in order:
            for q in range(self.cuts):
                i = self.order[n]
                total = self.column_sum(n, q)
                if n == s.first - 1:
                    self.out[q * self.rows : (q + 1) * self.rows] = total
                    continue
                down = jnp.where(i > s.a, 0, 1)
                z = (down * s.first + i) * self.cuts + q
                acc[...] = total

                @pl.when(jnp.where(i > s.a, s.a, s.first - 1 - s.a) > 0)
                def _(z=z):
                    s.arrived(self.z_buf.at[z], self.sems[5].at[z])
                    acc[...] = acc[...] + self.z_buf[z].astype(F32)

                self.core_buf[self.slot(i, s.b, q)] = acc[...].astype(BF)

                def make(n=n, q=q, i=i, down=down, z=z):
                    return s.copy(
                        self.core_buf.at[self.slot(i, s.b, q)], self.z_buf.at[z],
                        self.sems[4].at[n * self.cuts + q], self.sems[5].at[z], s.at(s.a + 1 - 2 * down, s.b, s.c),
                    )

                self.start(make)

    def finish_chain(self):
        s = self.spot
        for q in range(self.cuts):
            cut = slice(q * self.rows, (q + 1) * self.rows)
            for down, there in ((0, s.a), (1, s.first - 1 - s.a)):
                z = (down * s.first + s.a) * self.cuts + q

                @pl.when(there > 0)
                def _(z=z, cut=cut):
                    s.arrived(self.z_buf.at[z], self.sems[5].at[z])
                    self.out[cut] = self.out[cut] + self.z_buf[z].astype(F32)

    def wait_sends(self):
        for make in self.copies:
            make().wait_send()

    def finish(self):
        s = self.spot
        for i in range(1, s.first):
            for q in range(self.cuts):
                z = s.around(i) * self.cuts + q
                s.arrived(self.z_buf.at[z], self.sems[5].at[z])
                cut = slice(q * self.rows, (q + 1) * self.rows)
                self.out[cut] = self.out[cut] + self.z_buf[z].astype(F32)
        self.wait_sends()


def forward_kernel(
    place, heads, tok_ref, w_ref, aux_ref, cw_ref, cbw_ref, hp_ref, cot_own, out_own,
    pz_ref, raw_ref, mixed_ref, gated_ref, cv_ref, pre_ref, cbc_ref, pbc_ref, st_ref, stat_ref, out_all, cot_full,
    state, ubuf, bbuf, vd, yint, expand, tri_ref, send_sem, recv_sem, local_sem, cot_sem,
):
    inner = heads * HEADDIM
    pairs = heads // 2
    wide = 2 * inner
    now = pl.program_id(0) * pl.num_programs(1) + pl.program_id(1)
    last = place.steps - 1
    first = now == 0
    spot = Spot(place)
    gather = LineGather(spot, [(out_own, out_all)], send_sem, recv_sem, local_sem)
    swap = TokenSwap(spot, cot_own, cot_full, cot_sem) if place.pair else None

    @pl.when(first)
    def _():
        spot.greet(place.pair)
        gather.begin()
        if swap:
            swap.begin()

    for hop in range(1, place.first):

        @pl.when(now == min(hop, last))
        def _(hop=hop):
            gather.along(hop)
            gather.across(hop - 1)

    @pl.when(first)
    def _():
        for i, place in enumerate((AUX + heads, AUX + 2 * heads, AUX + 3 * heads)):
            expand[i] = expander(heads, inner, place)
        tri_ref[...] = jnp.where(iota2((CHUNK, CHUNK), 0) <= iota2((CHUNK, CHUNK), 1), 1.0, 0.0).astype(BF)

    @pl.when(pl.program_id(1) == 0)
    def _():
        state[...] = jnp.zeros_like(state)
        ubuf[0:HALO] = jnp.zeros((HALO, inner), F32)
        bbuf[0:HALO] = jnp.zeros((HALO, 2 * STATE), F32)

    tok = tok_ref[0]
    side = dot_nn(tok, w_ref[:, wide:])
    raw_ref[0] = side[:, 2 * STATE :].T[0:heads]
    pz_ref[0, :, wide:] = side[:, : 2 * STATE].astype(BF)
    for p in range(pairs):
        pz_ref[0, :, 256 * p : 256 * p + 256] = dot_nn(tok, w_ref[:, 256 * p : 256 * p + 256]).astype(BF)

    def chunk_step(step, carry):
        here = pl.ds(pl.multiple_of(step * CHUNK, CHUNK), CHUNK)
        aux = aux_ref[0, :, here]
        raw = raw_ref[0, :, here]
        bc = pz_ref[0, here, wide:]
        dt, cum, carried, toward = pieces(raw, hp_ref[0], hp_ref[1], aux, tri_ref[...])
        cols = compact([aux, cum, dt, carried, toward])
        both = hi_lo(cols)
        dtx = dot_nn(both, expand[0])
        carx = dot_nn(both, expand[1])
        towx = dot_nn(both, expand[2])
        pad = cols[:, 1:2]
        same = [None] + [cols[:, 1 + k : 2 + k] for k in range(1, TAPS)]
        low = iota2((CHUNK, 128), 1) < HEADDIM

        bbuf[HALO:] = bc.astype(F32) * pad
        maps = cbw_ref[TAPS : TAPS + 1] + cbw_ref[0:1] * bbuf[HALO:]
        for k in range(1, TAPS):
            maps = maps + cbw_ref[k : k + 1] * (same[k] * bbuf[HALO - k : HALO - k + CHUNK])
        pbc_ref[0, here] = maps.astype(BF)
        maps = (maps * sigmoid(maps)).astype(BF)
        cbc_ref[0, here] = maps
        bbuf[0:HALO] = bbuf[CHUNK : CHUNK + HALO]
        keys, queries = maps[:, :STATE], maps[:, STATE:]
        scores = dot_nt(queries, keys)
        keys_t = keys.astype(F32).T.astype(BF)

        for p in range(pairs):
            s = slice(128 * p, 128 * p + 128)
            x0 = pz_ref[0, here, 256 * p : 256 * p + 128].astype(F32)
            x1 = pz_ref[0, here, 256 * p + 128 : 256 * p + 256].astype(F32)
            value = jnp.where(low, pltpu.roll(x0, HEADDIM, 1), x1)
            ubuf[HALO:, s] = value * pad
            pre = cw_ref[TAPS : TAPS + 1, s] + cw_ref[0:1, s] * ubuf[HALO:, s]
            for k in range(1, TAPS):
                pre = pre + cw_ref[k : k + 1, s] * (same[k] * ubuf[HALO - k : HALO - k + CHUNK, s])
            pre_ref[0, here, s] = pre.astype(BF)
            cv = (pre * sigmoid(pre)).astype(BF)
            cv_ref[0, here, s] = cv
            vd[:, s] = (cv.astype(F32) * dtx[:, s]).astype(BF)
        ubuf[0:HALO] = ubuf[CHUNK : CHUNK + HALO]

        old = state[...]
        old_b = old.astype(BF)
        st_ref[0, step] = old_b
        yint[...] = dot_nn(queries, old_b) * carx
        state[...] = carx[CHUNK - 1 : CHUNK] * old + dot_nn(keys_t, (vd[...].astype(F32) * towx).astype(BF))

        inside = (iota2((CHUNK, CHUNK), 0) >= iota2((CHUNK, CHUNK), 1)) & (cols[:, 0:1] == aux[0:1])
        fence = jnp.where(inside, 0.0, FAR)
        squares = jnp.zeros((CHUNK, 128), F32)
        for p in range(pairs):
            s = slice(128 * p, 128 * p + 128)
            mix = []
            for h in (2 * p, 2 * p + 1):
                decay = jnp.exp2(cols[:, AUX + h : AUX + h + 1] - cum[h : h + 1] + fence)
                mix.append((scores * decay).astype(BF))
            v = vd[:, s]
            zero = jnp.zeros_like(v)
            stacked = jnp.concatenate([jnp.where(low, v, zero), jnp.where(low, zero, v)], axis=0)
            y = dot_nn(jnp.concatenate(mix, axis=1), stacked)
            mixed = y + yint[:, s] + cw_ref[5:6, s] * cv_ref[0, here, s].astype(F32)
            x0 = pz_ref[0, here, 256 * p : 256 * p + 128].astype(F32)
            x1 = pz_ref[0, here, 256 * p + 128 : 256 * p + 256].astype(F32)
            gate = jnp.where(low, x0, pltpu.roll(x1, HEADDIM, 1))
            gated = mixed * (gate * sigmoid(gate))
            mixed_ref[0, here, s] = mixed.astype(BF)
            gated_ref[0, here, s] = (gated * cw_ref[6:7, s]).astype(BF)
            squares = squares + gated * gated
        lane = iota2((CHUNK, 128), 1)
        sums = jnp.where(lane == 0, jnp.sum(squares, axis=1, keepdims=True), 0.0)
        stat_ref[0, :, here] = sums.T[0:8]
        return carry

    lax.fori_loop(0, BLOCK // CHUNK, chunk_step, 0, unroll=True)

    @pl.when(now == last)
    def _():
        gather.across(place.first - 1)
        gather.finish()
        if swap:
            swap.finish()


def backward_kernel(
    place, heads, inner_all, pz_ref, raw_ref, aux_ref, mixed_ref, cv_ref, pre_ref, cbc_ref, pbc_ref,
    st_ref, stat_ref, cw_ref, cbw_ref, hp_ref, g_ref, out_ref, gn_all, cot_all,
    ge_ref, flat_ref, y_keep, y_away, back_ref, grad_rows,
    dstate, cbuf, dbuf, vd, gm_s, gmc_s, ggate_s, bs_s, expand, collect, tri_ref, suf_ref, ghead_ref,
    y_s, g_s, fold, sums, theirs, normed_s, part_buf, core_buf, x_buf, z_buf,
    core_send, core_recv, x_send, x_recv, z_send, z_recv, y_sem, stat_sem,
):
    inner = heads * HEADDIM
    pairs = heads // 2
    wide = 2 * inner
    now = pl.program_id(0) * pl.num_programs(1) + pl.program_id(1)
    last = place.steps - 1
    first = now == 0
    gch_ref = flat_ref.at[8:16, 0:inner]
    gmap_ref = flat_ref.at[0:8, 0 : 2 * STATE]
    spot = Spot(place)
    if place.pair:
        scatter = LineScatter(
            spot, part_buf, core_buf, x_buf, z_buf, grad_rows, core_send, core_recv, x_send, x_recv, z_send, z_recv
        )
        half = HalfSwap(spot, y_s, y_away, y_sem)
        here_len = y_keep.shape[1]
        seqs = y_keep.shape[0]
        per_seq = place.length // CHUNK

        def out_terms(there):
            part_buf[there] = lax.dot_general(
                cot_all[:, there], normed_s[...], (((0,), (0,)), ((), ())), preferred_element_type=F32
            ).astype(BF)

        def keep():
            rows = y_s.at[:, pl.ds(pl.multiple_of(spot.me * here_len, here_len), here_len)]
            return pltpu.make_async_copy(rows, y_keep, y_sem.at[2])

        @pl.when(first)
        def _():
            spot.greet(True)
            for cut in range(out_ref.shape[0] // 256):
                cols = slice(256 * cut, 256 * cut + 256)
                for seq in range(seqs):
                    rows = slice(seq * place.length, (seq + 1) * place.length)
                    y = dot_nt(gn_all[rows], out_ref[cols])
                    y_s[seq, :, cols] = y.astype(BF)
                    y = y * cot_all[rows, cols].astype(F32)
                    y = y[:, :128] + y[:, 128:]
                    fold[rows] = y if cut == 0 else fold[rows] + y

            for step in range(seqs * per_seq):
                rows = slice(step * CHUNK, (step + 1) * CHUNK)
                seq, cut = divmod(step, per_seq)
                there = slice(cut * CHUNK, (cut + 1) * CHUNK)
                cross = jnp.sum(fold[rows], axis=1, keepdims=True)
                row = jnp.broadcast_to(cross, (CHUNK, 128)).T[0:8]
                sums[seq, :, there] = jnp.where(iota2(row.shape, 0) == 1, row, stat_ref[seq, :, there])
            swap = spot.copy(sums, theirs, stat_sem.at[0], stat_sem.at[1], spot.index, 1 - spot.me)
            swap.start()

            def out_back(step, carry):
                rows = pl.ds(pl.multiple_of(step * BLOCK, BLOCK), BLOCK)
                g_s[rows] = dot_nn(cot_all[rows], out_ref[...]).astype(BF)
                return carry

            lax.fori_loop(0, seqs * place.length // BLOCK, out_back, 0)
            swap.wait()
            half.begin()
            keep().start()
            back_ref[...] = finish_sums(sums[...] + theirs[...], inner_all)

            for step in range(seqs * per_seq):
                rows = slice(step * CHUNK, (step + 1) * CHUNK)
                seq, cut = divmod(step, per_seq)
                rms_col = compact([back_ref[seq, :, cut * CHUNK : (cut + 1) * CHUNK]])[:, 0:1]
                normed_s[rows] = (gn_all[rows].astype(F32) * rms_col).astype(BF)
            scatter.produce(out_terms, True)
            scatter.produce(out_terms, False)
            scatter.cross()

        @pl.when(now == min(2, last))
        def _():
            scatter.along()
    else:
        pl.when(first)(lambda: back_ref.__setitem__(Ellipsis, stat_ref[...]))

    @pl.when(first)
    def _():
        for i, place in enumerate((AUX + heads, AUX + 2 * heads, AUX + 3 * heads)):
            expand[i] = expander(heads, inner, place)
        collect[0] = collector(inner, heads)
        collect[1] = collector(inner, 2 * heads)
        r, c = iota2((CHUNK, CHUNK), 0), iota2((CHUNK, CHUNK), 1)
        tri_ref[...] = jnp.where(r <= c, 1.0, 0.0).astype(BF)
        suf_ref[...] = jnp.where(r >= c, 1.0, 0.0).astype(BF)
        flat_ref[...] = jnp.zeros_like(flat_ref)
        ghead_ref[...] = jnp.zeros_like(ghead_ref)

    @pl.when(pl.program_id(1) == 0)
    def _():
        dstate[...] = jnp.zeros_like(dstate)
        cbuf[CHUNK:] = jnp.zeros((HALO, inner), F32)
        dbuf[CHUNK:] = jnp.zeros((HALO, 2 * STATE), F32)

    seq_now = pl.program_id(0)
    block_start = (pl.num_programs(1) - 1 - pl.program_id(1)) * BLOCK

    def chunk_step(step, carry):
        here = pl.ds(pl.multiple_of(BLOCK - CHUNK - step * CHUNK, CHUNK), CHUNK)
        there = pl.ds(pl.multiple_of(block_start + BLOCK - CHUNK - step * CHUNK, CHUNK), CHUNK)
        flat_rows = pl.ds(pl.multiple_of(seq_now * place.length + block_start + BLOCK - CHUNK - step * CHUNK, CHUNK), CHUNK)
        aux = aux_ref[0, :, here]
        rate = hp_ref[1]
        dt, cum, carried, toward = pieces(raw_ref[0, :, here], hp_ref[0], rate, aux, tri_ref[...])
        cols = compact([aux, cum, dt, carried, toward, back_ref[seq_now, :, there]])
        both = hi_lo(cols)
        dtx = dot_nn(both, expand[0])
        carx = dot_nn(both, expand[1])
        towx = dot_nn(both, expand[2])
        pad = cols[:, 1:2]
        ahead = [None] + [cols[:, 7 + k : 8 + k] for k in range(1, TAPS)]
        base = AUX + 4 * heads
        rms, pull = cols[:, base : base + 1], cols[:, base + 1 : base + 2]
        low = iota2((CHUNK, 128), 1) < HEADDIM
        maps = cbc_ref[0, here]
        keys, queries = maps[:, :STATE], maps[:, STATE:]
        queries_t = queries.astype(F32).T.astype(BF)
        scores_t = dot_nt(keys, queries)

        for p in range(pairs):
            s = slice(128 * p, 128 * p + 128)
            x0 = pz_ref[0, here, 256 * p : 256 * p + 128].astype(F32)
            x1 = pz_ref[0, here, 256 * p + 128 : 256 * p + 256].astype(F32)
            gate = jnp.where(low, x0, pltpu.roll(x1, HEADDIM, 1))
            sig = sigmoid(gate)
            act = gate * sig
            mixed = mixed_ref[0, here, s].astype(F32)
            gated = mixed * act
            g = (g_s[flat_rows, s] if place.pair else g_ref[0, here, s]).astype(F32)
            grad_gated = rms * (g * cw_ref[6:7, s]) - gated * pull
            gm = grad_gated * act
            ggate_s[:, s] = (grad_gated * mixed * (sig * (1.0 + gate * (1.0 - sig)))).astype(BF)
            gm_s[:, s] = gm.astype(BF)
            gmc_s[:, s] = (gm * carx[:, s]).astype(BF)
            cv = cv_ref[0, here, s].astype(F32)
            vd[:, s] = (cv * dtx[:, s]).astype(BF)
            gch_ref[5:6, s] += jnp.sum(gm * cv, axis=0, keepdims=True)
            gch_ref[6:7, s] += jnp.sum(gated * rms * g, axis=0, keepdims=True)

        ds = dstate[...]
        ds_b = ds.astype(BF)
        st = st_ref[0, BLOCK // CHUNK - 1 - step]
        gmc = gmc_s[...]
        cs = dot_nn(queries, st)
        bs = dot_nn(keys, ds_b) * towx
        bs_s[...] = bs
        reach = dot_nn((gmc.astype(F32) * cs).astype(BF), collect[1])
        reach = reach + dot_nn((bs * cv_ref[0, here].astype(F32)).astype(BF), collect[0])
        grad_q = dot_nt(gmc, st)
        grad_k = dot_nt((vd[...].astype(F32) * towx).astype(BF), ds_b)
        keep = carx[CHUNK - 1 : CHUNK]
        held = jnp.sum(st.astype(F32) * ds, axis=0, keepdims=True) * keep
        dstate[...] = keep * ds + dot_nn(queries_t, gmc)

        inside = (iota2((CHUNK, CHUNK), 0) <= iota2((CHUNK, CHUNK), 1)) & (cols[:, 0:1] == aux[0:1])
        fence = jnp.where(inside, 0.0, FAR)
        grad_scores_t = jnp.zeros((CHUNK, CHUNK), F32)
        lane = iota2((CHUNK, 128), 1)
        gathered = reach
        row_sums = []
        for p in range(pairs):
            s = slice(128 * p, 128 * p + 128)
            gm_b = gm_s[:, s]
            zero = jnp.zeros_like(gm_b)
            gm_two = jnp.concatenate([jnp.where(low, gm_b, zero), jnp.where(low, zero, gm_b)], axis=0)
            near = dot_nt(vd[:, s], gm_two)
            mix = []
            for j in range(2):
                h = 2 * p + j
                decay = jnp.exp2(cum[h : h + 1] - cols[:, AUX + h : AUX + h + 1] + fence)
                mix.append((scores_t * decay).astype(BF))
                weighed = decay * near[:, CHUNK * j : CHUNK * j + CHUNK]
                grad_scores_t = grad_scores_t + weighed
                pairs_g = weighed * scores_t
                row_sums.append(jnp.sum(pairs_g, axis=0, keepdims=True))
                gathered = jnp.where(lane == h, jnp.sum(pairs_g, axis=1, keepdims=True), gathered)
            z = dot_nn(jnp.concatenate(mix, axis=1), gm_two)
            gm = gm_b.astype(F32)
            grad_v = cw_ref[5:6, s] * gm + dtx[:, s] * (z + bs_s[:, s])
            x0 = pz_ref[0, here, 256 * p : 256 * p + 128].astype(F32)
            x1 = pz_ref[0, here, 256 * p + 128 : 256 * p + 256].astype(F32)
            u = jnp.where(low, pltpu.roll(x0, HEADDIM, 1), x1) * pad
            pre = pre_ref[0, here, s].astype(F32)
            sig = sigmoid(pre)
            c = grad_v * (sig * (1.0 + pre * (1.0 - sig)))
            cbuf[0:CHUNK, s] = c
            gu = cw_ref[0:1, s] * c
            gch_ref[4:5, s] += jnp.sum(c, axis=0, keepdims=True)
            gch_ref[0:1, s] += jnp.sum(c * u, axis=0, keepdims=True)
            for k in range(1, TAPS):
                shifted = ahead[k] * cbuf[k : k + CHUNK, s]
                gu = gu + cw_ref[k : k + 1, s] * shifted
                gch_ref[k : k + 1, s] += jnp.sum(shifted * u, axis=0, keepdims=True)
            gu = gu * pad
            ggate = ggate_s[:, s].astype(F32)
            ge_ref[0, here, 256 * p : 256 * p + 128] = jnp.where(low, ggate, pltpu.roll(gu, HEADDIM, 1)).astype(BF)
            ge_ref[0, here, 256 * p + 128 : 256 * p + 256] = jnp.where(low, pltpu.roll(ggate, HEADDIM, 1), gu).astype(BF)
        cbuf[CHUNK:] = cbuf[0:HALO]

        gst = grad_scores_t.astype(BF)
        grad_k = grad_k + dot_nn(gst, queries)
        grad_q = grad_q + dot_nn(grad_scores_t.T.astype(BF), keys)
        pbc = pbc_ref[0, here].astype(F32)
        sig = sigmoid(pbc)
        c = jnp.concatenate([grad_k, grad_q], axis=1) * (sig * (1.0 + pbc * (1.0 - sig)))
        dbuf[0:CHUNK] = c
        u = pz_ref[0, here, wide:].astype(F32) * pad
        gu = cbw_ref[0:1] * c
        gmap_ref[4:5] += jnp.sum(c, axis=0, keepdims=True)
        gmap_ref[0:1] += jnp.sum(c * u, axis=0, keepdims=True)
        for k in range(1, TAPS):
            shifted = ahead[k] * dbuf[k : k + CHUNK]
            gu = gu + cbw_ref[k : k + 1] * shifted
            gmap_ref[k : k + 1] += jnp.sum(shifted * u, axis=0, keepdims=True)
        ge_ref[0, here, wide : wide + 2 * STATE] = (gu * pad).astype(BF)
        dbuf[CHUNK:] = dbuf[0:HALO]

        across = gathered.T
        col_sum = across[0:heads]
        kx = across[heads : 2 * heads]
        rint = across[2 * heads : 3 * heads]
        row_sum = jnp.concatenate(row_sums, axis=0)
        k_all = kx * dt
        held_head = exact_dot(jnp.broadcast_to(held, (16, inner)), collect[0])
        held_col = jnp.broadcast_to(held_head[0:1], (CHUNK, 128)).T[heads : 2 * heads]
        diff = row_sum + rint - col_sum - k_all
        grad_a = exact_dot(diff, suf_ref[...]) + jnp.sum(k_all, axis=1, keepdims=True) + held_col
        direct = jnp.where(dt > 0.0, col_sum / jnp.where(dt > 0.0, dt, 1.0), 0.0)
        grad_dt = direct + kx + rate * grad_a
        graw = grad_dt * aux[1:2] * sigmoid(raw_ref[0, :, here] + hp_ref[0])
        ge_ref[0, here, wide + 2 * STATE :] = compact([graw]).astype(BF)
        ghead_ref[0] += graw
        ghead_ref[1] += rate * dt * grad_a
        return carry

    lax.fori_loop(0, BLOCK // CHUNK, chunk_step, 0)
    @pl.when(now == last)
    def _():
        for i in range(2):
            sums = jnp.broadcast_to(jnp.sum(ghead_ref[i], axis=1, keepdims=True), (heads, 128))
            flat_ref[15:16, 128 * i : 128 * i + 128] = compact([sums])[0:1]
        if place.pair:
            scatter.finish()
            half.finish()
            keep().wait()
        else:
            grad_rows[...] = jnp.zeros_like(grad_rows)


def gather_kernel(
    place, heads, zx_ref, bc_ref, step_ref, hidden_ref, gain_ref, cxw_ref, cxb_ref, cbw_ref, cbb_ref, bias_ref, decay_ref,
    skip_ref, ngain_ref, seg_ref, pad_ref,
    w_all, tok_full, aux_ref, cw_ref, cbw_out, hp_ref,
    shard, tok_own, square, send_sem, recv_sem, local_sem, side_send, side_recv, side_local, tok_sem,
):
    inner = heads * HEADDIM
    wide = 2 * inner
    spot = Spot(place)
    rows = zx_ref.shape[0]
    shard[:, 0:wide] = zx_ref[...]
    shard[:, wide : wide + 2 * STATE] = bc_ref[...]
    square[...] = jnp.zeros_like(square)
    square[0:heads, 0:rows] = step_ref[...].astype(F32)
    shard[:, wide + 2 * STATE :] = square[...].T[0:rows].astype(BF)
    spot.greet(place.pair)
    main, other = slice(0, wide), slice(wide, wide + 2 * STATE + 128)
    half = rows // PIECES
    gathers = [
        LineGather(
            spot, [(shard.at[half * q : half * q + half, main], w_all)],
            send_sem.at[q], recv_sem.at[q], local_sem.at[q], main, q, PIECES,
        )
        for q in range(PIECES)
    ]
    side = RowGather(spot, [(shard.at[:, other], w_all)], side_send, side_recv, side_local, other)
    for gather in gathers:
        gather.begin()
    side.begin()

    size = 64
    seqs, here = hidden_ref.shape[0], hidden_ref.shape[1]

    def norm_rows(step, carry):
        seq, cut = lax.div(step, here // size), lax.rem(step, here // size)
        mine = pl.ds(pl.multiple_of(cut * size, size), size)
        hid = hidden_ref[seq, mine].astype(F32)
        inv = lax.rsqrt(jnp.mean(hid * hid, axis=-1, keepdims=True) + epsilon)
        tok_own[seq, mine] = (hid * inv * gain_ref[...]).astype(BF)
        return carry

    lax.fori_loop(0, seqs * (here // size), norm_rows, 0)
    if place.pair:
        swap = TokenSwap(spot, tok_own, tok_full, tok_sem)
        swap.begin()
    else:
        copy = pltpu.make_async_copy(tok_own, tok_full, tok_sem.at[2])
        copy.start()

    square[...] = jnp.zeros_like(square)
    square[0:1, 0:heads] = bias_ref[...]
    square[1:2, 0:heads] = decay_ref[...]
    square[2:3, 0:heads] = skip_ref[...]
    per_head = square[...].T
    hp_ref[0] = jnp.broadcast_to(per_head[0:heads, 0:1], (heads, 128))
    hp_ref[1] = jnp.broadcast_to(-jnp.exp(per_head[0:heads, 1:2]), (heads, 128))
    cw_ref[0:TAPS] = cxw_ref[...]
    cw_ref[TAPS : TAPS + 1] = cxb_ref[...]
    cw_ref[5:6] = exact_dot(square[0:16], expander(heads, inner, 0)[0:128])[2:3]
    cw_ref[6:7] = ngain_ref[...]
    cw_ref[7:8] = jnp.zeros((1, inner), F32)
    cbw_out[...] = jnp.zeros_like(cbw_out)
    cbw_out[0:TAPS] = cbw_ref[...]
    cbw_out[TAPS : TAPS + 1] = cbb_ref[...]

    length = place.length
    lane = iota2((8, length), 1)
    flag = lambda condition: jnp.where(condition, 1.0, 0.0)[0:1]
    for seq in range(aux_ref.shape[0]):
        seg = jnp.broadcast_to(seg_ref[seq : seq + 1], (8, length))
        aux_ref[seq] = jnp.zeros((AUX, length), F32)
        aux_ref[seq, 0:1] = seg[0:1].astype(F32)
        aux_ref[seq, 1:2] = pad_ref[seq : seq + 1].astype(F32)
        for k in range(1, TAPS):
            aux_ref[seq, 1 + k : 2 + k] = flag((pltpu.roll(seg, k, 1) == seg) & (lane >= k))
            aux_ref[seq, 7 + k : 8 + k] = flag((pltpu.roll(seg, length - k, 1) == seg) & (lane < length - k))
        before = jnp.full((8, CHUNK), -1, jnp.int32)
        for chunk in range(length // CHUNK):
            cut = slice(chunk * CHUNK, (chunk + 1) * CHUNK)
            block = seg[:, cut]
            tail = jnp.broadcast_to(block[:, CHUNK - 1 : CHUNK], (8, CHUNK))
            aux_ref[seq, 5:6, cut] = flag(block == before)
            aux_ref[seq, 6:7, cut] = flag(block == tail)
            before = tail

    for hop in range(1, place.first):
        for gather in gathers:
            gather.along(hop)
        side.cross() if hop == 1 else side.along(hop - 1)
        for gather in gathers:
            gather.across(hop - 1)
    side.along(place.first - 1) if place.first > 1 else side.cross()
    for gather in gathers:
        gather.across(place.first - 1)
    for gather in gathers:
        gather.finish()
    side.finish()
    swap.finish() if place.pair else copy.wait()


def finish_sums(total, inner_all):
    lines = lax.broadcasted_iota(jnp.int32, total.shape, 1)
    rms = lax.rsqrt(total[:, 0:1] / inner_all + epsilon)
    pull = rms * rms * rms * (total[:, 1:2] / inner_all)
    return jnp.where(lines == 0, rms, jnp.where(lines == 1, pull, 0.0))


def reduce_kernel(
    place, tok_ref, ge_ref, flat_ref, gain_ref, back_ref, w_hbm, hidden_hbm, cot_hbm, keep_hbm, away_hbm,
    own_ref, sum_ref, gh_ref, output_ref,
    w_ref, hidden_ref, cot_ref, keep_ref, away_ref, dg_ref, dg_send, dg_buf,
    part_buf, core_buf, x_buf, z_buf, acc, bc_buf, bc_send, y_flat, core_flat, x_flat, z_flat, stage,
    core_send, core_recv, x_send, x_recv, z_send, z_recv, flat_send, flat_recv, dg_sem, load_sem,
):
    spot = Spot(place)
    a, b, c, me, index = spot.a, spot.b, spot.c, spot.me, spot.index
    first, second = place.first, place.second
    scatter = LineScatter(
        spot, part_buf if place.pair else ge_ref, core_buf, x_buf, z_buf, own_ref,
        core_send, core_recv, x_send, x_recv, z_send, z_recv, PIECES,
    )
    loads = []
    if place.pair:
        pairs = ((w_hbm, w_ref), (hidden_hbm, hidden_ref), (cot_hbm, cot_ref), (keep_hbm, keep_ref), (away_hbm, away_ref))
        for k, (far, near) in enumerate(pairs):
            loads.append(pltpu.make_async_copy(far, near, load_sem.at[k]))
        loads[0].start()
    spot.greet(place.pair)
    started = []

    def send(*args):
        copy = spot.copy(*args)
        copy.start()
        started.append(copy)

    def terms(there):
        if place.pair:
            part_buf[there] = lax.dot_general(
                tok_ref[:, there], ge_ref[...], (((0,), (0,)), ((), ())), preferred_element_type=F32
            ).astype(BF)

    stage[0] = flat_ref[...]
    here = hidden_ref.shape[1]

    def token_gradient(side, to):
        for seq in range(hidden_ref.shape[0]):
            rows = pl.ds(pl.multiple_of(seq * place.length + side * here, here), here)
            for cut in range(w_ref.shape[0] // 256):
                cols = slice(256 * cut, 256 * cut + 256)
                dg = dot_nt(ge_ref[rows], w_ref[cols])
                to[seq, :, cols] = dg.astype(BF)
                stage[0, 5:6, cols] += jnp.sum(dg * tok_ref[rows, cols].astype(F32), axis=0, keepdims=True)

    far = [(n, j) for j in range(1, second) for n in range(first)]
    near = [(n, 0) for n in range(first)]
    for k, (n, j) in enumerate(far + near[:1]):
        terms(scatter.terms(n, j))
        scatter.give(n, j)
        if 1 <= k <= len(far):
            scatter.cross_over(*far[k - 1])
    if place.pair:
        loads[0].wait()
        for load in loads[1:]:
            load.start()
        token_gradient(1 - me, dg_send)
        send(dg_send, dg_buf, dg_sem.at[0], dg_sem.at[1], index, 1 - me)
    for n, j in near[1:]:
        terms(scatter.terms(n, j))
        scatter.give(n, j)
    scatter.chain(acc, range(1))
    if place.pair:
        token_gradient(me, dg_ref)

    z_flat[a] = stage[0]
    for i in range(1, first):
        send(
            stage.at[0], z_flat.at[a], flat_send.at[second + i], flat_recv.at[2 + second + a],
            spot.at(spot.around(i), b, c),
        )
    scatter.chain(acc, range(1, min(2, first)))
    for i in range(1, first):
        spot.arrived(z_flat.at[spot.around(i)], flat_recv.at[2 + second + spot.around(i)])
    total = z_flat[0]
    for i in range(1, first):
        total = total + z_flat[i]
    stage[1] = total
    x_flat[b] = total
    for j in range(1, second):
        send(stage.at[1], x_flat.at[b], flat_send.at[1 + j], flat_recv.at[2 + b], spot.at(a, spot.aside(j), c))
    scatter.chain(acc, range(2, first))
    for j in range(1, second):
        spot.arrived(x_flat.at[spot.aside(j)], flat_recv.at[2 + spot.aside(j)])
    total = x_flat[0]
    for j in range(1, second):
        total = total + x_flat[j]
    stage[2] = total
    send(stage.at[2], core_flat, flat_send.at[1], flat_recv.at[1], spot.sibling)

    if place.pair:
        for load in loads[1:]:
            load.wait()
        spot.arrived(dg_buf, dg_sem.at[1])
        size = 128

        def token_rows(step, carry):
            seq, cut = lax.div(step, here // size), lax.rem(step, here // size)
            mine = pl.ds(pl.multiple_of(cut * size, size), size)
            full = pl.ds(pl.multiple_of(me * here + cut * size, size), size)
            hid = hidden_ref[seq, mine].astype(F32)
            inv = lax.rsqrt(jnp.mean(hid * hid, axis=-1, keepdims=True) + epsilon)
            gain = (dg_ref[seq, mine].astype(F32) + dg_buf[seq, mine].astype(F32)) * gain_ref[...]
            pull = inv * inv * inv * jnp.mean(hid * gain, axis=-1, keepdims=True)
            gh_ref[seq, mine] = (cot_ref[seq, mine].astype(F32) + inv * gain - hid * pull).astype(BF)
            rms = compact([back_ref[seq, :, full]])[:, 0:1]
            mixed = keep_ref[seq, mine].astype(F32) + away_ref[seq, mine].astype(F32)
            output_ref[seq, mine] = (hid + rms * mixed).astype(BF)
            return carry

        lax.fori_loop(0, hidden_ref.shape[0] * (here // size), token_rows, 0)
    else:
        gh_ref[...] = jnp.zeros_like(gh_ref)
        output_ref[...] = jnp.zeros_like(output_ref)

    spot.arrived(core_flat, flat_recv.at[1])
    total = stage[2] + core_flat[...]
    sum_ref[...] = total
    if place.pair:
        stage[3, 0:8] = total[0:8]
        send(stage.at[3, 0:8], y_flat, flat_send.at[0], flat_recv.at[0], index, 1 - me)
    scatter.finish_chain()
    if place.pair:
        edge = own_ref.shape[1] - 128 - 2 * STATE
        bc_send[...] = own_ref[:, edge : edge + 2 * STATE]
        send(bc_send, bc_buf, dg_sem.at[2], dg_sem.at[3], index, 1 - me)
    scatter.wait_sends()
    if place.pair:
        spot.arrived(y_flat, flat_recv.at[0])
        sum_ref[0:8] = stage[3, 0:8] + y_flat[...]
        spot.arrived(bc_buf, dg_sem.at[3])
        own_ref[:, edge : edge + 2 * STATE] = bc_send[...] + bc_buf[...]
    for copy in started:
        copy.wait_send()


def last_kernel(
    heads, own_ref, sum_ref, gh_in, output_in, out_rows, gain_ref,
    output_ref, gh_ref, pre_ref, zx_ref, bc_ref, step_ref, cxw_ref, cxb_ref, cbw_ref, cbb_ref, bias_ref, decay_ref,
    skip_ref, ngain_ref, out_ref,
):
    inner = heads * HEADDIM
    wide = 2 * inner
    rows = own_ref.shape[0]
    output_ref[...] = output_in[...]
    gh_ref[...] = gh_in[...]
    pre_ref[...] = sum_ref[5:6] / gain_ref[...]
    zx_ref[...] = own_ref[:, 0:wide]
    bc_ref[...] = own_ref[:, wide : wide + 2 * STATE]
    steps = own_ref[:, wide + 2 * STATE :]
    if rows < 128:
        steps = jnp.concatenate([steps, jnp.zeros((128 - rows, 128), F32)], axis=0)
    step_ref[...] = steps.T[0:heads, 0:rows]
    cxw_ref[...] = sum_ref[8 : 8 + TAPS, 0:inner]
    cxb_ref[...] = sum_ref[8 + TAPS : 9 + TAPS, 0:inner]
    cbw_ref[...] = sum_ref[0:TAPS, 0 : 2 * STATE]
    cbb_ref[...] = sum_ref[TAPS : TAPS + 1, 0 : 2 * STATE]
    skip = exact_dot(jnp.broadcast_to(sum_ref[13:14, 0:inner], (16, inner)), collector(inner, 0))
    bias_ref[...] = sum_ref[15:16, 0:heads]
    decay_ref[...] = sum_ref[15:16, 128 : 128 + heads]
    skip_ref[...] = skip[0:1, 0:heads]
    ngain_ref[...] = sum_ref[14:15, 0:inner]
    out_ref[...] = out_rows[...]


SDS = jax.ShapeDtypeStruct
DMA = pltpu.SemaphoreType.DMA
ANY = pl.BlockSpec(memory_space=pl.ANY)
WHOLE = pl.BlockSpec(memory_space=pltpu.VMEM)


def params(collective=None):
    if collective is None:
        return pltpu.CompilerParams(vmem_limit_bytes=VMEM_LIMIT)
    return pltpu.CompilerParams(vmem_limit_bytes=VMEM_LIMIT, collective_id=collective, has_side_effects=True)


def whole_once(*shape):
    return pl.BlockSpec(shape, lambda s, c: (0,) * len(shape), pipeline_mode=pl.Buffered(1))


def line_sems(place, cuts, lines):
    columns = place.first * max(place.second - 1, 1) * cuts
    blocks = place.first * place.second * cuts
    return [DMA((blocks,)), DMA((blocks,)), DMA((columns,)), DMA((columns,)), DMA((place.first * cuts,)), DMA((lines,))]


def gather_all(place, size, zx, bc, step_t, hidden, gain, cxw, cxb, cbw, cbb, bias, decay, skip, ngain, seg, pad):
    seqs, here, width = hidden.shape
    heads, inner = bias.shape[1], cxw.shape[1]
    total = 2 * inner + 2 * STATE + 128
    rows = zx.shape[0]
    return pl.pallas_call(
        functools.partial(gather_kernel, place, heads),
        in_specs=[WHOLE] * 15,
        out_specs=[ANY, ANY] + [WHOLE] * 4,
        out_shape=[
            SDS((size * rows, total), BF), SDS((seqs, place.length if place.pair else here, width), BF),
            SDS((seqs, AUX, place.length), F32), SDS((8, inner), F32), SDS((8, 2 * STATE), F32), SDS((2, heads, 128), F32),
        ],
        scratch_shapes=[
            pltpu.VMEM((rows, total), BF), pltpu.VMEM(hidden.shape, BF), pltpu.VMEM((128, 128), F32),
            DMA((PIECES, 1, gather_sites(place.first, place.second))), DMA((PIECES, 1, size)), DMA((PIECES, 1)),
            DMA((1, row_sites(place.first, place.second))), DMA((1, size)), DMA((1,)), DMA((3,)),
        ],
        compiler_params=params(0),
        name="gather_all",
    )(zx, bc, step_t, hidden, gain, cxw, cxb, cbw, cbb, bias, decay, skip, ngain, seg, pad)


def mixer_forward(place, size, tok, weights, aux, cw, cbw, hp, cot_own, out_own):
    seqs, length, width = tok.shape
    heads, inner = hp.shape[1], cw.shape[1]
    wide = 2 * inner + 2 * STATE
    chunks = length // CHUNK
    token = lambda size: pl.BlockSpec((1, BLOCK, size), lambda s, c: (s, c, 0))
    row = lambda high: pl.BlockSpec((1, high, BLOCK), lambda s, c: (s, 0, c))
    return pl.pallas_call(
        functools.partial(forward_kernel, place, heads),
        grid=(seqs, length // BLOCK),
        in_specs=[
            token(width), whole_once(*weights.shape), row(AUX),
            whole_once(8, inner), whole_once(8, 2 * STATE), whole_once(2, heads, 128), WHOLE, ANY,
        ],
        out_specs=[
            token(wide), row(heads), token(inner), token(inner), token(inner), token(inner), token(2 * STATE),
            token(2 * STATE), pl.BlockSpec((1, BLOCK // CHUNK, STATE, inner), lambda s, c: (s, c, 0, 0)), row(8),
            ANY, ANY,
        ],
        out_shape=[
            SDS((seqs, length, wide), BF), SDS((seqs, heads, length), F32),
            SDS((seqs, length, inner), BF), SDS((seqs, length, inner), BF), SDS((seqs, length, inner), BF),
            SDS((seqs, length, inner), BF), SDS((seqs, length, 2 * STATE), BF), SDS((seqs, length, 2 * STATE), BF),
            SDS((seqs, chunks, STATE, inner), BF), SDS((seqs, 8, length), F32),
            SDS((size * out_own.shape[0], inner), BF), SDS((seqs, length, width) if place.pair else (8, 128), BF),
        ],
        scratch_shapes=[
            pltpu.VMEM((STATE, inner), F32), pltpu.VMEM((HALO + CHUNK, inner), F32),
            pltpu.VMEM((HALO + CHUNK, 2 * STATE), F32), pltpu.VMEM((CHUNK, inner), BF),
            pltpu.VMEM((CHUNK, inner), F32), pltpu.VMEM((3, 256, inner), BF), pltpu.VMEM((CHUNK, CHUNK), BF),
            DMA((1, gather_sites(place.first, place.second))), DMA((1, size)), DMA((1,)), DMA((3,)),
        ],
        compiler_params=params(1),
        name="mixer_forward",
    )(tok, weights, aux, cw, cbw, hp, cot_own, out_own)


def mixer_backward(
    place, size, inner_all, pz, raw, aux, mixed, cv, pre, cbc, pbc, st, stat, cw, cbw, hp, g, out_all, gn, cot
):
    seqs, length, inner = mixed.shape
    width, wide = out_all.shape[0], pz.shape[2] + 128
    heads = hp.shape[1]
    last = length // BLOCK - 1
    pair = place.pair
    here = length // 2 if pair else 16
    rows = width // size
    tokens = seqs * length
    token = lambda size: pl.BlockSpec((1, BLOCK, size), lambda s, c: (s, last - c, 0))
    row = lambda high: pl.BlockSpec((1, high, BLOCK), lambda s, c: (s, 0, last - c))
    fixed = lambda *shape: pl.BlockSpec(shape, lambda s, c: (0,) * len(shape))
    if pair:
        g = cbw
        gn_all, cot_all = gn.reshape(-1, inner), cot.reshape(-1, width)
    else:
        gn_all, cot_all, out_all = gn[0, :16, :128], cot[0, :16, :128], out_all[:16, :128]
    blocks = place.first * place.second
    columns = place.first * max(place.second - 1, 1)
    tile = lambda *shape: pltpu.VMEM(shape if pair else (1,) * (len(shape) - 2) + (16, 128), BF)
    rowed = pltpu.VMEM((seqs, 8, length), F32)
    return pl.pallas_call(
        functools.partial(backward_kernel, place, heads, inner_all),
        grid=(seqs, length // BLOCK),
        in_specs=[
            token(pz.shape[2]), row(heads), row(AUX), token(inner), token(inner),
            token(inner), token(2 * STATE), token(2 * STATE),
            pl.BlockSpec((1, BLOCK // CHUNK, STATE, inner), lambda s, c: (s, last - c, 0, 0)), whole_once(*stat.shape),
            whole_once(8, inner), whole_once(8, 2 * STATE), whole_once(2, heads, 128),
            whole_once(*g.shape) if pair else token(inner),
            whole_once(*out_all.shape), whole_once(*gn_all.shape), whole_once(*cot_all.shape),
        ],
        out_specs=[token(wide), fixed(16, width), ANY, ANY, fixed(seqs, 8, length), fixed(rows, inner)],
        out_shape=[
            SDS((seqs, length, wide), BF), SDS((16, width), F32), SDS((seqs, here, width), BF),
            SDS((seqs, here, width), BF), SDS((seqs, 8, length), F32), SDS((rows, inner), F32),
        ],
        scratch_shapes=[
            pltpu.VMEM((STATE, inner), F32), pltpu.VMEM((CHUNK + HALO, inner), F32),
            pltpu.VMEM((CHUNK + HALO, 2 * STATE), F32), pltpu.VMEM((CHUNK, inner), BF),
            pltpu.VMEM((CHUNK, inner), BF), pltpu.VMEM((CHUNK, inner), BF), pltpu.VMEM((CHUNK, inner), BF),
            pltpu.VMEM((CHUNK, inner), F32),
            pltpu.VMEM((3, 256, inner), BF), pltpu.VMEM((2, inner, 128), BF),
            pltpu.VMEM((CHUNK, CHUNK), BF), pltpu.VMEM((CHUNK, CHUNK), BF), pltpu.VMEM((2, heads, 128), F32),
            tile(seqs, length, width), tile(tokens, inner), pltpu.VMEM((tokens, 128), F32), rowed, rowed,
            tile(tokens, inner), tile(width, inner),
            tile(blocks, rows, inner), tile(columns, rows, inner), tile(place.first, rows, inner),
        ] + line_sems(place, 1, place.first) + [DMA((3,)), DMA((2,))],
        compiler_params=params(3 if pair else None),
        name="mixer_backward",
    )(
        pz, raw, aux, mixed, cv, pre, cbc, pbc, st, stat, cw, cbw, hp, g, out_all, gn_all, cot_all,
    )


def reduce_all(place, size, tok, ge, flat, gain, back, weights, hidden, cot_own, y_keep, y_away):
    seqs, length, depth = tok.shape
    width = ge.shape[2]
    rows = depth // size
    pair = place.pair
    if pair:
        tok, ge = tok.reshape(seqs * length, depth), ge.reshape(seqs * length, width)
    else:
        ge = jnp.einsum("stp,sty->py", tok, ge, preferred_element_type=F32).astype(BF)
        tok, weights = tok[0, :16], weights[:16, :128]
        flat = jnp.concatenate([lax.psum(flat[:8], "tensor"), flat[8:]])
        hidden, cot_own, y_keep, y_away = [jnp.zeros((1, 16, depth), BF)] * 4
        back = back[:1, :, :128]
    blocks = place.first * place.second * PIECES
    columns = place.first * max(place.second - 1, 1) * PIECES
    lines = 2 * place.first * PIECES
    cut = rows // PIECES
    tokens = pltpu.VMEM(hidden.shape, BF)
    small = pltpu.VMEM((rows, 2 * STATE), F32)
    own, flat, gh, output = pl.pallas_call(
        functools.partial(reduce_kernel, place),
        in_specs=[WHOLE] * 5 + [ANY] * 5,
        out_specs=[WHOLE] * 4,
        out_shape=[SDS((rows, width), F32), SDS(flat.shape, F32), SDS(hidden.shape, BF), SDS(hidden.shape, BF)],
        scratch_shapes=[
            pltpu.VMEM(weights.shape, BF), tokens, tokens, tokens, tokens, tokens, tokens, tokens,
            pltpu.VMEM((depth, width) if pair else (16, 128), BF),
            pltpu.VMEM((blocks, cut, width), BF),
            pltpu.VMEM((columns, cut, width), BF),
            pltpu.VMEM((lines, cut, width), BF),
            pltpu.VMEM((cut, width), F32),
            small, small,
            pltpu.VMEM((8, flat.shape[1]), F32),
            pltpu.VMEM(flat.shape, F32),
            pltpu.VMEM((place.second,) + flat.shape, F32),
            pltpu.VMEM((place.first,) + flat.shape, F32),
            pltpu.VMEM((4,) + flat.shape, F32),
        ] + line_sems(place, PIECES, lines) + [
            DMA((1 + place.first + place.second,)), DMA((2 + place.first + place.second,)), DMA((4,)), DMA((5,)),
        ],
        compiler_params=params(4),
        name="reduce_all",
    )(tok, ge, flat, gain, back, weights, hidden, cot_own, y_keep, y_away)
    if not pair:
        edge = width - 128 - 2 * STATE
        own = own.at[:, edge : edge + 2 * STATE].set(lax.psum(own[:, edge : edge + 2 * STATE], "tensor"))
    return own, flat, gh, output


def body(
    hidden, pre_gain, zx_weight, bc_weight, step_weight, conv_x_weight, conv_x_bias, conv_bc_weight, conv_bc_bias,
    step_bias, decay_log, skip_gain, norm_gain, out_weight, segment_ids, pad_mask, grad_out,
):
    n, size = lax.axis_size("tensor"), lax.axis_size("dp")
    heads = step_weight.shape[1]
    inner = heads * HEADDIM
    seqs, here, width = hidden.shape
    length = segment_ids.shape[1]
    first, second = factors(size)
    place = Place(first, second, n == 2 and (2 * width // size) % 128 == 0, seqs * length // BLOCK, length)
    line = lambda vector: vector.reshape(1, -1)
    gain = line(pre_gain)

    weights, tok, aux, cw, cbw, hp = gather_all(
        place, size, zx_weight, bc_weight, step_weight.T, hidden, gain, conv_x_weight, line(conv_x_bias),
        conv_bc_weight, line(conv_bc_bias), line(step_bias), line(decay_log), line(skip_gain), line(norm_gain),
        segment_ids, pad_mask,
    )
    if not place.pair:
        tok = lax.all_gather(tok, "tensor", axis=1, tiled=True)
    pz, raw, mixed, gn, cv, pre, cbc, pbc, st, stat, out_all, cot = mixer_forward(
        place, size, tok, weights, aux, cw, cbw, hp, grad_out, out_weight.T
    )
    if not place.pair:
        cot = lax.all_gather(grad_out, "tensor", axis=1, tiled=True)
    g = y = None
    if not place.pair:
        y = jnp.einsum("stc,rc->str", gn, out_all, preferred_element_type=F32)
        cross = jnp.sum(y * cot.astype(F32), axis=-1)
        stat = finish_sums(lax.psum(stat.at[:, 1].set(cross), "tensor"), inner * n)
        g = jnp.einsum("str,rc->stc", cot, out_all, preferred_element_type=F32).astype(BF)
    ge, flat, y_keep, y_away, back, out_rows = mixer_backward(
        place, size, inner * n, pz, raw, aux, mixed, cv, pre, cbc, pbc, st, stat, cw, cbw, hp, g, out_all, gn, cot
    )
    if not place.pair:
        normed_out = (gn.astype(F32) * back[:, 0, :, None]).astype(BF)
        terms = jnp.einsum("str,stc->rc", cot, normed_out, preferred_element_type=F32).astype(BF)
        out_rows = lax.psum_scatter(terms, "dp", scatter_dimension=0, tiled=True).astype(F32)
        dg = jnp.einsum("sty,py->stp", ge, weights, preferred_element_type=F32)
        flat = flat.at[5].add(jnp.sum(dg * tok.astype(F32), axis=(0, 1)))
    own, sums, grad_hidden, output = reduce_all(
        place, size, tok, ge, flat, gain, back, weights, hidden, grad_out, y_keep, y_away
    )
    if not place.pair:
        hidden_f = hidden.astype(F32)
        inv_rms = lax.rsqrt(jnp.mean(hidden_f * hidden_f, axis=-1, keepdims=True) + epsilon)
        scatter = lambda rows: lax.psum_scatter(rows, "tensor", scatter_dimension=1, tiled=True)
        gain_grad = scatter(dg) * pre_gain
        pull = inv_rms**3 * jnp.mean(hidden_f * gain_grad, axis=-1, keepdims=True)
        grad_hidden = (grad_out.astype(F32) + inv_rms * gain_grad - hidden_f * pull).astype(BF)
        output = (hidden_f + scatter(y * back[:, 0, :, None])).astype(BF)
    rows = own.shape[0]
    output, grad_hidden, grad_pre, gzx, gbc, gstep, gcxw, gcxb, gcbw, gcbb, gbias, gdecay, gskip, gnorm, gout = pl.pallas_call(
        functools.partial(last_kernel, heads),
        in_specs=[WHOLE] * 6,
        out_specs=[WHOLE] * 15,
        out_shape=[
            SDS(hidden.shape, BF), SDS(hidden.shape, BF), SDS((1, width), F32), SDS((rows, 2 * inner), F32),
            SDS((rows, 2 * STATE), F32), SDS((heads, rows), F32), SDS((TAPS, inner), F32), SDS((1, inner), F32),
            SDS((TAPS, 2 * STATE), F32), SDS((1, 2 * STATE), F32), SDS((1, heads), F32), SDS((1, heads), F32),
            SDS((1, heads), F32), SDS((1, inner), F32), SDS((rows, inner), F32),
        ],
        compiler_params=params(),
        name="outputs",
    )(own, sums, grad_hidden, output, out_rows, gain)
    return (
        output, grad_hidden, grad_pre[0], gzx, gbc, gstep.T, gcxw, gcxb[0], gcbw, gcbb[0], gbias[0], gdecay[0],
        gskip[0], gnorm[0], gout.T,
    )


def solution(mesh):
    placed = (
        P("dp", "tensor", None), P(), P("dp", "tensor"), P("dp", None), P("dp", "tensor"), P(None, "tensor"),
        P("tensor"), P(), P(), P("tensor"), P("tensor"), P("tensor"), P("tensor"), P("tensor", "dp"),
        P("dp", None), P("dp", None), P("dp", "tensor", None),
    )
    return jax.shard_map(
        body,
        mesh=mesh,
        in_specs=placed,
        out_specs=(
            P("dp", "tensor", None), P("dp", "tensor", None), P(), P("dp", "tensor"), P("dp", None), P("dp", "tensor"),
            P(None, "tensor"), P("tensor"), P(), P(), P("tensor"), P("tensor"), P("tensor"), P("tensor"),
            P("tensor", "dp"),
        ),
        check_vma=False,
    )
```

```python
import collections
import functools
import jax
import jax.numpy as jnp
from jax import lax
from jax.experimental import pallas as pl
from jax.experimental.pallas import tpu as pltpu
from jax.sharding import PartitionSpec as P

HEADDIM = 64
STATE = 128
CHUNK = 128
TAPS = 4
HALO = 8
AUX = 16
LOG2E = 1.4426950408889634
FAR = -1e30
BLOCK = 256
VMEM_LIMIT = 58 * 1024 * 1024
MESH = pl.DeviceIdType.MESH
PIECES = 2
epsilon = 1e-05
BF = jnp.bfloat16
F32 = jnp.float32


def sigmoid(v):
    return 0.5 * jnp.tanh(0.5 * v) + 0.5


def split3(v):
    a = v.astype(BF)
    r = v - a.astype(F32)
    b = r.astype(BF)
    c = (r - b.astype(F32)).astype(BF)
    return a, b, c


def dot_nn(a, b):
    return lax.dot_general(a, b, (((1,), (0,)), ((), ())), preferred_element_type=F32)


def dot_nt(a, b):
    return lax.dot_general(a, b, (((1,), (1,)), ((), ())), preferred_element_type=F32)


def exact_dot(v, ones):
    rows = v.shape[0]
    out = dot_nn(jnp.concatenate(split3(v), axis=0), ones)
    return out[:rows] + out[rows : 2 * rows] + out[2 * rows :]


def iota2(shape, dim):
    return lax.broadcasted_iota(jnp.int32, shape, dim)


def pieces(raw, bias, rate, aux, tri):
    pad = aux[1:2]
    pre = raw + bias
    soft = jnp.maximum(pre, 0.0) + jnp.log1p(jnp.exp(-jnp.abs(pre)))
    dt = soft * pad
    cum = exact_dot(dt * rate, tri) * LOG2E
    carried = jnp.exp2(cum) * aux[5:6]
    toward = jnp.exp2(cum[:, CHUNK - 1 : CHUNK] - cum) * aux[6:7]
    return dt, cum, carried, toward


def expander(heads, inner, place):
    row = lax.rem(iota2((256, inner), 0), 128)
    head = lax.div(iota2((256, inner), 1), HEADDIM)
    return jnp.where(row == head + place, 1.0, 0.0).astype(BF)


def collector(inner, place):
    head = lax.div(iota2((inner, 128), 0), HEADDIM)
    lane = iota2((inner, 128), 1)
    return jnp.where(lane == head + place, 1.0, 0.0).astype(BF)


def hi_lo(cols):
    hi = cols.astype(BF)
    return jnp.concatenate([hi, (cols - hi.astype(F32)).astype(BF)], axis=1)


def compact(rows_list):
    used = sum(r.shape[0] for r in rows_list)
    if used < 128:
        rows_list = list(rows_list) + [jnp.zeros((128 - used, CHUNK), F32)]
    return jnp.concatenate(rows_list, axis=0).T


def split_pair(first, second, low):
    gate = jnp.where(low, first, pltpu.roll(second, HEADDIM, 1))
    value = jnp.where(low, pltpu.roll(first, HEADDIM, 1), second)
    return gate, value


Place = collections.namedtuple("Place", ("first", "second", "pair", "steps", "length"))


def factors(size):
    first = 4 if size % 8 == 0 else 1
    return first, size // (2 * first)


class Spot:
    def __init__(self, place):
        self.first, self.second = place.first, place.second
        self.index = lax.axis_index("dp")
        self.me = lax.axis_index("tensor")
        self.a = lax.div(self.index, 2 * self.second)
        self.b = lax.rem(lax.div(self.index, 2), self.second)
        self.c = lax.rem(self.index, 2)

    def at(self, i, j, k):
        return (i * self.second + j) * 2 + k

    def around(self, i):
        return lax.rem(self.a + i, self.first)

    def aside(self, j):
        return lax.rem(self.b + j, self.second)

    @property
    def sibling(self):
        return self.at(self.a, self.b, 1 - self.c)

    def greet(self, pair):
        barrier = pltpu.get_barrier_semaphore()
        peers = [(self.sibling, self.me)]
        peers += [(self.at(self.a, self.aside(j), self.c), self.me) for j in range(1, self.second)]
        peers += [(self.at(self.around(i), self.b, self.c), self.me) for i in range(1, self.first)]
        if pair:
            peers.append((self.index, 1 - self.me))
        for peer in peers:
            pl.semaphore_signal(barrier, inc=1, device_id=peer, device_id_type=MESH)
        pl.semaphore_wait(barrier, len(peers))

    def copy(self, src, dst, ss, rs, target, tensor=None):
        return pltpu.make_async_remote_copy(
            src_ref=src, dst_ref=dst, send_sem=ss, recv_sem=rs,
            device_id=(target, self.me if tensor is None else tensor), device_id_type=MESH,
        )

    def arrived(self, dst, rs):
        self.copy(dst, dst, rs, rs, self.sibling).wait_recv()


def when(valid, run):
    def quiet():
        run()

    quiet() if valid is None else pl.when(valid)(quiet)


def gather_sites(first, second):
    return (2 + second) + (first - 1) * 2 * (1 + second) + (2 * first - 1) * (second - 1)


def row_sites(first, second):
    return (2 + second) + 3 * (second - 1) + (first - 1) * 4 * second


class LineGather:
    def __init__(self, spot, arrays, send_sem, recv_sem, local_sem, columns=None, part=0, parts=1):
        self.spot, self.arrays, self.columns = spot, arrays, columns
        self.part, self.parts = part, parts
        self.send_sem, self.recv_sem, self.local_sem = send_sem, recv_sem, local_sem
        self.sites = []

    def rows(self, which, shard):
        own, full = self.arrays[which]
        rows = own.shape[0]
        there = pl.ds(pl.multiple_of((shard * self.parts + self.part) * rows, rows), rows)
        return full.at[there] if self.columns is None else full.at[there, self.columns]

    def copies(self, site, shard, target, mine=False):
        return [
            self.spot.copy(
                own if mine else self.rows(w, shard), self.rows(w, shard),
                self.send_sem.at[w, site], self.recv_sem.at[w, shard], target,
            )
            for w, (own, full) in enumerate(self.arrays)
        ]

    def send(self, valid, shard, target, mine=False):
        site = len(self.sites)
        self.sites.append((valid, shard, target, mine))
        when(valid and valid(), lambda: [copy.start() for copy in self.copies(site, shard(), target(), mine)])

    def arrive(self, valid, shard):
        def wait():
            for w in range(len(self.arrays)):
                self.spot.arrived(self.rows(w, shard), self.recv_sem.at[w, shard])

        when(valid, wait)

    def local(self):
        return [
            pltpu.make_async_copy(own, self.rows(w, self.spot.index), self.local_sem.at[w])
            for w, (own, full) in enumerate(self.arrays)
        ]

    def begin(self):
        s = self.spot
        self.send(lambda: s.a < s.first - 1, lambda: s.index, lambda: s.at(s.a + 1, s.b, s.c), True)
        self.send(lambda: s.a > 0, lambda: s.index, lambda: s.at(s.a - 1, s.b, s.c), True)
        for j in range(1, s.second):
            self.send(None, lambda: s.index, lambda j=j: s.at(s.a, s.aside(j), s.c), True)
        self.send(None, lambda: s.index, lambda: s.sibling, True)
        for copy in self.local():
            copy.start()

    def sides(self, hop):
        s = self.spot
        if hop == 0:
            return [(None, lambda: s.a, None, None)]
        return [
            (lambda: s.a - hop >= 0, lambda: s.a - hop, lambda: s.a < s.first - 1, lambda: s.at(s.a + 1, s.b, s.c)),
            (lambda: s.a + hop < s.first, lambda: s.a + hop, lambda: s.a > 0, lambda: s.at(s.a - 1, s.b, s.c)),
        ]

    def along(self, hop):
        s = self.spot
        for valid, origin, onward, target in self.sides(hop):
            shard = lambda origin=origin: s.at(origin(), s.b, s.c)
            self.arrive(valid(), shard())
            self.send(lambda valid=valid, onward=onward: valid() & onward(), shard, target)
            for j in range(1, s.second):
                self.send(valid, shard, lambda j=j: s.at(s.a, s.aside(j), s.c))
            self.send(valid, shard, lambda: s.sibling)

    def across(self, hop):
        s = self.spot
        for j in range(1, s.second):
            for valid, origin, onward, target in self.sides(hop):
                shard = lambda origin=origin, j=j: s.at(origin(), s.aside(j), s.c)
                self.arrive(valid and valid(), shard())
                self.send(valid, shard, lambda: s.sibling)

    def finish(self):
        s = self.spot
        for i in range(s.first):
            for j in range(s.second):
                self.arrive(None, s.at(i, j, 1 - s.c))
        for site, (valid, shard, target, mine) in enumerate(self.sites):
            when(
                valid and valid(),
                lambda site=site, shard=shard, target=target, mine=mine: [
                    copy.wait_send() for copy in self.copies(site, shard(), target(), mine)
                ],
            )
        for copy in self.local():
            copy.wait()


class RowGather(LineGather):
    def cross(self):
        s = self.spot
        for j in range(1, s.second):
            shard = lambda j=j: s.at(s.a, s.aside(j), s.c)
            self.arrive(None, shard())
            self.send(lambda: s.a < s.first - 1, shard, lambda: s.at(s.a + 1, s.b, s.c))
            self.send(lambda: s.a > 0, shard, lambda: s.at(s.a - 1, s.b, s.c))
            self.send(None, shard, lambda: s.sibling)

    def along(self, hop):
        s = self.spot
        for j in range(s.second):
            for valid, origin, onward, target in self.sides(hop):
                shard = lambda origin=origin, j=j: s.at(origin(), s.aside(j), s.c)
                self.arrive(valid(), shard())
                self.send(lambda valid=valid, onward=onward: valid() & onward(), shard, target)
                self.send(valid, shard, lambda: s.sibling)


class TokenSwap:
    def __init__(self, spot, own, full, sem):
        self.spot, self.own, self.full, self.sem = spot, own, full, sem

    def target(self):
        here = self.own.shape[1]
        return self.full.at[:, pl.ds(pl.multiple_of(self.spot.me * here, here), here)]

    def remote(self):
        s = self.spot
        return s.copy(self.own, self.target(), self.sem.at[0], self.sem.at[1], s.index, 1 - s.me)

    def local(self):
        return pltpu.make_async_copy(self.own, self.target(), self.sem.at[2])

    def begin(self):
        self.remote().start()
        self.local().start()

    def finish(self):
        self.remote().wait()
        self.local().wait()


class HalfSwap:
    def __init__(self, spot, whole, away, sem):
        self.spot, self.whole, self.away, self.sem = spot, whole, away, sem

    def remote(self):
        s = self.spot
        here = self.away.shape[1]
        rows = self.whole.at[:, pl.ds(pl.multiple_of((1 - s.me) * here, here), here)]
        return s.copy(rows, self.away, self.sem.at[0], self.sem.at[1], s.index, 1 - s.me)

    def begin(self):
        self.remote().start()

    def finish(self):
        self.remote().wait()


class LineScatter:
    def __init__(
        self, spot, part, core_buf, x_buf, z_buf, out, core_send, core_recv, x_send, x_recv, z_send, z_recv, cuts=1
    ):
        self.spot, self.part, self.out, self.cuts = spot, part, out, cuts
        self.core_buf, self.x_buf, self.z_buf = core_buf, x_buf, z_buf
        self.sems = (core_send, core_recv, x_send, x_recv, z_send, z_recv)
        self.rows = out.shape[0] // cuts
        self.copies = []
        a = spot.a
        if spot.first == 4:
            near = jnp.minimum(a, 3 - a)
            self.order = [jnp.where(a < 2, d, 3 - d) for d in (3 + 0 * a, 2 - 2 * near, 1 + near)] + [a]
        else:
            self.order = [a]

    def block(self, i, j, k, q):
        rows = self.rows
        return self.part.at[pl.ds(pl.multiple_of((self.spot.at(i, j, k) * self.cuts + q) * rows, rows), rows)]

    def slot(self, i, j, q):
        return (i * self.spot.second + j) * self.cuts + q

    def start(self, make):
        make().start()
        self.copies.append(make)

    def give(self, n, j):
        s, i = self.spot, self.order[n]
        for q in range(self.cuts):

            def make(q=q):
                t = self.slot(i, s.aside(j), q)
                return s.copy(
                    self.block(i, s.aside(j), 1 - s.c, q), self.core_buf.at[t], self.sems[0].at[t],
                    self.sems[1].at[t], s.sibling,
                )

            self.start(make)

    def terms(self, n, j):
        rows = 2 * self.rows * self.cuts
        first_row = self.spot.at(self.order[n], self.spot.aside(j), 0) * self.rows * self.cuts
        return pl.ds(pl.multiple_of(first_row, rows), rows)

    def cross_over(self, n, j):
        s, i = self.spot, self.order[n]
        for q in range(self.cuts):
            t = self.slot(i, s.aside(j), q)
            s.arrived(self.core_buf.at[t], self.sems[1].at[t])
            own = self.block(i, s.aside(j), s.c, q)[...].astype(F32)
            self.core_buf[t] = (own + self.core_buf[t].astype(F32)).astype(BF)

            def make(q=q):
                t = self.slot(i, s.aside(j), q)
                there = (i * (s.second - 1) + s.second - j - 1) * self.cuts + q
                here = (i * (s.second - 1) + j - 1) * self.cuts + q
                return s.copy(
                    self.core_buf.at[t], self.x_buf.at[there], self.sems[2].at[here], self.sems[3].at[there],
                    s.at(s.a, s.aside(j), s.c),
                )

            self.start(make)

    def column_sum(self, n, q):
        s, i = self.spot, self.order[n]
        t = self.slot(i, s.b, q)
        s.arrived(self.core_buf.at[t], self.sems[1].at[t])
        total = self.block(i, s.b, s.c, q)[...].astype(F32) + self.core_buf[t].astype(F32)
        for j in range(1, s.second):
            u = (i * (s.second - 1) + j - 1) * self.cuts + q
            s.arrived(self.x_buf.at[u], self.sems[3].at[u])
            total = total + self.x_buf[u].astype(F32)
        return total

    def produce(self, make_terms, far):
        s = self.spot
        for j in range(1, s.second) if far else [0]:
            for n in range(s.first):
                make_terms(self.terms(n, j))
                self.give(n, j)

    def cross(self):
        for j in range(1, self.spot.second):
            for n in range(self.spot.first):
                self.cross_over(n, j)

    def along(self):
        s = self.spot
        for n in range(s.first):
            for q in range(self.cuts):
                total = self.column_sum(n, q)
                if n == s.first - 1:
                    self.out[q * self.rows : (q + 1) * self.rows] = total
                    continue
                self.core_buf[self.slot(self.order[n], s.b, q)] = total.astype(BF)

                def make(n=n, q=q):
                    z = s.a * self.cuts + q
                    return s.copy(
                        self.core_buf.at[self.slot(self.order[n], s.b, q)], self.z_buf.at[z],
                        self.sems[4].at[n * self.cuts + q], self.sems[5].at[z], s.at(self.order[n], s.b, s.c),
                    )

                self.start(make)

    def chain(self, acc, order):
        s = self.spot
        for n in order:
            for q in range(self.cuts):
                i = self.order[n]
                total = self.column_sum(n, q)
                if n == s.first - 1:
                    self.out[q * self.rows : (q + 1) * self.rows] = total
                    continue
                down = jnp.where(i > s.a, 0, 1)
                z = (down * s.first + i) * self.cuts + q
                acc[...] = total

                @pl.when(jnp.where(i > s.a, s.a, s.first - 1 - s.a) > 0)
                def _(z=z):
                    s.arrived(self.z_buf.at[z], self.sems[5].at[z])
                    acc[...] = acc[...] + self.z_buf[z].astype(F32)

                self.core_buf[self.slot(i, s.b, q)] = acc[...].astype(BF)

                def make(n=n, q=q, i=i, down=down, z=z):
                    return s.copy(
                        self.core_buf.at[self.slot(i, s.b, q)], self.z_buf.at[z],
                        self.sems[4].at[n * self.cuts + q], self.sems[5].at[z], s.at(s.a + 1 - 2 * down, s.b, s.c),
                    )

                self.start(make)

    def finish_chain(self):
        s = self.spot
        for q in range(self.cuts):
            cut = slice(q * self.rows, (q + 1) * self.rows)
            for down, there in ((0, s.a), (1, s.first - 1 - s.a)):
                z = (down * s.first + s.a) * self.cuts + q

                @pl.when(there > 0)
                def _(z=z, cut=cut):
                    s.arrived(self.z_buf.at[z], self.sems[5].at[z])
                    self.out[cut] = self.out[cut] + self.z_buf[z].astype(F32)

    def wait_sends(self):
        for make in self.copies:
            make().wait_send()

    def finish(self):
        s = self.spot
        for i in range(1, s.first):
            for q in range(self.cuts):
                z = s.around(i) * self.cuts + q
                s.arrived(self.z_buf.at[z], self.sems[5].at[z])
                cut = slice(q * self.rows, (q + 1) * self.rows)
                self.out[cut] = self.out[cut] + self.z_buf[z].astype(F32)
        self.wait_sends()


def forward_kernel(
    place, heads, tok_ref, w_hbm, aux_ref, cw_ref, cbw_ref, hp_ref, cot_own, out_own,
    pz_ref, raw_ref, mixed_ref, gated_ref, cv_ref, pre_ref, cbc_ref, pbc_ref, st_ref, stat_ref, out_all, cot_full,
    state, ubuf, bbuf, vd, yint, expand, tri_ref, w_ref, send_sem, recv_sem, local_sem, cot_sem, load_sem,
):
    inner = heads * HEADDIM
    pairs = heads // 2
    wide = 2 * inner
    now = pl.program_id(0) * pl.num_programs(1) + pl.program_id(1)
    last = place.steps - 1
    first = now == 0
    spot = Spot(place)
    gather = LineGather(spot, [(out_own, out_all)], send_sem, recv_sem, local_sem)
    swap = TokenSwap(spot, cot_own, cot_full, cot_sem) if place.pair else None

    @pl.when(first)
    def _():
        load = pltpu.make_async_copy(w_hbm, w_ref, load_sem)
        load.start()
        spot.greet(place.pair)
        gather.begin()
        if swap:
            swap.begin()
        load.wait()

    for hop in range(1, place.first):

        @pl.when(now == min(hop, last))
        def _(hop=hop):
            gather.along(hop)
            gather.across(hop - 1)

    @pl.when(first)
    def _():
        for i, place in enumerate((AUX + heads, AUX + 2 * heads, AUX + 3 * heads)):
            expand[i] = expander(heads, inner, place)
        tri_ref[...] = jnp.where(iota2((CHUNK, CHUNK), 0) <= iota2((CHUNK, CHUNK), 1), 1.0, 0.0).astype(BF)

    @pl.when(pl.program_id(1) == 0)
    def _():
        state[...] = jnp.zeros_like(state)
        ubuf[0:HALO] = jnp.zeros((HALO, inner), F32)
        bbuf[0:HALO] = jnp.zeros((HALO, 2 * STATE), F32)

    tok = tok_ref[0]
    side = dot_nn(tok, w_ref[:, wide:])
    raw_ref[0] = side[:, 2 * STATE :].T[0:heads]
    pz_ref[0, :, wide:] = side[:, : 2 * STATE].astype(BF)
    for p in range(pairs):
        pz_ref[0, :, 256 * p : 256 * p + 256] = dot_nn(tok, w_ref[:, 256 * p : 256 * p + 256]).astype(BF)

    def chunk_step(step, carry):
        here = pl.ds(pl.multiple_of(step * CHUNK, CHUNK), CHUNK)
        aux = aux_ref[0, :, here]
        raw = raw_ref[0, :, here]
        bc = pz_ref[0, here, wide:]
        dt, cum, carried, toward = pieces(raw, hp_ref[0], hp_ref[1], aux, tri_ref[...])
        cols = compact([aux, cum, dt, carried, toward])
        both = hi_lo(cols)
        dtx = dot_nn(both, expand[0])
        carx = dot_nn(both, expand[1])
        towx = dot_nn(both, expand[2])
        pad = cols[:, 1:2]
        same = [None] + [cols[:, 1 + k : 2 + k] for k in range(1, TAPS)]
        low = iota2((CHUNK, 128), 1) < HEADDIM

        bbuf[HALO:] = bc.astype(F32) * pad
        maps = cbw_ref[TAPS : TAPS + 1] + cbw_ref[0:1] * bbuf[HALO:]
        for k in range(1, TAPS):
            maps = maps + cbw_ref[k : k + 1] * (same[k] * bbuf[HALO - k : HALO - k + CHUNK])
        pbc_ref[0, here] = maps.astype(BF)
        maps = (maps * sigmoid(maps)).astype(BF)
        cbc_ref[0, here] = maps
        bbuf[0:HALO] = bbuf[CHUNK : CHUNK + HALO]
        keys, queries = maps[:, :STATE], maps[:, STATE:]
        scores = dot_nt(queries, keys)
        keys_t = keys.astype(F32).T.astype(BF)

        for p in range(pairs):
            s = slice(128 * p, 128 * p + 128)
            x0 = pz_ref[0, here, 256 * p : 256 * p + 128].astype(F32)
            x1 = pz_ref[0, here, 256 * p + 128 : 256 * p + 256].astype(F32)
            value = jnp.where(low, pltpu.roll(x0, HEADDIM, 1), x1)
            ubuf[HALO:, s] = value * pad
            pre = cw_ref[TAPS : TAPS + 1, s] + cw_ref[0:1, s] * ubuf[HALO:, s]
            for k in range(1, TAPS):
                pre = pre + cw_ref[k : k + 1, s] * (same[k] * ubuf[HALO - k : HALO - k + CHUNK, s])
            pre_ref[0, here, s] = pre.astype(BF)
            cv = (pre * sigmoid(pre)).astype(BF)
            cv_ref[0, here, s] = cv
            vd[:, s] = (cv.astype(F32) * dtx[:, s]).astype(BF)
        ubuf[0:HALO] = ubuf[CHUNK : CHUNK + HALO]

        old = state[...]
        old_b = old.astype(BF)
        st_ref[0, step] = old_b
        yint[...] = dot_nn(queries, old_b) * carx
        state[...] = carx[CHUNK - 1 : CHUNK] * old + dot_nn(keys_t, (vd[...].astype(F32) * towx).astype(BF))

        inside = (iota2((CHUNK, CHUNK), 0) >= iota2((CHUNK, CHUNK), 1)) & (cols[:, 0:1] == aux[0:1])
        fence = jnp.where(inside, 0.0, FAR)
        squares = jnp.zeros((CHUNK, 128), F32)
        for p in range(pairs):
            s = slice(128 * p, 128 * p + 128)
            mix = []
            for h in (2 * p, 2 * p + 1):
                decay = jnp.exp2(cols[:, AUX + h : AUX + h + 1] - cum[h : h + 1] + fence)
                mix.append((scores * decay).astype(BF))
            v = vd[:, s]
            zero = jnp.zeros_like(v)
            stacked = jnp.concatenate([jnp.where(low, v, zero), jnp.where(low, zero, v)], axis=0)
            y = dot_nn(jnp.concatenate(mix, axis=1), stacked)
            mixed = y + yint[:, s] + cw_ref[5:6, s] * cv_ref[0, here, s].astype(F32)
            x0 = pz_ref[0, here, 256 * p : 256 * p + 128].astype(F32)
            x1 = pz_ref[0, here, 256 * p + 128 : 256 * p + 256].astype(F32)
            gate = jnp.where(low, x0, pltpu.roll(x1, HEADDIM, 1))
            gated = mixed * (gate * sigmoid(gate))
            mixed_ref[0, here, s] = mixed.astype(BF)
            gated_ref[0, here, s] = (gated * cw_ref[6:7, s]).astype(BF)
            squares = squares + gated * gated
        lane = iota2((CHUNK, 128), 1)
        sums = jnp.where(lane == 0, jnp.sum(squares, axis=1, keepdims=True), 0.0)
        stat_ref[0, :, here] = sums.T[0:8]
        return carry

    lax.fori_loop(0, BLOCK // CHUNK, chunk_step, 0, unroll=True)

    @pl.when(now == last)
    def _():
        gather.across(place.first - 1)
        gather.finish()
        if swap:
            swap.finish()


def backward_kernel(
    place, heads, inner_all, pz_ref, raw_ref, aux_ref, mixed_ref, cv_ref, pre_ref, cbc_ref, pbc_ref,
    st_ref, stat_ref, cw_ref, cbw_ref, hp_ref, g_ref, out_hbm, gn_hbm, cot_hbm,
    ge_ref, flat_ref, y_keep, y_away, back_ref, grad_rows,
    dstate, cbuf, dbuf, vd, gm_s, gmc_s, ggate_s, bs_s, expand, collect, tri_ref, suf_ref, ghead_ref,
    y_s, g_s, fold, sums, theirs, normed_s, part_buf, core_buf, x_buf, z_buf,
    core_send, core_recv, x_send, x_recv, z_send, z_recv, y_sem, stat_sem,
    out_ref, gn_all, cot_all, load_sem,
):
    inner = heads * HEADDIM
    pairs = heads // 2
    wide = 2 * inner
    now = pl.program_id(0) * pl.num_programs(1) + pl.program_id(1)
    last = place.steps - 1
    first = now == 0
    gch_ref = flat_ref.at[8:16, 0:inner]
    gmap_ref = flat_ref.at[0:8, 0 : 2 * STATE]
    spot = Spot(place)
    if place.pair:
        scatter = LineScatter(
            spot, part_buf, core_buf, x_buf, z_buf, grad_rows, core_send, core_recv, x_send, x_recv, z_send, z_recv
        )
        half = HalfSwap(spot, y_s, y_away, y_sem)
        here_len = y_keep.shape[1]
        seqs = y_keep.shape[0]
        per_seq = place.length // CHUNK

        def out_terms(there):
            part_buf[there] = lax.dot_general(
                cot_all[:, there], normed_s[...], (((0,), (0,)), ((), ())), preferred_element_type=F32
            ).astype(BF)

        def keep():
            rows = y_s.at[:, pl.ds(pl.multiple_of(spot.me * here_len, here_len), here_len)]
            return pltpu.make_async_copy(rows, y_keep, y_sem.at[2])

        @pl.when(first)
        def _():
            loads = [
                pltpu.make_async_copy(far, near, load_sem.at[k])
                for k, (far, near) in enumerate(((gn_hbm, gn_all), (out_hbm, out_ref), (cot_hbm, cot_all)))
            ]
            for load in loads:
                load.start()
            spot.greet(True)
            for load in loads:
                load.wait()
            for cut in range(out_ref.shape[0] // 256):
                cols = slice(256 * cut, 256 * cut + 256)
                for seq in range(seqs):
                    rows = slice(seq * place.length, (seq + 1) * place.length)
                    y = dot_nt(gn_all[rows], out_ref[cols])
                    y_s[seq, :, cols] = y.astype(BF)
                    y = y * cot_all[rows, cols].astype(F32)
                    y = y[:, :128] + y[:, 128:]
                    fold[rows] = y if cut == 0 else fold[rows] + y

            for step in range(seqs * per_seq):
                rows = slice(step * CHUNK, (step + 1) * CHUNK)
                seq, cut = divmod(step, per_seq)
                there = slice(cut * CHUNK, (cut + 1) * CHUNK)
                cross = jnp.sum(fold[rows], axis=1, keepdims=True)
                row = jnp.broadcast_to(cross, (CHUNK, 128)).T[0:8]
                sums[seq, :, there] = jnp.where(iota2(row.shape, 0) == 1, row, stat_ref[seq, :, there])
            swap = spot.copy(sums, theirs, stat_sem.at[0], stat_sem.at[1], spot.index, 1 - spot.me)
            swap.start()

            def out_back(step, carry):
                rows = pl.ds(pl.multiple_of(step * BLOCK, BLOCK), BLOCK)
                g_s[rows] = dot_nn(cot_all[rows], out_ref[...]).astype(BF)
                return carry

            lax.fori_loop(0, seqs * place.length // BLOCK, out_back, 0)
            swap.wait()
            half.begin()
            keep().start()
            back_ref[...] = finish_sums(sums[...] + theirs[...], inner_all)

            for step in range(seqs * per_seq):
                rows = slice(step * CHUNK, (step + 1) * CHUNK)
                seq, cut = divmod(step, per_seq)
                rms_col = compact([back_ref[seq, :, cut * CHUNK : (cut + 1) * CHUNK]])[:, 0:1]
                normed_s[rows] = (gn_all[rows].astype(F32) * rms_col).astype(BF)
            scatter.produce(out_terms, True)
            scatter.produce(out_terms, False)
            scatter.cross()

        @pl.when(now == min(2, last))
        def _():
            scatter.along()
    else:
        pl.when(first)(lambda: back_ref.__setitem__(Ellipsis, stat_ref[...]))

    @pl.when(first)
    def _():
        for i, place in enumerate((AUX + heads, AUX + 2 * heads, AUX + 3 * heads)):
            expand[i] = expander(heads, inner, place)
        collect[0] = collector(inner, heads)
        collect[1] = collector(inner, 2 * heads)
        r, c = iota2((CHUNK, CHUNK), 0), iota2((CHUNK, CHUNK), 1)
        tri_ref[...] = jnp.where(r <= c, 1.0, 0.0).astype(BF)
        suf_ref[...] = jnp.where(r >= c, 1.0, 0.0).astype(BF)
        flat_ref[...] = jnp.zeros_like(flat_ref)
        ghead_ref[...] = jnp.zeros_like(ghead_ref)

    @pl.when(pl.program_id(1) == 0)
    def _():
        dstate[...] = jnp.zeros_like(dstate)
        cbuf[CHUNK:] = jnp.zeros((HALO, inner), F32)
        dbuf[CHUNK:] = jnp.zeros((HALO, 2 * STATE), F32)

    seq_now = pl.program_id(0)
    block_start = (pl.num_programs(1) - 1 - pl.program_id(1)) * BLOCK

    def chunk_step(step, carry):
        here = pl.ds(pl.multiple_of(BLOCK - CHUNK - step * CHUNK, CHUNK), CHUNK)
        there = pl.ds(pl.multiple_of(block_start + BLOCK - CHUNK - step * CHUNK, CHUNK), CHUNK)
        flat_rows = pl.ds(pl.multiple_of(seq_now * place.length + block_start + BLOCK - CHUNK - step * CHUNK, CHUNK), CHUNK)
        aux = aux_ref[0, :, here]
        rate = hp_ref[1]
        dt, cum, carried, toward = pieces(raw_ref[0, :, here], hp_ref[0], rate, aux, tri_ref[...])
        cols = compact([aux, cum, dt, carried, toward, back_ref[seq_now, :, there]])
        both = hi_lo(cols)
        dtx = dot_nn(both, expand[0])
        carx = dot_nn(both, expand[1])
        towx = dot_nn(both, expand[2])
        pad = cols[:, 1:2]
        ahead = [None] + [cols[:, 7 + k : 8 + k] for k in range(1, TAPS)]
        base = AUX + 4 * heads
        rms, pull = cols[:, base : base + 1], cols[:, base + 1 : base + 2]
        low = iota2((CHUNK, 128), 1) < HEADDIM
        maps = cbc_ref[0, here]
        keys, queries = maps[:, :STATE], maps[:, STATE:]
        queries_t = queries.astype(F32).T.astype(BF)
        scores_t = dot_nt(keys, queries)

        for p in range(pairs):
            s = slice(128 * p, 128 * p + 128)
            x0 = pz_ref[0, here, 256 * p : 256 * p + 128].astype(F32)
            x1 = pz_ref[0, here, 256 * p + 128 : 256 * p + 256].astype(F32)
            gate = jnp.where(low, x0, pltpu.roll(x1, HEADDIM, 1))
            sig = sigmoid(gate)
            act = gate * sig
            mixed = mixed_ref[0, here, s].astype(F32)
            gated = mixed * act
            g = (g_s[flat_rows, s] if place.pair else g_ref[0, here, s]).astype(F32)
            grad_gated = rms * (g * cw_ref[6:7, s]) - gated * pull
            gm = grad_gated * act
            ggate_s[:, s] = (grad_gated * mixed * (sig * (1.0 + gate * (1.0 - sig)))).astype(BF)
            gm_s[:, s] = gm.astype(BF)
            gmc_s[:, s] = (gm * carx[:, s]).astype(BF)
            cv = cv_ref[0, here, s].astype(F32)
            vd[:, s] = (cv * dtx[:, s]).astype(BF)
            gch_ref[5:6, s] += jnp.sum(gm * cv, axis=0, keepdims=True)
            gch_ref[6:7, s] += jnp.sum(gated * rms * g, axis=0, keepdims=True)

        ds = dstate[...]
        ds_b = ds.astype(BF)
        st = st_ref[0, BLOCK // CHUNK - 1 - step]
        gmc = gmc_s[...]
        cs = dot_nn(queries, st)
        bs = dot_nn(keys, ds_b) * towx
        bs_s[...] = bs
        reach = dot_nn((gmc.astype(F32) * cs).astype(BF), collect[1])
        reach = reach + dot_nn((bs * cv_ref[0, here].astype(F32)).astype(BF), collect[0])
        grad_q = dot_nt(gmc, st)
        grad_k = dot_nt((vd[...].astype(F32) * towx).astype(BF), ds_b)
        keep = carx[CHUNK - 1 : CHUNK]
        held = jnp.sum(st.astype(F32) * ds, axis=0, keepdims=True) * keep
        dstate[...] = keep * ds + dot_nn(queries_t, gmc)

        inside = (iota2((CHUNK, CHUNK), 0) <= iota2((CHUNK, CHUNK), 1)) & (cols[:, 0:1] == aux[0:1])
        fence = jnp.where(inside, 0.0, FAR)
        grad_scores_t = jnp.zeros((CHUNK, CHUNK), F32)
        lane = iota2((CHUNK, 128), 1)
        gathered = reach
        row_sums = []
        for p in range(pairs):
            s = slice(128 * p, 128 * p + 128)
            gm_b = gm_s[:, s]
            zero = jnp.zeros_like(gm_b)
            gm_two = jnp.concatenate([jnp.where(low, gm_b, zero), jnp.where(low, zero, gm_b)], axis=0)
            near = dot_nt(vd[:, s], gm_two)
            mix = []
            for j in range(2):
                h = 2 * p + j
                decay = jnp.exp2(cum[h : h + 1] - cols[:, AUX + h : AUX + h + 1] + fence)
                mix.append((scores_t * decay).astype(BF))
                weighed = decay * near[:, CHUNK * j : CHUNK * j + CHUNK]
                grad_scores_t = grad_scores_t + weighed
                pairs_g = weighed * scores_t
                row_sums.append(jnp.sum(pairs_g, axis=0, keepdims=True))
                gathered = jnp.where(lane == h, jnp.sum(pairs_g, axis=1, keepdims=True), gathered)
            z = dot_nn(jnp.concatenate(mix, axis=1), gm_two)
            gm = gm_b.astype(F32)
            grad_v = cw_ref[5:6, s] * gm + dtx[:, s] * (z + bs_s[:, s])
            x0 = pz_ref[0, here, 256 * p : 256 * p + 128].astype(F32)
            x1 = pz_ref[0, here, 256 * p + 128 : 256 * p + 256].astype(F32)
            u = jnp.where(low, pltpu.roll(x0, HEADDIM, 1), x1) * pad
            pre = pre_ref[0, here, s].astype(F32)
            sig = sigmoid(pre)
            c = grad_v * (sig * (1.0 + pre * (1.0 - sig)))
            cbuf[0:CHUNK, s] = c
            gu = cw_ref[0:1, s] * c
            gch_ref[4:5, s] += jnp.sum(c, axis=0, keepdims=True)
            gch_ref[0:1, s] += jnp.sum(c * u, axis=0, keepdims=True)
            for k in range(1, TAPS):
                shifted = ahead[k] * cbuf[k : k + CHUNK, s]
                gu = gu + cw_ref[k : k + 1, s] * shifted
                gch_ref[k : k + 1, s] += jnp.sum(shifted * u, axis=0, keepdims=True)
            gu = gu * pad
            ggate = ggate_s[:, s].astype(F32)
            ge_ref[0, here, 256 * p : 256 * p + 128] = jnp.where(low, ggate, pltpu.roll(gu, HEADDIM, 1)).astype(BF)
            ge_ref[0, here, 256 * p + 128 : 256 * p + 256] = jnp.where(low, pltpu.roll(ggate, HEADDIM, 1), gu).astype(BF)
        cbuf[CHUNK:] = cbuf[0:HALO]

        gst = grad_scores_t.astype(BF)
        grad_k = grad_k + dot_nn(gst, queries)
        grad_q = grad_q + dot_nn(grad_scores_t.T.astype(BF), keys)
        pbc = pbc_ref[0, here].astype(F32)
        sig = sigmoid(pbc)
        c = jnp.concatenate([grad_k, grad_q], axis=1) * (sig * (1.0 + pbc * (1.0 - sig)))
        dbuf[0:CHUNK] = c
        u = pz_ref[0, here, wide:].astype(F32) * pad
        gu = cbw_ref[0:1] * c
        gmap_ref[4:5] += jnp.sum(c, axis=0, keepdims=True)
        gmap_ref[0:1] += jnp.sum(c * u, axis=0, keepdims=True)
        for k in range(1, TAPS):
            shifted = ahead[k] * dbuf[k : k + CHUNK]
            gu = gu + cbw_ref[k : k + 1] * shifted
            gmap_ref[k : k + 1] += jnp.sum(shifted * u, axis=0, keepdims=True)
        ge_ref[0, here, wide : wide + 2 * STATE] = (gu * pad).astype(BF)
        dbuf[CHUNK:] = dbuf[0:HALO]

        across = gathered.T
        col_sum = across[0:heads]
        kx = across[heads : 2 * heads]
        rint = across[2 * heads : 3 * heads]
        row_sum = jnp.concatenate(row_sums, axis=0)
        k_all = kx * dt
        held_head = exact_dot(jnp.broadcast_to(held, (16, inner)), collect[0])
        held_col = jnp.broadcast_to(held_head[0:1], (CHUNK, 128)).T[heads : 2 * heads]
        diff = row_sum + rint - col_sum - k_all
        grad_a = exact_dot(diff, suf_ref[...]) + jnp.sum(k_all, axis=1, keepdims=True) + held_col
        direct = jnp.where(dt > 0.0, col_sum / jnp.where(dt > 0.0, dt, 1.0), 0.0)
        grad_dt = direct + kx + rate * grad_a
        graw = grad_dt * aux[1:2] * sigmoid(raw_ref[0, :, here] + hp_ref[0])
        ge_ref[0, here, wide + 2 * STATE :] = compact([graw]).astype(BF)
        ghead_ref[0] += graw
        ghead_ref[1] += rate * dt * grad_a
        return carry

    lax.fori_loop(0, BLOCK // CHUNK, chunk_step, 0)
    @pl.when(now == last)
    def _():
        for i in range(2):
            sums = jnp.broadcast_to(jnp.sum(ghead_ref[i], axis=1, keepdims=True), (heads, 128))
            flat_ref[15:16, 128 * i : 128 * i + 128] = compact([sums])[0:1]
        if place.pair:
            scatter.finish()
            half.finish()
            keep().wait()
        else:
            grad_rows[...] = jnp.zeros_like(grad_rows)


def gather_kernel(
    place, heads, zx_ref, bc_ref, step_ref, hidden_ref, gain_ref, cxw_ref, cxb_ref, cbw_ref, cbb_ref, bias_ref, decay_ref,
    skip_ref, ngain_ref, seg_ref, pad_ref,
    w_all, tok_full, aux_ref, cw_ref, cbw_out, hp_ref,
    shard, tok_own, square, send_sem, recv_sem, local_sem, side_send, side_recv, side_local, tok_sem,
):
    inner = heads * HEADDIM
    wide = 2 * inner
    spot = Spot(place)
    rows = zx_ref.shape[0]
    shard[:, 0:wide] = zx_ref[...]
    shard[:, wide : wide + 2 * STATE] = bc_ref[...]
    square[...] = jnp.zeros_like(square)
    square[0:heads, 0:rows] = step_ref[...].astype(F32)
    shard[:, wide + 2 * STATE :] = square[...].T[0:rows].astype(BF)
    spot.greet(place.pair)
    main, other = slice(0, wide), slice(wide, wide + 2 * STATE + 128)
    half = rows // PIECES
    gathers = [
        LineGather(
            spot, [(shard.at[half * q : half * q + half, main], w_all)],
            send_sem.at[q], recv_sem.at[q], local_sem.at[q], main, q, PIECES,
        )
        for q in range(PIECES)
    ]
    side = RowGather(spot, [(shard.at[:, other], w_all)], side_send, side_recv, side_local, other)
    for gather in gathers:
        gather.begin()
    side.begin()

    size = 64
    seqs, here = hidden_ref.shape[0], hidden_ref.shape[1]

    def norm_rows(step, carry):
        seq, cut = lax.div(step, here // size), lax.rem(step, here // size)
        mine = pl.ds(pl.multiple_of(cut * size, size), size)
        hid = hidden_ref[seq, mine].astype(F32)
        inv = lax.rsqrt(jnp.mean(hid * hid, axis=-1, keepdims=True) + epsilon)
        tok_own[seq, mine] = (hid * inv * gain_ref[...]).astype(BF)
        return carry

    lax.fori_loop(0, seqs * (here // size), norm_rows, 0)
    if place.pair:
        swap = TokenSwap(spot, tok_own, tok_full, tok_sem)
        swap.begin()
    else:
        copy = pltpu.make_async_copy(tok_own, tok_full, tok_sem.at[2])
        copy.start()

    square[...] = jnp.zeros_like(square)
    square[0:1, 0:heads] = bias_ref[...]
    square[1:2, 0:heads] = decay_ref[...]
    square[2:3, 0:heads] = skip_ref[...]
    per_head = square[...].T
    hp_ref[0] = jnp.broadcast_to(per_head[0:heads, 0:1], (heads, 128))
    hp_ref[1] = jnp.broadcast_to(-jnp.exp(per_head[0:heads, 1:2]), (heads, 128))
    cw_ref[0:TAPS] = cxw_ref[...]
    cw_ref[TAPS : TAPS + 1] = cxb_ref[...]
    cw_ref[5:6] = exact_dot(square[0:16], expander(heads, inner, 0)[0:128])[2:3]
    cw_ref[6:7] = ngain_ref[...]
    cw_ref[7:8] = jnp.zeros((1, inner), F32)
    cbw_out[...] = jnp.zeros_like(cbw_out)
    cbw_out[0:TAPS] = cbw_ref[...]
    cbw_out[TAPS : TAPS + 1] = cbb_ref[...]

    length = place.length
    lane = iota2((8, length), 1)
    flag = lambda condition: jnp.where(condition, 1.0, 0.0)[0:1]
    for seq in range(aux_ref.shape[0]):
        seg = jnp.broadcast_to(seg_ref[seq : seq + 1], (8, length))
        aux_ref[seq] = jnp.zeros((AUX, length), F32)
        aux_ref[seq, 0:1] = seg[0:1].astype(F32)
        aux_ref[seq, 1:2] = pad_ref[seq : seq + 1].astype(F32)
        for k in range(1, TAPS):
            aux_ref[seq, 1 + k : 2 + k] = flag((pltpu.roll(seg, k, 1) == seg) & (lane >= k))
            aux_ref[seq, 7 + k : 8 + k] = flag((pltpu.roll(seg, length - k, 1) == seg) & (lane < length - k))
        before = jnp.full((8, CHUNK), -1, jnp.int32)
        for chunk in range(length // CHUNK):
            cut = slice(chunk * CHUNK, (chunk + 1) * CHUNK)
            block = seg[:, cut]
            tail = jnp.broadcast_to(block[:, CHUNK - 1 : CHUNK], (8, CHUNK))
            aux_ref[seq, 5:6, cut] = flag(block == before)
            aux_ref[seq, 6:7, cut] = flag(block == tail)
            before = tail

    for hop in range(1, place.first):
        for gather in gathers:
            gather.along(hop)
        side.cross() if hop == 1 else side.along(hop - 1)
        for gather in gathers:
            gather.across(hop - 1)
    side.along(place.first - 1) if place.first > 1 else side.cross()
    for gather in gathers:
        gather.across(place.first - 1)
    for gather in gathers:
        gather.finish()
    side.finish()
    swap.finish() if place.pair else copy.wait()


def finish_sums(total, inner_all):
    lines = lax.broadcasted_iota(jnp.int32, total.shape, 1)
    rms = lax.rsqrt(total[:, 0:1] / inner_all + epsilon)
    pull = rms * rms * rms * (total[:, 1:2] / inner_all)
    return jnp.where(lines == 0, rms, jnp.where(lines == 1, pull, 0.0))


def reduce_kernel(
    place, tok_hbm, ge_hbm, flat_ref, gain_ref, back_ref, w_hbm, hidden_hbm, cot_hbm, keep_hbm, away_hbm,
    own_ref, sum_ref, gh_ref, output_ref,
    tok_ref, ge_ref, w_ref, hidden_ref, cot_ref, keep_ref, away_ref, dg_ref, dg_send, dg_buf,
    part_buf, core_buf, x_buf, z_buf, acc, bc_buf, bc_send, y_flat, core_flat, x_flat, z_flat, stage,
    core_send, core_recv, x_send, x_recv, z_send, z_recv, flat_send, flat_recv, dg_sem, load_sem, first_sem,
):
    spot = Spot(place)
    a, b, c, me, index = spot.a, spot.b, spot.c, spot.me, spot.index
    first, second = place.first, place.second
    scatter = LineScatter(
        spot, part_buf if place.pair else ge_ref, core_buf, x_buf, z_buf, own_ref,
        core_send, core_recv, x_send, x_recv, z_send, z_recv, PIECES,
    )
    ahead = [
        pltpu.make_async_copy(ge_hbm, ge_ref, first_sem.at[0]), pltpu.make_async_copy(tok_hbm, tok_ref, first_sem.at[1])
    ]
    for load in ahead:
        load.start()
    loads = []
    if place.pair:
        pairs = ((w_hbm, w_ref), (hidden_hbm, hidden_ref), (cot_hbm, cot_ref), (keep_hbm, keep_ref), (away_hbm, away_ref))
        for k, (far, near) in enumerate(pairs):
            loads.append(pltpu.make_async_copy(far, near, load_sem.at[k]))
        loads[0].start()
    spot.greet(place.pair)
    for load in ahead:
        load.wait()
    started = []

    def send(*args):
        copy = spot.copy(*args)
        copy.start()
        started.append(copy)

    def terms(there):
        if place.pair:
            part_buf[there] = lax.dot_general(
                tok_ref[:, there], ge_ref[...], (((0,), (0,)), ((), ())), preferred_element_type=F32
            ).astype(BF)

    stage[0] = flat_ref[...]
    here = hidden_ref.shape[1]

    def token_gradient(side, to):
        for seq in range(hidden_ref.shape[0]):
            rows = pl.ds(pl.multiple_of(seq * place.length + side * here, here), here)
            for cut in range(w_ref.shape[0] // 256):
                cols = slice(256 * cut, 256 * cut + 256)
                dg = dot_nt(ge_ref[rows], w_ref[cols])
                to[seq, :, cols] = dg.astype(BF)
                stage[0, 5:6, cols] += jnp.sum(dg * tok_ref[rows, cols].astype(F32), axis=0, keepdims=True)

    far = [(n, j) for j in range(1, second) for n in range(first)]
    near = [(n, 0) for n in range(first)]
    for k, (n, j) in enumerate(far + near[:1]):
        terms(scatter.terms(n, j))
        scatter.give(n, j)
        if 1 <= k <= len(far):
            scatter.cross_over(*far[k - 1])
    if place.pair:
        loads[0].wait()
        for load in loads[1:]:
            load.start()
        token_gradient(1 - me, dg_send)
        send(dg_send, dg_buf, dg_sem.at[0], dg_sem.at[1], index, 1 - me)
    for n, j in near[1:]:
        terms(scatter.terms(n, j))
        scatter.give(n, j)
    scatter.chain(acc, range(1))
    if place.pair:
        token_gradient(me, dg_ref)

    z_flat[a] = stage[0]
    for i in range(1, first):
        send(
            stage.at[0], z_flat.at[a], flat_send.at[second + i], flat_recv.at[2 + second + a],
            spot.at(spot.around(i), b, c),
        )
    scatter.chain(acc, range(1, min(2, first)))
    for i in range(1, first):
        spot.arrived(z_flat.at[spot.around(i)], flat_recv.at[2 + second + spot.around(i)])
    total = z_flat[0]
    for i in range(1, first):
        total = total + z_flat[i]
    stage[1] = total
    x_flat[b] = total
    for j in range(1, second):
        send(stage.at[1], x_flat.at[b], flat_send.at[1 + j], flat_recv.at[2 + b], spot.at(a, spot.aside(j), c))
    scatter.chain(acc, range(2, first))
    for j in range(1, second):
        spot.arrived(x_flat.at[spot.aside(j)], flat_recv.at[2 + spot.aside(j)])
    total = x_flat[0]
    for j in range(1, second):
        total = total + x_flat[j]
    stage[2] = total
    send(stage.at[2], core_flat, flat_send.at[1], flat_recv.at[1], spot.sibling)

    if place.pair:
        for load in loads[1:]:
            load.wait()
        spot.arrived(dg_buf, dg_sem.at[1])
        size = 128

        def token_rows(step, carry):
            seq, cut = lax.div(step, here // size), lax.rem(step, here // size)
            mine = pl.ds(pl.multiple_of(cut * size, size), size)
            full = pl.ds(pl.multiple_of(me * here + cut * size, size), size)
            hid = hidden_ref[seq, mine].astype(F32)
            inv = lax.rsqrt(jnp.mean(hid * hid, axis=-1, keepdims=True) + epsilon)
            gain = (dg_ref[seq, mine].astype(F32) + dg_buf[seq, mine].astype(F32)) * gain_ref[...]
            pull = inv * inv * inv * jnp.mean(hid * gain, axis=-1, keepdims=True)
            gh_ref[seq, mine] = (cot_ref[seq, mine].astype(F32) + inv * gain - hid * pull).astype(BF)
            rms = compact([back_ref[seq, :, full]])[:, 0:1]
            mixed = keep_ref[seq, mine].astype(F32) + away_ref[seq, mine].astype(F32)
            output_ref[seq, mine] = (hid + rms * mixed).astype(BF)
            return carry

        lax.fori_loop(0, hidden_ref.shape[0] * (here // size), token_rows, 0)
    else:
        gh_ref[...] = jnp.zeros_like(gh_ref)
        output_ref[...] = jnp.zeros_like(output_ref)

    spot.arrived(core_flat, flat_recv.at[1])
    total = stage[2] + core_flat[...]
    sum_ref[...] = total
    if place.pair:
        stage[3, 0:8] = total[0:8]
        send(stage.at[3, 0:8], y_flat, flat_send.at[0], flat_recv.at[0], index, 1 - me)
    scatter.finish_chain()
    if place.pair:
        edge = own_ref.shape[1] - 128 - 2 * STATE
        bc_send[...] = own_ref[:, edge : edge + 2 * STATE]
        send(bc_send, bc_buf, dg_sem.at[2], dg_sem.at[3], index, 1 - me)
    scatter.wait_sends()
    if place.pair:
        spot.arrived(y_flat, flat_recv.at[0])
        sum_ref[0:8] = stage[3, 0:8] + y_flat[...]
        spot.arrived(bc_buf, dg_sem.at[3])
        own_ref[:, edge : edge + 2 * STATE] = bc_send[...] + bc_buf[...]
    for copy in started:
        copy.wait_send()


def last_kernel(
    heads, own_ref, sum_ref, gh_in, output_in, out_rows, gain_ref,
    output_ref, gh_ref, pre_ref, zx_ref, bc_ref, step_ref, cxw_ref, cxb_ref, cbw_ref, cbb_ref, bias_ref, decay_ref,
    skip_ref, ngain_ref, out_ref,
):
    inner = heads * HEADDIM
    wide = 2 * inner
    rows = own_ref.shape[0]
    output_ref[...] = output_in[...]
    gh_ref[...] = gh_in[...]
    pre_ref[...] = sum_ref[5:6] / gain_ref[...]
    zx_ref[...] = own_ref[:, 0:wide]
    bc_ref[...] = own_ref[:, wide : wide + 2 * STATE]
    steps = own_ref[:, wide + 2 * STATE :]
    if rows < 128:
        steps = jnp.concatenate([steps, jnp.zeros((128 - rows, 128), F32)], axis=0)
    step_ref[...] = steps.T[0:heads, 0:rows]
    cxw_ref[...] = sum_ref[8 : 8 + TAPS, 0:inner]
    cxb_ref[...] = sum_ref[8 + TAPS : 9 + TAPS, 0:inner]
    cbw_ref[...] = sum_ref[0:TAPS, 0 : 2 * STATE]
    cbb_ref[...] = sum_ref[TAPS : TAPS + 1, 0 : 2 * STATE]
    skip = exact_dot(jnp.broadcast_to(sum_ref[13:14, 0:inner], (16, inner)), collector(inner, 0))
    bias_ref[...] = sum_ref[15:16, 0:heads]
    decay_ref[...] = sum_ref[15:16, 128 : 128 + heads]
    skip_ref[...] = skip[0:1, 0:heads]
    ngain_ref[...] = sum_ref[14:15, 0:inner]
    out_ref[...] = out_rows[...]


SDS = jax.ShapeDtypeStruct
DMA = pltpu.SemaphoreType.DMA
ANY = pl.BlockSpec(memory_space=pl.ANY)
WHOLE = pl.BlockSpec(memory_space=pltpu.VMEM)


def params(collective=None):
    if collective is None:
        return pltpu.CompilerParams(vmem_limit_bytes=VMEM_LIMIT)
    return pltpu.CompilerParams(vmem_limit_bytes=VMEM_LIMIT, collective_id=collective, has_side_effects=True)


def whole_once(*shape):
    return pl.BlockSpec(shape, lambda s, c: (0,) * len(shape), pipeline_mode=pl.Buffered(1))


def line_sems(place, cuts, lines):
    columns = place.first * max(place.second - 1, 1) * cuts
    blocks = place.first * place.second * cuts
    return [DMA((blocks,)), DMA((blocks,)), DMA((columns,)), DMA((columns,)), DMA((place.first * cuts,)), DMA((lines,))]


def gather_all(place, size, zx, bc, step_t, hidden, gain, cxw, cxb, cbw, cbb, bias, decay, skip, ngain, seg, pad):
    seqs, here, width = hidden.shape
    heads, inner = bias.shape[1], cxw.shape[1]
    total = 2 * inner + 2 * STATE + 128
    rows = zx.shape[0]
    return pl.pallas_call(
        functools.partial(gather_kernel, place, heads),
        in_specs=[WHOLE] * 15,
        out_specs=[ANY, ANY] + [WHOLE] * 4,
        out_shape=[
            SDS((size * rows, total), BF), SDS((seqs, place.length if place.pair else here, width), BF),
            SDS((seqs, AUX, place.length), F32), SDS((8, inner), F32), SDS((8, 2 * STATE), F32), SDS((2, heads, 128), F32),
        ],
        scratch_shapes=[
            pltpu.VMEM((rows, total), BF), pltpu.VMEM(hidden.shape, BF), pltpu.VMEM((128, 128), F32),
            DMA((PIECES, 1, gather_sites(place.first, place.second))), DMA((PIECES, 1, size)), DMA((PIECES, 1)),
            DMA((1, row_sites(place.first, place.second))), DMA((1, size)), DMA((1,)), DMA((3,)),
        ],
        compiler_params=params(0),
        name="gather_all",
    )(zx, bc, step_t, hidden, gain, cxw, cxb, cbw, cbb, bias, decay, skip, ngain, seg, pad)


def mixer_forward(place, size, tok, weights, aux, cw, cbw, hp, cot_own, out_own):
    seqs, length, width = tok.shape
    heads, inner = hp.shape[1], cw.shape[1]
    wide = 2 * inner + 2 * STATE
    chunks = length // CHUNK
    token = lambda size: pl.BlockSpec((1, BLOCK, size), lambda s, c: (s, c, 0))
    row = lambda high: pl.BlockSpec((1, high, BLOCK), lambda s, c: (s, 0, c))
    return pl.pallas_call(
        functools.partial(forward_kernel, place, heads),
        grid=(seqs, length // BLOCK),
        in_specs=[
            token(width), ANY, row(AUX),
            whole_once(8, inner), whole_once(8, 2 * STATE), whole_once(2, heads, 128), WHOLE, ANY,
        ],
        out_specs=[
            token(wide), row(heads), token(inner), token(inner), token(inner), token(inner), token(2 * STATE),
            token(2 * STATE), pl.BlockSpec((1, BLOCK // CHUNK, STATE, inner), lambda s, c: (s, c, 0, 0)), row(8),
            ANY, ANY,
        ],
        out_shape=[
            SDS((seqs, length, wide), BF), SDS((seqs, heads, length), F32),
            SDS((seqs, length, inner), BF), SDS((seqs, length, inner), BF), SDS((seqs, length, inner), BF),
            SDS((seqs, length, inner), BF), SDS((seqs, length, 2 * STATE), BF), SDS((seqs, length, 2 * STATE), BF),
            SDS((seqs, chunks, STATE, inner), BF), SDS((seqs, 8, length), F32),
            SDS((size * out_own.shape[0], inner), BF), SDS((seqs, length, width) if place.pair else (8, 128), BF),
        ],
        scratch_shapes=[
            pltpu.VMEM((STATE, inner), F32), pltpu.VMEM((HALO + CHUNK, inner), F32),
            pltpu.VMEM((HALO + CHUNK, 2 * STATE), F32), pltpu.VMEM((CHUNK, inner), BF),
            pltpu.VMEM((CHUNK, inner), F32), pltpu.VMEM((3, 256, inner), BF), pltpu.VMEM((CHUNK, CHUNK), BF),
            pltpu.VMEM(weights.shape, BF),
            DMA((1, gather_sites(place.first, place.second))), DMA((1, size)), DMA((1,)), DMA((3,)), DMA,
        ],
        compiler_params=params(1),
        name="mixer_forward",
    )(tok, weights, aux, cw, cbw, hp, cot_own, out_own)


def mixer_backward(
    place, size, inner_all, pz, raw, aux, mixed, cv, pre, cbc, pbc, st, stat, cw, cbw, hp, g, out_all, gn, cot
):
    seqs, length, inner = mixed.shape
    width, wide = out_all.shape[0], pz.shape[2] + 128
    heads = hp.shape[1]
    last = length // BLOCK - 1
    pair = place.pair
    here = length // 2 if pair else 16
    rows = width // size
    tokens = seqs * length
    token = lambda size: pl.BlockSpec((1, BLOCK, size), lambda s, c: (s, last - c, 0))
    row = lambda high: pl.BlockSpec((1, high, BLOCK), lambda s, c: (s, 0, last - c))
    fixed = lambda *shape: pl.BlockSpec(shape, lambda s, c: (0,) * len(shape))
    if pair:
        g = cbw
        gn_all, cot_all = gn.reshape(-1, inner), cot.reshape(-1, width)
    else:
        gn_all, cot_all, out_all = gn[0, :16, :128], cot[0, :16, :128], out_all[:16, :128]
    blocks = place.first * place.second
    columns = place.first * max(place.second - 1, 1)
    tile = lambda *shape: pltpu.VMEM(shape if pair else (1,) * (len(shape) - 2) + (16, 128), BF)
    rowed = pltpu.VMEM((seqs, 8, length), F32)
    return pl.pallas_call(
        functools.partial(backward_kernel, place, heads, inner_all),
        grid=(seqs, length // BLOCK),
        in_specs=[
            token(pz.shape[2]), row(heads), row(AUX), token(inner), token(inner),
            token(inner), token(2 * STATE), token(2 * STATE),
            pl.BlockSpec((1, BLOCK // CHUNK, STATE, inner), lambda s, c: (s, last - c, 0, 0)), whole_once(*stat.shape),
            whole_once(8, inner), whole_once(8, 2 * STATE), whole_once(2, heads, 128),
            whole_once(*g.shape) if pair else token(inner),
            ANY, ANY, ANY,
        ],
        out_specs=[token(wide), fixed(16, width), ANY, ANY, fixed(seqs, 8, length), fixed(rows, inner)],
        out_shape=[
            SDS((seqs, length, wide), BF), SDS((16, width), F32), SDS((seqs, here, width), BF),
            SDS((seqs, here, width), BF), SDS((seqs, 8, length), F32), SDS((rows, inner), F32),
        ],
        scratch_shapes=[
            pltpu.VMEM((STATE, inner), F32), pltpu.VMEM((CHUNK + HALO, inner), F32),
            pltpu.VMEM((CHUNK + HALO, 2 * STATE), F32), pltpu.VMEM((CHUNK, inner), BF),
            pltpu.VMEM((CHUNK, inner), BF), pltpu.VMEM((CHUNK, inner), BF), pltpu.VMEM((CHUNK, inner), BF),
            pltpu.VMEM((CHUNK, inner), F32),
            pltpu.VMEM((3, 256, inner), BF), pltpu.VMEM((2, inner, 128), BF),
            pltpu.VMEM((CHUNK, CHUNK), BF), pltpu.VMEM((CHUNK, CHUNK), BF), pltpu.VMEM((2, heads, 128), F32),
            tile(seqs, length, width), tile(tokens, inner), pltpu.VMEM((tokens, 128), F32), rowed, rowed,
            tile(tokens, inner), tile(width, inner),
            tile(blocks, rows, inner), tile(columns, rows, inner), tile(place.first, rows, inner),
        ] + line_sems(place, 1, place.first) + [DMA((3,)), DMA((2,))] + [
            pltpu.VMEM(out_all.shape, BF), pltpu.VMEM(gn_all.shape, BF), pltpu.VMEM(cot_all.shape, BF), DMA((3,)),
        ],
        compiler_params=params(3 if pair else None),
        name="mixer_backward",
    )(
        pz, raw, aux, mixed, cv, pre, cbc, pbc, st, stat, cw, cbw, hp, g, out_all, gn_all, cot_all,
    )


def reduce_all(place, size, tok, ge, flat, gain, back, weights, hidden, cot_own, y_keep, y_away):
    seqs, length, depth = tok.shape
    width = ge.shape[2]
    rows = depth // size
    pair = place.pair
    if pair:
        tok, ge = tok.reshape(seqs * length, depth), ge.reshape(seqs * length, width)
    else:
        ge = jnp.einsum("stp,sty->py", tok, ge, preferred_element_type=F32).astype(BF)
        tok, weights = tok[0, :16], weights[:16, :128]
        flat = jnp.concatenate([lax.psum(flat[:8], "tensor"), flat[8:]])
        hidden, cot_own, y_keep, y_away = [jnp.zeros((1, 16, depth), BF)] * 4
        back = back[:1, :, :128]
    blocks = place.first * place.second * PIECES
    columns = place.first * max(place.second - 1, 1) * PIECES
    lines = 2 * place.first * PIECES
    cut = rows // PIECES
    tokens = pltpu.VMEM(hidden.shape, BF)
    small = pltpu.VMEM((rows, 2 * STATE), F32)
    own, flat, gh, output = pl.pallas_call(
        functools.partial(reduce_kernel, place),
        in_specs=[ANY] * 2 + [WHOLE] * 3 + [ANY] * 5,
        out_specs=[WHOLE] * 4,
        out_shape=[SDS((rows, width), F32), SDS(flat.shape, F32), SDS(hidden.shape, BF), SDS(hidden.shape, BF)],
        scratch_shapes=[
            pltpu.VMEM(tok.shape, BF), pltpu.VMEM(ge.shape, BF), pltpu.VMEM(weights.shape, BF), tokens, tokens, tokens, tokens, tokens, tokens, tokens,
            pltpu.VMEM((depth, width) if pair else (16, 128), BF),
            pltpu.VMEM((blocks, cut, width), BF),
            pltpu.VMEM((columns, cut, width), BF),
            pltpu.VMEM((lines, cut, width), BF),
            pltpu.VMEM((cut, width), F32),
            small, small,
            pltpu.VMEM((8, flat.shape[1]), F32),
            pltpu.VMEM(flat.shape, F32),
            pltpu.VMEM((place.second,) + flat.shape, F32),
            pltpu.VMEM((place.first,) + flat.shape, F32),
            pltpu.VMEM((4,) + flat.shape, F32),
        ] + line_sems(place, PIECES, lines) + [
            DMA((1 + place.first + place.second,)), DMA((2 + place.first + place.second,)), DMA((4,)), DMA((5,)), DMA((2,)),
        ],
        compiler_params=params(4),
        name="reduce_all",
    )(tok, ge, flat, gain, back, weights, hidden, cot_own, y_keep, y_away)
    if not pair:
        edge = width - 128 - 2 * STATE
        own = own.at[:, edge : edge + 2 * STATE].set(lax.psum(own[:, edge : edge + 2 * STATE], "tensor"))
    return own, flat, gh, output


def body(
    hidden, pre_gain, zx_weight, bc_weight, step_weight, conv_x_weight, conv_x_bias, conv_bc_weight, conv_bc_bias,
    step_bias, decay_log, skip_gain, norm_gain, out_weight, segment_ids, pad_mask, grad_out,
):
    n, size = lax.axis_size("tensor"), lax.axis_size("dp")
    heads = step_weight.shape[1]
    inner = heads * HEADDIM
    seqs, here, width = hidden.shape
    length = segment_ids.shape[1]
    first, second = factors(size)
    place = Place(first, second, n == 2 and (2 * width // size) % 128 == 0, seqs * length // BLOCK, length)
    line = lambda vector: vector.reshape(1, -1)
    gain = line(pre_gain)

    weights, tok, aux, cw, cbw, hp = gather_all(
        place, size, zx_weight, bc_weight, step_weight.T, hidden, gain, conv_x_weight, line(conv_x_bias),
        conv_bc_weight, line(conv_bc_bias), line(step_bias), line(decay_log), line(skip_gain), line(norm_gain),
        segment_ids, pad_mask,
    )
    if not place.pair:
        tok = lax.all_gather(tok, "tensor", axis=1, tiled=True)
    pz, raw, mixed, gn, cv, pre, cbc, pbc, st, stat, out_all, cot = mixer_forward(
        place, size, tok, weights, aux, cw, cbw, hp, grad_out, out_weight.T
    )
    if not place.pair:
        cot = lax.all_gather(grad_out, "tensor", axis=1, tiled=True)
    g = y = None
    if not place.pair:
        y = jnp.einsum("stc,rc->str", gn, out_all, preferred_element_type=F32)
        cross = jnp.sum(y * cot.astype(F32), axis=-1)
        stat = finish_sums(lax.psum(stat.at[:, 1].set(cross), "tensor"), inner * n)
        g = jnp.einsum("str,rc->stc", cot, out_all, preferred_element_type=F32).astype(BF)
    ge, flat, y_keep, y_away, back, out_rows = mixer_backward(
        place, size, inner * n, pz, raw, aux, mixed, cv, pre, cbc, pbc, st, stat, cw, cbw, hp, g, out_all, gn, cot
    )
    if not place.pair:
        normed_out = (gn.astype(F32) * back[:, 0, :, None]).astype(BF)
        terms = jnp.einsum("str,stc->rc", cot, normed_out, preferred_element_type=F32).astype(BF)
        out_rows = lax.psum_scatter(terms, "dp", scatter_dimension=0, tiled=True).astype(F32)
        dg = jnp.einsum("sty,py->stp", ge, weights, preferred_element_type=F32)
        flat = flat.at[5].add(jnp.sum(dg * tok.astype(F32), axis=(0, 1)))
    own, sums, grad_hidden, output = reduce_all(
        place, size, tok, ge, flat, gain, back, weights, hidden, grad_out, y_keep, y_away
    )
    if not place.pair:
        hidden_f = hidden.astype(F32)
        inv_rms = lax.rsqrt(jnp.mean(hidden_f * hidden_f, axis=-1, keepdims=True) + epsilon)
        scatter = lambda rows: lax.psum_scatter(rows, "tensor", scatter_dimension=1, tiled=True)
        gain_grad = scatter(dg) * pre_gain
        pull = inv_rms**3 * jnp.mean(hidden_f * gain_grad, axis=-1, keepdims=True)
        grad_hidden = (grad_out.astype(F32) + inv_rms * gain_grad - hidden_f * pull).astype(BF)
        output = (hidden_f + scatter(y * back[:, 0, :, None])).astype(BF)
    rows = own.shape[0]
    output, grad_hidden, grad_pre, gzx, gbc, gstep, gcxw, gcxb, gcbw, gcbb, gbias, gdecay, gskip, gnorm, gout = pl.pallas_call(
        functools.partial(last_kernel, heads),
        in_specs=[WHOLE] * 6,
        out_specs=[WHOLE] * 15,
        out_shape=[
            SDS(hidden.shape, BF), SDS(hidden.shape, BF), SDS((1, width), F32), SDS((rows, 2 * inner), F32),
            SDS((rows, 2 * STATE), F32), SDS((heads, rows), F32), SDS((TAPS, inner), F32), SDS((1, inner), F32),
            SDS((TAPS, 2 * STATE), F32), SDS((1, 2 * STATE), F32), SDS((1, heads), F32), SDS((1, heads), F32),
            SDS((1, heads), F32), SDS((1, inner), F32), SDS((rows, inner), F32),
        ],
        compiler_params=params(),
        name="outputs",
    )(own, sums, grad_hidden, output, out_rows, gain)
    return (
        output, grad_hidden, grad_pre[0], gzx, gbc, gstep.T, gcxw, gcxb[0], gcbw, gcbb[0], gbias[0], gdecay[0],
        gskip[0], gnorm[0], gout.T,
    )


def solution(mesh):
    placed = (
        P("dp", "tensor", None), P(), P("dp", "tensor"), P("dp", None), P("dp", "tensor"), P(None, "tensor"),
        P("tensor"), P(), P(), P("tensor"), P("tensor"), P("tensor"), P("tensor"), P("tensor", "dp"),
        P("dp", None), P("dp", None), P("dp", "tensor", None),
    )
    return jax.shard_map(
        body,
        mesh=mesh,
        in_specs=placed,
        out_specs=(
            P("dp", "tensor", None), P("dp", "tensor", None), P(), P("dp", "tensor"), P("dp", None), P("dp", "tensor"),
            P(None, "tensor"), P("tensor"), P(), P(), P("tensor"), P("tensor"), P("tensor"), P("tensor"),
            P("tensor", "dp"),
        ),
        check_vma=False,
    )
```

```python
import collections
import functools
import jax
import jax.numpy as jnp
from jax import lax
from jax.experimental import pallas as pl
from jax.experimental.pallas import tpu as pltpu
from jax.sharding import PartitionSpec as P

HEADDIM = 64
STATE = 128
CHUNK = 128
TAPS = 4
HALO = 8
AUX = 16
LOG2E = 1.4426950408889634
FAR = -1e30
BLOCK = 256
VMEM_LIMIT = 58 * 1024 * 1024
MESH = pl.DeviceIdType.MESH
PIECES = 2
epsilon = 1e-05
BF = jnp.bfloat16
F32 = jnp.float32


def sigmoid(v):
    return 0.5 * jnp.tanh(0.5 * v) + 0.5


def split3(v):
    a = v.astype(BF)
    r = v - a.astype(F32)
    b = r.astype(BF)
    c = (r - b.astype(F32)).astype(BF)
    return a, b, c


def dot_nn(a, b):
    return lax.dot_general(a, b, (((1,), (0,)), ((), ())), preferred_element_type=F32)


def dot_nt(a, b):
    return lax.dot_general(a, b, (((1,), (1,)), ((), ())), preferred_element_type=F32)


def exact_dot(v, ones):
    rows = v.shape[0]
    out = dot_nn(jnp.concatenate(split3(v), axis=0), ones)
    return out[:rows] + out[rows : 2 * rows] + out[2 * rows :]


def iota2(shape, dim):
    return lax.broadcasted_iota(jnp.int32, shape, dim)


def pieces(raw, bias, rate, aux, tri):
    pad = aux[1:2]
    pre = raw + bias
    soft = jnp.maximum(pre, 0.0) + jnp.log1p(jnp.exp(-jnp.abs(pre)))
    dt = soft * pad
    cum = exact_dot(dt * rate, tri) * LOG2E
    carried = jnp.exp2(cum) * aux[5:6]
    toward = jnp.exp2(cum[:, CHUNK - 1 : CHUNK] - cum) * aux[6:7]
    return dt, cum, carried, toward


def expander(heads, inner, place):
    row = lax.rem(iota2((256, inner), 0), 128)
    head = lax.div(iota2((256, inner), 1), HEADDIM)
    return jnp.where(row == head + place, 1.0, 0.0).astype(BF)


def collector(inner, place):
    head = lax.div(iota2((inner, 128), 0), HEADDIM)
    lane = iota2((inner, 128), 1)
    return jnp.where(lane == head + place, 1.0, 0.0).astype(BF)


def hi_lo(cols):
    hi = cols.astype(BF)
    return jnp.concatenate([hi, (cols - hi.astype(F32)).astype(BF)], axis=1)


def compact(rows_list):
    used = sum(r.shape[0] for r in rows_list)
    if used < 128:
        rows_list = list(rows_list) + [jnp.zeros((128 - used, CHUNK), F32)]
    return jnp.concatenate(rows_list, axis=0).T


def split_pair(first, second, low):
    gate = jnp.where(low, first, pltpu.roll(second, HEADDIM, 1))
    value = jnp.where(low, pltpu.roll(first, HEADDIM, 1), second)
    return gate, value


Place = collections.namedtuple("Place", ("first", "second", "pair", "steps", "length"))


def factors(size):
    first = 4 if size % 8 == 0 else 1
    return first, size // (2 * first)


class Spot:
    def __init__(self, place):
        self.first, self.second = place.first, place.second
        self.index = lax.axis_index("dp")
        self.me = lax.axis_index("tensor")
        self.a = lax.div(self.index, 2 * self.second)
        self.b = lax.rem(lax.div(self.index, 2), self.second)
        self.c = lax.rem(self.index, 2)

    def at(self, i, j, k):
        return (i * self.second + j) * 2 + k

    def around(self, i):
        return lax.rem(self.a + i, self.first)

    def aside(self, j):
        return lax.rem(self.b + j, self.second)

    @property
    def sibling(self):
        return self.at(self.a, self.b, 1 - self.c)

    def greet(self, pair):
        barrier = pltpu.get_barrier_semaphore()
        peers = [(self.sibling, self.me)]
        peers += [(self.at(self.a, self.aside(j), self.c), self.me) for j in range(1, self.second)]
        peers += [(self.at(self.around(i), self.b, self.c), self.me) for i in range(1, self.first)]
        if pair:
            peers.append((self.index, 1 - self.me))
        for peer in peers:
            pl.semaphore_signal(barrier, inc=1, device_id=peer, device_id_type=MESH)
        pl.semaphore_wait(barrier, len(peers))

    def copy(self, src, dst, ss, rs, target, tensor=None):
        return pltpu.make_async_remote_copy(
            src_ref=src, dst_ref=dst, send_sem=ss, recv_sem=rs,
            device_id=(target, self.me if tensor is None else tensor), device_id_type=MESH,
        )

    def arrived(self, dst, rs):
        self.copy(dst, dst, rs, rs, self.sibling).wait_recv()


def when(valid, run):
    def quiet():
        run()

    quiet() if valid is None else pl.when(valid)(quiet)


def gather_sites(first, second):
    return (2 + second) + (first - 1) * 2 * (1 + second) + (2 * first - 1) * (second - 1)


def row_sites(first, second):
    return (2 + second) + 3 * (second - 1) + (first - 1) * 4 * second


class LineGather:
    def __init__(self, spot, arrays, send_sem, recv_sem, local_sem, columns=None, part=0, parts=1):
        self.spot, self.arrays, self.columns = spot, arrays, columns
        self.part, self.parts = part, parts
        self.send_sem, self.recv_sem, self.local_sem = send_sem, recv_sem, local_sem
        self.sites = []

    def rows(self, which, shard):
        own, full = self.arrays[which]
        rows = own.shape[0]
        there = pl.ds(pl.multiple_of((shard * self.parts + self.part) * rows, rows), rows)
        return full.at[there] if self.columns is None else full.at[there, self.columns]

    def copies(self, site, shard, target, mine=False):
        return [
            self.spot.copy(
                own if mine else self.rows(w, shard), self.rows(w, shard),
                self.send_sem.at[w, site], self.recv_sem.at[w, shard], target,
            )
            for w, (own, full) in enumerate(self.arrays)
        ]

    def send(self, valid, shard, target, mine=False):
        site = len(self.sites)
        self.sites.append((valid, shard, target, mine))
        when(valid and valid(), lambda: [copy.start() for copy in self.copies(site, shard(), target(), mine)])

    def arrive(self, valid, shard):
        def wait():
            for w in range(len(self.arrays)):
                self.spot.arrived(self.rows(w, shard), self.recv_sem.at[w, shard])

        when(valid, wait)

    def local(self):
        return [
            pltpu.make_async_copy(own, self.rows(w, self.spot.index), self.local_sem.at[w])
            for w, (own, full) in enumerate(self.arrays)
        ]

    def begin(self):
        s = self.spot
        self.send(lambda: s.a < s.first - 1, lambda: s.index, lambda: s.at(s.a + 1, s.b, s.c), True)
        self.send(lambda: s.a > 0, lambda: s.index, lambda: s.at(s.a - 1, s.b, s.c), True)
        for j in range(1, s.second):
            self.send(None, lambda: s.index, lambda j=j: s.at(s.a, s.aside(j), s.c), True)
        self.send(None, lambda: s.index, lambda: s.sibling, True)
        for copy in self.local():
            copy.start()

    def sides(self, hop):
        s = self.spot
        if hop == 0:
            return [(None, lambda: s.a, None, None)]
        return [
            (lambda: s.a - hop >= 0, lambda: s.a - hop, lambda: s.a < s.first - 1, lambda: s.at(s.a + 1, s.b, s.c)),
            (lambda: s.a + hop < s.first, lambda: s.a + hop, lambda: s.a > 0, lambda: s.at(s.a - 1, s.b, s.c)),
        ]

    def along(self, hop):
        s = self.spot
        for valid, origin, onward, target in self.sides(hop):
            shard = lambda origin=origin: s.at(origin(), s.b, s.c)
            self.arrive(valid(), shard())
            self.send(lambda valid=valid, onward=onward: valid() & onward(), shard, target)
            for j in range(1, s.second):
                self.send(valid, shard, lambda j=j: s.at(s.a, s.aside(j), s.c))
            self.send(valid, shard, lambda: s.sibling)

    def across(self, hop):
        s = self.spot
        for j in range(1, s.second):
            for valid, origin, onward, target in self.sides(hop):
                shard = lambda origin=origin, j=j: s.at(origin(), s.aside(j), s.c)
                self.arrive(valid and valid(), shard())
                self.send(valid, shard, lambda: s.sibling)

    def finish(self):
        s = self.spot
        for i in range(s.first):
            for j in range(s.second):
                self.arrive(None, s.at(i, j, 1 - s.c))
        for site, (valid, shard, target, mine) in enumerate(self.sites):
            when(
                valid and valid(),
                lambda site=site, shard=shard, target=target, mine=mine: [
                    copy.wait_send() for copy in self.copies(site, shard(), target(), mine)
                ],
            )
        for copy in self.local():
            copy.wait()


class RowGather(LineGather):
    def cross(self):
        s = self.spot
        for j in range(1, s.second):
            shard = lambda j=j: s.at(s.a, s.aside(j), s.c)
            self.arrive(None, shard())
            self.send(lambda: s.a < s.first - 1, shard, lambda: s.at(s.a + 1, s.b, s.c))
            self.send(lambda: s.a > 0, shard, lambda: s.at(s.a - 1, s.b, s.c))
            self.send(None, shard, lambda: s.sibling)

    def along(self, hop):
        s = self.spot
        for j in range(s.second):
            for valid, origin, onward, target in self.sides(hop):
                shard = lambda origin=origin, j=j: s.at(origin(), s.aside(j), s.c)
                self.arrive(valid(), shard())
                self.send(lambda valid=valid, onward=onward: valid() & onward(), shard, target)
                self.send(valid, shard, lambda: s.sibling)


class TokenSwap:
    def __init__(self, spot, own, full, sem):
        self.spot, self.own, self.full, self.sem = spot, own, full, sem

    def target(self):
        here = self.own.shape[1]
        return self.full.at[:, pl.ds(pl.multiple_of(self.spot.me * here, here), here)]

    def remote(self):
        s = self.spot
        return s.copy(self.own, self.target(), self.sem.at[0], self.sem.at[1], s.index, 1 - s.me)

    def local(self):
        return pltpu.make_async_copy(self.own, self.target(), self.sem.at[2])

    def begin(self):
        self.remote().start()
        self.local().start()

    def finish(self):
        self.remote().wait()
        self.local().wait()


class HalfSwap:
    def __init__(self, spot, whole, away, sem):
        self.spot, self.whole, self.away, self.sem = spot, whole, away, sem

    def remote(self):
        s = self.spot
        here = self.away.shape[1]
        rows = self.whole.at[:, pl.ds(pl.multiple_of((1 - s.me) * here, here), here)]
        return s.copy(rows, self.away, self.sem.at[0], self.sem.at[1], s.index, 1 - s.me)

    def begin(self):
        self.remote().start()

    def finish(self):
        self.remote().wait()


class LineScatter:
    def __init__(
        self, spot, part, core_buf, x_buf, z_buf, out, core_send, core_recv, x_send, x_recv, z_send, z_recv, cuts=1
    ):
        self.spot, self.part, self.out, self.cuts = spot, part, out, cuts
        self.core_buf, self.x_buf, self.z_buf = core_buf, x_buf, z_buf
        self.sems = (core_send, core_recv, x_send, x_recv, z_send, z_recv)
        self.rows = out.shape[0] // cuts
        self.copies = []
        a = spot.a
        if spot.first == 4:
            near = jnp.minimum(a, 3 - a)
            self.order = [jnp.where(a < 2, d, 3 - d) for d in (3 + 0 * a, 2 - 2 * near, 1 + near)] + [a]
        else:
            self.order = [a]

    def block(self, i, j, k, q):
        rows = self.rows
        return self.part.at[pl.ds(pl.multiple_of((self.spot.at(i, j, k) * self.cuts + q) * rows, rows), rows)]

    def slot(self, i, j, q):
        return (i * self.spot.second + j) * self.cuts + q

    def start(self, make):
        make().start()
        self.copies.append(make)

    def give(self, n, j):
        s, i = self.spot, self.order[n]
        for q in range(self.cuts):

            def make(q=q):
                t = self.slot(i, s.aside(j), q)
                return s.copy(
                    self.block(i, s.aside(j), 1 - s.c, q), self.core_buf.at[t], self.sems[0].at[t],
                    self.sems[1].at[t], s.sibling,
                )

            self.start(make)

    def terms(self, n, j):
        rows = 2 * self.rows * self.cuts
        first_row = self.spot.at(self.order[n], self.spot.aside(j), 0) * self.rows * self.cuts
        return pl.ds(pl.multiple_of(first_row, rows), rows)

    def cross_over(self, n, j):
        s, i = self.spot, self.order[n]
        for q in range(self.cuts):
            t = self.slot(i, s.aside(j), q)
            s.arrived(self.core_buf.at[t], self.sems[1].at[t])
            own = self.block(i, s.aside(j), s.c, q)[...].astype(F32)
            self.core_buf[t] = (own + self.core_buf[t].astype(F32)).astype(BF)

            def make(q=q):
                t = self.slot(i, s.aside(j), q)
                there = (i * (s.second - 1) + s.second - j - 1) * self.cuts + q
                here = (i * (s.second - 1) + j - 1) * self.cuts + q
                return s.copy(
                    self.core_buf.at[t], self.x_buf.at[there], self.sems[2].at[here], self.sems[3].at[there],
                    s.at(s.a, s.aside(j), s.c),
                )

            self.start(make)

    def column_sum(self, n, q):
        s, i = self.spot, self.order[n]
        t = self.slot(i, s.b, q)
        s.arrived(self.core_buf.at[t], self.sems[1].at[t])
        total = self.block(i, s.b, s.c, q)[...].astype(F32) + self.core_buf[t].astype(F32)
        for j in range(1, s.second):
            u = (i * (s.second - 1) + j - 1) * self.cuts + q
            s.arrived(self.x_buf.at[u], self.sems[3].at[u])
            total = total + self.x_buf[u].astype(F32)
        return total

    def produce(self, make_terms, far):
        s = self.spot
        for j in range(1, s.second) if far else [0]:
            for n in range(s.first):
                make_terms(self.terms(n, j))
                self.give(n, j)

    def cross(self):
        for j in range(1, self.spot.second):
            for n in range(self.spot.first):
                self.cross_over(n, j)

    def along(self):
        s = self.spot
        for n in range(s.first):
            for q in range(self.cuts):
                total = self.column_sum(n, q)
                if n == s.first - 1:
                    self.out[q * self.rows : (q + 1) * self.rows] = total
                    continue
                self.core_buf[self.slot(self.order[n], s.b, q)] = total.astype(BF)

                def make(n=n, q=q):
                    z = s.a * self.cuts + q
                    return s.copy(
                        self.core_buf.at[self.slot(self.order[n], s.b, q)], self.z_buf.at[z],
                        self.sems[4].at[n * self.cuts + q], self.sems[5].at[z], s.at(self.order[n], s.b, s.c),
                    )

                self.start(make)

    def chain(self, acc, order):
        s = self.spot
        for n in order:
            for q in range(self.cuts):
                i = self.order[n]
                total = self.column_sum(n, q)
                if n == s.first - 1:
                    self.out[q * self.rows : (q + 1) * self.rows] = total
                    continue
                down = jnp.where(i > s.a, 0, 1)
                z = (down * s.first + i) * self.cuts + q
                acc[...] = total

                @pl.when(jnp.where(i > s.a, s.a, s.first - 1 - s.a) > 0)
                def _(z=z):
                    s.arrived(self.z_buf.at[z], self.sems[5].at[z])
                    acc[...] = acc[...] + self.z_buf[z].astype(F32)

                self.core_buf[self.slot(i, s.b, q)] = acc[...].astype(BF)

                def make(n=n, q=q, i=i, down=down, z=z):
                    return s.copy(
                        self.core_buf.at[self.slot(i, s.b, q)], self.z_buf.at[z],
                        self.sems[4].at[n * self.cuts + q], self.sems[5].at[z], s.at(s.a + 1 - 2 * down, s.b, s.c),
                    )

                self.start(make)

    def finish_chain(self):
        s = self.spot
        for q in range(self.cuts):
            cut = slice(q * self.rows, (q + 1) * self.rows)
            for down, there in ((0, s.a), (1, s.first - 1 - s.a)):
                z = (down * s.first + s.a) * self.cuts + q

                @pl.when(there > 0)
                def _(z=z, cut=cut):
                    s.arrived(self.z_buf.at[z], self.sems[5].at[z])
                    self.out[cut] = self.out[cut] + self.z_buf[z].astype(F32)

    def wait_sends(self):
        for make in self.copies:
            make().wait_send()

    def finish(self):
        s = self.spot
        for i in range(1, s.first):
            for q in range(self.cuts):
                z = s.around(i) * self.cuts + q
                s.arrived(self.z_buf.at[z], self.sems[5].at[z])
                cut = slice(q * self.rows, (q + 1) * self.rows)
                self.out[cut] = self.out[cut] + self.z_buf[z].astype(F32)
        self.wait_sends()


def forward_kernel(
    place, heads, tok_ref, w_hbm, aux_ref, cw_ref, cbw_ref, hp_ref, cot_own, out_own,
    pz_ref, raw_ref, mixed_ref, gated_ref, cv_ref, pre_ref, cbc_ref, pbc_ref, st_ref, stat_ref, out_all, cot_full,
    state, ubuf, bbuf, vd, yint, expand, tri_ref, w_ref, send_sem, recv_sem, local_sem, cot_sem, load_sem,
):
    inner = heads * HEADDIM
    pairs = heads // 2
    wide = 2 * inner
    now = pl.program_id(0) * pl.num_programs(1) + pl.program_id(1)
    last = place.steps - 1
    first = now == 0
    spot = Spot(place)
    gather = LineGather(spot, [(out_own, out_all)], send_sem, recv_sem, local_sem)
    swap = TokenSwap(spot, cot_own, cot_full, cot_sem) if place.pair else None

    @pl.when(first)
    def _():
        load = pltpu.make_async_copy(w_hbm, w_ref, load_sem)
        load.start()
        spot.greet(place.pair)
        gather.begin()
        if swap:
            swap.begin()
        load.wait()

    for hop in range(1, place.first):

        @pl.when(now == min(hop, last))
        def _(hop=hop):
            gather.along(hop)
            gather.across(hop - 1)

    @pl.when(first)
    def _():
        for i, place in enumerate((AUX + heads, AUX + 2 * heads, AUX + 3 * heads)):
            expand[i] = expander(heads, inner, place)
        tri_ref[...] = jnp.where(iota2((CHUNK, CHUNK), 0) <= iota2((CHUNK, CHUNK), 1), 1.0, 0.0).astype(BF)

    @pl.when(pl.program_id(1) == 0)
    def _():
        state[...] = jnp.zeros_like(state)
        ubuf[0:HALO] = jnp.zeros((HALO, inner), F32)
        bbuf[0:HALO] = jnp.zeros((HALO, 2 * STATE), F32)

    tok = tok_ref[0]
    side = dot_nn(tok, w_ref[:, wide:])
    raw_ref[0] = side[:, 2 * STATE :].T[0:heads]
    pz_ref[0, :, wide:] = side[:, : 2 * STATE].astype(BF)
    for p in range(pairs):
        pz_ref[0, :, 256 * p : 256 * p + 256] = dot_nn(tok, w_ref[:, 256 * p : 256 * p + 256]).astype(BF)

    def chunk_step(step, carry):
        here = pl.ds(pl.multiple_of(step * CHUNK, CHUNK), CHUNK)
        aux = aux_ref[0, :, here]
        raw = raw_ref[0, :, here]
        bc = pz_ref[0, here, wide:]
        dt, cum, carried, toward = pieces(raw, hp_ref[0], hp_ref[1], aux, tri_ref[...])
        cols = compact([aux, cum, dt, carried, toward])
        both = hi_lo(cols)
        dtx = dot_nn(both, expand[0])
        carx = dot_nn(both, expand[1])
        towx = dot_nn(both, expand[2])
        pad = cols[:, 1:2]
        same = [None] + [cols[:, 1 + k : 2 + k] for k in range(1, TAPS)]
        low = iota2((CHUNK, 128), 1) < HEADDIM

        bbuf[HALO:] = bc.astype(F32) * pad
        maps = cbw_ref[TAPS : TAPS + 1] + cbw_ref[0:1] * bbuf[HALO:]
        for k in range(1, TAPS):
            maps = maps + cbw_ref[k : k + 1] * (same[k] * bbuf[HALO - k : HALO - k + CHUNK])
        pbc_ref[0, here] = maps.astype(BF)
        maps = (maps * sigmoid(maps)).astype(BF)
        cbc_ref[0, here] = maps
        bbuf[0:HALO] = bbuf[CHUNK : CHUNK + HALO]
        keys, queries = maps[:, :STATE], maps[:, STATE:]
        scores = dot_nt(queries, keys)
        keys_t = keys.astype(F32).T.astype(BF)

        for p in range(pairs):
            s = slice(128 * p, 128 * p + 128)
            x0 = pz_ref[0, here, 256 * p : 256 * p + 128].astype(F32)
            x1 = pz_ref[0, here, 256 * p + 128 : 256 * p + 256].astype(F32)
            value = jnp.where(low, pltpu.roll(x0, HEADDIM, 1), x1)
            ubuf[HALO:, s] = value * pad
            pre = cw_ref[TAPS : TAPS + 1, s] + cw_ref[0:1, s] * ubuf[HALO:, s]
            for k in range(1, TAPS):
                pre = pre + cw_ref[k : k + 1, s] * (same[k] * ubuf[HALO - k : HALO - k + CHUNK, s])
            pre_ref[0, here, s] = pre.astype(BF)
            cv = (pre * sigmoid(pre)).astype(BF)
            cv_ref[0, here, s] = cv
            vd[:, s] = (cv.astype(F32) * dtx[:, s]).astype(BF)
        ubuf[0:HALO] = ubuf[CHUNK : CHUNK + HALO]

        old = state[...]
        old_b = old.astype(BF)
        st_ref[0, step] = old_b
        yint[...] = dot_nn(queries, old_b) * carx
        state[...] = carx[CHUNK - 1 : CHUNK] * old + dot_nn(keys_t, (vd[...].astype(F32) * towx).astype(BF))

        inside = (iota2((CHUNK, CHUNK), 0) >= iota2((CHUNK, CHUNK), 1)) & (cols[:, 0:1] == aux[0:1])
        fence = jnp.where(inside, 0.0, FAR)
        squares = jnp.zeros((CHUNK, 128), F32)
        for p in range(pairs):
            s = slice(128 * p, 128 * p + 128)
            mix = []
            for h in (2 * p, 2 * p + 1):
                decay = jnp.exp2(cols[:, AUX + h : AUX + h + 1] - cum[h : h + 1] + fence)
                mix.append((scores * decay).astype(BF))
            v = vd[:, s]
            zero = jnp.zeros_like(v)
            stacked = jnp.concatenate([jnp.where(low, v, zero), jnp.where(low, zero, v)], axis=0)
            y = dot_nn(jnp.concatenate(mix, axis=1), stacked)
            mixed = y + yint[:, s] + cw_ref[5:6, s] * cv_ref[0, here, s].astype(F32)
            x0 = pz_ref[0, here, 256 * p : 256 * p + 128].astype(F32)
            x1 = pz_ref[0, here, 256 * p + 128 : 256 * p + 256].astype(F32)
            gate = jnp.where(low, x0, pltpu.roll(x1, HEADDIM, 1))
            gated = mixed * (gate * sigmoid(gate))
            mixed_ref[0, here, s] = mixed.astype(BF)
            gated_ref[0, here, s] = (gated * cw_ref[6:7, s]).astype(BF)
            squares = squares + gated * gated
        lane = iota2((CHUNK, 128), 1)
        sums = jnp.where(lane == 0, jnp.sum(squares, axis=1, keepdims=True), 0.0)
        stat_ref[0, :, here] = sums.T[0:8]
        return carry

    lax.fori_loop(0, BLOCK // CHUNK, chunk_step, 0, unroll=True)

    @pl.when(now == last)
    def _():
        gather.across(place.first - 1)
        gather.finish()
        if swap:
            swap.finish()


def backward_kernel(
    place, heads, inner_all, pz_ref, raw_ref, aux_ref, mixed_ref, cv_ref, pre_ref, cbc_ref, pbc_ref,
    st_ref, stat_ref, cw_ref, cbw_ref, hp_ref, g_ref, out_hbm, gn_hbm, cot_hbm,
    ge_ref, flat_ref, y_keep, y_away, back_ref, grad_rows,
    dstate, cbuf, dbuf, vd, gm_s, gmc_s, ggate_s, bs_s, expand, collect, tri_ref, suf_ref, ghead_ref,
    y_s, g_s, fold, sums, theirs, normed_s, part_buf, core_buf, x_buf, z_buf,
    core_send, core_recv, x_send, x_recv, z_send, z_recv, y_sem, stat_sem,
    out_ref, gn_all, cot_all, load_sem,
):
    inner = heads * HEADDIM
    pairs = heads // 2
    wide = 2 * inner
    now = pl.program_id(0) * pl.num_programs(1) + pl.program_id(1)
    last = place.steps - 1
    first = now == 0
    gch_ref = flat_ref.at[8:16, 0:inner]
    gmap_ref = flat_ref.at[0:8, 0 : 2 * STATE]
    spot = Spot(place)
    if place.pair:
        scatter = LineScatter(
            spot, part_buf, core_buf, x_buf, z_buf, grad_rows, core_send, core_recv, x_send, x_recv, z_send, z_recv
        )
        half = HalfSwap(spot, y_s, y_away, y_sem)
        here_len = y_keep.shape[1]
        seqs = y_keep.shape[0]
        per_seq = place.length // CHUNK

        def out_terms(there):
            part_buf[there] = lax.dot_general(
                cot_all[:, there], normed_s[...], (((0,), (0,)), ((), ())), preferred_element_type=F32
            ).astype(BF)

        def keep():
            rows = y_s.at[:, pl.ds(pl.multiple_of(spot.me * here_len, here_len), here_len)]
            return pltpu.make_async_copy(rows, y_keep, y_sem.at[2])

        @pl.when(first)
        def _():
            loads = [
                pltpu.make_async_copy(far, near, load_sem.at[k])
                for k, (far, near) in enumerate(((gn_hbm, gn_all), (out_hbm, out_ref), (cot_hbm, cot_all)))
            ]
            for load in loads:
                load.start()
            spot.greet(True)
            for load in loads:
                load.wait()
            for cut in range(out_ref.shape[0] // 256):
                cols = slice(256 * cut, 256 * cut + 256)
                for seq in range(seqs):
                    rows = slice(seq * place.length, (seq + 1) * place.length)
                    y = dot_nt(gn_all[rows], out_ref[cols])
                    y_s[seq, :, cols] = y.astype(BF)
                    y = y * cot_all[rows, cols].astype(F32)
                    y = y[:, :128] + y[:, 128:]
                    fold[rows] = y if cut == 0 else fold[rows] + y

            for step in range(seqs * per_seq):
                rows = slice(step * CHUNK, (step + 1) * CHUNK)
                seq, cut = divmod(step, per_seq)
                there = slice(cut * CHUNK, (cut + 1) * CHUNK)
                cross = jnp.sum(fold[rows], axis=1, keepdims=True)
                row = jnp.broadcast_to(cross, (CHUNK, 128)).T[0:8]
                sums[seq, :, there] = jnp.where(iota2(row.shape, 0) == 1, row, stat_ref[seq, :, there])
            swap = spot.copy(sums, theirs, stat_sem.at[0], stat_sem.at[1], spot.index, 1 - spot.me)
            swap.start()

            def out_back(step, carry):
                rows = pl.ds(pl.multiple_of(step * BLOCK, BLOCK), BLOCK)
                g_s[rows] = dot_nn(cot_all[rows], out_ref[...]).astype(BF)
                return carry

            lax.fori_loop(0, seqs * place.length // BLOCK, out_back, 0)
            swap.wait()
            half.begin()
            keep().start()
            back_ref[...] = finish_sums(sums[...] + theirs[...], inner_all)

            for step in range(seqs * per_seq):
                rows = slice(step * CHUNK, (step + 1) * CHUNK)
                seq, cut = divmod(step, per_seq)
                rms_col = compact([back_ref[seq, :, cut * CHUNK : (cut + 1) * CHUNK]])[:, 0:1]
                normed_s[rows] = (gn_all[rows].astype(F32) * rms_col).astype(BF)
            scatter.produce(out_terms, True)
            scatter.produce(out_terms, False)
            scatter.cross()

        @pl.when(now == min(2, last))
        def _():
            scatter.along()
    else:
        pl.when(first)(lambda: back_ref.__setitem__(Ellipsis, stat_ref[...]))

    @pl.when(first)
    def _():
        for i, place in enumerate((AUX + heads, AUX + 2 * heads, AUX + 3 * heads)):
            expand[i] = expander(heads, inner, place)
        collect[0] = collector(inner, heads)
        collect[1] = collector(inner, 2 * heads)
        r, c = iota2((CHUNK, CHUNK), 0), iota2((CHUNK, CHUNK), 1)
        tri_ref[...] = jnp.where(r <= c, 1.0, 0.0).astype(BF)
        suf_ref[...] = jnp.where(r >= c, 1.0, 0.0).astype(BF)
        flat_ref[...] = jnp.zeros_like(flat_ref)
        ghead_ref[...] = jnp.zeros_like(ghead_ref)

    @pl.when(pl.program_id(1) == 0)
    def _():
        dstate[...] = jnp.zeros_like(dstate)
        cbuf[CHUNK:] = jnp.zeros((HALO, inner), F32)
        dbuf[CHUNK:] = jnp.zeros((HALO, 2 * STATE), F32)

    seq_now = pl.program_id(0)
    block_start = (pl.num_programs(1) - 1 - pl.program_id(1)) * BLOCK

    def chunk_step(step, carry):
        here = pl.ds(pl.multiple_of(BLOCK - CHUNK - step * CHUNK, CHUNK), CHUNK)
        there = pl.ds(pl.multiple_of(block_start + BLOCK - CHUNK - step * CHUNK, CHUNK), CHUNK)
        flat_rows = pl.ds(pl.multiple_of(seq_now * place.length + block_start + BLOCK - CHUNK - step * CHUNK, CHUNK), CHUNK)
        aux = aux_ref[0, :, here]
        rate = hp_ref[1]
        dt, cum, carried, toward = pieces(raw_ref[0, :, here], hp_ref[0], rate, aux, tri_ref[...])
        cols = compact([aux, cum, dt, carried, toward, back_ref[seq_now, :, there]])
        both = hi_lo(cols)
        dtx = dot_nn(both, expand[0])
        carx = dot_nn(both, expand[1])
        towx = dot_nn(both, expand[2])
        pad = cols[:, 1:2]
        ahead = [None] + [cols[:, 7 + k : 8 + k] for k in range(1, TAPS)]
        base = AUX + 4 * heads
        rms, pull = cols[:, base : base + 1], cols[:, base + 1 : base + 2]
        low = iota2((CHUNK, 128), 1) < HEADDIM
        maps = cbc_ref[0, here]
        keys, queries = maps[:, :STATE], maps[:, STATE:]
        queries_t = queries.astype(F32).T.astype(BF)
        scores_t = dot_nt(keys, queries)

        for p in range(pairs):
            s = slice(128 * p, 128 * p + 128)
            x0 = pz_ref[0, here, 256 * p : 256 * p + 128].astype(F32)
            x1 = pz_ref[0, here, 256 * p + 128 : 256 * p + 256].astype(F32)
            gate = jnp.where(low, x0, pltpu.roll(x1, HEADDIM, 1))
            sig = sigmoid(gate)
            act = gate * sig
            mixed = mixed_ref[0, here, s].astype(F32)
            gated = mixed * act
            g = (g_s[flat_rows, s] if place.pair else g_ref[0, here, s]).astype(F32)
            grad_gated = rms * (g * cw_ref[6:7, s]) - gated * pull
            gm = grad_gated * act
            ggate_s[:, s] = (grad_gated * mixed * (sig * (1.0 + gate * (1.0 - sig)))).astype(BF)
            gm_s[:, s] = gm.astype(BF)
            gmc_s[:, s] = (gm * carx[:, s]).astype(BF)
            cv = cv_ref[0, here, s].astype(F32)
            vd[:, s] = (cv * dtx[:, s]).astype(BF)
            gch_ref[5:6, s] += jnp.sum(gm * cv, axis=0, keepdims=True)
            gch_ref[6:7, s] += jnp.sum(gated * rms * g, axis=0, keepdims=True)

        ds = dstate[...]
        ds_b = ds.astype(BF)
        st = st_ref[0, BLOCK // CHUNK - 1 - step]
        gmc = gmc_s[...]
        cs = dot_nn(queries, st)
        bs = dot_nn(keys, ds_b) * towx
        bs_s[...] = bs
        reach = dot_nn((gmc.astype(F32) * cs).astype(BF), collect[1])
        reach = reach + dot_nn((bs * cv_ref[0, here].astype(F32)).astype(BF), collect[0])
        grad_q = dot_nt(gmc, st)
        grad_k = dot_nt((vd[...].astype(F32) * towx).astype(BF), ds_b)
        keep = carx[CHUNK - 1 : CHUNK]
        held = jnp.sum(st.astype(F32) * ds, axis=0, keepdims=True) * keep
        dstate[...] = keep * ds + dot_nn(queries_t, gmc)

        inside = (iota2((CHUNK, CHUNK), 0) <= iota2((CHUNK, CHUNK), 1)) & (cols[:, 0:1] == aux[0:1])
        fence = jnp.where(inside, 0.0, FAR)
        grad_scores_t = jnp.zeros((CHUNK, CHUNK), F32)
        lane = iota2((CHUNK, 128), 1)
        gathered = reach
        row_sums = []
        for p in range(pairs):
            s = slice(128 * p, 128 * p + 128)
            gm_b = gm_s[:, s]
            zero = jnp.zeros_like(gm_b)
            gm_two = jnp.concatenate([jnp.where(low, gm_b, zero), jnp.where(low, zero, gm_b)], axis=0)
            near = dot_nt(vd[:, s], gm_two)
            mix = []
            for j in range(2):
                h = 2 * p + j
                decay = jnp.exp2(cum[h : h + 1] - cols[:, AUX + h : AUX + h + 1] + fence)
                mix.append((scores_t * decay).astype(BF))
                weighed = decay * near[:, CHUNK * j : CHUNK * j + CHUNK]
                grad_scores_t = grad_scores_t + weighed
                pairs_g = weighed * scores_t
                row_sums.append(jnp.sum(pairs_g, axis=0, keepdims=True))
                gathered = jnp.where(lane == h, jnp.sum(pairs_g, axis=1, keepdims=True), gathered)
            z = dot_nn(jnp.concatenate(mix, axis=1), gm_two)
            gm = gm_b.astype(F32)
            grad_v = cw_ref[5:6, s] * gm + dtx[:, s] * (z + bs_s[:, s])
            x0 = pz_ref[0, here, 256 * p : 256 * p + 128].astype(F32)
            x1 = pz_ref[0, here, 256 * p + 128 : 256 * p + 256].astype(F32)
            u = jnp.where(low, pltpu.roll(x0, HEADDIM, 1), x1) * pad
            pre = pre_ref[0, here, s].astype(F32)
            sig = sigmoid(pre)
            c = grad_v * (sig * (1.0 + pre * (1.0 - sig)))
            cbuf[0:CHUNK, s] = c
            gu = cw_ref[0:1, s] * c
            gch_ref[4:5, s] += jnp.sum(c, axis=0, keepdims=True)
            gch_ref[0:1, s] += jnp.sum(c * u, axis=0, keepdims=True)
            for k in range(1, TAPS):
                shifted = ahead[k] * cbuf[k : k + CHUNK, s]
                gu = gu + cw_ref[k : k + 1, s] * shifted
                gch_ref[k : k + 1, s] += jnp.sum(shifted * u, axis=0, keepdims=True)
            gu = gu * pad
            ggate = ggate_s[:, s].astype(F32)
            ge_ref[0, here, 256 * p : 256 * p + 128] = jnp.where(low, ggate, pltpu.roll(gu, HEADDIM, 1)).astype(BF)
            ge_ref[0, here, 256 * p + 128 : 256 * p + 256] = jnp.where(low, pltpu.roll(ggate, HEADDIM, 1), gu).astype(BF)
        cbuf[CHUNK:] = cbuf[0:HALO]

        gst = grad_scores_t.astype(BF)
        grad_k = grad_k + dot_nn(gst, queries)
        grad_q = grad_q + dot_nn(grad_scores_t.T.astype(BF), keys)
        pbc = pbc_ref[0, here].astype(F32)
        sig = sigmoid(pbc)
        c = jnp.concatenate([grad_k, grad_q], axis=1) * (sig * (1.0 + pbc * (1.0 - sig)))
        dbuf[0:CHUNK] = c
        u = pz_ref[0, here, wide:].astype(F32) * pad
        gu = cbw_ref[0:1] * c
        gmap_ref[4:5] += jnp.sum(c, axis=0, keepdims=True)
        gmap_ref[0:1] += jnp.sum(c * u, axis=0, keepdims=True)
        for k in range(1, TAPS):
            shifted = ahead[k] * dbuf[k : k + CHUNK]
            gu = gu + cbw_ref[k : k + 1] * shifted
            gmap_ref[k : k + 1] += jnp.sum(shifted * u, axis=0, keepdims=True)
        ge_ref[0, here, wide : wide + 2 * STATE] = (gu * pad).astype(BF)
        dbuf[CHUNK:] = dbuf[0:HALO]

        across = gathered.T
        col_sum = across[0:heads]
        kx = across[heads : 2 * heads]
        rint = across[2 * heads : 3 * heads]
        row_sum = jnp.concatenate(row_sums, axis=0)
        k_all = kx * dt
        held_head = exact_dot(jnp.broadcast_to(held, (16, inner)), collect[0])
        held_col = jnp.broadcast_to(held_head[0:1], (CHUNK, 128)).T[heads : 2 * heads]
        diff = row_sum + rint - col_sum - k_all
        grad_a = exact_dot(diff, suf_ref[...]) + jnp.sum(k_all, axis=1, keepdims=True) + held_col
        direct = jnp.where(dt > 0.0, col_sum / jnp.where(dt > 0.0, dt, 1.0), 0.0)
        grad_dt = direct + kx + rate * grad_a
        graw = grad_dt * aux[1:2] * sigmoid(raw_ref[0, :, here] + hp_ref[0])
        ge_ref[0, here, wide + 2 * STATE :] = compact([graw]).astype(BF)
        ghead_ref[0] += graw
        ghead_ref[1] += rate * dt * grad_a
        return carry

    lax.fori_loop(0, BLOCK // CHUNK, chunk_step, 0)
    @pl.when(now == last)
    def _():
        for i in range(2):
            sums = jnp.broadcast_to(jnp.sum(ghead_ref[i], axis=1, keepdims=True), (heads, 128))
            flat_ref[15:16, 128 * i : 128 * i + 128] = compact([sums])[0:1]
        if place.pair:
            scatter.finish()
            half.finish()
            keep().wait()
        else:
            grad_rows[...] = jnp.zeros_like(grad_rows)


def gather_kernel(
    place, heads, zx_ref, bc_ref, step_ref, hidden_ref, gain_ref, cxw_ref, cxb_ref, cbw_ref, cbb_ref, bias_ref, decay_ref,
    skip_ref, ngain_ref, seg_ref, pad_ref,
    w_all, tok_full, aux_ref, cw_ref, cbw_out, hp_ref,
    shard, tok_own, square, send_sem, recv_sem, local_sem, side_send, side_recv, side_local, tok_sem,
):
    inner = heads * HEADDIM
    wide = 2 * inner
    spot = Spot(place)
    rows = zx_ref.shape[0]
    shard[:, 0:wide] = zx_ref[...]
    shard[:, wide : wide + 2 * STATE] = bc_ref[...]
    square[...] = jnp.zeros_like(square)
    square[0:heads, 0:rows] = step_ref[...].astype(F32)
    shard[:, wide + 2 * STATE :] = square[...].T[0:rows].astype(BF)
    spot.greet(place.pair)
    main, other = slice(0, wide), slice(wide, wide + 2 * STATE + 128)
    half = rows // PIECES
    gathers = [
        LineGather(
            spot, [(shard.at[half * q : half * q + half, main], w_all)],
            send_sem.at[q], recv_sem.at[q], local_sem.at[q], main, q, PIECES,
        )
        for q in range(PIECES)
    ]
    side = RowGather(spot, [(shard.at[:, other], w_all)], side_send, side_recv, side_local, other)
    for gather in gathers:
        gather.begin()
    side.begin()

    size = 64
    seqs, here = hidden_ref.shape[0], hidden_ref.shape[1]

    def norm_rows(step, carry):
        seq, cut = lax.div(step, here // size), lax.rem(step, here // size)
        mine = pl.ds(pl.multiple_of(cut * size, size), size)
        hid = hidden_ref[seq, mine].astype(F32)
        inv = lax.rsqrt(jnp.mean(hid * hid, axis=-1, keepdims=True) + epsilon)
        tok_own[seq, mine] = (hid * inv * gain_ref[...]).astype(BF)
        return carry

    lax.fori_loop(0, seqs * (here // size), norm_rows, 0)
    if place.pair:
        swap = TokenSwap(spot, tok_own, tok_full, tok_sem)
        swap.begin()
    else:
        copy = pltpu.make_async_copy(tok_own, tok_full, tok_sem.at[2])
        copy.start()

    square[...] = jnp.zeros_like(square)
    square[0:1, 0:heads] = bias_ref[...]
    square[1:2, 0:heads] = decay_ref[...]
    square[2:3, 0:heads] = skip_ref[...]
    per_head = square[...].T
    hp_ref[0] = jnp.broadcast_to(per_head[0:heads, 0:1], (heads, 128))
    hp_ref[1] = jnp.broadcast_to(-jnp.exp(per_head[0:heads, 1:2]), (heads, 128))
    cw_ref[0:TAPS] = cxw_ref[...]
    cw_ref[TAPS : TAPS + 1] = cxb_ref[...]
    cw_ref[5:6] = exact_dot(square[0:16], expander(heads, inner, 0)[0:128])[2:3]
    cw_ref[6:7] = ngain_ref[...]
    cw_ref[7:8] = jnp.zeros((1, inner), F32)
    cbw_out[...] = jnp.zeros_like(cbw_out)
    cbw_out[0:TAPS] = cbw_ref[...]
    cbw_out[TAPS : TAPS + 1] = cbb_ref[...]

    length = place.length
    lane = iota2((8, length), 1)
    flag = lambda condition: jnp.where(condition, 1.0, 0.0)[0:1]
    for seq in range(aux_ref.shape[0]):
        seg = jnp.broadcast_to(seg_ref[seq : seq + 1], (8, length))
        aux_ref[seq] = jnp.zeros((AUX, length), F32)
        aux_ref[seq, 0:1] = seg[0:1].astype(F32)
        aux_ref[seq, 1:2] = pad_ref[seq : seq + 1].astype(F32)
        for k in range(1, TAPS):
            aux_ref[seq, 1 + k : 2 + k] = flag((pltpu.roll(seg, k, 1) == seg) & (lane >= k))
            aux_ref[seq, 7 + k : 8 + k] = flag((pltpu.roll(seg, length - k, 1) == seg) & (lane < length - k))
        before = jnp.full((8, CHUNK), -1, jnp.int32)
        for chunk in range(length // CHUNK):
            cut = slice(chunk * CHUNK, (chunk + 1) * CHUNK)
            block = seg[:, cut]
            tail = jnp.broadcast_to(block[:, CHUNK - 1 : CHUNK], (8, CHUNK))
            aux_ref[seq, 5:6, cut] = flag(block == before)
            aux_ref[seq, 6:7, cut] = flag(block == tail)
            before = tail

    for hop in range(1, place.first):
        for gather in gathers:
            gather.along(hop)
        side.cross() if hop == 1 else side.along(hop - 1)
        for gather in gathers:
            gather.across(hop - 1)
    side.along(place.first - 1) if place.first > 1 else side.cross()
    for gather in gathers:
        gather.across(place.first - 1)
    for gather in gathers:
        gather.finish()
    side.finish()
    swap.finish() if place.pair else copy.wait()


def finish_sums(total, inner_all):
    lines = lax.broadcasted_iota(jnp.int32, total.shape, 1)
    rms = lax.rsqrt(total[:, 0:1] / inner_all + epsilon)
    pull = rms * rms * rms * (total[:, 1:2] / inner_all)
    return jnp.where(lines == 0, rms, jnp.where(lines == 1, pull, 0.0))


def reduce_kernel(
    place, tok_hbm, ge_hbm, flat_ref, gain_ref, back_ref, w_hbm, hidden_hbm, cot_hbm, keep_hbm, away_hbm,
    own_ref, sum_ref, gh_hbm, output_hbm,
    gh_ref, output_ref, tok_ref, ge_ref, w_ref, hidden_ref, cot_ref, keep_ref, away_ref, dg_ref, dg_send, dg_buf,
    part_buf, core_buf, x_buf, z_buf, acc, bc_buf, bc_send, y_flat, core_flat, x_flat, z_flat, stage,
    core_send, core_recv, x_send, x_recv, z_send, z_recv, flat_send, flat_recv, dg_sem, load_sem, first_sem, leave_sem,
):
    spot = Spot(place)
    a, b, c, me, index = spot.a, spot.b, spot.c, spot.me, spot.index
    first, second = place.first, place.second
    scatter = LineScatter(
        spot, part_buf if place.pair else ge_ref, core_buf, x_buf, z_buf, own_ref,
        core_send, core_recv, x_send, x_recv, z_send, z_recv, PIECES,
    )
    ahead = [
        pltpu.make_async_copy(ge_hbm, ge_ref, first_sem.at[0]), pltpu.make_async_copy(tok_hbm, tok_ref, first_sem.at[1])
    ]
    for load in ahead:
        load.start()
    loads = []
    if place.pair:
        pairs = ((w_hbm, w_ref), (hidden_hbm, hidden_ref), (cot_hbm, cot_ref), (keep_hbm, keep_ref), (away_hbm, away_ref))
        for k, (far, near) in enumerate(pairs):
            loads.append(pltpu.make_async_copy(far, near, load_sem.at[k]))
        loads[0].start()
    spot.greet(place.pair)
    for load in ahead:
        load.wait()
    started = []

    def send(*args):
        copy = spot.copy(*args)
        copy.start()
        started.append(copy)

    def terms(there):
        if place.pair:
            part_buf[there] = lax.dot_general(
                tok_ref[:, there], ge_ref[...], (((0,), (0,)), ((), ())), preferred_element_type=F32
            ).astype(BF)

    stage[0] = flat_ref[...]
    here = hidden_ref.shape[1]

    def token_gradient(side, to):
        for seq in range(hidden_ref.shape[0]):
            rows = pl.ds(pl.multiple_of(seq * place.length + side * here, here), here)
            for cut in range(w_ref.shape[0] // 256):
                cols = slice(256 * cut, 256 * cut + 256)
                dg = dot_nt(ge_ref[rows], w_ref[cols])
                to[seq, :, cols] = dg.astype(BF)
                stage[0, 5:6, cols] += jnp.sum(dg * tok_ref[rows, cols].astype(F32), axis=0, keepdims=True)

    far = [(n, j) for j in range(1, second) for n in range(first)]
    near = [(n, 0) for n in range(first)]
    for k, (n, j) in enumerate(far + near[:1]):
        terms(scatter.terms(n, j))
        scatter.give(n, j)
        if 1 <= k <= len(far):
            scatter.cross_over(*far[k - 1])
    if place.pair:
        loads[0].wait()
        for load in loads[1:]:
            load.start()
        token_gradient(1 - me, dg_send)
        send(dg_send, dg_buf, dg_sem.at[0], dg_sem.at[1], index, 1 - me)
    for n, j in near[1:]:
        terms(scatter.terms(n, j))
        scatter.give(n, j)
    scatter.chain(acc, range(1))
    if place.pair:
        token_gradient(me, dg_ref)

    z_flat[a] = stage[0]
    for i in range(1, first):
        send(
            stage.at[0], z_flat.at[a], flat_send.at[second + i], flat_recv.at[2 + second + a],
            spot.at(spot.around(i), b, c),
        )
    scatter.chain(acc, range(1, min(2, first)))
    for i in range(1, first):
        spot.arrived(z_flat.at[spot.around(i)], flat_recv.at[2 + second + spot.around(i)])
    total = z_flat[0]
    for i in range(1, first):
        total = total + z_flat[i]
    stage[1] = total
    x_flat[b] = total
    for j in range(1, second):
        send(stage.at[1], x_flat.at[b], flat_send.at[1 + j], flat_recv.at[2 + b], spot.at(a, spot.aside(j), c))
    scatter.chain(acc, range(2, first))
    for j in range(1, second):
        spot.arrived(x_flat.at[spot.aside(j)], flat_recv.at[2 + spot.aside(j)])
    total = x_flat[0]
    for j in range(1, second):
        total = total + x_flat[j]
    stage[2] = total
    send(stage.at[2], core_flat, flat_send.at[1], flat_recv.at[1], spot.sibling)

    if place.pair:
        for load in loads[1:]:
            load.wait()
        spot.arrived(dg_buf, dg_sem.at[1])
        size = 128

        def token_rows(step, carry):
            seq, cut = lax.div(step, here // size), lax.rem(step, here // size)
            mine = pl.ds(pl.multiple_of(cut * size, size), size)
            full = pl.ds(pl.multiple_of(me * here + cut * size, size), size)
            hid = hidden_ref[seq, mine].astype(F32)
            inv = lax.rsqrt(jnp.mean(hid * hid, axis=-1, keepdims=True) + epsilon)
            gain = (dg_ref[seq, mine].astype(F32) + dg_buf[seq, mine].astype(F32)) * gain_ref[...]
            pull = inv * inv * inv * jnp.mean(hid * gain, axis=-1, keepdims=True)
            gh_ref[seq, mine] = (cot_ref[seq, mine].astype(F32) + inv * gain - hid * pull).astype(BF)
            rms = compact([back_ref[seq, :, full]])[:, 0:1]
            mixed = keep_ref[seq, mine].astype(F32) + away_ref[seq, mine].astype(F32)
            output_ref[seq, mine] = (hid + rms * mixed).astype(BF)
            return carry

        lax.fori_loop(0, hidden_ref.shape[0] * (here // size), token_rows, 0)
    else:
        gh_ref[...] = jnp.zeros_like(gh_ref)
        output_ref[...] = jnp.zeros_like(output_ref)
    leaving = [
        pltpu.make_async_copy(gh_ref, gh_hbm, leave_sem.at[0]),
        pltpu.make_async_copy(output_ref, output_hbm, leave_sem.at[1]),
    ]
    for copy in leaving:
        copy.start()

    spot.arrived(core_flat, flat_recv.at[1])
    total = stage[2] + core_flat[...]
    sum_ref[...] = total
    if place.pair:
        stage[3, 0:8] = total[0:8]
        send(stage.at[3, 0:8], y_flat, flat_send.at[0], flat_recv.at[0], index, 1 - me)
    scatter.finish_chain()
    if place.pair:
        edge = own_ref.shape[1] - 128 - 2 * STATE
        bc_send[...] = own_ref[:, edge : edge + 2 * STATE]
        send(bc_send, bc_buf, dg_sem.at[2], dg_sem.at[3], index, 1 - me)
    scatter.wait_sends()
    if place.pair:
        spot.arrived(y_flat, flat_recv.at[0])
        sum_ref[0:8] = stage[3, 0:8] + y_flat[...]
        spot.arrived(bc_buf, dg_sem.at[3])
        own_ref[:, edge : edge + 2 * STATE] = bc_send[...] + bc_buf[...]
    for copy in started:
        copy.wait_send()
    for copy in leaving:
        copy.wait()


def last_kernel(
    heads, own_ref, sum_ref, gh_in, output_in, out_rows, gain_ref,
    output_ref, gh_ref, pre_ref, zx_ref, bc_ref, step_ref, cxw_ref, cxb_ref, cbw_ref, cbb_ref, bias_ref, decay_ref,
    skip_ref, ngain_ref, out_ref,
):
    inner = heads * HEADDIM
    wide = 2 * inner
    rows = own_ref.shape[0]
    output_ref[...] = output_in[...]
    gh_ref[...] = gh_in[...]
    pre_ref[...] = sum_ref[5:6] / gain_ref[...]
    zx_ref[...] = own_ref[:, 0:wide]
    bc_ref[...] = own_ref[:, wide : wide + 2 * STATE]
    steps = own_ref[:, wide + 2 * STATE :]
    if rows < 128:
        steps = jnp.concatenate([steps, jnp.zeros((128 - rows, 128), F32)], axis=0)
    step_ref[...] = steps.T[0:heads, 0:rows]
    cxw_ref[...] = sum_ref[8 : 8 + TAPS, 0:inner]
    cxb_ref[...] = sum_ref[8 + TAPS : 9 + TAPS, 0:inner]
    cbw_ref[...] = sum_ref[0:TAPS, 0 : 2 * STATE]
    cbb_ref[...] = sum_ref[TAPS : TAPS + 1, 0 : 2 * STATE]
    skip = exact_dot(jnp.broadcast_to(sum_ref[13:14, 0:inner], (16, inner)), collector(inner, 0))
    bias_ref[...] = sum_ref[15:16, 0:heads]
    decay_ref[...] = sum_ref[15:16, 128 : 128 + heads]
    skip_ref[...] = skip[0:1, 0:heads]
    ngain_ref[...] = sum_ref[14:15, 0:inner]
    out_ref[...] = out_rows[...]


SDS = jax.ShapeDtypeStruct
DMA = pltpu.SemaphoreType.DMA
ANY = pl.BlockSpec(memory_space=pl.ANY)
WHOLE = pl.BlockSpec(memory_space=pltpu.VMEM)


def params(collective=None):
    if collective is None:
        return pltpu.CompilerParams(vmem_limit_bytes=VMEM_LIMIT)
    return pltpu.CompilerParams(vmem_limit_bytes=VMEM_LIMIT, collective_id=collective, has_side_effects=True)


def whole_once(*shape):
    return pl.BlockSpec(shape, lambda s, c: (0,) * len(shape), pipeline_mode=pl.Buffered(1))


def line_sems(place, cuts, lines):
    columns = place.first * max(place.second - 1, 1) * cuts
    blocks = place.first * place.second * cuts
    return [DMA((blocks,)), DMA((blocks,)), DMA((columns,)), DMA((columns,)), DMA((place.first * cuts,)), DMA((lines,))]


def gather_all(place, size, zx, bc, step_t, hidden, gain, cxw, cxb, cbw, cbb, bias, decay, skip, ngain, seg, pad):
    seqs, here, width = hidden.shape
    heads, inner = bias.shape[1], cxw.shape[1]
    total = 2 * inner + 2 * STATE + 128
    rows = zx.shape[0]
    return pl.pallas_call(
        functools.partial(gather_kernel, place, heads),
        in_specs=[WHOLE] * 15,
        out_specs=[ANY, ANY] + [WHOLE] * 4,
        out_shape=[
            SDS((size * rows, total), BF), SDS((seqs, place.length if place.pair else here, width), BF),
            SDS((seqs, AUX, place.length), F32), SDS((8, inner), F32), SDS((8, 2 * STATE), F32), SDS((2, heads, 128), F32),
        ],
        scratch_shapes=[
            pltpu.VMEM((rows, total), BF), pltpu.VMEM(hidden.shape, BF), pltpu.VMEM((128, 128), F32),
            DMA((PIECES, 1, gather_sites(place.first, place.second))), DMA((PIECES, 1, size)), DMA((PIECES, 1)),
            DMA((1, row_sites(place.first, place.second))), DMA((1, size)), DMA((1,)), DMA((3,)),
        ],
        compiler_params=params(0),
        name="gather_all",
    )(zx, bc, step_t, hidden, gain, cxw, cxb, cbw, cbb, bias, decay, skip, ngain, seg, pad)


def mixer_forward(place, size, tok, weights, aux, cw, cbw, hp, cot_own, out_own):
    seqs, length, width = tok.shape
    heads, inner = hp.shape[1], cw.shape[1]
    wide = 2 * inner + 2 * STATE
    chunks = length // CHUNK
    token = lambda size: pl.BlockSpec((1, BLOCK, size), lambda s, c: (s, c, 0))
    row = lambda high: pl.BlockSpec((1, high, BLOCK), lambda s, c: (s, 0, c))
    return pl.pallas_call(
        functools.partial(forward_kernel, place, heads),
        grid=(seqs, length // BLOCK),
        in_specs=[
            token(width), ANY, row(AUX),
            whole_once(8, inner), whole_once(8, 2 * STATE), whole_once(2, heads, 128), WHOLE, ANY,
        ],
        out_specs=[
            token(wide), row(heads), token(inner), token(inner), token(inner), token(inner), token(2 * STATE),
            token(2 * STATE), pl.BlockSpec((1, BLOCK // CHUNK, STATE, inner), lambda s, c: (s, c, 0, 0)), row(8),
            ANY, ANY,
        ],
        out_shape=[
            SDS((seqs, length, wide), BF), SDS((seqs, heads, length), F32),
            SDS((seqs, length, inner), BF), SDS((seqs, length, inner), BF), SDS((seqs, length, inner), BF),
            SDS((seqs, length, inner), BF), SDS((seqs, length, 2 * STATE), BF), SDS((seqs, length, 2 * STATE), BF),
            SDS((seqs, chunks, STATE, inner), BF), SDS((seqs, 8, length), F32),
            SDS((size * out_own.shape[0], inner), BF), SDS((seqs, length, width) if place.pair else (8, 128), BF),
        ],
        scratch_shapes=[
            pltpu.VMEM((STATE, inner), F32), pltpu.VMEM((HALO + CHUNK, inner), F32),
            pltpu.VMEM((HALO + CHUNK, 2 * STATE), F32), pltpu.VMEM((CHUNK, inner), BF),
            pltpu.VMEM((CHUNK, inner), F32), pltpu.VMEM((3, 256, inner), BF), pltpu.VMEM((CHUNK, CHUNK), BF),
            pltpu.VMEM(weights.shape, BF),
            DMA((1, gather_sites(place.first, place.second))), DMA((1, size)), DMA((1,)), DMA((3,)), DMA,
        ],
        compiler_params=params(1),
        name="mixer_forward",
    )(tok, weights, aux, cw, cbw, hp, cot_own, out_own)


def mixer_backward(
    place, size, inner_all, pz, raw, aux, mixed, cv, pre, cbc, pbc, st, stat, cw, cbw, hp, g, out_all, gn, cot
):
    seqs, length, inner = mixed.shape
    width, wide = out_all.shape[0], pz.shape[2] + 128
    heads = hp.shape[1]
    last = length // BLOCK - 1
    pair = place.pair
    here = length // 2 if pair else 16
    rows = width // size
    tokens = seqs * length
    token = lambda size: pl.BlockSpec((1, BLOCK, size), lambda s, c: (s, last - c, 0))
    row = lambda high: pl.BlockSpec((1, high, BLOCK), lambda s, c: (s, 0, last - c))
    fixed = lambda *shape: pl.BlockSpec(shape, lambda s, c: (0,) * len(shape))
    if pair:
        g = cbw
        gn_all, cot_all = gn.reshape(-1, inner), cot.reshape(-1, width)
    else:
        gn_all, cot_all, out_all = gn[0, :16, :128], cot[0, :16, :128], out_all[:16, :128]
    blocks = place.first * place.second
    columns = place.first * max(place.second - 1, 1)
    tile = lambda *shape: pltpu.VMEM(shape if pair else (1,) * (len(shape) - 2) + (16, 128), BF)
    rowed = pltpu.VMEM((seqs, 8, length), F32)
    return pl.pallas_call(
        functools.partial(backward_kernel, place, heads, inner_all),
        grid=(seqs, length // BLOCK),
        in_specs=[
            token(pz.shape[2]), row(heads), row(AUX), token(inner), token(inner),
            token(inner), token(2 * STATE), token(2 * STATE),
            pl.BlockSpec((1, BLOCK // CHUNK, STATE, inner), lambda s, c: (s, last - c, 0, 0)), whole_once(*stat.shape),
            whole_once(8, inner), whole_once(8, 2 * STATE), whole_once(2, heads, 128),
            whole_once(*g.shape) if pair else token(inner),
            ANY, ANY, ANY,
        ],
        out_specs=[token(wide), fixed(16, width), ANY, ANY, fixed(seqs, 8, length), fixed(rows, inner)],
        out_shape=[
            SDS((seqs, length, wide), BF), SDS((16, width), F32), SDS((seqs, here, width), BF),
            SDS((seqs, here, width), BF), SDS((seqs, 8, length), F32), SDS((rows, inner), F32),
        ],
        scratch_shapes=[
            pltpu.VMEM((STATE, inner), F32), pltpu.VMEM((CHUNK + HALO, inner), F32),
            pltpu.VMEM((CHUNK + HALO, 2 * STATE), F32), pltpu.VMEM((CHUNK, inner), BF),
            pltpu.VMEM((CHUNK, inner), BF), pltpu.VMEM((CHUNK, inner), BF), pltpu.VMEM((CHUNK, inner), BF),
            pltpu.VMEM((CHUNK, inner), F32),
            pltpu.VMEM((3, 256, inner), BF), pltpu.VMEM((2, inner, 128), BF),
            pltpu.VMEM((CHUNK, CHUNK), BF), pltpu.VMEM((CHUNK, CHUNK), BF), pltpu.VMEM((2, heads, 128), F32),
            tile(seqs, length, width), tile(tokens, inner), pltpu.VMEM((tokens, 128), F32), rowed, rowed,
            tile(tokens, inner), tile(width, inner),
            tile(blocks, rows, inner), tile(columns, rows, inner), tile(place.first, rows, inner),
        ] + line_sems(place, 1, place.first) + [DMA((3,)), DMA((2,))] + [
            pltpu.VMEM(out_all.shape, BF), pltpu.VMEM(gn_all.shape, BF), pltpu.VMEM(cot_all.shape, BF), DMA((3,)),
        ],
        compiler_params=params(3 if pair else None),
        name="mixer_backward",
    )(
        pz, raw, aux, mixed, cv, pre, cbc, pbc, st, stat, cw, cbw, hp, g, out_all, gn_all, cot_all,
    )


def reduce_all(place, size, tok, ge, flat, gain, back, weights, hidden, cot_own, y_keep, y_away):
    seqs, length, depth = tok.shape
    width = ge.shape[2]
    rows = depth // size
    pair = place.pair
    if pair:
        tok, ge = tok.reshape(seqs * length, depth), ge.reshape(seqs * length, width)
    else:
        ge = jnp.einsum("stp,sty->py", tok, ge, preferred_element_type=F32).astype(BF)
        tok, weights = tok[0, :16], weights[:16, :128]
        flat = jnp.concatenate([lax.psum(flat[:8], "tensor"), flat[8:]])
        hidden, cot_own, y_keep, y_away = [jnp.zeros((1, 16, depth), BF)] * 4
        back = back[:1, :, :128]
    blocks = place.first * place.second * PIECES
    columns = place.first * max(place.second - 1, 1) * PIECES
    lines = 2 * place.first * PIECES
    cut = rows // PIECES
    tokens = pltpu.VMEM(hidden.shape, BF)
    small = pltpu.VMEM((rows, 2 * STATE), F32)
    own, flat, gh, output = pl.pallas_call(
        functools.partial(reduce_kernel, place),
        in_specs=[ANY] * 2 + [WHOLE] * 3 + [ANY] * 5,
        out_specs=[WHOLE] * 2 + [ANY] * 2,
        out_shape=[SDS((rows, width), F32), SDS(flat.shape, F32), SDS(hidden.shape, BF), SDS(hidden.shape, BF)],
        scratch_shapes=[
            tokens, tokens, pltpu.VMEM(tok.shape, BF), pltpu.VMEM(ge.shape, BF), pltpu.VMEM(weights.shape, BF), tokens, tokens, tokens, tokens, tokens, tokens, tokens,
            pltpu.VMEM((depth, width) if pair else (16, 128), BF),
            pltpu.VMEM((blocks, cut, width), BF),
            pltpu.VMEM((columns, cut, width), BF),
            pltpu.VMEM((lines, cut, width), BF),
            pltpu.VMEM((cut, width), F32),
            small, small,
            pltpu.VMEM((8, flat.shape[1]), F32),
            pltpu.VMEM(flat.shape, F32),
            pltpu.VMEM((place.second,) + flat.shape, F32),
            pltpu.VMEM((place.first,) + flat.shape, F32),
            pltpu.VMEM((4,) + flat.shape, F32),
        ] + line_sems(place, PIECES, lines) + [
            DMA((1 + place.first + place.second,)), DMA((2 + place.first + place.second,)), DMA((4,)), DMA((5,)), DMA((2,)), DMA((2,)),
        ],
        compiler_params=params(4),
        name="reduce_all",
    )(tok, ge, flat, gain, back, weights, hidden, cot_own, y_keep, y_away)
    if not pair:
        edge = width - 128 - 2 * STATE
        own = own.at[:, edge : edge + 2 * STATE].set(lax.psum(own[:, edge : edge + 2 * STATE], "tensor"))
    return own, flat, gh, output


def body(
    hidden, pre_gain, zx_weight, bc_weight, step_weight, conv_x_weight, conv_x_bias, conv_bc_weight, conv_bc_bias,
    step_bias, decay_log, skip_gain, norm_gain, out_weight, segment_ids, pad_mask, grad_out,
):
    n, size = lax.axis_size("tensor"), lax.axis_size("dp")
    heads = step_weight.shape[1]
    inner = heads * HEADDIM
    seqs, here, width = hidden.shape
    length = segment_ids.shape[1]
    first, second = factors(size)
    place = Place(first, second, n == 2 and (2 * width // size) % 128 == 0, seqs * length // BLOCK, length)
    line = lambda vector: vector.reshape(1, -1)
    gain = line(pre_gain)

    weights, tok, aux, cw, cbw, hp = gather_all(
        place, size, zx_weight, bc_weight, step_weight.T, hidden, gain, conv_x_weight, line(conv_x_bias),
        conv_bc_weight, line(conv_bc_bias), line(step_bias), line(decay_log), line(skip_gain), line(norm_gain),
        segment_ids, pad_mask,
    )
    if not place.pair:
        tok = lax.all_gather(tok, "tensor", axis=1, tiled=True)
    pz, raw, mixed, gn, cv, pre, cbc, pbc, st, stat, out_all, cot = mixer_forward(
        place, size, tok, weights, aux, cw, cbw, hp, grad_out, out_weight.T
    )
    if not place.pair:
        cot = lax.all_gather(grad_out, "tensor", axis=1, tiled=True)
    g = y = None
    if not place.pair:
        y = jnp.einsum("stc,rc->str", gn, out_all, preferred_element_type=F32)
        cross = jnp.sum(y * cot.astype(F32), axis=-1)
        stat = finish_sums(lax.psum(stat.at[:, 1].set(cross), "tensor"), inner * n)
        g = jnp.einsum("str,rc->stc", cot, out_all, preferred_element_type=F32).astype(BF)
    ge, flat, y_keep, y_away, back, out_rows = mixer_backward(
        place, size, inner * n, pz, raw, aux, mixed, cv, pre, cbc, pbc, st, stat, cw, cbw, hp, g, out_all, gn, cot
    )
    if not place.pair:
        normed_out = (gn.astype(F32) * back[:, 0, :, None]).astype(BF)
        terms = jnp.einsum("str,stc->rc", cot, normed_out, preferred_element_type=F32).astype(BF)
        out_rows = lax.psum_scatter(terms, "dp", scatter_dimension=0, tiled=True).astype(F32)
        dg = jnp.einsum("sty,py->stp", ge, weights, preferred_element_type=F32)
        flat = flat.at[5].add(jnp.sum(dg * tok.astype(F32), axis=(0, 1)))
    own, sums, grad_hidden, output = reduce_all(
        place, size, tok, ge, flat, gain, back, weights, hidden, grad_out, y_keep, y_away
    )
    if not place.pair:
        hidden_f = hidden.astype(F32)
        inv_rms = lax.rsqrt(jnp.mean(hidden_f * hidden_f, axis=-1, keepdims=True) + epsilon)
        scatter = lambda rows: lax.psum_scatter(rows, "tensor", scatter_dimension=1, tiled=True)
        gain_grad = scatter(dg) * pre_gain
        pull = inv_rms**3 * jnp.mean(hidden_f * gain_grad, axis=-1, keepdims=True)
        grad_hidden = (grad_out.astype(F32) + inv_rms * gain_grad - hidden_f * pull).astype(BF)
        output = (hidden_f + scatter(y * back[:, 0, :, None])).astype(BF)
    rows = own.shape[0]
    output, grad_hidden, grad_pre, gzx, gbc, gstep, gcxw, gcxb, gcbw, gcbb, gbias, gdecay, gskip, gnorm, gout = pl.pallas_call(
        functools.partial(last_kernel, heads),
        in_specs=[WHOLE] * 6,
        out_specs=[WHOLE] * 15,
        out_shape=[
            SDS(hidden.shape, BF), SDS(hidden.shape, BF), SDS((1, width), F32), SDS((rows, 2 * inner), F32),
            SDS((rows, 2 * STATE), F32), SDS((heads, rows), F32), SDS((TAPS, inner), F32), SDS((1, inner), F32),
            SDS((TAPS, 2 * STATE), F32), SDS((1, 2 * STATE), F32), SDS((1, heads), F32), SDS((1, heads), F32),
            SDS((1, heads), F32), SDS((1, inner), F32), SDS((rows, inner), F32),
        ],
        compiler_params=params(),
        name="outputs",
    )(own, sums, grad_hidden, output, out_rows, gain)
    return (
        output, grad_hidden, grad_pre[0], gzx, gbc, gstep.T, gcxw, gcxb[0], gcbw, gcbb[0], gbias[0], gdecay[0],
        gskip[0], gnorm[0], gout.T,
    )


def solution(mesh):
    placed = (
        P("dp", "tensor", None), P(), P("dp", "tensor"), P("dp", None), P("dp", "tensor"), P(None, "tensor"),
        P("tensor"), P(), P(), P("tensor"), P("tensor"), P("tensor"), P("tensor"), P("tensor", "dp"),
        P("dp", None), P("dp", None), P("dp", "tensor", None),
    )
    return jax.shard_map(
        body,
        mesh=mesh,
        in_specs=placed,
        out_specs=(
            P("dp", "tensor", None), P("dp", "tensor", None), P(), P("dp", "tensor"), P("dp", None), P("dp", "tensor"),
            P(None, "tensor"), P("tensor"), P(), P(), P("tensor"), P("tensor"), P("tensor"), P("tensor"),
            P("tensor", "dp"),
        ),
        check_vma=False,
    )
```
